32 devices in a mesh: section: 2 (over x), dp: 16 (over z, y, core).
Axes of the slice: x: 2, y: 2, z: 4, core: 2. Of those that a mesh axis runs over, the one named last changes fastest.
Arguments:
- block_input: bfloat16 [2, 16, 96, 768], P(None, 'dp'), may hold values from -6 to 6
- cotangent: bfloat16 [2, 16, 96, 768], P(None, 'dp'), may hold values from -8 to 8
- lengths: int32 [2, 16], P(None, 'dp'), may hold values from 1 to 96, 1152 in all within a row
- leads: int32 [2, 16], P(None, 'dp'), may hold values from 0 to 23
- norm_gain1: float32 [2, 768], P('section', 'dp'), may hold values from 0.25 to 1.75
- norm_bias1: float32 [2, 768], P('section', 'dp'), may hold values from -1.75 to 1.75
- lead_table: float32 [2, 768, 24], P('section', 'dp'), may hold values from -3 to 3
- qkv_weight: float32 [2, 768, 2304], P('section', 'dp'), may hold values from -0.21875 to 0.21875
- query_bias: float32 [2, 768], P('section', 'dp'), may hold values from -1.75 to 1.75
- value_bias: float32 [2, 768], P('section', 'dp'), may hold values from -1.75 to 1.75
- out_weight: float32 [2, 768, 768], P('section', 'dp'), may hold values from -0.875 to 0.875
- out_bias: float32 [2, 768], P('section', 'dp'), may hold values from -1.75 to 1.75
- norm_gain2: float32 [2, 768], P('section', 'dp'), may hold values from 0.25 to 1.75
- norm_bias2: float32 [2, 768], P('section', 'dp'), may hold values from -1.75 to 1.75
- up_weight: float32 [2, 768, 3072], P('section', 'dp'), may hold values from -0.21875 to 0.21875
- up_bias: float32 [2, 3072], P('section', 'dp'), may hold values from -1.75 to 1.75
- down_weight: float32 [2, 3072, 768], P('section', 'dp'), may hold values from -0.109375 to 0.109375
- down_bias: float32 [2, 768], P('section', 'dp'), may hold values from -1.75 to 1.75
Outputs:
- activations: bfloat16 [2, 2, 16, 96, 768], P('section', None, 'dp')
- input_grads: float32 [2, 2, 16, 96, 768], P('section', None, 'dp')
- grad_norm_gain1: float32 [2, 768], P('section', 'dp')
- grad_norm_bias1: float32 [2, 768], P('section', 'dp')
- grad_lead_table: float32 [2, 768, 24], P('section', 'dp')
- grad_qkv_weight: float32 [2, 768, 2304], P('section', 'dp')
- grad_query_bias: float32 [2, 768], P('section', 'dp')
- grad_value_bias: float32 [2, 768], P('section', 'dp')
- grad_out_weight: float32 [2, 768, 768], P('section', 'dp')
- grad_out_bias: float32 [2, 768], P('section', 'dp')
- grad_norm_gain2: float32 [2, 768], P('section', 'dp')
- grad_norm_bias2: float32 [2, 768], P('section', 'dp')
- grad_up_weight: float32 [2, 768, 3072], P('section', 'dp')
- grad_up_bias: float32 [2, 3072], P('section', 'dp')
- grad_down_weight: float32 [2, 3072, 768], P('section', 'dp')
- grad_down_bias: float32 [2, 768], P('section', 'dp')
The draws below stay inside these ranges and needn't reach their ends.
Inputs may be any that keep to these rules, and one draw needn't show every extreme that they name: In each micro-batch the lengths of the 16 items sum to 1152 and the longest is 96.
All inputs are finite; a program needn't handle non-finite values. No bound on the sum of `lengths` on one device may be relied on, other than what follows from the above.
Results may differ from the reference program's by a relative error of at most 0.013.
The reference program's roundings to bfloat16 on the way count: a program that leaves them out, or rounds other values in their place, can miss the bound.
Values may be sent and summed in bfloat16 or wider, within the bound.
No kernel may reach another device: no remote copies, remote signals or barrier semaphores. Data moves between devices by JAX's collectives and lax.ppermute only.
A program may use at most 128 MiB of HBM per device.

```python
import math
import jax
import jax.numpy as jnp
import numpy as np
from jax import lax

D = 768
HEADS = 12
HEAD = 64
FF = 3072
LEADS = 24
LEN = 96
MICRO = 2
ITEMS = 16
LAYERS = 2


def set_ends(drawn, key, least, top_value):
    place = [jax.random.randint(jax.random.fold_in(key, axis), (), 0, length) for axis, length in enumerate(drawn.shape)]
    widest = drawn.shape.index(max(drawn.shape))
    next_to = place[:widest] + [(place[widest] + 1) % drawn.shape[widest]] + place[widest + 1:]
    return drawn.at[tuple(place)].set(least).at[tuple(next_to)].set(top_value)


def raised(drawn, rng, source, target, shards_of, factor):
    def block_of(dim):
        return (jnp.arange(drawn.shape[dim]) // (drawn.shape[dim] // shards_of)).reshape((-1,) + (1,) * (drawn.ndim - 1 - dim))

    one_side = jax.random.permutation(rng, shards_of)[block_of(target)]
    other_side = (block_of(target) + shards_of // 2) % shards_of
    return jnp.where((block_of(source) == one_side) | (block_of(source) == other_side), factor * drawn, drawn)


def levels(rng, extent, cuts, least, high):
    level = 1.0
    for dim, shards_of in cuts:
        draws = jax.random.uniform(jax.random.fold_in(jax.random.fold_in(rng, 6), dim), (shards_of,), jnp.float32, least / len(cuts), high / len(cuts))
        level = level * jnp.repeat(jnp.exp(draws), extent[dim] // shards_of).reshape((-1,) + (1,) * (len(extent) - 1 - dim))
    return level


def split_up(count, total, most, skew):
    weights = [(1 << 20) // math.isqrt(rank ** skew) + 1 for rank in range(2, count + 1)]
    spare, holding = total - most - (count - 1), [1] * (count - 1)
    while spare > 0:
        candidates = [i for i in range(count - 1) if holding[i] < most]
        whole, remaining = sum([weights[i] for i in candidates]), spare
        for i in candidates:
            more = min(most - holding[i], max(1, remaining * weights[i] // whole), spare)
            holding[i] = holding[i] + more
            spare = spare - more
    return np.array([most] + holding)


def uneven_parts(rng, count, total, bound, lean):
    if count == 2:
        one = jax.random.randint(rng, (), max(1, total - bound), min(bound, total - 1) + 1)
        return jnp.stack([one, total - one])
    sizes = jnp.asarray(split_up(count, total, bound, lean), jnp.int32)
    twos = (count - 1) // 2
    giver, receiver = sizes[1:1 + 2 * twos:2], sizes[2:2 + 2 * twos:2]
    slack = jnp.minimum(giver - 1, bound - receiver)
    shifted = jax.random.randint(jax.random.fold_in(rng, 1), (twos,), 0, 1 << 20) % (slack + 1)
    sizes = sizes.at[1:1 + 2 * twos:2].set(giver - shifted).at[2:2 + 2 * twos:2].set(receiver + shifted)
    return sizes[jax.random.permutation(jax.random.fold_in(rng, 2), count)]


def scatter_about(rng, extent, scale, limit, cuts=(), kind=jnp.bfloat16):
    array = jax.random.normal(rng, extent, jnp.float32) * scale
    if len(cuts) > 0:
        array = levels(rng, extent, cuts, -0.22, 0.18) * array
    return jnp.clip(array, min=-limit, max=limit).astype(kind)


def noise_with(rng, dims, spread, reach, cuts, heavy, held_as=jnp.bfloat16):
    array = spread * jax.random.normal(rng, dims, jnp.float32)
    if cuts:
        array = array * levels(rng, dims, cuts, -0.22, 0.18)
    return jnp.clip(raised(array, jax.random.fold_in(rng, 3), *heavy), -reach, reach).astype(held_as)


def setup_inputs(seed: int = 0) -> dict:
    arg_keys = jax.random.split(jax.random.key(seed), 19)
    block_input = scatter_about(arg_keys[0], (MICRO, ITEMS, LEN, D), 1.0, 6.0, ((1, 16),))
    cotangent = noise_with(arg_keys[1], (MICRO, ITEMS, LEN, D), 1.0, 8.0, ((1, 16),), (1, 3, 16, 2.0))
    lengths = jax.vmap(lambda own: uneven_parts(own, ITEMS, ITEMS * LEN * 3 // 4, LEN, 2))(jax.random.split(arg_keys[2], MICRO)).reshape((MICRO, ITEMS)).astype(jnp.int32)
    leads = set_ends(jax.random.randint(arg_keys[3], (MICRO, ITEMS), 0, LEADS), jax.random.fold_in(arg_keys[3], 1), 0, LEADS - 1).astype(jnp.int32)
    norm_gain1 = jnp.clip(1.0 + 0.15 * jax.random.normal(arg_keys[4], (LAYERS, D), jnp.float32), 0.25, 1.75)
    norm_bias1 = scatter_about(arg_keys[5], (LAYERS, D), 0.3, 1.75, ((0, 2), (1, 16)), jnp.float32)
    lead_table = scatter_about(arg_keys[6], (LAYERS, D, LEADS), 0.5, 3.0, ((0, 2), (1, 16)), jnp.float32)
    qkv_weight = scatter_about(arg_keys[7], (LAYERS, D, 3 * D), D ** -0.5, 0.21875, ((0, 2), (1, 16)), jnp.float32)
    query_bias = scatter_about(arg_keys[8], (LAYERS, D), 0.3, 1.75, ((0, 2), (1, 16)), jnp.float32)
    value_bias = scatter_about(arg_keys[9], (LAYERS, D), 0.3, 1.75, ((0, 2), (1, 16)), jnp.float32)
    out_weight = scatter_about(arg_keys[10], (LAYERS, D, D), (D // 16) ** -0.5, 0.875, ((0, 2), (1, 16)), jnp.float32)
    out_bias = scatter_about(arg_keys[11], (LAYERS, D), 0.3, 1.75, ((0, 2), (1, 16)), jnp.float32)
    norm_gain2 = jnp.clip(1.0 + 0.15 * jax.random.normal(arg_keys[12], (LAYERS, D), jnp.float32), 0.25, 1.75)
    norm_bias2 = scatter_about(arg_keys[13], (LAYERS, D), 0.3, 1.75, ((0, 2), (1, 16)), jnp.float32)
    up_weight = scatter_about(arg_keys[14], (LAYERS, D, FF), D ** -0.5, 0.21875, ((0, 2), (1, 16)), jnp.float32)
    up_bias = scatter_about(arg_keys[15], (LAYERS, FF), 0.3, 1.75, ((0, 2), (1, 16)), jnp.float32)
    down_weight = scatter_about(arg_keys[16], (LAYERS, FF, D), FF ** -0.5, 0.109375, ((0, 2), (1, 16)), jnp.float32)
    down_bias = scatter_about(arg_keys[17], (LAYERS, D), 0.3, 1.75, ((0, 2), (1, 16)), jnp.float32)
    return dict(block_input=block_input, cotangent=cotangent, lengths=lengths, leads=leads, norm_gain1=norm_gain1, norm_bias1=norm_bias1, lead_table=lead_table, qkv_weight=qkv_weight, query_bias=query_bias, value_bias=value_bias, out_weight=out_weight, out_bias=out_bias, norm_gain2=norm_gain2, norm_bias2=norm_bias2, up_weight=up_weight, up_bias=up_bias, down_weight=down_weight, down_bias=down_bias)


EPS = 1e-06
SCALE_FACTOR = 0.125
HIGHEST = lax.Precision.HIGHEST

@jax.custom_vjp
def low(v):
    return lax.optimization_barrier(v.astype(jnp.bfloat16)).astype(jnp.float32)

@jax.custom_vjp
def low_back(v):
    return v

def low_keep(v):
    return (low(v), None)

def low_pass(kept, grad):
    return (grad,)

def back_keep(v):
    return (v, None)

def back_low(kept, grad):
    return (low(grad),)
low.defvjp(low_keep, low_pass)
low_back.defvjp(back_keep, back_low)

def layer_norm(values, gain, shift):
    mean = lax.optimization_barrier(jnp.mean(values, -1, keepdims=True))
    centred = values - mean
    variance = lax.optimization_barrier(jnp.mean(centred * centred, -1, keepdims=True))
    return centred * lax.rsqrt(variance + EPS) * gain + shift

def gelu_tanh(values):
    return 0.5 * values * (1.0 + jnp.tanh(0.7978845608028654 * (values + 0.044715 * values * values * values)))

def layer_group(weights, inputs, length, lead):
    gain_one, shift_one, lead_table, qkv_weight, query_bias, value_bias, out_weight, out_bias, gain_two, shift_two, up_weight, up_bias, down_weight, down_bias = weights
    group = inputs.shape[0]
    onehot = (jnp.arange(LEADS, dtype=jnp.int32)[None, :] == lead[:, None]).astype(jnp.float32)
    embedded = jnp.einsum('gl,dl->gd', onehot, lead_table, precision=HIGHEST)
    normed = low(layer_norm(inputs, gain_one, shift_one) + embedded[:, None, :])
    joined = jnp.einsum('gtd,de->gte', normed, qkv_weight, precision=HIGHEST)
    query = low(low_back(joined[..., :D] + query_bias)).reshape(group, LEN, HEADS, HEAD)
    key_rows = low(low_back(joined[..., D:2 * D])).reshape(group, LEN, HEADS, HEAD)
    value = low(low_back(joined[..., 2 * D:] + value_bias)).reshape(group, LEN, HEADS, HEAD)
    logits = low_back(jnp.einsum('gqhd,gkhd->ghqk', query, key_rows, precision=HIGHEST) * SCALE_FACTOR)
    valid_keys = jnp.arange(LEN, dtype=jnp.int32)[None, :] < length[:, None]
    logits = jnp.where(valid_keys[:, None, None, :], logits, -1000000000.0)
    top = lax.optimization_barrier(jnp.max(logits, -1, keepdims=True))
    expo = jnp.exp(logits - top)
    probs = expo / lax.optimization_barrier(jnp.sum(expo, -1, keepdims=True))
    mixed = jnp.einsum('ghqk,gkhd->gqhd', low(probs), value, precision=HIGHEST).reshape(group, LEN, D)
    attended = low(low_back(mixed))
    branch = low_back(jnp.einsum('gtd,de->gte', attended, out_weight, precision=HIGHEST) + out_bias)
    middle = inputs + branch
    hidden = low(layer_norm(middle, gain_two, shift_two))
    pre_act = low_back(jnp.einsum('gtd,df->gtf', hidden, up_weight, precision=HIGHEST) + up_bias)
    activated = low(gelu_tanh(pre_act))
    return middle + low_back(jnp.einsum('gtf,fd->gtd', activated, down_weight, precision=HIGHEST) + down_bias)

def reference(block_input, cotangent, lengths, leads, norm_gain1, norm_bias1, lead_table, qkv_weight, query_bias, value_bias, out_weight, out_bias, norm_gain2, norm_bias2, up_weight, up_bias, down_weight, down_bias):
    masters = (norm_gain1, norm_bias1, lead_table, qkv_weight, query_bias, value_bias, out_weight, out_bias, norm_gain2, norm_bias2, up_weight, up_bias, down_weight, down_bias)
    count = MICRO * ITEMS
    group = math.gcd(count, max(1, 4096 // LEN))
    batches = count // group
    length_groups = lengths.reshape(batches, group).astype(jnp.int32)
    lead_groups = leads.reshape(batches, group).astype(jnp.int32)
    inputs = block_input.astype(jnp.float32).reshape(count, LEN, D)
    extra = jnp.zeros((count, LEN, D), jnp.float32)

    def run_layer(weights, layer, values):
        rounded = tuple((low(weight[layer]) for weight in weights))

        def one_group(pieces):
            return layer_group(rounded, pieces[0], pieces[1], pieces[2])
        outputs = lax.map(jax.checkpoint(one_group), (values.reshape(batches, group, LEN, D), length_groups, lead_groups))
        return outputs.reshape(count, LEN, D)

    def forward(values, added, weights):
        first_out = run_layer(weights, 0, values)
        second_in = low(low_back(first_out)) + added
        second_out = run_layer(weights, 1, second_in)
        return (first_out, second_out)
    (first_out, second_out), backward = jax.vjp(forward, inputs, extra, masters)
    grad_in, grad_extra, grads = backward((jnp.zeros_like(first_out), cotangent.astype(jnp.float32).reshape(count, LEN, D)))
    shape_five = (MICRO, ITEMS, LEN, D)
    activations = jnp.stack([first_out.reshape(shape_five), second_out.reshape(shape_five)]).astype(jnp.bfloat16)
    input_grads = jnp.stack([grad_in.reshape(shape_five), grad_extra.reshape(shape_five)])
    return (activations, input_grads, grads[0], grads[1], grads[2], grads[3], grads[4], grads[5], grads[6], grads[7], grads[8], grads[9], grads[10], grads[11], grads[12], grads[13])
```

```python
import functools

import jax
import jax.numpy as jnp
from jax import lax
from jax.experimental import pallas as pl
from jax.experimental.pallas import tpu as pltpu
from jax.sharding import PartitionSpec as P

HEAD = 64
PAIR = 2 * HEAD
EPS = 1e-06
SCALE_FACTOR = 0.125
GELU_A = 0.7978845608028654
GELU_B = 0.044715
LIMIT = 60 * 1024 * 1024
F32 = jnp.float32
BF16 = jnp.bfloat16
BLOCKS = 12
QKV, OUT, UP, DOWN = (0, 3), (3, 1), (4, 4), (8, 4)


def mm(left, right):
    return jnp.dot(left, right, preferred_element_type=F32)


def mm_nt(left, right):
    return lax.dot_general(left, right, (((1,), (1,)), ((), ())), preferred_element_type=F32)


def mm_tn(left, right):
    return lax.dot_general(left, right, (((0,), (0,)), ((), ())), preferred_element_type=F32)


def normalised(values):
    mean = jnp.mean(values, -1, keepdims=True)
    centred = values - mean
    variance = jnp.mean(centred * centred, -1, keepdims=True)
    rstd = lax.rsqrt(variance + EPS)
    return centred * rstd, rstd


def norm_back(grad, xhat, rstd, gain):
    scaled = grad * gain
    first = jnp.mean(scaled, -1, keepdims=True)
    second = jnp.mean(scaled * xhat, -1, keepdims=True)
    return rstd * (scaled - first - xhat * second)


def gelu_both(values):
    square = values * values
    slope = GELU_A * (1.0 + 3.0 * GELU_B * square)
    bend = jnp.tanh(GELU_A * values * (1.0 + GELU_B * square))
    half = 0.5 * (1.0 + bend)
    return values * half, half + 0.5 * values * (1.0 - bend * bend) * slope


def split_pair(rows):
    lane = lax.broadcasted_iota(jnp.int32, rows.shape, 1)
    zero = jnp.zeros_like(rows)
    return jnp.concatenate(
        [jnp.where(lane < HEAD, rows, zero), jnp.where(lane < HEAD, zero, rows)], 0
    )


def join_pair(stacked):
    count = stacked.shape[0] // 2
    lane = lax.broadcasted_iota(jnp.int32, (count, PAIR), 1)
    return jnp.where(lane < HEAD, stacked[:count], stacked[count:])


class Plan:
    def __init__(self, shards, rows, order, items, length, width):
        self.shards, self.rows, self.order = shards, rows, order
        self.items, self.length, self.width = items, length, width
        self.tokens = items * length
        self.pairs = width // PAIR


def weight_copies(plan, gathered, held, sem, group):
    first, count = group
    copies = []
    for place, device in enumerate(plan.order):
        if group is DOWN:
            for block in range(count):
                row = count * device + block
                copies.append(
                    pltpu.make_async_copy(
                        gathered.at[place, first + block],
                        held.at[first + row // plan.shards, row % plan.shards],
                        sem,
                    )
                )
        else:
            copies.append(
                pltpu.make_async_copy(
                    gathered.at[place, pl.ds(first, count)],
                    held.at[pl.ds(first, count), device],
                    sem,
                )
            )
    return copies


def start_weights(plan, gathered, held, sem, group):
    for copy in weight_copies(plan, gathered, held, sem, group):
        copy.start()


def wait_weights(held, sem, group):
    first, count = group
    part = held.at[pl.ds(first, count)]
    pltpu.make_async_copy(part, part, sem).wait()


def block_of(plan, held, index):
    return held[index].reshape(plan.width, plan.width)


def forward(plan, inputs, lengths, vec, gathered, held, sems, scratch, keep):
    width, length = plan.width, plan.length
    normed_ref, qkv_ref, attended_ref, middle_ref, hidden_ref = scratch[:5]
    start_weights(plan, gathered, held, sems.at[0], QKV)
    start_weights(plan, gathered, held, sems.at[1], OUT)
    values = inputs.astype(F32)
    xhat, _ = normalised(values)
    base = xhat * vec[0:1, :] + vec[1:2, :]
    for item in range(plan.items):
        rows = slice(item * length, (item + 1) * length)
        normed_ref[rows, :] = (base[rows] + vec[12 + item : 13 + item, :]).astype(BF16)
    wait_weights(held, sems.at[0], QKV)
    start_weights(plan, gathered, held, sems.at[2], UP)
    for part, bias in enumerate((2, None, 3)):
        joined = mm(normed_ref[...], block_of(plan, held, part))
        if bias is not None:
            joined = joined + vec[bias : bias + 1, :]
        qkv_ref[:, part * width : (part + 1) * width] = joined.astype(BF16)
    start_weights(plan, gathered, held, sems.at[3], DOWN)
    key_index = lax.broadcasted_iota(jnp.int32, (2 * length, length), 1)
    for item in range(plan.items):
        rows = slice(item * length, (item + 1) * length)
        valid = key_index < lengths[item]
        for pair in range(plan.pairs):
            at = pair * PAIR
            query = split_pair(qkv_ref[rows, at : at + PAIR])
            key = qkv_ref[rows, width + at : width + at + PAIR]
            value = qkv_ref[rows, 2 * width + at : 2 * width + at + PAIR]
            logits = jnp.where(valid, mm_nt(query, key) * SCALE_FACTOR, -1000000000.0)
            expo = jnp.exp(logits - jnp.max(logits, -1, keepdims=True))
            probs = expo / jnp.sum(expo, -1, keepdims=True)
            if keep:
                scratch[5][item * plan.pairs + pair] = probs
            attended_ref[rows, at : at + PAIR] = join_pair(mm(probs.astype(BF16), value)).astype(
                BF16
            )
    wait_weights(held, sems.at[1], OUT)
    middle = values + (mm(attended_ref[...], block_of(plan, held, OUT[0])) + vec[4:5, :])
    middle_ref[...] = middle
    xhat, _ = normalised(middle)
    hidden_ref[...] = (xhat * vec[5:6, :] + vec[6:7, :]).astype(BF16)
    wait_weights(held, sems.at[2], UP)
    wait_weights(held, sems.at[3], DOWN)
    total = None
    for part in range(UP[1]):
        pre_act = mm(hidden_ref[...], block_of(plan, held, UP[0] + part)) + vec[8 + part : 9 + part, :]
        act, slope = gelu_both(pre_act)
        act = act.astype(BF16)
        if keep:
            scratch[6][:, part * width : (part + 1) * width] = act
            scratch[7][:, part * width : (part + 1) * width] = slope
        term = mm(act, block_of(plan, held, DOWN[0] + part))
        total = term if total is None else total + term
    return middle_ref[...] + (total + vec[7:8, :])


def attention_back(plan, probs_ref, qkv_ref, grad_attended_ref, rows_ref):
    width, length = plan.width, plan.length
    for item in range(plan.items):
        rows = slice(item * length, (item + 1) * length)
        for pair in range(plan.pairs):
            at = pair * PAIR
            query = split_pair(qkv_ref[rows, at : at + PAIR])
            key = qkv_ref[rows, width + at : width + at + PAIR]
            value = qkv_ref[rows, 2 * width + at : 2 * width + at + PAIR]
            grad = split_pair(grad_attended_ref[rows, at : at + PAIR])
            probs = probs_ref[item * plan.pairs + pair]
            grad_probs = mm_nt(grad, value)
            centre = jnp.sum(grad_probs * probs, -1, keepdims=True)
            grad_logits = (probs * (grad_probs - centre)).astype(BF16)
            grad_query = join_pair(mm(grad_logits, key)) * SCALE_FACTOR
            grad_key = mm_tn(grad_logits, query) * SCALE_FACTOR
            grad_value = mm_tn(probs.astype(BF16), grad)
            rows_ref[rows, at : at + PAIR] = grad_query.astype(BF16)
            rows_ref[rows, width + at : width + at + PAIR] = grad_key.astype(BF16)
            rows_ref[rows, 2 * width + at : 2 * width + at + PAIR] = grad_value.astype(BF16)


def column_sum(values):
    return jnp.sum(values.astype(F32), 0, keepdims=True)


def forward_kernel(plan, lengths, x_ref, vec, gathered, y_ref, held, normed, qkv, attended, middle, hidden, sems):
    out = forward(
        plan, x_ref[...], lengths, vec, gathered, held, sems,
        (normed, qkv, attended, middle, hidden), False,
    )
    y_ref[...] = out.astype(BF16)


def chain_kernel(
    plan, lengths, flag, x_ref, recv_ref, cot_ref, vec, gathered,
    y_ref, xin_ref, dx_ref, normed_out, qkv_out, attended_out, middle_out, hidden_out, probs_out, act_out, slope_out,
    held, normed, qkv, attended, middle, hidden, probs, act, slope, grad_attended, grad_rows, sems, out_sems,
):
    width = plan.width
    xin_ref[...] = jnp.where(flag[0] == 0, x_ref[...], recv_ref[...])
    scratch = (normed, qkv, attended, middle, hidden, probs, act, slope)
    out = forward(plan, xin_ref[...], lengths, vec, gathered, held, sems, scratch, True)
    y_ref[...] = out.astype(BF16)
    outs = (normed_out, qkv_out, attended_out, middle_out, hidden_out, probs_out, act_out, slope_out)
    copies = [
        pltpu.make_async_copy(source, target, out_sems.at[index])
        for index, (source, target) in enumerate(zip(scratch, outs))
    ]
    for copy in copies:
        copy.start()
    branch = cot_ref[...]
    grad_hidden = None
    for part in range(UP[1]):
        grad_act = mm_nt(branch, block_of(plan, held, DOWN[0] + part))
        grad_pre = (slope[:, part * width : (part + 1) * width] * grad_act).astype(BF16)
        term = mm_nt(grad_pre, block_of(plan, held, UP[0] + part))
        grad_hidden = term if grad_hidden is None else grad_hidden + term
    xhat, rstd = normalised(middle[...])
    grad_middle = branch.astype(F32) + norm_back(grad_hidden, xhat, rstd, vec[5:6, :])
    grad_attended[...] = mm_nt(grad_middle.astype(BF16), block_of(plan, held, OUT[0])).astype(BF16)
    attention_back(plan, probs, qkv, grad_attended, grad_rows)
    grad_normed = None
    for part in range(QKV[1]):
        term = mm_nt(grad_rows[:, part * width : (part + 1) * width], block_of(plan, held, part))
        grad_normed = term if grad_normed is None else grad_normed + term
    xhat, rstd = normalised(xin_ref[...].astype(F32))
    dx_ref[...] = (grad_middle + norm_back(grad_normed, xhat, rstd, vec[0:1, :])).astype(BF16)
    for copy in copies:
        copy.wait()


def grad_copies(plan, stage, grads, sem, index):
    copies = []
    for place, device in enumerate(plan.order):
        if index >= DOWN[0]:
            for block in range(DOWN[1]):
                row = DOWN[1] * device + block
                if DOWN[0] + row // plan.shards == index:
                    copies.append(
                        pltpu.make_async_copy(
                            stage.at[row % plan.shards], grads.at[place, DOWN[0] + block], sem
                        )
                    )
        else:
            copies.append(pltpu.make_async_copy(stage.at[device], grads.at[place, index], sem))
    return copies


def backward_kernel(
    plan, flag, arr_ref, cot_ref, xin_ref, vec, gathered,
    normed_in, qkv_in, attended_in, middle_in, hidden_in, probs_in, act_in, slope_in,
    dx_ref, small_ref, grads,
    held, normed, qkv, attended, middle, hidden, probs, act, slope, grad_attended, grad_rows, grad_pre_ref, stage,
    sems, in_sems, stage_sems,
):
    width, length = plan.width, plan.length
    start_weights(plan, gathered, held, sems.at[3], DOWN)
    ins = (normed_in, qkv_in, attended_in, middle_in, hidden_in, probs_in, act_in, slope_in)
    scratch = (normed, qkv, attended, middle, hidden, probs, act, slope)
    copies = [
        pltpu.make_async_copy(source, target, in_sems.at[index])
        for index, (source, target) in enumerate(zip(ins, scratch))
    ]
    copies[7].start()
    copies[6].start()
    start_weights(plan, gathered, held, sems.at[2], UP)
    for index in (4, 3, 2):
        copies[index].start()
    start_weights(plan, gathered, held, sems.at[1], OUT)
    for index in (5, 1, 0):
        copies[index].start()
    start_weights(plan, gathered, held, sems.at[0], QKV)
    branch = jnp.where(flag[0] == 0, arr_ref[...], cot_ref[...])
    used = [False, False]

    def emit(index, value):
        slot = index % 2
        if used[slot]:
            pltpu.make_async_copy(stage.at[slot], stage.at[slot], stage_sems.at[slot]).wait()
        used[slot] = True
        stage[slot] = value.astype(BF16).reshape(plan.shards, plan.rows, width)
        for copy in grad_copies(plan, stage.at[slot], grads, stage_sems.at[slot], index):
            copy.start()

    small_ref[7:8, :] = column_sum(branch)
    wait_weights(held, sems.at[3], DOWN)
    copies[7].wait()
    copies[6].wait()
    wait_weights(held, sems.at[2], UP)
    grad_hidden = None
    for part in range(UP[1]):
        columns = slice(part * width, (part + 1) * width)
        grad_act = mm_nt(branch, block_of(plan, held, DOWN[0] + part))
        grad_pre = (slope[:, columns] * grad_act).astype(BF16)
        grad_pre_ref[:, columns] = grad_pre
        small_ref[8 + part : 9 + part, :] = column_sum(grad_pre)
        term = mm_nt(grad_pre, block_of(plan, held, UP[0] + part))
        grad_hidden = term if grad_hidden is None else grad_hidden + term
        emit(DOWN[0] + part, mm_tn(act[:, columns], branch))
    copies[4].wait()
    for part in range(UP[1]):
        columns = slice(part * width, (part + 1) * width)
        emit(UP[0] + part, mm_tn(hidden[...], grad_pre_ref[:, columns]))
    copies[3].wait()
    copies[2].wait()
    xhat, rstd = normalised(middle[...])
    small_ref[5:6, :] = column_sum(grad_hidden * xhat)
    small_ref[6:7, :] = column_sum(grad_hidden)
    grad_middle = branch.astype(F32) + norm_back(grad_hidden, xhat, rstd, vec[5:6, :])
    middle[...] = grad_middle
    attn_grad = grad_middle.astype(BF16)
    small_ref[4:5, :] = column_sum(attn_grad)
    emit(OUT[0], mm_tn(attended[...], attn_grad))
    wait_weights(held, sems.at[1], OUT)
    grad_attended[...] = mm_nt(attn_grad, block_of(plan, held, OUT[0])).astype(BF16)
    copies[5].wait()
    copies[1].wait()
    attention_back(plan, probs, qkv, grad_attended, grad_rows)
    copies[0].wait()
    wait_weights(held, sems.at[0], QKV)
    grad_normed = None
    for part in range(QKV[1]):
        rows = grad_rows[:, part * width : (part + 1) * width]
        term = mm_nt(rows, block_of(plan, held, part))
        grad_normed = term if grad_normed is None else grad_normed + term
        emit(part, mm_tn(normed[...], rows))
        if part != 1:
            small_ref[2 + part // 2 : 3 + part // 2, :] = column_sum(rows)
    xhat, rstd = normalised(xin_ref[...].astype(F32))
    small_ref[0:1, :] = column_sum(grad_normed * xhat)
    small_ref[1:2, :] = column_sum(grad_normed)
    for item in range(plan.items):
        small_ref[12 + item : 13 + item, :] = column_sum(
            grad_normed[item * length : (item + 1) * length]
        )
    dx_ref[...] = middle[...] + norm_back(grad_normed, xhat, rstd, vec[0:1, :])
    for slot in range(2):
        pltpu.make_async_copy(stage.at[slot], stage.at[slot], stage_sems.at[slot]).wait()


SMEM = pl.BlockSpec(memory_space=pltpu.SMEM)
VMEM = pl.BlockSpec(memory_space=pltpu.VMEM)
ANY = pl.BlockSpec(memory_space=pl.ANY)


def kept_shapes(plan):
    tokens, width = plan.tokens, plan.width
    return [
        ((tokens, width), BF16),
        ((tokens, 3 * width), BF16),
        ((tokens, width), BF16),
        ((tokens, width), F32),
        ((tokens, width), BF16),
        ((plan.items * plan.pairs, 2 * plan.length, plan.length), F32),
        ((tokens, 4 * width), BF16),
        ((tokens, 4 * width), F32),
    ]


def params():
    return pltpu.CompilerParams(vmem_limit_bytes=LIMIT)


def run_forward(plan, lengths, x, vec, gathered):
    kept = [pltpu.VMEM(*shape) for shape in kept_shapes(plan)]
    held = pltpu.VMEM((BLOCKS, plan.shards, plan.rows, plan.width), BF16)
    return pl.pallas_call(
        functools.partial(forward_kernel, plan),
        out_shape=jax.ShapeDtypeStruct(x.shape, BF16),
        in_specs=[SMEM, VMEM, VMEM, ANY],
        out_specs=VMEM,
        scratch_shapes=[held] + kept[:5] + [pltpu.SemaphoreType.DMA((4,))],
        compiler_params=params(),
        name="layer_forward",
    )(lengths, x, vec, gathered)


def run_chain(plan, lengths, flag, x, recv, cot, vec, gathered):
    tokens, width = plan.tokens, plan.width
    shapes = kept_shapes(plan)
    held = pltpu.VMEM((BLOCKS, plan.shards, plan.rows, plan.width), BF16)
    rows = jax.ShapeDtypeStruct((tokens, width), BF16)
    return pl.pallas_call(
        functools.partial(chain_kernel, plan),
        out_shape=[rows] * 3 + [jax.ShapeDtypeStruct(*shape) for shape in shapes],
        in_specs=[SMEM, SMEM, VMEM, VMEM, VMEM, VMEM, ANY],
        out_specs=[VMEM] * 3 + [ANY] * len(shapes),
        scratch_shapes=[held]
        + [pltpu.VMEM(*shape) for shape in shapes]
        + [
            pltpu.VMEM((tokens, width), BF16),
            pltpu.VMEM((tokens, 3 * width), BF16),
            pltpu.SemaphoreType.DMA((4,)),
            pltpu.SemaphoreType.DMA((len(shapes),)),
        ],
        compiler_params=params(),
        name="layer_chain",
    )(lengths, flag, x, recv, cot, vec, gathered)


def run_backward(plan, flag, arriving, cot, xin, vec, gathered, kept):
    tokens, width = plan.tokens, plan.width
    shapes = kept_shapes(plan)
    blocks = (BLOCKS, plan.shards, plan.rows, plan.width)
    return pl.pallas_call(
        functools.partial(backward_kernel, plan),
        out_shape=[
            jax.ShapeDtypeStruct((tokens, width), F32),
            jax.ShapeDtypeStruct((16, width), F32),
            jax.ShapeDtypeStruct((plan.shards, BLOCKS, plan.rows, plan.width), BF16),
        ],
        in_specs=[SMEM, VMEM, VMEM, VMEM, VMEM, ANY] + [ANY] * len(shapes),
        out_specs=[VMEM, VMEM, ANY],
        scratch_shapes=[pltpu.VMEM(blocks, BF16)]
        + [pltpu.VMEM(*shape) for shape in shapes]
        + [
            pltpu.VMEM((tokens, width), BF16),
            pltpu.VMEM((tokens, 3 * width), BF16),
            pltpu.VMEM((tokens, 4 * width), BF16),
            pltpu.VMEM((2,) + blocks[1:], BF16),
            pltpu.SemaphoreType.DMA((4,)),
            pltpu.SemaphoreType.DMA((len(shapes),)),
            pltpu.SemaphoreType.DMA((2,)),
        ],
        compiler_params=params(),
        name="layer_backward",
    )(flag, arriving, cot, xin, vec, gathered, *kept)


def shifted(value, axis, steps):
    count = lax.axis_size(axis)
    first, last = (max(0, -steps), min(count, count - steps))
    return lax.ppermute(value, axis, [(source, source + steps) for source in range(first, last)])


def small_gather(value, count):
    value = value[None]
    if count & (count - 1):
        return lax.all_gather(value, "dp", axis=0, tiled=True)
    index = lax.axis_index("dp")
    step = 1
    while step < count:
        other = lax.ppermute(value, "dp", [(i, i ^ step) for i in range(count)])
        value = jnp.where(
            (index & step) == 0,
            jnp.concatenate([value, other], 0),
            jnp.concatenate([other, value], 0),
        )
        step *= 2
    return value


def small_scatter(value, count):
    if count & (count - 1):
        return lax.psum_scatter(value, "dp", scatter_dimension=0, tiled=True)[0]
    index = lax.axis_index("dp")
    step = count // 2
    while step:
        upper = (index & step) != 0
        keep = jnp.where(upper, value[step:], value[:step])
        send = jnp.where(upper, value[:step], value[step:])
        value = keep + lax.ppermute(send, "dp", [(i, i ^ step) for i in range(count)])
        step //= 2
    return value[0]


def cycle(count):
    chips = count // 2
    walk = list(range(0, chips, 2)) + list(range(chips - 1, 0, -2))
    return [2 * chip + core for chip in walk for core in range(2)]


def body(
    block_input, cotangent, lengths, leads,
    norm_gain1, norm_bias1, lead_table, qkv_weight, query_bias, value_bias, out_weight, out_bias,
    norm_gain2, norm_bias2, up_weight, up_bias, down_weight, down_bias,
):
    count = lax.axis_size("dp")
    micro, local, length, width = block_input.shape
    items = micro * local
    rows = width // count
    leads_count = lead_table.shape[2]
    section = lax.axis_index("section")
    flag = section.astype(jnp.int32).reshape(1)
    flat = lambda value: value.reshape(items * length, width)
    x, cot = flat(block_input), flat(cotangent)
    lens, lead = lengths.reshape(items), leads.reshape(items)

    qkv_part = qkv_weight[0].astype(BF16).reshape(rows, 3, width).transpose(1, 0, 2)
    up_part = up_weight[0].astype(BF16).reshape(rows, 4, width).transpose(1, 0, 2)
    packed = jnp.concatenate(
        [
            qkv_part,
            out_weight.astype(BF16),
            up_part,
            down_weight[0].astype(BF16).reshape(4, rows, width),
        ],
        0,
    )
    aligned = rows % 16 == 0
    order = cycle(count) if aligned else list(range(count))
    if aligned:
        gathered = lax.all_gather(packed, "dp", axis=0, tiled=True, axis_index_groups=[order])
        gathered = gathered.reshape(count, BLOCKS, rows, width)
        plan = Plan(count, rows, order, items, length, width)
    else:
        gathered = lax.all_gather(packed, "dp", axis=0).reshape(count, BLOCKS, rows, width)
        head = gathered[:, :8].transpose(1, 0, 2, 3).reshape(8, width, width)
        tail = gathered[:, 8:].reshape(4, width, width)
        gathered = jnp.concatenate([head, tail], 0)[None]
        plan = Plan(1, width, [0], items, length, width)

    small = jnp.concatenate(
        [
            norm_gain1, norm_bias1, query_bias, value_bias, out_bias, norm_gain2, norm_bias2, down_bias,
            up_bias.reshape(4, rows), lead_table[0].T,
        ],
        0,
    ).astype(BF16)
    small = small_gather(small, count)
    wide = small.transpose(1, 0, 2).reshape(12 + leads_count, width).astype(F32)
    vec = jnp.concatenate(
        [wide[:8], small[:, 8:12].reshape(4, width).astype(F32)]
        + [lax.dynamic_slice_in_dim(wide, 12 + lead[item], 1, 0) for item in range(items)]
        + [jnp.zeros((4 - items, width), F32)],
        0,
    )

    first_out = run_forward(plan, lens, x, vec, gathered)
    recv = shifted(first_out, "section", 1)
    output, xin, first_grad, *kept = run_chain(plan, lens, flag, x, recv, cot, vec, gathered)
    arriving = shifted(first_grad, "section", -1)
    input_grad, sums, grads = run_backward(plan, flag, arriving, cot, xin, vec, gathered, kept)

    if aligned:
        grads = lax.psum_scatter(
            grads.reshape(count * BLOCKS, rows, width),
            "dp", scatter_dimension=0, tiled=True, axis_index_groups=[order],
        )
    else:
        grads = grads.reshape(BLOCKS, width, width)
        head = grads[:8].reshape(8, count, rows, width).transpose(1, 0, 2, 3)
        tail = grads[8:].reshape(count, 4, rows, width)
        grads = lax.psum_scatter(
            jnp.concatenate([head, tail], 1), "dp", scatter_dimension=0, tiled=False
        )
    hot = (jnp.arange(leads_count)[:, None] == lead[None, :]).astype(F32)
    table = sum(hot[:, item : item + 1] * sums[12 + item : 13 + item] for item in range(items))
    spread = jnp.concatenate(
        [
            sums[:8].reshape(8, count, rows).transpose(1, 0, 2),
            sums[8:12].reshape(count, 4, rows),
            table.reshape(leads_count, count, rows).transpose(1, 0, 2),
        ],
        1,
    )
    spread = small_scatter(spread, count)

    grads = grads.astype(F32)
    vector = lambda index: spread[index : index + 1]
    across = lambda value: value.transpose(1, 0, 2).reshape(1, rows, -1)
    shape = (1, micro, local, length, width)
    return (
        output.reshape(shape),
        input_grad.reshape(shape),
        vector(0),
        vector(1),
        spread[12:].T[None],
        across(grads[:3]),
        vector(2),
        vector(3),
        grads[3:4],
        vector(4),
        vector(5),
        vector(6),
        across(grads[4:8]),
        spread[8:12].reshape(1, 4 * rows),
        grads[8:].reshape(1, 4 * rows, width),
        vector(7),
    )


def solution(mesh):
    weights = (
        P("section", "dp"),
        P("section", "dp"),
        P("section", "dp", None),
        P("section", "dp", None),
        P("section", "dp"),
        P("section", "dp"),
        P("section", "dp", None),
        P("section", "dp"),
        P("section", "dp"),
        P("section", "dp"),
        P("section", "dp", None),
        P("section", "dp"),
        P("section", "dp", None),
        P("section", "dp"),
    )
    rows = P(None, "dp", None, None)
    layers = P("section", None, "dp", None, None)
    return jax.shard_map(
        body,
        mesh=mesh,
        in_specs=(rows, rows, P(None, "dp"), P(None, "dp")) + weights,
        out_specs=(layers, layers) + weights,
        check_vma=False,
    )
```

```python
import functools

import jax
import jax.numpy as jnp
from jax import lax
from jax.experimental import pallas as pl
from jax.experimental.pallas import tpu as pltpu
from jax.sharding import PartitionSpec as P

HEAD = 64
PAIR = 2 * HEAD
EPS = 1e-06
SCALE_FACTOR = 0.125
GELU_A = 0.7978845608028654
GELU_B = 0.044715
F32 = jnp.float32
BF16 = jnp.bfloat16
OUT = 3
FIRST = 4
SECOND = 8
QUART = 4


def mm(left, right):
    return jnp.dot(left, right, preferred_element_type=F32)


def mm_nt(left, right):
    return lax.dot_general(left, right, (((1,), (1,)), ((), ())), preferred_element_type=F32)


def mm_tn(left, right):
    return lax.dot_general(left, right, (((0,), (0,)), ((), ())), preferred_element_type=F32)


def normalised(values):
    mean = jnp.mean(values, -1, keepdims=True)
    centred = values - mean
    variance = jnp.mean(centred * centred, -1, keepdims=True)
    rstd = lax.rsqrt(variance + EPS)
    return centred * rstd, rstd


def norm_back(grad, xhat, rstd, gain):
    scaled = grad * gain
    first = jnp.mean(scaled, -1, keepdims=True)
    second = jnp.mean(scaled * xhat, -1, keepdims=True)
    return rstd * (scaled - first - xhat * second)


def gelu_both(values):
    square = values * values
    slope = GELU_A * (1.0 + 3.0 * GELU_B * square)
    bend = jnp.tanh(GELU_A * values * (1.0 + GELU_B * square))
    half = 0.5 * (1.0 + bend)
    return values * half, half + 0.5 * values * (1.0 - bend * bend) * slope


def split_pair(rows):
    lane = lax.broadcasted_iota(jnp.int32, rows.shape, 1)
    zero = jnp.zeros_like(rows)
    return jnp.concatenate(
        [jnp.where(lane < HEAD, rows, zero), jnp.where(lane < HEAD, zero, rows)], 0
    )


def join_pair(stacked):
    count = stacked.shape[0] // 2
    lane = lax.broadcasted_iota(jnp.int32, (count, PAIR), 1)
    return jnp.where(lane < HEAD, stacked[:count], stacked[count:])


class Plan:
    def __init__(self, shards, rows, order, items, length, width):
        self.shards, self.rows, self.order = shards, rows, order
        self.items, self.length, self.width = items, length, width
        self.tokens = items * length
        self.pairs = width // PAIR


def first_copies(pieces, devs, held, sem, blocks):
    return [
        pltpu.make_async_copy(piece.at[blocks], held.at[blocks, devs[slot]], sem)
        for slot, piece in enumerate(pieces)
    ]


def down_rows(plan, device):
    whole = plan.shards % QUART == 0
    parts = [(0, QUART)] if whole else [(block, 1) for block in range(QUART)]
    return [
        (first, count, *divmod(QUART * device + first, plan.shards)) for first, count in parts
    ]


def up_copies(plan, gathered, held, sem, part):
    return [
        pltpu.make_async_copy(gathered.at[place, part], held.at[part, device], sem)
        for place, device in enumerate(plan.order)
    ]


def down_copies(plan, gathered, held, sem, part):
    return [
        pltpu.make_async_copy(
            gathered.at[place, pl.ds(QUART + first, count)],
            held.at[QUART + block, pl.ds(row, count)],
            sem,
        )
        for place, device in enumerate(plan.order)
        for first, count, block, row in down_rows(plan, device)
        if block == part
    ]


def start_all(copies):
    for copy in copies:
        copy.start()


def wait_bytes(part, sem):
    pltpu.make_async_copy(part, part, sem).wait()


def block_of(plan, held, index):
    return held[index].reshape(plan.width, plan.width)


def columns_of(plan, index):
    return slice(index * plan.width, (index + 1) * plan.width)


def attention_forward(plan, lengths, qkv_ref, attended_ref, probs_ref):
    width, length = plan.width, plan.length
    key_index = lax.broadcasted_iota(jnp.int32, (2 * length, length), 1)
    for item in range(plan.items):
        rows = slice(item * length, (item + 1) * length)
        valid = key_index < lengths[item]
        for pair in range(plan.pairs):
            at = pair * PAIR
            query = split_pair(qkv_ref[rows, at : at + PAIR])
            key = qkv_ref[rows, width + at : width + at + PAIR]
            value = qkv_ref[rows, 2 * width + at : 2 * width + at + PAIR]
            logits = jnp.where(valid, mm_nt(query, key) * SCALE_FACTOR, -1000000000.0)
            expo = jnp.exp(logits - jnp.max(logits, -1, keepdims=True))
            probs = expo / jnp.sum(expo, -1, keepdims=True)
            if probs_ref is not None:
                probs_ref[item * plan.pairs + pair] = probs
            attended_ref[rows, at : at + PAIR] = join_pair(mm(probs.astype(BF16), value)).astype(
                BF16
            )


def first_half(plan, inputs, lengths, vec, held, wait, normed_ref, qkv_ref, attended_ref, probs_ref, hidden_ref):
    width, length = plan.width, plan.length
    values = inputs.astype(F32)
    xhat, _ = normalised(values)
    base = xhat * vec[0:1, :] + vec[1:2, :]
    for item in range(plan.items):
        rows = slice(item * length, (item + 1) * length)
        normed_ref[rows, :] = (base[rows] + vec[12 + item : 13 + item, :]).astype(BF16)
    wait(0)
    for part, bias in enumerate((2, None, 3)):
        joined = mm(normed_ref[...], block_of(plan, held, part))
        if bias is not None:
            joined = joined + vec[bias : bias + 1, :]
        qkv_ref[:, columns_of(plan, part)] = joined.astype(BF16)
    attention_forward(plan, lengths, qkv_ref, attended_ref, probs_ref)
    wait(1)
    middle = values + (mm(attended_ref[...], block_of(plan, held, OUT)) + vec[4:5, :])
    xhat, _ = normalised(middle)
    hidden_ref[...] = (xhat * vec[5:6, :] + vec[6:7, :]).astype(BF16)
    return middle


def second_half(plan, hidden_ref, vec, held, act_ref=None, slope_ref=None, wait=None):
    total = None
    for part in range(QUART):
        if wait is not None:
            wait(part)
        pre_act = mm(hidden_ref[...], block_of(plan, held, part)) + vec[8 + part : 9 + part, :]
        act, slope = gelu_both(pre_act)
        act = act.astype(BF16)
        if act_ref is not None:
            act_ref[:, columns_of(plan, part)] = act
            slope_ref[:, columns_of(plan, part)] = slope
        if wait is not None:
            wait(QUART + part)
        term = mm(act, block_of(plan, held, QUART + part))
        total = term if total is None else total + term
    return total + vec[7:8, :]


def attention_back(plan, probs_ref, qkv_ref, grad_attended_ref, rows_ref):
    width, length = plan.width, plan.length
    for item in range(plan.items):
        rows = slice(item * length, (item + 1) * length)
        for pair in range(plan.pairs):
            at = pair * PAIR
            query = split_pair(qkv_ref[rows, at : at + PAIR])
            key = qkv_ref[rows, width + at : width + at + PAIR]
            value = qkv_ref[rows, 2 * width + at : 2 * width + at + PAIR]
            grad = split_pair(grad_attended_ref[rows, at : at + PAIR])
            probs = probs_ref[item * plan.pairs + pair]
            grad_probs = mm_nt(grad, value)
            centre = jnp.sum(grad_probs * probs, -1, keepdims=True)
            grad_logits = (probs * (grad_probs - centre)).astype(BF16)
            grad_query = join_pair(mm(grad_logits, key)) * SCALE_FACTOR
            grad_key = mm_tn(grad_logits, query) * SCALE_FACTOR
            grad_value = mm_tn(probs.astype(BF16), grad)
            rows_ref[rows, at : at + PAIR] = grad_query.astype(BF16)
            rows_ref[rows, width + at : width + at + PAIR] = grad_key.astype(BF16)
            rows_ref[rows, 2 * width + at : 2 * width + at + PAIR] = grad_value.astype(BF16)


def column_sum(values):
    return jnp.sum(values.astype(F32), 0, keepdims=True)


def load_first(held, pieces, devs, sems):
    start_all(first_copies(pieces, devs, held, sems.at[0], pl.ds(0, OUT)))
    start_all(first_copies(pieces, devs, held, sems.at[1], pl.ds(OUT, 1)))

    def wait(group):
        blocks = pl.ds(OUT, 1) if group else pl.ds(0, OUT)
        wait_bytes(held.at[blocks], sems.at[group])

    return wait


def attend_kernel(plan, lengths, flag, devs, x_ref, vec, *refs):
    pieces, (middle_ref, hidden_ref, held, normed, qkv, attended, sems) = refs[:-7], refs[-7:]
    wait = load_first(held, pieces, devs, sems)
    middle_ref[...] = first_half(
        plan, x_ref[...], lengths, vec, held, wait, normed, qkv, attended, None, hidden_ref
    )


def mlp_kernel(plan, middle_ref, hidden_ref, vec, gathered, y_ref, held, sems):
    for part in range(QUART):
        start_all(up_copies(plan, gathered, held, sems.at[part], part))
        start_all(down_copies(plan, gathered, held, sems.at[QUART + part], part))

    def wait(block):
        wait_bytes(held.at[block], sems.at[block])

    total = second_half(plan, hidden_ref, vec, held, wait=wait)
    y_ref[...] = (middle_ref[...] + total).astype(BF16)


def load_kernel(plan, devs, after, gathered, *refs):
    pieces, (held1, held2, sems) = refs[:-3], refs[-3:]
    copies = first_copies(pieces, devs, held1, sems.at[0], pl.ds(0, FIRST))
    for part in range(QUART):
        copies += up_copies(plan, gathered, held2, sems.at[1], part)
        copies += down_copies(plan, gathered, held2, sems.at[1], part)
    start_all(copies)
    wait_bytes(held1, sems.at[0])
    wait_bytes(held2, sems.at[1])


def chain_kernel(
    plan, lengths, flag, x_ref, recv_ref, cot_ref, vec, held1, held2,
    y_ref, xin_ref, dx_ref, normed, qkv, attended, middle, hidden, probs, act, slope, grad_attended, grad_rows,
):
    xin_ref[...] = jnp.where(flag[0] == 0, x_ref[...], recv_ref[...])
    middle[...] = first_half(
        plan, xin_ref[...], lengths, vec, held1, lambda group: None, normed, qkv, attended, probs, hidden
    )
    y_ref[...] = (middle[...] + second_half(plan, hidden, vec, held2, act, slope)).astype(BF16)
    branch = cot_ref[...]
    grad_hidden = None
    for part in range(QUART):
        grad_act = mm_nt(branch, block_of(plan, held2, QUART + part))
        grad_pre = (slope[:, columns_of(plan, part)] * grad_act).astype(BF16)
        term = mm_nt(grad_pre, block_of(plan, held2, part))
        grad_hidden = term if grad_hidden is None else grad_hidden + term
    xhat, rstd = normalised(middle[...])
    grad_middle = branch.astype(F32) + norm_back(grad_hidden, xhat, rstd, vec[5:6, :])
    grad_attended[...] = mm_nt(grad_middle.astype(BF16), block_of(plan, held1, OUT)).astype(BF16)
    attention_back(plan, probs, qkv, grad_attended, grad_rows)
    grad_normed = None
    for part in range(OUT):
        term = mm_nt(grad_rows[:, columns_of(plan, part)], block_of(plan, held1, part))
        grad_normed = term if grad_normed is None else grad_normed + term
    xhat, rstd = normalised(xin_ref[...].astype(F32))
    dx_ref[...] = (grad_middle + norm_back(grad_normed, xhat, rstd, vec[0:1, :])).astype(BF16)


class Stage:
    def __init__(self, plan, stage, sems):
        self.plan, self.stage, self.sems, self.sent = plan, stage, sems, 0

    def put(self, value, copies_of):
        slot = self.sent % 2
        if self.sent >= 2:
            wait_bytes(self.stage.at[slot], self.sems.at[slot])
        self.sent += 1
        plan = self.plan
        self.stage[slot] = value.astype(BF16).reshape(plan.shards, plan.rows, plan.width)
        start_all(copies_of(self.stage.at[slot], self.sems.at[slot]))

    def drain(self):
        for slot in range(min(2, self.sent)):
            wait_bytes(self.stage.at[slot], self.sems.at[slot])


def backward_kernel(
    plan, flag, arr_ref, cot_ref, xin_ref, vec, held1, held2,
    normed, qkv, attended, middle_ref, hidden, probs, act, slope,
    dx_ref, small_ref, grads, grad_pre_ref, grad_middle_ref, grad_attended, grad_rows, stage, stage_sems,
):
    length = plan.length
    branch = jnp.where(flag[0] == 0, arr_ref[...], cot_ref[...])
    small_ref[...] = jnp.zeros_like(small_ref)
    small_ref[7:8, :] = column_sum(branch)
    out = Stage(plan, stage, stage_sems)

    def copies_of(block):
        def copies(source, sem):
            return [
                pltpu.make_async_copy(source.at[device], grads.at[place, block], sem)
                for place, device in enumerate(plan.order)
            ]

        return copies

    def copies_of_down(part):
        def copies(source, sem):
            return [
                pltpu.make_async_copy(
                    source.at[pl.ds(row, count)],
                    grads.at[place, pl.ds(FIRST + QUART + first, count)],
                    sem,
                )
                for place, device in enumerate(plan.order)
                for first, count, block, row in down_rows(plan, device)
                if block == part
            ]

        return copies

    grad_hidden = None
    for part in range(QUART):
        columns = columns_of(plan, part)
        grad_act = mm_nt(branch, block_of(plan, held2, QUART + part))
        grad_pre = (slope[:, columns] * grad_act).astype(BF16)
        grad_pre_ref[:, columns] = grad_pre
        small_ref[8 + part : 9 + part, :] = column_sum(grad_pre)
        term = mm_nt(grad_pre, block_of(plan, held2, part))
        grad_hidden = term if grad_hidden is None else grad_hidden + term
        out.put(mm_tn(act[:, columns], branch), copies_of_down(part))
    for part in range(QUART):
        out.put(
            mm_tn(hidden[...], grad_pre_ref[:, columns_of(plan, part)]), copies_of(FIRST + part)
        )
    xhat, rstd = normalised(middle_ref[...])
    small_ref[5:6, :] = column_sum(grad_hidden * xhat)
    small_ref[6:7, :] = column_sum(grad_hidden)
    grad_middle = branch.astype(F32) + norm_back(grad_hidden, xhat, rstd, vec[5:6, :])
    grad_middle_ref[...] = grad_middle
    attn_grad = grad_middle.astype(BF16)
    small_ref[4:5, :] = column_sum(attn_grad)
    grad_attended[...] = mm_nt(attn_grad, block_of(plan, held1, OUT)).astype(BF16)
    out.put(mm_tn(attended[...], attn_grad), copies_of(OUT))
    attention_back(plan, probs, qkv, grad_attended, grad_rows)
    grad_normed = None
    for part in range(OUT):
        rows = grad_rows[:, columns_of(plan, part)]
        out.put(mm_tn(normed[...], rows), copies_of(part))
        term = mm_nt(rows, block_of(plan, held1, part))
        grad_normed = term if grad_normed is None else grad_normed + term
        if part != 1:
            small_ref[2 + part // 2 : 3 + part // 2, :] = column_sum(rows)
    xhat, rstd = normalised(xin_ref[...].astype(F32))
    small_ref[0:1, :] = column_sum(grad_normed * xhat)
    small_ref[1:2, :] = column_sum(grad_normed)
    for item in range(plan.items):
        small_ref[12 + item : 13 + item, :] = column_sum(
            grad_normed[item * length : (item + 1) * length]
        )
    dx_ref[...] = grad_middle_ref[...] + norm_back(grad_normed, xhat, rstd, vec[0:1, :])
    out.drain()


def pack_kernel(qkv_ref, out_ref, up_ref, down_ref, first_ref, second_ref):
    rows, width = out_ref.shape
    for part in range(OUT):
        first_ref[part] = qkv_ref[:, part * width : (part + 1) * width].astype(BF16)
    first_ref[OUT] = out_ref[...].astype(BF16)
    for part in range(QUART):
        second_ref[part] = up_ref[:, part * width : (part + 1) * width].astype(BF16)
        second_ref[QUART + part] = down_ref[part * rows : (part + 1) * rows, :].astype(BF16)


def unpack_kernel(grads_ref, qkv_ref, out_ref, up_ref, down_ref):
    _, rows, width = grads_ref.shape
    for part in range(OUT):
        qkv_ref[:, part * width : (part + 1) * width] = grads_ref[part].astype(F32)
    out_ref[...] = grads_ref[OUT].astype(F32)
    for part in range(QUART):
        up_ref[:, part * width : (part + 1) * width] = grads_ref[FIRST + part].astype(F32)
        down_ref[part * rows : (part + 1) * rows, :] = grads_ref[FIRST + QUART + part].astype(F32)


SMEM = pl.BlockSpec(memory_space=pltpu.SMEM)
VMEM = pl.BlockSpec(memory_space=pltpu.VMEM)
HBM = pl.BlockSpec(memory_space=pltpu.HBM)


def kept_shapes(plan):
    tokens, width = plan.tokens, plan.width
    return [
        ((tokens, width), BF16),
        ((tokens, 3 * width), BF16),
        ((tokens, width), BF16),
        ((tokens, width), F32),
        ((tokens, width), BF16),
        ((plan.items * plan.pairs, 2 * plan.length, plan.length), F32),
        ((tokens, 4 * width), BF16),
        ((tokens, 4 * width), F32),
    ]


def held_blocks(plan, blocks):
    return pltpu.VMEM((blocks, plan.shards, plan.rows, plan.width), BF16)


def call(kernel, outs, in_specs, out_specs, scratch, name, work, limit, args):
    args = [
        pltpu.with_memory_space_constraint(arg, pltpu.HBM) if spec is HBM else arg
        for arg, spec in zip(args, in_specs)
    ]
    return pl.pallas_call(
        kernel,
        out_shape=outs,
        in_specs=in_specs,
        out_specs=out_specs,
        scratch_shapes=scratch,
        compiler_params=pltpu.CompilerParams(vmem_limit_bytes=limit * 1024 * 1024),
        cost_estimate=pl.CostEstimate(flops=2 * work[0], bytes_accessed=work[1], transcendentals=0),
        name=name,
    )(*args)


def of(shape):
    return jax.ShapeDtypeStruct(*shape)


def inside(shape):
    return pltpu.VMEM(*shape)


def run_attend(plan, lengths, flag, devs, x, vec, pieces):
    kept = kept_shapes(plan)
    block = plan.width * plan.width
    return call(
        functools.partial(attend_kernel, plan),
        [of(kept[3]), of(kept[4])],
        [SMEM, SMEM, SMEM, VMEM, VMEM] + [HBM] * len(pieces),
        [VMEM, VMEM],
        [held_blocks(plan, FIRST)] + [inside(shape) for shape in kept[:3]] + [pltpu.SemaphoreType.DMA((2,))],
        "attend",
        (FIRST * block * plan.tokens, FIRST * block * 2),
        14,
        (lengths, flag, devs, x, vec, *pieces),
    )


def run_mlp(plan, middle, hidden, vec, gathered):
    block = plan.width * plan.width
    return call(
        functools.partial(mlp_kernel, plan),
        jax.ShapeDtypeStruct(hidden.shape, BF16),
        [VMEM, VMEM, VMEM, HBM],
        VMEM,
        [held_blocks(plan, SECOND), pltpu.SemaphoreType.DMA((SECOND,))],
        "mlp",
        (SECOND * block * plan.tokens, SECOND * block * 2),
        16,
        (middle, hidden, vec, gathered),
    )


def run_load(plan, devs, after, gathered, pieces):
    block = plan.width * plan.width
    return call(
        functools.partial(load_kernel, plan),
        [held_blocks(plan, FIRST), held_blocks(plan, SECOND)],
        [SMEM, pl.BlockSpec(memory_space=pl.ANY)] + [HBM] * (1 + len(pieces)),
        [VMEM, VMEM],
        [pltpu.SemaphoreType.DMA((2,))],
        "load",
        (0, (FIRST + SECOND) * block * 4),
        2,
        (devs, after, gathered, *pieces),
    )


def run_chain(plan, lengths, flag, x, recv, cot, vec, held1, held2):
    shapes = kept_shapes(plan)
    block = plan.width * plan.width
    return call(
        functools.partial(chain_kernel, plan),
        [of(shapes[0]), inside(shapes[0]), of(shapes[0])] + [inside(shape) for shape in shapes],
        [SMEM] * 2 + [VMEM] * 6,
        [VMEM] * (3 + len(shapes)),
        [inside(shapes[0]), inside(shapes[1])],
        "chain",
        (24 * block * plan.tokens, 12 * block),
        10,
        (lengths, flag, x, recv, cot, vec, held1, held2),
    )


def run_backward(plan, flag, arriving, cot, xin, vec, held1, held2, kept):
    shapes = kept_shapes(plan)
    block = plan.width * plan.width
    stage = (2, plan.shards, plan.rows, plan.width)
    return call(
        functools.partial(backward_kernel, plan),
        [
            of(shapes[3]),
            jax.ShapeDtypeStruct((16, plan.width), F32),
            pltpu.HBM((plan.shards, FIRST + SECOND, plan.rows, plan.width), BF16),
        ],
        [SMEM] + [VMEM] * (6 + len(kept)),
        [VMEM, VMEM, HBM],
        [inside(shapes[index]) for index in (6, 3, 0, 1)]
        + [pltpu.VMEM(stage, BF16), pltpu.SemaphoreType.DMA((2,))],
        "backward",
        (24 * block * plan.tokens, 12 * block * 2),
        12,
        (flag, arriving, cot, xin, vec, held1, held2, *kept),
    )


def shifted(value, axis, steps):
    count = lax.axis_size(axis)
    first, last = (max(0, -steps), min(count, count - steps))
    return lax.ppermute(value, axis, [(source, source + steps) for source in range(first, last)])


def small_gather(value, count):
    value = value[None]
    if count & (count - 1):
        return lax.all_gather(value, "dp", axis=0, tiled=True)
    index = lax.axis_index("dp")
    step = 1
    while step < count:
        other = lax.ppermute(value, "dp", [(i, i ^ step) for i in range(count)])
        value = jnp.where(
            (index & step) == 0,
            jnp.concatenate([value, other], 0),
            jnp.concatenate([other, value], 0),
        )
        step *= 2
    return value


def small_scatter(value, count):
    if count & (count - 1):
        return lax.psum_scatter(value, "dp", scatter_dimension=0, tiled=True)[0]
    index = lax.axis_index("dp")
    step = count // 2
    while step:
        upper = (index & step) != 0
        keep = jnp.where(upper, value[step:], value[:step])
        send = jnp.where(upper, value[:step], value[step:])
        value = keep + lax.ppermute(send, "dp", [(i, i ^ step) for i in range(count)])
        step //= 2
    return value[0]


class Ring:
    def __init__(self, count):
        self.chips = count // 2
        self.walk = list(range(0, self.chips, 2)) + list(range(self.chips - 1, 0, -2))
        self.order = [2 * chip + core for chip in self.walk for core in range(2)]
        after = self.walk[1:] + self.walk[:1]
        self.onward = [
            (2 * here + core, 2 * there + core)
            for here, there in zip(self.walk, after)
            for core in range(2)
        ]
        self.back = [(there, here) for here, there in self.onward]
        self.sibling = [(index, index ^ 1) for index in range(count)]

    def slots(self):
        index = lax.axis_index("dp")
        chip, core = index // 2, index % 2
        place = jnp.where(chip % 2 == 0, chip // 2, self.chips - 1 - chip // 2)
        ahead = (place + jnp.arange(self.chips, dtype=jnp.int32)) % self.chips
        chips = jnp.where(ahead < (self.chips + 1) // 2, 2 * ahead, 2 * (self.chips - 1 - ahead) + 1)
        return jnp.concatenate([2 * chips + core, 2 * chips + 1 - core]).astype(jnp.int32)

    def gather(self, shard, beside):
        half = self.chips // 2
        own = [None] * self.chips
        own[0] = shard
        ahead = behind = shard
        for step in range(1, half + 1):
            if step == 3:
                ahead, beside = lax.optimization_barrier((ahead, beside))
            ahead = lax.ppermute(ahead, "dp", self.onward)
            own[self.chips - step] = ahead
            if step < self.chips - half:
                behind = lax.ppermute(behind, "dp", self.back)
                own[step] = behind
        return own + [lax.ppermute(piece, "dp", self.sibling) for piece in own], beside


def body(
    block_input, cotangent, lengths, leads,
    norm_gain1, norm_bias1, lead_table, qkv_weight, query_bias, value_bias, out_weight, out_bias,
    norm_gain2, norm_bias2, up_weight, up_bias, down_weight, down_bias,
):
    count = lax.axis_size("dp")
    micro, local, length, width = block_input.shape
    items = micro * local
    rows = width // count
    leads_count = lead_table.shape[2]
    flag = lax.axis_index("section").astype(jnp.int32).reshape(1)
    flat = lambda value: value.reshape(items * length, width)
    x, cot = flat(block_input), flat(cotangent)
    lens, lead = lengths.reshape(items), leads.reshape(items)

    small = jnp.concatenate(
        [
            norm_gain1, norm_bias1, query_bias, value_bias, out_bias, norm_gain2, norm_bias2, down_bias,
            up_bias.reshape(4, rows), lead_table[0].T,
        ],
        0,
    ).astype(BF16)
    small = small_gather(small, count)
    wide = small.transpose(1, 0, 2).reshape(12 + leads_count, width).astype(F32)
    vec = jnp.concatenate(
        [wide[:8], small[:, 8:12].reshape(4, width).astype(F32)]
        + [lax.dynamic_slice_in_dim(wide, 12 + lead[item], 1, 0) for item in range(items)]
        + [jnp.zeros((4 - items, width), F32)],
        0,
    )

    aligned = rows % 16 == 0 and count % 4 == 0
    if aligned:
        ring = Ring(count)
        first, second = pl.pallas_call(
            pack_kernel,
            out_shape=[
                jax.ShapeDtypeStruct((FIRST, rows, width), BF16),
                jax.ShapeDtypeStruct((SECOND, rows, width), BF16),
            ],
            name="pack",
        )(qkv_weight[0], out_weight[0], up_weight[0], down_weight[0])
        gathered = lax.all_gather(second, "dp", axis=0, tiled=True, axis_index_groups=[ring.order])
        gathered = gathered.reshape(count, SECOND, rows, width)
        pieces, vec = ring.gather(first, vec)
        devs = ring.slots()
        plan = Plan(count, rows, ring.order, items, length, width)
    else:
        wide_blocks = lambda value: value[0].reshape(rows, -1, width).transpose(1, 0, 2)
        packed = jnp.concatenate(
            [wide_blocks(qkv_weight), out_weight, wide_blocks(up_weight), down_weight.reshape(QUART, rows, width)], 0
        )
        everything = lax.all_gather(packed.astype(BF16), "dp", axis=0)
        across_blocks = lambda value: value.transpose(1, 0, 2, 3).reshape(-1, width, width)
        pieces = [across_blocks(everything[:, :FIRST])]
        gathered = jnp.concatenate(
            [
                across_blocks(everything[:, FIRST : FIRST + QUART]),
                everything[:, FIRST + QUART :].reshape(QUART, width, width),
            ],
            0,
        )[None]
        devs = jnp.zeros((1,), jnp.int32)
        plan = Plan(1, width, [0], items, length, width)

    middle, hidden = run_attend(plan, lens, flag, devs, x, vec, pieces)
    first_out = run_mlp(plan, middle, hidden, vec, gathered)
    recv = shifted(first_out, "section", 1)
    held1, held2 = run_load(plan, devs, first_out, gathered, pieces)
    output, xin, first_grad, *kept = run_chain(plan, lens, flag, x, recv, cot, vec, held1, held2)
    arriving = shifted(first_grad, "section", -1)
    input_grad, sums, grads = run_backward(
        plan, flag, arriving, cot, xin, vec, held1, held2, kept
    )
    blocks = FIRST + SECOND
    if aligned:
        grads = lax.psum_scatter(
            grads.reshape(count * blocks, rows, width),
            "dp", scatter_dimension=0, tiled=True, axis_index_groups=[ring.order],
        )
        shapes = [(rows, OUT * width), (rows, width), (rows, QUART * width), (QUART * rows, width)]
        grads = pl.pallas_call(
            unpack_kernel,
            out_shape=[jax.ShapeDtypeStruct(shape, F32) for shape in shapes],
            name="unpack",
        )(grads)
    else:
        head, tail = grads[0, : FIRST + QUART], grads[0, FIRST + QUART :]
        grads = jnp.concatenate(
            [
                head.reshape(-1, count, rows, width).transpose(1, 0, 2, 3),
                tail.reshape(count, QUART, rows, width),
            ],
            1,
        )
        grads = lax.psum_scatter(grads, "dp", scatter_dimension=0, tiled=False).astype(F32)
        across = lambda value: value.transpose(1, 0, 2).reshape(rows, -1)
        grads = (
            across(grads[:OUT]),
            grads[OUT],
            across(grads[FIRST : FIRST + QUART]),
            grads[FIRST + QUART :].reshape(QUART * rows, width),
        )
    hot = (jnp.arange(leads_count)[:, None] == lead[None, :]).astype(F32)
    table = sum(hot[:, item : item + 1] * sums[12 + item : 13 + item] for item in range(items))
    spread = jnp.concatenate(
        [
            sums[:8].reshape(8, count, rows).transpose(1, 0, 2),
            sums[8:12].reshape(count, 4, rows),
            table.reshape(leads_count, count, rows).transpose(1, 0, 2),
        ],
        1,
    )
    spread = small_scatter(spread, count)

    vector = lambda index: spread[index : index + 1]
    shape = (1, micro, local, length, width)
    return (
        output.reshape(shape),
        input_grad.reshape(shape),
        vector(0),
        vector(1),
        spread[12:].T[None],
        grads[0][None],
        vector(2),
        vector(3),
        grads[1][None],
        vector(4),
        vector(5),
        vector(6),
        grads[2][None],
        spread[8:12].reshape(1, 4 * rows),
        grads[3][None],
        vector(7),
    )


def solution(mesh):
    weights = (
        P("section", "dp"),
        P("section", "dp"),
        P("section", "dp", None),
        P("section", "dp", None),
        P("section", "dp"),
        P("section", "dp"),
        P("section", "dp", None),
        P("section", "dp"),
        P("section", "dp"),
        P("section", "dp"),
        P("section", "dp", None),
        P("section", "dp"),
        P("section", "dp", None),
        P("section", "dp"),
    )
    rows = P(None, "dp", None, None)
    layers = P("section", None, "dp", None, None)
    return jax.shard_map(
        body,
        mesh=mesh,
        in_specs=(rows, rows, P(None, "dp"), P(None, "dp")) + weights,
        out_specs=(layers, layers) + weights,
        check_vma=False,
    )
```

```python
import functools

import jax
import jax.numpy as jnp
from jax import lax
from jax.experimental import pallas as pl
from jax.experimental.pallas import tpu as pltpu
from jax.sharding import PartitionSpec as P

HEAD = 64
PAIR = 2 * HEAD
EPS = 1e-06
SCALE_FACTOR = 0.125
GELU_A = 0.7978845608028654
GELU_B = 0.044715
F32 = jnp.float32
BF16 = jnp.bfloat16
OUT = 3
FIRST = 4
SECOND = 8
QUART = 4
EXTRA = 16


def mm(left, right):
    return jnp.dot(left, right, preferred_element_type=F32)


def mm_nt(left, right):
    return lax.dot_general(left, right, (((1,), (1,)), ((), ())), preferred_element_type=F32)


def mm_tn(left, right):
    return lax.dot_general(left, right, (((0,), (0,)), ((), ())), preferred_element_type=F32)


def normalised(values):
    mean = jnp.mean(values, -1, keepdims=True)
    centred = values - mean
    variance = jnp.mean(centred * centred, -1, keepdims=True)
    rstd = lax.rsqrt(variance + EPS)
    return centred * rstd, rstd


def norm_back(grad, xhat, rstd, gain):
    scaled = grad * gain
    first = jnp.mean(scaled, -1, keepdims=True)
    second = jnp.mean(scaled * xhat, -1, keepdims=True)
    return rstd * (scaled - first - xhat * second)


def gelu_both(values):
    square = values * values
    slope = GELU_A * (1.0 + 3.0 * GELU_B * square)
    bend = jnp.tanh(GELU_A * values * (1.0 + GELU_B * square))
    half = 0.5 * (1.0 + bend)
    return values * half, half + 0.5 * values * (1.0 - bend * bend) * slope


def split_pair(rows):
    lane = lax.broadcasted_iota(jnp.int32, rows.shape, 1)
    zero = jnp.zeros_like(rows)
    return jnp.concatenate(
        [jnp.where(lane < HEAD, rows, zero), jnp.where(lane < HEAD, zero, rows)], 0
    )


def join_pair(stacked):
    count = stacked.shape[0] // 2
    lane = lax.broadcasted_iota(jnp.int32, (count, PAIR), 1)
    return jnp.where(lane < HEAD, stacked[:count], stacked[count:])


class Plan:
    def __init__(self, order, rows, items, length, width):
        self.order, self.shards, self.rows = order, len(order), rows
        self.items, self.length, self.width = items, length, width
        self.tokens = items * length
        self.pairs = width // PAIR
        whole = self.shards % QUART == 0
        self.runs = [(0, QUART)] if whole else [(block, 1) for block in range(QUART)]
        self.parts = 2 if self.shards > 1 else 1


def first_copies(plan, pieces, devs, held, sem, blocks):
    if plan.shards == 1:
        return block_copies(pieces, devs, held, sem, blocks)
    return [
        pltpu.make_async_copy(
            piece.at[pl.ds(block * plan.rows, plan.rows)], held.at[block, devs[slot]], sem
        )
        for slot, piece in enumerate(pieces)
        for block in range(blocks.start, blocks.start + blocks.size)
    ]


def block_copies(pieces, devs, held, sem, blocks, at=0):
    return [
        pltpu.make_async_copy(
            piece.at[blocks], held.at[pl.ds(at + blocks.start, blocks.size), devs[slot]], sem
        )
        for slot, piece in enumerate(pieces)
    ]


def down_copies(plan, pieces, devs, held, sems):
    copies = []
    for slot, piece in enumerate(pieces):
        for first, count in plan.runs:
            row = QUART * devs[slot] + first
            block = row // plan.shards
            copies.append(
                pltpu.make_async_copy(
                    piece.at[pl.ds(first, count)],
                    held.at[QUART + block, pl.ds(row % plan.shards, count)],
                    sems.at[block],
                )
            )
    return copies


def second_pieces(plan, gathered):
    ups = [gathered.at[place, pl.ds(0, QUART)] for place in range(plan.shards)]
    downs = [gathered.at[place, pl.ds(QUART, QUART)] for place in range(plan.shards)]
    return ups, downs


def start_all(copies):
    for copy in copies:
        copy.start()


def wait_bytes(part, sem):
    pltpu.make_async_copy(part, part, sem).wait()


def block_of(plan, held, index):
    return held[index].reshape(plan.width, plan.width)


def columns_of(plan, index):
    return slice(index * plan.width, (index + 1) * plan.width)


def attention_forward(plan, lengths, qkv_ref, attended_ref, probs_ref):
    width, length = plan.width, plan.length
    key_index = lax.broadcasted_iota(jnp.int32, (2 * length, length), 1)
    for item in range(plan.items):
        rows = slice(item * length, (item + 1) * length)
        valid = key_index < lengths[item]
        for pair in range(plan.pairs):
            at = pair * PAIR
            query = split_pair(qkv_ref[rows, at : at + PAIR])
            key = qkv_ref[rows, width + at : width + at + PAIR]
            value = qkv_ref[rows, 2 * width + at : 2 * width + at + PAIR]
            logits = jnp.where(valid, mm_nt(query, key) * SCALE_FACTOR, -1000000000.0)
            expo = jnp.exp(logits - jnp.max(logits, -1, keepdims=True))
            probs = expo / jnp.sum(expo, -1, keepdims=True)
            if probs_ref is not None:
                probs_ref[item * plan.pairs + pair] = probs
            attended_ref[rows, at : at + PAIR] = join_pair(mm(probs.astype(BF16), value)).astype(
                BF16
            )


def first_half(plan, inputs, lengths, vec, held, wait, normed_ref, qkv_ref, attended_ref, probs_ref, hidden_ref):
    width, length = plan.width, plan.length
    values = inputs.astype(F32)
    xhat, _ = normalised(values)
    base = xhat * vec[0:1, :] + vec[1:2, :]
    for item in range(plan.items):
        rows = slice(item * length, (item + 1) * length)
        normed_ref[rows, :] = (base[rows] + vec[12 + item : 13 + item, :]).astype(BF16)
    wait(0)
    for part, bias in enumerate((2, None, 3)):
        joined = mm(normed_ref[...], block_of(plan, held, part))
        if bias is not None:
            joined = joined + vec[bias : bias + 1, :]
        qkv_ref[:, columns_of(plan, part)] = joined.astype(BF16)
    attention_forward(plan, lengths, qkv_ref, attended_ref, probs_ref)
    wait(1)
    middle = values + (mm(attended_ref[...], block_of(plan, held, OUT)) + vec[4:5, :])
    xhat, _ = normalised(middle)
    hidden_ref[...] = (xhat * vec[5:6, :] + vec[6:7, :]).astype(BF16)
    return middle


def second_half(plan, hidden_ref, vec, held, act_ref=None, slope_ref=None, wait=None):
    total = None
    for part in range(QUART):
        if wait is not None:
            wait(part)
        pre_act = mm(hidden_ref[...], block_of(plan, held, part)) + vec[8 + part : 9 + part, :]
        act, slope = gelu_both(pre_act)
        act = act.astype(BF16)
        if act_ref is not None:
            act_ref[:, columns_of(plan, part)] = act
            slope_ref[:, columns_of(plan, part)] = slope
        if wait is not None:
            wait(QUART + part)
        term = mm(act, block_of(plan, held, QUART + part))
        total = term if total is None else total + term
    return total + vec[7:8, :]


def attention_back(plan, probs_ref, qkv_ref, grad_attended_ref, rows_ref):
    width, length = plan.width, plan.length
    for item in range(plan.items):
        rows = slice(item * length, (item + 1) * length)
        for pair in range(plan.pairs):
            at = pair * PAIR
            query = split_pair(qkv_ref[rows, at : at + PAIR])
            key = qkv_ref[rows, width + at : width + at + PAIR]
            value = qkv_ref[rows, 2 * width + at : 2 * width + at + PAIR]
            grad = split_pair(grad_attended_ref[rows, at : at + PAIR])
            probs = probs_ref[item * plan.pairs + pair]
            grad_probs = mm_nt(grad, value)
            centre = jnp.sum(grad_probs * probs, -1, keepdims=True)
            grad_logits = (probs * (grad_probs - centre)).astype(BF16)
            grad_query = join_pair(mm(grad_logits, key)) * SCALE_FACTOR
            grad_key = mm_tn(grad_logits, query) * SCALE_FACTOR
            grad_value = mm_tn(probs.astype(BF16), grad)
            rows_ref[rows, at : at + PAIR] = grad_query.astype(BF16)
            rows_ref[rows, width + at : width + at + PAIR] = grad_key.astype(BF16)
            rows_ref[rows, 2 * width + at : 2 * width + at + PAIR] = grad_value.astype(BF16)


def column_sum(values):
    return jnp.sum(values.astype(F32), 0, keepdims=True)


def attend_kernel(plan, lengths, flag, devs, x_ref, vec, *refs):
    pieces, (middle_ref, hidden_ref, held, normed, qkv, attended, sems) = refs[:-7], refs[-7:]
    start_all(first_copies(plan, pieces, devs, held, sems.at[0], pl.ds(0, OUT)))
    start_all(first_copies(plan, pieces, devs, held, sems.at[1], pl.ds(OUT, 1)))

    def wait(group):
        blocks = pl.ds(OUT, 1) if group else pl.ds(0, OUT)
        wait_bytes(held.at[blocks], sems.at[group])

    middle_ref[...] = first_half(
        plan, x_ref[...], lengths, vec, held, wait, normed, qkv, attended, None, hidden_ref
    )


def mlp_kernel(plan, middle_ref, hidden_ref, vec, gathered, y_ref, held, sems, down_sems):
    (ups, downs), devs = second_pieces(plan, gathered), plan.order
    start_all(block_copies(ups, devs, held, sems.at[0], pl.ds(0, 1)))
    start_all(down_copies(plan, downs, devs, held, down_sems))
    for part in range(1, QUART):
        start_all(block_copies(ups, devs, held, sems.at[part], pl.ds(part, 1)))

    def wait(block):
        sem = sems.at[block] if block < QUART else down_sems.at[block - QUART]
        wait_bytes(held.at[block], sem)

    total = second_half(plan, hidden_ref, vec, held, wait=wait)
    y_ref[...] = (middle_ref[...] + total).astype(BF16)


def load_kernel(plan, devs, after, gathered, *refs):
    firsts, (held1, held2, sems, down_sems) = refs[:-4], refs[-4:]
    ups, downs = second_pieces(plan, gathered)
    start_all(first_copies(plan, firsts, devs, held1, sems.at[0], pl.ds(0, FIRST)))
    start_all(block_copies(ups, plan.order, held2, sems.at[1], pl.ds(0, QUART)))
    start_all(down_copies(plan, downs, plan.order, held2, down_sems))
    wait_bytes(held1, sems.at[0])
    wait_bytes(held2.at[pl.ds(0, QUART)], sems.at[1])
    for part in range(QUART):
        wait_bytes(held2.at[QUART + part], down_sems.at[part])


def chain_kernel(
    plan, lengths, flag, x_ref, recv_ref, cot_ref, vec, held1, held2,
    y_ref, dx_ref, hidden, act, slope, *refs,
):
    outs, (xin_ref, normed, qkv, attended, middle, probs, grad_attended, grad_rows, sems) = refs[:6], refs[6:]
    kept = (xin_ref, normed, qkv, attended, middle, probs)
    copies = [
        pltpu.make_async_copy(source, target, sems.at[index])
        for index, (source, target) in enumerate(zip(kept, outs))
    ]
    xin_ref[...] = jnp.where(flag[0] == 0, x_ref[...], recv_ref[...])
    middle[...] = first_half(
        plan, xin_ref[...], lengths, vec, held1, lambda group: None, normed, qkv, attended, probs, hidden
    )
    start_all(copies)
    y_ref[...] = (middle[...] + second_half(plan, hidden, vec, held2, act, slope)).astype(BF16)
    branch = cot_ref[...]
    grad_hidden = None
    for part in range(QUART):
        grad_act = mm_nt(branch, block_of(plan, held2, QUART + part))
        grad_pre = (slope[:, columns_of(plan, part)] * grad_act).astype(BF16)
        term = mm_nt(grad_pre, block_of(plan, held2, part))
        grad_hidden = term if grad_hidden is None else grad_hidden + term
    xhat, rstd = normalised(middle[...])
    grad_middle = branch.astype(F32) + norm_back(grad_hidden, xhat, rstd, vec[5:6, :])
    grad_attended[...] = mm_nt(grad_middle.astype(BF16), block_of(plan, held1, OUT)).astype(BF16)
    attention_back(plan, probs, qkv, grad_attended, grad_rows)
    grad_normed = None
    for part in range(OUT):
        term = mm_nt(grad_rows[:, columns_of(plan, part)], block_of(plan, held1, part))
        grad_normed = term if grad_normed is None else grad_normed + term
    xhat, rstd = normalised(xin_ref[...].astype(F32))
    dx_ref[...] = (grad_middle + norm_back(grad_normed, xhat, rstd, vec[0:1, :])).astype(BF16)
    for copy in copies:
        copy.wait()


class Stage:
    def __init__(self, plan, stage, sems):
        self.plan, self.stage, self.sems, self.sent = plan, stage, sems, 0

    def put(self, value, copies_of):
        slot = self.sent % 2
        if self.sent >= 2:
            wait_bytes(self.stage.at[slot], self.sems.at[slot])
        self.sent += 1
        plan = self.plan
        self.stage[slot] = value.astype(BF16).reshape(plan.shards, plan.rows, plan.width)
        start_all(copies_of(self.stage.at[slot], self.sems.at[slot]))

    def drain(self):
        for slot in range(min(2, self.sent)):
            wait_bytes(self.stage.at[slot], self.sems.at[slot])


def mlp_back_kernel(
    plan, flag, arr_ref, cot_ref, held2, hidden, act, slope,
    grad_hidden_ref, small_ref, grads, grad_pre_ref, stage, stage_sems,
):
    branch = jnp.where(flag[0] == 0, arr_ref[...], cot_ref[...])
    small_ref[...] = jnp.zeros_like(small_ref)
    small_ref[7:8, :] = column_sum(branch)
    out = Stage(plan, stage, stage_sems)

    def copies_of_up(part):
        def copies(source, sem):
            return [
                pltpu.make_async_copy(source.at[device], grads.at[place, part], sem)
                for place, device in enumerate(plan.order)
            ]

        return copies

    def copies_of_down(part):
        def copies(source, sem):
            made = []
            for place, device in enumerate(plan.order):
                for first, count in plan.runs:
                    block, row = divmod(QUART * device + first, plan.shards)
                    if block == part:
                        made.append(
                            pltpu.make_async_copy(
                                source.at[pl.ds(row, count)],
                                grads.at[place, pl.ds(QUART + first, count)],
                                sem,
                            )
                        )
            return made

        return copies

    grad_hidden = None
    for part in range(QUART):
        columns = columns_of(plan, part)
        grad_act = mm_nt(branch, block_of(plan, held2, QUART + part))
        grad_pre = (slope[:, columns] * grad_act).astype(BF16)
        grad_pre_ref[:, columns] = grad_pre
        small_ref[8 + part : 9 + part, :] = column_sum(grad_pre)
        term = mm_nt(grad_pre, block_of(plan, held2, part))
        grad_hidden = term if grad_hidden is None else grad_hidden + term
        out.put(mm_tn(act[:, columns], branch), copies_of_down(part))
    grad_hidden_ref[...] = grad_hidden
    for part in range(QUART):
        out.put(mm_tn(hidden[...], grad_pre_ref[:, columns_of(plan, part)]), copies_of_up(part))
    out.drain()


def slot_copies(plan, devs, grads, block):
    each = plan.shards // plan.parts

    def copies(source, sem):
        return [
            pltpu.make_async_copy(
                source.at[devs[slot]],
                grads[slot // each].at[slot % each, pl.ds(block * plan.rows, plan.rows)],
                sem,
            )
            for slot in range(plan.shards)
        ]

    return copies


def pack_sums(plan, lead, many, sums, stack, lines):
    rows, width = plan.rows, plan.width
    across = width // rows
    groups = pl.cdiv(many, across)
    high = groups * across
    leads = many - 12
    entry = lax.broadcasted_iota(jnp.int32, (high - 12, width), 0)
    table = jnp.zeros((high - 12, width), F32)
    for item in range(plan.items):
        table = table + jnp.where(entry == lead[item], sums[12 + item : 13 + item], 0.0)
    top, ups = sums[:8], sums[8:12]
    for device in range(plan.shards):
        columns = slice(device * rows, (device + 1) * rows)
        line, place = divmod(QUART * device * rows, width)
        parts = [
            ups[line : line + 1, place + part * rows : place + (part + 1) * rows]
            for part in range(QUART)
        ]
        share = jnp.concatenate([top[:, columns], *parts, table[:, columns]], 0)
        stack[device * high : (device + 1) * high, :] = share.astype(BF16)
    entry = lax.broadcasted_iota(jnp.int32, (rows, width), 0)
    column = lax.broadcasted_iota(jnp.int32, (rows, width), 1)
    tile = jnp.where(lax.rem(column, rows) == entry, 1.0, 0.0).astype(BF16)
    line = lax.broadcasted_iota(jnp.int32, (high, width), 0)
    lane = lax.broadcasted_iota(jnp.int32, (high, width), 1)
    place = lax.rem(line, across) * rows
    chosen = (lane >= place) & (lane < place + rows)
    lines[...] = jnp.zeros_like(lines)
    for device in range(plan.shards):
        spread = mm(stack[device * high : (device + 1) * high, :], tile)
        spread = jnp.where(chosen, spread, 0.0).reshape(groups, across, width)
        lines[device, 0:groups, :] = jnp.sum(spread, 1)


def rest_kernel(
    plan, many, flag, devs, lead, arr_ref, cot_ref, grad_hidden_ref, small_in, vec, *refs,
):
    kept_in, pieces, refs = refs[:6], refs[6 : 6 + plan.shards], refs[6 + plan.shards :]
    dx_ref, small_ref = refs[:2]
    grads, refs = refs[2 : 2 + plan.parts], refs[2 + plan.parts :]
    kept, refs = refs[:6], refs[6:]
    held, grad_middle_ref, grad_attended, grad_rows, sems, kept_sems, stage, stage_sems, out_sem, stack, lines, packed = refs
    xin_ref, normed, qkv, attended, middle_ref, probs = kept
    start_all(first_copies(plan, pieces, devs, held, sems.at[1], pl.ds(OUT, 1)))
    copies = [
        pltpu.make_async_copy(source, target, kept_sems.at[index])
        for index, (source, target) in enumerate(zip(kept_in, kept))
    ]
    for index in (4, 3, 2, 5, 1, 0):
        copies[index].start()
    start_all(first_copies(plan, pieces, devs, held, sems.at[0], pl.ds(0, OUT)))
    length = plan.length
    branch = jnp.where(flag[0] == 0, arr_ref[...], cot_ref[...])
    out = Stage(plan, stage, stage_sems)
    small_ref[...] = small_in[...]
    grad_hidden = grad_hidden_ref[...]
    copies[4].wait()
    xhat, rstd = normalised(middle_ref[...])
    small_ref[5:6, :] = column_sum(grad_hidden * xhat)
    small_ref[6:7, :] = column_sum(grad_hidden)
    grad_middle = branch.astype(F32) + norm_back(grad_hidden, xhat, rstd, vec[5:6, :])
    grad_middle_ref[...] = grad_middle
    attn_grad = grad_middle.astype(BF16)
    small_ref[4:5, :] = column_sum(attn_grad)
    wait_bytes(held.at[pl.ds(OUT, 1)], sems.at[1])
    grad_attended[...] = mm_nt(attn_grad, block_of(plan, held, OUT)).astype(BF16)
    copies[3].wait()
    out.put(mm_tn(attended[...], attn_grad), slot_copies(plan, devs, grads, OUT))
    copies[2].wait()
    copies[5].wait()
    attention_back(plan, probs, qkv, grad_attended, grad_rows)
    copies[1].wait()
    copies[0].wait()
    wait_bytes(held.at[pl.ds(0, OUT)], sems.at[0])
    grad_normed = None
    for part in range(OUT):
        rows = grad_rows[:, columns_of(plan, part)]
        term = mm_nt(rows, block_of(plan, held, part))
        grad_normed = term if grad_normed is None else grad_normed + term
        if part != 1:
            small_ref[2 + part // 2 : 3 + part // 2, :] = column_sum(rows)
        out.put(mm_tn(normed[...], rows), slot_copies(plan, devs, grads, part))
    xhat, rstd = normalised(xin_ref[...].astype(F32))
    small_ref[0:1, :] = column_sum(grad_normed * xhat)
    small_ref[1:2, :] = column_sum(grad_normed)
    for item in range(plan.items):
        small_ref[12 + item : 13 + item, :] = column_sum(
            grad_normed[item * length : (item + 1) * length]
        )
    dx_ref[...] = grad_middle_ref[...] + norm_back(grad_normed, xhat, rstd, vec[0:1, :])
    if plan.parts == 2:
        pack_sums(plan, lead, many, small_ref[...], stack, lines)
        packed[...] = lines[...].astype(BF16)
        each = plan.shards // plan.parts
        start_all(
            [
                pltpu.make_async_copy(
                    packed.at[devs[slot]],
                    grads[slot // each].at[slot % each, pl.ds(FIRST * plan.rows, EXTRA)],
                    out_sem.at[0],
                )
                for slot in range(plan.shards)
            ]
        )
        wait_bytes(packed, out_sem.at[0])
    out.drain()


def pack_kernel(qkv_ref, out_ref, up_ref, down_ref, *refs):
    rows, width = out_ref.shape
    vectors, (up_bias, table, first_ref, second_ref, small, wide) = refs[:8], refs[8:]
    for index, vector in enumerate(vectors):
        small[index : index + 1, :] = vector[...]
    for part in range(QUART):
        small[8 + part : 9 + part, :] = up_bias[:, part * rows : (part + 1) * rows]
    many = 12 + table.shape[0]
    small[12:many, :] = table[...]
    across = width // rows
    wide[...] = jnp.zeros_like(wide)
    for index in range(many):
        line, place = divmod(index, across)
        wide[line : line + 1, place * rows : (place + 1) * rows] = small[index : index + 1, :]
    for part in range(OUT):
        first_ref[part * rows : (part + 1) * rows, :] = qkv_ref[:, part * width : (part + 1) * width].astype(BF16)
    first_ref[OUT * rows : FIRST * rows, :] = out_ref[...].astype(BF16)
    first_ref[FIRST * rows :, :] = wide[...].astype(BF16)
    for part in range(QUART):
        second_ref[part] = up_ref[:, part * width : (part + 1) * width].astype(BF16)
        second_ref[QUART + part] = down_ref[part * rows : (part + 1) * rows, :].astype(BF16)


def vectors_kernel(plan, many, devs, *refs):
    pieces, (out_ref, lines, spread, sem) = refs[: plan.shards], refs[plan.shards :]
    rows, width = plan.rows, plan.width
    across = width // rows
    groups = pl.cdiv(many, across)
    start_all(
        [
            pltpu.make_async_copy(piece.at[pl.ds(FIRST * rows, EXTRA)], lines.at[slot], sem.at[0])
            for slot, piece in enumerate(pieces)
        ]
    )
    wait_bytes(lines, sem.at[0])
    line = lax.broadcasted_iota(jnp.int32, (across, width), 0)
    lane = lax.broadcasted_iota(jnp.int32, (across, width), 1)
    chosen = (lane >= line * rows) & (lane < (line + 1) * rows)
    for slot in range(plan.shards):
        values = lines[slot].astype(F32)
        for group in range(groups):
            at = (slot * groups + group) * across
            picked = jnp.where(chosen, jnp.broadcast_to(values[group : group + 1], chosen.shape), 0.0)
            spread[at : at + across, :] = picked.astype(BF16)
    source = lax.broadcasted_iota(jnp.int32, (width, rows), 0)
    target = lax.broadcasted_iota(jnp.int32, (width, rows), 1)
    fold = sum(jnp.where(source == target + place * rows, 1.0, 0.0) for place in range(across))
    narrow = mm(spread[...], fold.astype(BF16)).astype(BF16)
    entry = lax.broadcasted_iota(jnp.int32, (rows, width), 0)
    column = lax.broadcasted_iota(jnp.int32, (rows, width), 1)
    total = None
    for slot in range(plan.shards):
        at = slot * groups * across
        place = jnp.where(column == entry + devs[slot] * rows, 1.0, 0.0).astype(BF16)
        term = mm(narrow[at : at + groups * across], place)
        total = term if total is None else total + term
    out_ref[...] = total


def unpack_kernel(grads_ref, up_ref, down_ref):
    _, rows, width = grads_ref.shape
    for part in range(QUART):
        up_ref[:, part * width : (part + 1) * width] = grads_ref[part].astype(F32)
        down_ref[part * rows : (part + 1) * rows, :] = grads_ref[QUART + part].astype(F32)


def add_kernel(work, *refs):
    outs, at = refs[len(refs) - len(work) :], 0
    for (terms, first), out in zip(work, outs):
        rows = out.shape[0] // terms
        came = refs[at + 2 * terms] if first is not None else None
        for term in range(terms):
            low = term * rows
            value = refs[at][0].astype(F32) + refs[at + 1][0].astype(F32)
            if came is not None and first <= low < first + came.shape[0]:
                value = value + came[low - first : low - first + rows, :].astype(F32)
            out[low : low + rows, :] = value.astype(BF16)
            at += 2
        at += came is not None


def total_kernel(terms, many, *refs):
    pairs, (ahead, behind) = refs[: 2 * terms], refs[2 * terms : 2 * terms + 2]
    outs = refs[2 * terms + 2 :]
    high, width = pairs[0].shape[1:]

    def rows_of(low, count):
        term, first = divmod(low, high)
        value = pairs[2 * term][0, first : first + count, :].astype(F32)
        value = value + pairs[2 * term + 1][0, first : first + count, :].astype(F32)
        came = ahead[low : low + count, :].astype(F32) + behind[low : low + count, :].astype(F32)
        return value + came

    rows = (high - (EXTRA if many else 0)) // FIRST
    low = 0
    for out in outs[:2]:
        for row in range(out.shape[0] // rows):
            for column in range(out.shape[1] // width):
                out[row * rows : (row + 1) * rows, column * width : (column + 1) * width] = rows_of(low, rows)
                low += rows
    if many:
        vectors, (up_bias, table, small) = outs[2:10], outs[10:]
        lines = rows_of(low, EXTRA)
        for index in range(many):
            line, place = divmod(index, width // rows)
            small[index : index + 1, :] = lines[line : line + 1, place * rows : (place + 1) * rows]
        for index, vector in enumerate(vectors):
            vector[...] = small[index : index + 1, :]
        for part in range(QUART):
            up_bias[:, part * rows : (part + 1) * rows] = small[8 + part : 9 + part, :]
        table[...] = small[12:many, :]


SMEM = pl.BlockSpec(memory_space=pltpu.SMEM)
VMEM = pl.BlockSpec(memory_space=pltpu.VMEM)
HBM = pl.BlockSpec(memory_space=pltpu.HBM)
ANY = pl.BlockSpec(memory_space=pl.ANY)


def kept_shapes(plan):
    tokens, width = plan.tokens, plan.width
    return [
        ((tokens, width), BF16),
        ((tokens, 3 * width), BF16),
        ((tokens, width), BF16),
        ((tokens, width), F32),
        ((tokens, width), BF16),
        ((plan.items * plan.pairs, 2 * plan.length, plan.length), F32),
        ((tokens, 4 * width), BF16),
        ((tokens, 4 * width), F32),
    ]


def held_blocks(plan, blocks):
    return pltpu.VMEM((blocks, plan.shards, plan.rows, plan.width), BF16)


def call(kernel, outs, in_specs, out_specs, scratch, name, work, limit, args):
    args = [
        pltpu.with_memory_space_constraint(arg, pltpu.HBM) if spec is HBM else arg
        for arg, spec in zip(args, in_specs)
    ]
    return pl.pallas_call(
        kernel,
        out_shape=outs,
        in_specs=in_specs,
        out_specs=out_specs,
        scratch_shapes=scratch,
        compiler_params=pltpu.CompilerParams(vmem_limit_bytes=limit * 1024 * 1024),
        cost_estimate=pl.CostEstimate(flops=2 * work[0], bytes_accessed=work[1], transcendentals=0),
        name=name,
    )(*args)


def of(shape):
    return jax.ShapeDtypeStruct(*shape)


def inside(shape):
    return pltpu.VMEM(*shape)


def run_attend(plan, lengths, flag, devs, x, vec, pieces):
    kept = kept_shapes(plan)
    block = plan.width * plan.width
    return call(
        functools.partial(attend_kernel, plan),
        [of(kept[3]), of(kept[4])],
        [SMEM, SMEM, SMEM, VMEM, VMEM] + [HBM] * len(pieces),
        [VMEM, VMEM],
        [held_blocks(plan, FIRST)] + [inside(shape) for shape in kept[:3]] + [pltpu.SemaphoreType.DMA((2,))],
        "attend",
        (FIRST * block * plan.tokens, FIRST * block * 2),
        14,
        (lengths, flag, devs, x, vec, *pieces),
    )


def run_vectors(plan, many, devs, pieces):
    groups = pl.cdiv(many, plan.width // plan.rows) * (plan.width // plan.rows)
    return call(
        functools.partial(vectors_kernel, plan, many),
        jax.ShapeDtypeStruct((groups, plan.width), F32),
        [SMEM] + [HBM] * len(pieces),
        VMEM,
        [
            pltpu.VMEM((plan.shards, EXTRA, plan.width), BF16),
            pltpu.VMEM((plan.shards * groups, plan.width), BF16),
            pltpu.SemaphoreType.DMA((1,)),
        ],
        "vectors",
        (plan.width * plan.width * plan.rows, plan.width * plan.width * 4),
        12,
        (devs, *pieces),
    )


def run_mlp(plan, middle, hidden, vec, gathered):
    block = plan.width * plan.width
    return call(
        functools.partial(mlp_kernel, plan),
        jax.ShapeDtypeStruct(hidden.shape, BF16),
        [VMEM, VMEM, VMEM, HBM],
        VMEM,
        [held_blocks(plan, SECOND), pltpu.SemaphoreType.DMA((QUART,)), pltpu.SemaphoreType.DMA((QUART,))],
        "mlp",
        (SECOND * block * plan.tokens, SECOND * block * 2),
        16,
        (middle, hidden, vec, gathered),
    )


def run_load(plan, devs, after, firsts, gathered):
    block = plan.width * plan.width
    return call(
        functools.partial(load_kernel, plan),
        [held_blocks(plan, FIRST), held_blocks(plan, SECOND)],
        [SMEM, ANY] + [HBM] * (1 + len(firsts)),
        [VMEM, VMEM],
        [pltpu.SemaphoreType.DMA((2,)), pltpu.SemaphoreType.DMA((QUART,))],
        "load",
        (0, (FIRST + SECOND) * block * 4),
        2,
        (devs, after, gathered, *firsts),
    )


def run_chain(plan, lengths, flag, x, recv, cot, vec, held1, held2):
    shapes = kept_shapes(plan)
    block = plan.width * plan.width
    rest = [shapes[index] for index in (0, 0, 1, 2, 3, 5)]
    return call(
        functools.partial(chain_kernel, plan),
        [of(shapes[0]), of(shapes[0])]
        + [inside(shapes[index]) for index in (4, 6, 7)]
        + [pltpu.HBM(*shape) for shape in rest],
        [SMEM] * 2 + [VMEM] * 6,
        [VMEM] * 5 + [HBM] * len(rest),
        [inside(shape) for shape in rest]
        + [inside(shapes[0]), inside(shapes[1]), pltpu.SemaphoreType.DMA((len(rest),))],
        "chain",
        (24 * block * plan.tokens, 12 * block),
        14,
        (lengths, flag, x, recv, cot, vec, held1, held2),
    )


def grad_shapes(plan, extra=0):
    rows = FIRST * plan.rows + (extra if plan.parts == 2 else 0)
    return [pltpu.HBM((plan.shards // plan.parts, rows, plan.width), BF16)] * plan.parts


def stage_scratch(plan):
    return [
        pltpu.VMEM((2, plan.shards, plan.rows, plan.width), BF16),
        pltpu.SemaphoreType.DMA((2,)),
    ]


def run_mlp_back(plan, flag, arriving, cot, held2, hidden, act, slope):
    shapes = kept_shapes(plan)
    block = plan.width * plan.width
    return call(
        functools.partial(mlp_back_kernel, plan),
        [
            of(shapes[3]),
            jax.ShapeDtypeStruct((16, plan.width), F32),
            pltpu.HBM((plan.shards, SECOND, plan.rows, plan.width), BF16),
        ],
        [SMEM] + [VMEM] * 6,
        [VMEM, VMEM, HBM],
        [inside(shapes[6])] + stage_scratch(plan),
        "mlp_back",
        (2 * SECOND * block * plan.tokens, SECOND * block * 2),
        10,
        (flag, arriving, cot, held2, hidden, act, slope),
    )


def run_rest(plan, many, flag, devs, lead, arriving, cot, grad_hidden, small, vec, kept, pieces):
    shapes = kept_shapes(plan)
    block = plan.width * plan.width
    across = plan.width // plan.rows
    high = pl.cdiv(many, across) * across
    lines = (plan.shards, EXTRA, plan.width)
    rest = [shapes[index] for index in (0, 0, 1, 2, 3, 5)]
    input_grad, small, *grads = call(
        functools.partial(rest_kernel, plan, many),
        [of(shapes[3]), jax.ShapeDtypeStruct((16, plan.width), F32)] + grad_shapes(plan, EXTRA),
        [SMEM] * 3 + [VMEM] * 5 + [HBM] * (len(rest) + len(pieces)),
        [VMEM] * 2 + [HBM] * plan.parts,
        [inside(shape) for shape in rest]
        + [held_blocks(plan, FIRST)]
        + [inside(shapes[index]) for index in (3, 0, 1)]
        + [pltpu.SemaphoreType.DMA((2,)), pltpu.SemaphoreType.DMA((len(rest),))]
        + stage_scratch(plan)
        + [pltpu.SemaphoreType.DMA((1,)), pltpu.VMEM((plan.shards * high, plan.rows), BF16)]
        + [pltpu.VMEM(lines, F32), pltpu.VMEM(lines, BF16)],
        "rest",
        (2 * FIRST * block * plan.tokens, 2 * FIRST * block * 2),
        26,
        (flag, devs, lead, arriving, cot, grad_hidden, small, vec, *kept, *pieces),
    )
    return input_grad, small, grads


def run_add(work, beside):
    specs, args, plans, outs = [], [], [], []
    for slot, terms, came in work:
        _, rows, width = terms[0][0].shape
        for pair in terms:
            one = pl.BlockSpec((1, rows, width), lambda index, slot=slot: (slot, 0, 0))
            specs += [one, one]
            args += [pltpu.with_memory_space_constraint(array, pltpu.HBM) for array in pair]
        first = None
        if came is not None:
            specs.append(pl.BlockSpec(came.shape, lambda index: (0, 0)))
            args.append(came)
            alone = came.shape[0] == len(terms) * rows
            first = 0 if alone or not outs else rows
        plans.append((len(terms), first))
        outs.append((len(terms) * rows, width))
    kernel = functools.partial(add_kernel, plans)
    return pl.pallas_call(
        lambda *refs: kernel(*refs[len(beside) :]),
        out_shape=[jax.ShapeDtypeStruct(shape, BF16) for shape in outs],
        grid=(1,),
        in_specs=[ANY] * len(beside) + specs,
        out_specs=[pl.BlockSpec(shape, lambda index: (0, 0)) for shape in outs],
        compiler_params=pltpu.CompilerParams(vmem_limit_bytes=14 * 1024 * 1024),
        name="add",
    )(*beside, *args)


def run_total(one, many, shapes):
    args = [
        pltpu.with_memory_space_constraint(array, pltpu.HBM) for pair in one.terms for array in pair
    ]
    _, rows, width = args[0].shape
    first = pl.BlockSpec((1, rows, width), lambda index: (0, 0, 0))
    whole = pl.BlockSpec((len(one.terms) * rows, width), lambda index: (0, 0))
    return pl.pallas_call(
        functools.partial(total_kernel, len(one.terms), many),
        out_shape=[jax.ShapeDtypeStruct(shape, F32) for shape in shapes],
        grid=(1,),
        in_specs=[first] * len(args) + [whole] * 2,
        out_specs=[pl.BlockSpec(shape, lambda index: (0, 0)) for shape in shapes],
        scratch_shapes=[pltpu.VMEM((many, shapes[2][1]), F32)] if many else [],
        compiler_params=pltpu.CompilerParams(vmem_limit_bytes=14 * 1024 * 1024),
        name="total",
    )(*args, *one.carried)


def after(value, *others):
    return lax.optimization_barrier((value, *others))[0]


def shifted(value, axis, steps):
    count = lax.axis_size(axis)
    first, last = (max(0, -steps), min(count, count - steps))
    return lax.ppermute(value, axis, [(source, source + steps) for source in range(first, last)])


class Ring:
    def __init__(self, count):
        self.count, self.chips = count, count // 2
        self.walk = list(range(0, self.chips, 2)) + list(range(self.chips - 1, 0, -2))
        self.order = [2 * chip + core for chip in self.walk for core in range(2)]
        after = self.walk[1:] + self.walk[:1]
        self.onward = [
            (2 * here + core, 2 * there + core)
            for here, there in zip(self.walk, after)
            for core in range(2)
        ]
        self.back = [(there, here) for here, there in self.onward]
        self.sibling = [(index, index ^ 1) for index in range(count)]

    def slots(self):
        index = lax.axis_index("dp")
        chip, core = index // 2, index % 2
        place_of = lambda chip: jnp.where(chip % 2 == 0, chip // 2, self.chips - 1 - chip // 2)
        steps = jnp.arange(self.chips, dtype=jnp.int32)
        ahead = (place_of(chip) + steps) % self.chips
        chips = jnp.where(ahead < (self.chips + 1) // 2, 2 * ahead, 2 * (self.chips - 1 - ahead) + 1)
        devs = jnp.concatenate([2 * chips + core, 2 * chips + 1 - core]).astype(jnp.int32)
        return devs

    def step(self, ahead, behind):
        return lax.ppermute(ahead, "dp", self.onward), lax.ppermute(behind, "dp", self.back)

    def gather(self, shard):
        half = self.chips // 2
        own = [shard] + [None] * (self.chips - 1)
        ahead = behind = shard
        for step in range(1, half):
            ahead, behind = self.step(ahead, behind)
            own[self.chips - step], own[step] = ahead, behind
            ahead, behind = lax.optimization_barrier((ahead, behind))
        own[half] = lax.ppermute(ahead, "dp", self.onward)
        return own

    def siblings(self, pieces):
        return [lax.ppermute(piece, "dp", self.sibling) for piece in pieces]


class RingSum:
    def __init__(self, ring, terms):
        self.ring, self.terms = ring, terms
        self.time = ring.chips // 2
        self.carried = [None, None]

    def add(self, *beside):
        opposite = self.time == self.ring.chips // 2
        work = []
        for way in range(2):
            slot = self.time if way == 0 else self.ring.chips - self.time
            terms = self.terms
            if opposite:
                terms = self.terms[way : way + 1]
            if terms:
                work.append((way, slot, terms, self.carried[way]))
        sums = run_add([entry[1:] for entry in work], beside)
        for entry, value in zip(work, sums):
            self.carried[entry[0]] = value
        return sums[0]

    def send(self):
        for way, route in enumerate((self.ring.onward, self.ring.back)):
            if self.carried[way] is not None:
                self.carried[way] = lax.ppermute(self.carried[way], "dp", route)
        self.time -= 1


def body(
    block_input, cotangent, lengths, leads,
    norm_gain1, norm_bias1, lead_table, qkv_weight, query_bias, value_bias, out_weight, out_bias,
    norm_gain2, norm_bias2, up_weight, up_bias, down_weight, down_bias,
):
    count = lax.axis_size("dp")
    micro, local, length, width = block_input.shape
    items = micro * local
    rows = width // count
    leads_count = lead_table.shape[2]
    flag = lax.axis_index("section").astype(jnp.int32).reshape(1)
    flat = lambda value: value.reshape(items * length, width)
    x, cot = flat(block_input), flat(cotangent)
    lens, lead = lengths.reshape(items), leads.reshape(items)

    vectors = (
        norm_gain1, norm_bias1, query_bias, value_bias, out_bias, norm_gain2, norm_bias2, down_bias
    )
    many = 12 + leads_count
    aligned = rows % 16 == 0 and count % 4 == 0 and pl.cdiv(many, width // rows) <= EXTRA
    if aligned:
        ring = Ring(count)
        first, second = pl.pallas_call(
            pack_kernel,
            out_shape=[jax.ShapeDtypeStruct((FIRST * rows + EXTRA, width), BF16)]
            + [jax.ShapeDtypeStruct((SECOND, rows, width), BF16)],
            scratch_shapes=[pltpu.VMEM((many, rows), F32), pltpu.VMEM((EXTRA, width), F32)],
            name="pack",
        )(qkv_weight[0], out_weight[0], up_weight[0], down_weight[0], *vectors, up_bias, lead_table[0].T)
        gathered = lax.all_gather(second, "dp", axis=0, tiled=True, axis_index_groups=[ring.order])
        gathered = gathered.reshape(count, SECOND, rows, width)
        firsts = ring.gather(first)
        firsts = firsts + ring.siblings(firsts)
        devs = ring.slots()
        plan = Plan(ring.order, rows, items, length, width)
        wide = run_vectors(plan, many, devs, firsts)
    else:
        wide_blocks = lambda value: value[0].reshape(rows, -1, width).transpose(1, 0, 2)
        packed = jnp.concatenate(
            [wide_blocks(qkv_weight), out_weight, wide_blocks(up_weight), down_weight.reshape(QUART, rows, width)], 0
        )
        everything = lax.all_gather(packed.astype(BF16), "dp", axis=0)
        across_blocks = lambda value: value.transpose(1, 0, 2, 3).reshape(-1, width, width)
        firsts = [across_blocks(everything[:, :FIRST])]
        gathered = jnp.concatenate(
            [
                across_blocks(everything[:, FIRST : FIRST + QUART]),
                everything[:, FIRST + QUART :].reshape(QUART, width, width),
            ],
            0,
        )[None]
        devs = jnp.zeros((1,), jnp.int32)
        plan = Plan([0], width, items, length, width)
        small = jnp.concatenate([*vectors, up_bias.reshape(4, rows), lead_table[0].T], 0).astype(BF16)
        wide = lax.all_gather(small, "dp", axis=1, tiled=True).astype(F32)

    vec = jnp.concatenate(
        [wide[:8], wide[8:12].reshape(4, count, rows).transpose(1, 0, 2).reshape(4, width)]
        + [lax.dynamic_slice_in_dim(wide, 12 + lead[item], 1, 0) for item in range(items)]
        + [jnp.zeros((4 - items, width), F32)],
        0,
    )

    middle, hidden = run_attend(plan, lens, flag, devs, x, vec, firsts)
    first_out = run_mlp(plan, middle, hidden, vec, gathered)
    recv = shifted(first_out, "section", 1)
    held1, held2 = run_load(plan, devs, first_out, firsts, gathered)
    output, first_grad, hidden, act, slope, *kept = run_chain(
        plan, lens, flag, x, recv, cot, vec, held1, held2
    )
    arriving = shifted(first_grad, "section", -1)
    grad_hidden, sums, grads2 = run_mlp_back(plan, flag, arriving, cot, held2, hidden, act, slope)
    input_grad, sums, grads1 = run_rest(
        plan, many, flag, devs, lead, arriving, cot, grad_hidden, sums, vec, kept, firsts
    )
    if aligned:
        first_sum = RingSum(ring, [(grads1[0], *ring.siblings(grads1[1:]))])
        while first_sum.time:
            first_sum.add()
            first_sum.send()
        grads2 = lax.psum_scatter(
            grads2.reshape(count * SECOND, rows, width),
            "dp", scatter_dimension=0, tiled=True, axis_index_groups=[ring.order],
        )
        grad_up, grad_down = pl.pallas_call(
            unpack_kernel,
            out_shape=[
                jax.ShapeDtypeStruct((rows, QUART * width), F32),
                jax.ShapeDtypeStruct((QUART * rows, width), F32),
            ],
            name="unpack",
        )(grads2)
        grad_qkv, grad_out, *small_grads = run_total(
            first_sum, many,
            [(rows, OUT * width), (rows, width)] + [(1, rows)] * 8 + [(1, QUART * rows), (leads_count, rows)],
        )
    else:
        split = lambda value: value[0].reshape(-1, count, rows, width).transpose(1, 0, 2, 3)
        grads = jnp.concatenate(
            [
                split(grads1[0]),
                split(grads2[0, :QUART].reshape(1, QUART * width, width)),
                grads2[0, QUART:].reshape(count, QUART, rows, width),
            ],
            1,
        )
        grads = lax.psum_scatter(grads, "dp", scatter_dimension=0, tiled=False).astype(F32)
        across = lambda value: value.transpose(1, 0, 2).reshape(rows, -1)
        grad_qkv, grad_out = across(grads[:OUT]), grads[OUT]
        grad_up = across(grads[FIRST : FIRST + QUART])
        grad_down = grads[FIRST + QUART :].reshape(QUART * rows, width)
        hot = (jnp.arange(leads_count)[:, None] == lead[None, :]).astype(F32)
        table = sum(hot[:, item : item + 1] * sums[12 + item : 13 + item] for item in range(items))
        up_sums = sums[8:12].reshape(count, 4, rows).transpose(1, 0, 2).reshape(4, width)
        spread = lax.psum_scatter(
            jnp.concatenate([sums[:8], up_sums, table], 0), "dp", scatter_dimension=1, tiled=True
        )
        small_grads = [spread[index : index + 1] for index in range(8)]
        small_grads += [spread[8:12].reshape(1, 4 * rows), spread[12:]]
    vector = small_grads
    shape = (1, micro, local, length, width)
    return (
        output.reshape(shape),
        input_grad.reshape(shape),
        vector[0],
        vector[1],
        vector[9].T[None],
        grad_qkv[None],
        vector[2],
        vector[3],
        grad_out[None],
        vector[4],
        vector[5],
        vector[6],
        grad_up[None],
        vector[8],
        grad_down[None],
        vector[7],
    )


def solution(mesh):
    weights = (
        P("section", "dp"),
        P("section", "dp"),
        P("section", "dp", None),
        P("section", "dp", None),
        P("section", "dp"),
        P("section", "dp"),
        P("section", "dp", None),
        P("section", "dp"),
        P("section", "dp"),
        P("section", "dp"),
        P("section", "dp", None),
        P("section", "dp"),
        P("section", "dp", None),
        P("section", "dp"),
    )
    rows = P(None, "dp", None, None)
    layers = P("section", None, "dp", None, None)
    return jax.shard_map(
        body,
        mesh=mesh,
        in_specs=(rows, rows, P(None, "dp"), P(None, "dp")) + weights,
        out_specs=(layers, layers) + weights,
        check_vma=False,
    )
```

```python
import functools

import jax
import jax.numpy as jnp
from jax import lax
from jax.experimental import pallas as pl
from jax.experimental.pallas import tpu as pltpu
from jax.sharding import PartitionSpec as P

HEAD = 64
PAIR = 2 * HEAD
EPS = 1e-06
SCALE_FACTOR = 0.125
GELU_A = 0.7978845608028654
GELU_B = 0.044715
F32 = jnp.float32
BF16 = jnp.bfloat16
OUT = 3
FIRST = 4
SECOND = 8
QUART = 4
EXTRA = 16
LOW = 2


def mm(left, right):
    return jnp.dot(left, right, preferred_element_type=F32)


def mm_nt(left, right):
    return lax.dot_general(left, right, (((1,), (1,)), ((), ())), preferred_element_type=F32)


def mm_tn(left, right):
    return lax.dot_general(left, right, (((0,), (0,)), ((), ())), preferred_element_type=F32)


def normalised(values):
    mean = jnp.mean(values, -1, keepdims=True)
    centred = values - mean
    variance = jnp.mean(centred * centred, -1, keepdims=True)
    rstd = lax.rsqrt(variance + EPS)
    return centred * rstd, rstd


def norm_back(grad, xhat, rstd, gain):
    scaled = grad * gain
    first = jnp.mean(scaled, -1, keepdims=True)
    second = jnp.mean(scaled * xhat, -1, keepdims=True)
    return rstd * (scaled - first - xhat * second)


def gelu_both(values):
    square = values * values
    slope = GELU_A * (1.0 + 3.0 * GELU_B * square)
    bend = jnp.tanh(GELU_A * values * (1.0 + GELU_B * square))
    half = 0.5 * (1.0 + bend)
    return values * half, half + 0.5 * values * (1.0 - bend * bend) * slope


def split_pair(rows):
    lane = lax.broadcasted_iota(jnp.int32, rows.shape, 1)
    zero = jnp.zeros_like(rows)
    return jnp.concatenate(
        [jnp.where(lane < HEAD, rows, zero), jnp.where(lane < HEAD, zero, rows)], 0
    )


def join_pair(stacked):
    count = stacked.shape[0] // 2
    lane = lax.broadcasted_iota(jnp.int32, (count, PAIR), 1)
    return jnp.where(lane < HEAD, stacked[:count], stacked[count:])


class Plan:
    def __init__(self, order, rows, items, length, width):
        self.order, self.shards, self.rows = order, len(order), rows
        self.items, self.length, self.width = items, length, width
        self.tokens = items * length
        self.low = LOW * rows
        self.pairs = width // PAIR
        whole = self.shards % QUART == 0
        self.runs = [(0, QUART)] if whole else [(block, 1) for block in range(QUART)]
        self.parts = 2 if self.shards > 1 else 1


def slot_pieces(plan, refs):
    if plan.shards == 1:
        return [[(0, refs[0])]]
    refs, slots, half = list(refs), [], plan.shards // 4
    for slot in range(plan.shards):
        parts = [(0, refs.pop(0))]
        if slot % (plan.shards // 2) == half:
            parts.append((plan.low, refs.pop(0)))
        slots.append(parts)
    return slots


def piece_rows(parts, row, count):
    start, ref = [part for part in parts if part[0] <= row][-1]
    return ref.at[pl.ds(row - start, count)]


def first_copies(plan, refs, devs, held, sem, blocks):
    if plan.shards == 1:
        return block_copies(refs, devs, held, sem, blocks)
    return [
        pltpu.make_async_copy(
            piece_rows(parts, block * plan.rows, plan.rows), held.at[block, devs[slot]], sem
        )
        for slot, parts in enumerate(slot_pieces(plan, refs))
        for block in range(blocks.start, blocks.start + blocks.size)
    ]


def block_copies(pieces, devs, held, sem, blocks, at=0):
    return [
        pltpu.make_async_copy(
            piece.at[blocks], held.at[pl.ds(at + blocks.start, blocks.size), devs[slot]], sem
        )
        for slot, piece in enumerate(pieces)
    ]


def down_copies(plan, pieces, devs, held, sems):
    copies = []
    for slot, piece in enumerate(pieces):
        for first, count in plan.runs:
            block, row = divmod(QUART * devs[slot] + first, plan.shards)
            copy = pltpu.make_async_copy(
                piece.at[pl.ds(first, count)],
                held.at[QUART + block, pl.ds(row, count)],
                sems.at[block],
            )
            copies.append((block, copy))
    return copies


def second_pieces(plan, gathered):
    ups = [gathered.at[place, pl.ds(0, QUART)] for place in range(plan.shards)]
    downs = [gathered.at[place, pl.ds(QUART, QUART)] for place in range(plan.shards)]
    return ups, downs


def start_all(copies):
    for copy in copies:
        copy.start()


def wait_bytes(part, sem):
    pltpu.make_async_copy(part, part, sem).wait()


def block_of(plan, held, index):
    return held[index].reshape(plan.width, plan.width)


def columns_of(plan, index):
    return slice(index * plan.width, (index + 1) * plan.width)


def attention_forward(plan, lengths, qkv_ref, attended_ref, probs_ref):
    width, length = plan.width, plan.length
    key_index = lax.broadcasted_iota(jnp.int32, (2 * length, length), 1)
    for item in range(plan.items):
        rows = slice(item * length, (item + 1) * length)
        valid = key_index < lengths[item]
        for pair in range(plan.pairs):
            at = pair * PAIR
            query = split_pair(qkv_ref[rows, at : at + PAIR])
            key = qkv_ref[rows, width + at : width + at + PAIR]
            value = qkv_ref[rows, 2 * width + at : 2 * width + at + PAIR]
            logits = jnp.where(valid, mm_nt(query, key) * SCALE_FACTOR, -1000000000.0)
            expo = jnp.exp(logits - jnp.max(logits, -1, keepdims=True))
            probs = expo / jnp.sum(expo, -1, keepdims=True)
            if probs_ref is not None:
                probs_ref[item * plan.pairs + pair] = probs
            attended_ref[rows, at : at + PAIR] = join_pair(mm(probs.astype(BF16), value)).astype(
                BF16
            )


def first_half(plan, inputs, lengths, vec, held, wait, normed_ref, qkv_ref, attended_ref, probs_ref, hidden_ref):
    width, length = plan.width, plan.length
    values = inputs.astype(F32)
    xhat, _ = normalised(values)
    base = xhat * vec[0:1, :] + vec[1:2, :]
    for item in range(plan.items):
        rows = slice(item * length, (item + 1) * length)
        normed_ref[rows, :] = (base[rows] + vec[12 + item : 13 + item, :]).astype(BF16)
    wait(0)
    for part, bias in enumerate((2, None, 3)):
        joined = mm(normed_ref[...], block_of(plan, held, part))
        if bias is not None:
            joined = joined + vec[bias : bias + 1, :]
        qkv_ref[:, columns_of(plan, part)] = joined.astype(BF16)
    attention_forward(plan, lengths, qkv_ref, attended_ref, probs_ref)
    wait(1)
    middle = values + (mm(attended_ref[...], block_of(plan, held, OUT)) + vec[4:5, :])
    xhat, _ = normalised(middle)
    hidden_ref[...] = (xhat * vec[5:6, :] + vec[6:7, :]).astype(BF16)
    return middle


def second_half(plan, hidden_ref, vec, held, act_ref=None, slope_ref=None, wait=None):
    total = None
    for part in range(QUART):
        if wait is not None:
            wait(part)
        pre_act = mm(hidden_ref[...], block_of(plan, held, part)) + vec[8 + part : 9 + part, :]
        act, slope = gelu_both(pre_act)
        act = act.astype(BF16)
        if act_ref is not None:
            act_ref[:, columns_of(plan, part)] = act
            slope_ref[:, columns_of(plan, part)] = slope
        if wait is not None:
            wait(QUART + part)
        term = mm(act, block_of(plan, held, QUART + part))
        total = term if total is None else total + term
    return total + vec[7:8, :]


def attention_back(plan, probs_ref, qkv_ref, grad_attended_ref, rows_ref):
    width, length = plan.width, plan.length
    for item in range(plan.items):
        rows = slice(item * length, (item + 1) * length)
        for pair in range(plan.pairs):
            at = pair * PAIR
            query = split_pair(qkv_ref[rows, at : at + PAIR])
            key = qkv_ref[rows, width + at : width + at + PAIR]
            value = qkv_ref[rows, 2 * width + at : 2 * width + at + PAIR]
            grad = split_pair(grad_attended_ref[rows, at : at + PAIR])
            probs = probs_ref[item * plan.pairs + pair]
            grad_probs = mm_nt(grad, value)
            centre = jnp.sum(grad_probs * probs, -1, keepdims=True)
            grad_logits = (probs * (grad_probs - centre)).astype(BF16)
            grad_query = join_pair(mm(grad_logits, key)) * SCALE_FACTOR
            grad_key = mm_tn(grad_logits, query) * SCALE_FACTOR
            grad_value = mm_tn(probs.astype(BF16), grad)
            rows_ref[rows, at : at + PAIR] = grad_query.astype(BF16)
            rows_ref[rows, width + at : width + at + PAIR] = grad_key.astype(BF16)
            rows_ref[rows, 2 * width + at : 2 * width + at + PAIR] = grad_value.astype(BF16)


def column_sum(values):
    return jnp.sum(values.astype(F32), 0, keepdims=True)


def attend_kernel(plan, lengths, flag, devs, x_ref, vec, *refs):
    pieces, (middle_ref, hidden_ref, held, normed, qkv, attended, sems) = refs[:-7], refs[-7:]
    start_all(first_copies(plan, pieces, devs, held, sems.at[0], pl.ds(0, OUT)))
    start_all(first_copies(plan, pieces, devs, held, sems.at[1], pl.ds(OUT, 1)))

    def wait(group):
        blocks = pl.ds(OUT, 1) if group else pl.ds(0, OUT)
        wait_bytes(held.at[blocks], sems.at[group])

    middle_ref[...] = first_half(
        plan, x_ref[...], lengths, vec, held, wait, normed, qkv, attended, None, hidden_ref
    )


def mlp_kernel(plan, middle_ref, hidden_ref, vec, gathered, y_ref, held, sems, down_sems):
    (ups, downs), devs = second_pieces(plan, gathered), plan.order
    down = down_copies(plan, downs, devs, held, down_sems)
    for part in range(QUART):
        start_all(block_copies(ups, devs, held, sems.at[part], pl.ds(part, 1)))
        start_all([copy for block, copy in down if block == part])

    def wait(block):
        sem = sems.at[block] if block < QUART else down_sems.at[block - QUART]
        wait_bytes(held.at[block], sem)

    total = second_half(plan, hidden_ref, vec, held, wait=wait)
    y_ref[...] = (middle_ref[...] + total).astype(BF16)


def load_kernel(plan, devs, after, gathered, *refs):
    firsts, (held1, held2, sems, down_sems) = refs[:-4], refs[-4:]
    ups, downs = second_pieces(plan, gathered)
    start_all(first_copies(plan, firsts, devs, held1, sems.at[0], pl.ds(0, FIRST)))
    start_all(block_copies(ups, plan.order, held2, sems.at[1], pl.ds(0, QUART)))
    start_all([copy for _, copy in down_copies(plan, downs, plan.order, held2, down_sems)])
    wait_bytes(held1, sems.at[0])
    wait_bytes(held2.at[pl.ds(0, QUART)], sems.at[1])
    for part in range(QUART):
        wait_bytes(held2.at[QUART + part], down_sems.at[part])


def chain_kernel(
    plan, lengths, flag, x_ref, recv_ref, cot_ref, vec, held1, held2,
    y_ref, dx_ref, hidden, act, slope, *refs,
):
    outs, (xin_ref, normed, qkv, attended, middle, probs, grad_attended, grad_rows, sems) = refs[:6], refs[6:]
    kept = (xin_ref, normed, qkv, attended, middle, probs)
    copies = [
        pltpu.make_async_copy(source, target, sems.at[index])
        for index, (source, target) in enumerate(zip(kept, outs))
    ]
    xin_ref[...] = jnp.where(flag[0] == 0, x_ref[...], recv_ref[...])
    middle[...] = first_half(
        plan, xin_ref[...], lengths, vec, held1, lambda group: None, normed, qkv, attended, probs, hidden
    )
    start_all(copies)
    y_ref[...] = (middle[...] + second_half(plan, hidden, vec, held2, act, slope)).astype(BF16)
    branch = cot_ref[...]
    grad_hidden = None
    for part in range(QUART):
        grad_act = mm_nt(branch, block_of(plan, held2, QUART + part))
        grad_pre = (slope[:, columns_of(plan, part)] * grad_act).astype(BF16)
        term = mm_nt(grad_pre, block_of(plan, held2, part))
        grad_hidden = term if grad_hidden is None else grad_hidden + term
    xhat, rstd = normalised(middle[...])
    grad_middle = branch.astype(F32) + norm_back(grad_hidden, xhat, rstd, vec[5:6, :])
    grad_attended[...] = mm_nt(grad_middle.astype(BF16), block_of(plan, held1, OUT)).astype(BF16)
    attention_back(plan, probs, qkv, grad_attended, grad_rows)
    grad_normed = None
    for part in range(OUT):
        term = mm_nt(grad_rows[:, columns_of(plan, part)], block_of(plan, held1, part))
        grad_normed = term if grad_normed is None else grad_normed + term
    xhat, rstd = normalised(xin_ref[...].astype(F32))
    dx_ref[...] = (grad_middle + norm_back(grad_normed, xhat, rstd, vec[0:1, :])).astype(BF16)
    for copy in copies:
        copy.wait()


class Stage:
    def __init__(self, plan, stage, sems):
        self.plan, self.stage, self.sems, self.sent = plan, stage, sems, 0

    def put(self, value, copies_of):
        slot = self.sent % 2
        if self.sent >= 2:
            wait_bytes(self.stage.at[slot], self.sems.at[slot])
        self.sent += 1
        plan = self.plan
        self.stage[slot] = value.astype(BF16).reshape(plan.shards, plan.rows, plan.width)
        start_all(copies_of(self.stage.at[slot], self.sems.at[slot]))

    def drain(self):
        for slot in range(min(2, self.sent)):
            wait_bytes(self.stage.at[slot], self.sems.at[slot])


def mlp_back_kernel(
    plan, flag, arr_ref, cot_ref, held2, hidden, act, slope,
    grad_hidden_ref, small_ref, grads, grad_pre_ref, stage, stage_sems,
):
    branch = jnp.where(flag[0] == 0, arr_ref[...], cot_ref[...])
    small_ref[...] = jnp.zeros_like(small_ref)
    small_ref[7:8, :] = column_sum(branch)
    out = Stage(plan, stage, stage_sems)

    def copies_of_up(part):
        def copies(source, sem):
            return [
                pltpu.make_async_copy(source.at[device], grads.at[place, part], sem)
                for place, device in enumerate(plan.order)
            ]

        return copies

    def copies_of_down(part):
        def copies(source, sem):
            made = []
            for place, device in enumerate(plan.order):
                for first, count in plan.runs:
                    block, row = divmod(QUART * device + first, plan.shards)
                    if block == part:
                        made.append(
                            pltpu.make_async_copy(
                                source.at[pl.ds(row, count)],
                                grads.at[place, pl.ds(QUART + first, count)],
                                sem,
                            )
                        )
            return made

        return copies

    grad_hidden = None
    for part in range(QUART):
        columns = columns_of(plan, part)
        grad_act = mm_nt(branch, block_of(plan, held2, QUART + part))
        grad_pre = (slope[:, columns] * grad_act).astype(BF16)
        grad_pre_ref[:, columns] = grad_pre
        small_ref[8 + part : 9 + part, :] = column_sum(grad_pre)
        term = mm_nt(grad_pre, block_of(plan, held2, part))
        grad_hidden = term if grad_hidden is None else grad_hidden + term
        out.put(mm_tn(act[:, columns], branch), copies_of_down(part))
    grad_hidden_ref[...] = grad_hidden
    for part in range(QUART):
        out.put(mm_tn(hidden[...], grad_pre_ref[:, columns_of(plan, part)]), copies_of_up(part))
    out.drain()


def slot_copies(plan, devs, grads, block):
    each = plan.shards // plan.parts

    def copies(source, sem):
        return [
            pltpu.make_async_copy(
                source.at[devs[slot]],
                grads[slot // each].at[slot % each, pl.ds(block * plan.rows, plan.rows)],
                sem,
            )
            for slot in range(plan.shards)
        ]

    return copies


def pack_sums(plan, lead, many, sums, stack, lines):
    rows, width = plan.rows, plan.width
    across = width // rows
    groups = pl.cdiv(many, across)
    high = groups * across
    leads = many - 12
    entry = lax.broadcasted_iota(jnp.int32, (high - 12, width), 0)
    table = jnp.zeros((high - 12, width), F32)
    for item in range(plan.items):
        table = table + jnp.where(entry == lead[item], sums[12 + item : 13 + item], 0.0)
    top, ups = sums[:8], sums[8:12]
    for device in range(plan.shards):
        columns = slice(device * rows, (device + 1) * rows)
        line, place = divmod(QUART * device * rows, width)
        parts = [
            ups[line : line + 1, place + part * rows : place + (part + 1) * rows]
            for part in range(QUART)
        ]
        share = jnp.concatenate([top[:, columns], *parts, table[:, columns]], 0)
        stack[device * high : (device + 1) * high, :] = share.astype(BF16)
    entry = lax.broadcasted_iota(jnp.int32, (rows, width), 0)
    column = lax.broadcasted_iota(jnp.int32, (rows, width), 1)
    tile = jnp.where(lax.rem(column, rows) == entry, 1.0, 0.0).astype(BF16)
    line = lax.broadcasted_iota(jnp.int32, (high, width), 0)
    lane = lax.broadcasted_iota(jnp.int32, (high, width), 1)
    place = lax.rem(line, across) * rows
    chosen = (lane >= place) & (lane < place + rows)
    lines[...] = jnp.zeros_like(lines)
    for device in range(plan.shards):
        spread = mm(stack[device * high : (device + 1) * high, :], tile)
        spread = jnp.where(chosen, spread, 0.0).reshape(groups, across, width)
        lines[device, 0:groups, :] = jnp.sum(spread, 1)


def rest_kernel(
    plan, many, flag, devs, lead, arr_ref, cot_ref, grad_hidden_ref, small_in, vec, *refs,
):
    count = plan.shards + plan.parts * (plan.parts - 1)
    kept_in, pieces, refs = refs[:6], refs[6 : 6 + count], refs[6 + count :]
    dx_ref, small_ref = refs[:2]
    grads, refs = refs[2 : 2 + plan.parts], refs[2 + plan.parts :]
    kept, refs = refs[:6], refs[6:]
    held, grad_middle_ref, grad_attended, grad_rows, sems, kept_sems, stage, stage_sems, out_sem, stack, lines, packed = refs
    xin_ref, normed, qkv, attended, middle_ref, probs = kept
    start_all(first_copies(plan, pieces, devs, held, sems.at[1], pl.ds(OUT, 1)))
    copies = [
        pltpu.make_async_copy(source, target, kept_sems.at[index])
        for index, (source, target) in enumerate(zip(kept_in, kept))
    ]
    for index in (4, 3, 2, 5, 1, 0):
        copies[index].start()
    start_all(first_copies(plan, pieces, devs, held, sems.at[0], pl.ds(0, OUT)))
    length = plan.length
    branch = jnp.where(flag[0] == 0, arr_ref[...], cot_ref[...])
    out = Stage(plan, stage, stage_sems)
    small_ref[...] = small_in[...]
    grad_hidden = grad_hidden_ref[...]
    copies[4].wait()
    xhat, rstd = normalised(middle_ref[...])
    small_ref[5:6, :] = column_sum(grad_hidden * xhat)
    small_ref[6:7, :] = column_sum(grad_hidden)
    grad_middle = branch.astype(F32) + norm_back(grad_hidden, xhat, rstd, vec[5:6, :])
    grad_middle_ref[...] = grad_middle
    attn_grad = grad_middle.astype(BF16)
    small_ref[4:5, :] = column_sum(attn_grad)
    wait_bytes(held.at[pl.ds(OUT, 1)], sems.at[1])
    grad_attended[...] = mm_nt(attn_grad, block_of(plan, held, OUT)).astype(BF16)
    copies[3].wait()
    out.put(mm_tn(attended[...], attn_grad), slot_copies(plan, devs, grads, OUT))
    copies[2].wait()
    copies[5].wait()
    attention_back(plan, probs, qkv, grad_attended, grad_rows)
    copies[1].wait()
    copies[0].wait()
    wait_bytes(held.at[pl.ds(0, OUT)], sems.at[0])
    grad_normed = None
    for part in range(OUT):
        rows = grad_rows[:, columns_of(plan, part)]
        term = mm_nt(rows, block_of(plan, held, part))
        grad_normed = term if grad_normed is None else grad_normed + term
        if part != 1:
            small_ref[2 + part // 2 : 3 + part // 2, :] = column_sum(rows)
        out.put(mm_tn(normed[...], rows), slot_copies(plan, devs, grads, part))
    xhat, rstd = normalised(xin_ref[...].astype(F32))
    small_ref[0:1, :] = column_sum(grad_normed * xhat)
    small_ref[1:2, :] = column_sum(grad_normed)
    for item in range(plan.items):
        small_ref[12 + item : 13 + item, :] = column_sum(
            grad_normed[item * length : (item + 1) * length]
        )
    dx_ref[...] = grad_middle_ref[...] + norm_back(grad_normed, xhat, rstd, vec[0:1, :])
    if plan.parts == 2:
        pack_sums(plan, lead, many, small_ref[...], stack, lines)
        packed[...] = lines[...].astype(BF16)
        each = plan.shards // plan.parts
        start_all(
            [
                pltpu.make_async_copy(
                    packed.at[devs[slot]],
                    grads[slot // each].at[slot % each, pl.ds(FIRST * plan.rows, EXTRA)],
                    out_sem.at[0],
                )
                for slot in range(plan.shards)
            ]
        )
        wait_bytes(packed, out_sem.at[0])
    out.drain()


def pack_kernel(qkv_ref, out_ref, up_ref, down_ref, *refs):
    rows, width = out_ref.shape
    vectors, (up_bias, table, first_ref, second_ref, small, wide) = refs[:8], refs[8:]
    for index, vector in enumerate(vectors):
        small[index : index + 1, :] = vector[...]
    for part in range(QUART):
        small[8 + part : 9 + part, :] = up_bias[:, part * rows : (part + 1) * rows]
    many = 12 + table.shape[0]
    small[12:many, :] = table[...]
    across = width // rows
    wide[...] = jnp.zeros_like(wide)
    for index in range(many):
        line, place = divmod(index, across)
        wide[line : line + 1, place * rows : (place + 1) * rows] = small[index : index + 1, :]
    for part in range(OUT):
        first_ref[part * rows : (part + 1) * rows, :] = qkv_ref[:, part * width : (part + 1) * width].astype(BF16)
    first_ref[OUT * rows : FIRST * rows, :] = out_ref[...].astype(BF16)
    first_ref[FIRST * rows :, :] = wide[...].astype(BF16)
    for part in range(QUART):
        second_ref[part] = up_ref[:, part * width : (part + 1) * width].astype(BF16)
        second_ref[QUART + part] = down_ref[part * rows : (part + 1) * rows, :].astype(BF16)


def vectors_kernel(plan, many, devs, lead, *refs):
    pieces, (out_ref, lines, spread, sem) = slot_pieces(plan, refs[:-4]), refs[-4:]
    rows, width = plan.rows, plan.width
    across = width // rows
    groups = pl.cdiv(many, across)
    start_all(
        [
            pltpu.make_async_copy(piece_rows(parts, FIRST * rows, EXTRA), lines.at[slot], sem.at[0])
            for slot, parts in enumerate(pieces)
        ]
    )
    wait_bytes(lines, sem.at[0])
    line = lax.broadcasted_iota(jnp.int32, (across, width), 0)
    lane = lax.broadcasted_iota(jnp.int32, (across, width), 1)
    chosen = (lane >= line * rows) & (lane < (line + 1) * rows)
    up_line = lax.broadcasted_iota(jnp.int32, (QUART, width), 0)
    up_lane = lax.broadcasted_iota(jnp.int32, (QUART, width), 1)
    ups = jnp.zeros((QUART, width), F32)
    for slot in range(plan.shards):
        values = lines[slot].astype(F32)
        for group in range(groups):
            at = (slot * groups + group) * across
            picked = jnp.where(chosen, jnp.broadcast_to(values[group : group + 1], chosen.shape), 0.0)
            spread[at : at + across, :] = picked.astype(BF16)
        first = QUART * rows * devs[slot]
        there = lax.rem(first, width)
        moved = jnp.broadcast_to(values[8 // across : 8 // across + 1], (8, width))
        moved = pltpu.roll(moved, lax.rem(there + width - 8 % across * rows, width), 1)[:QUART]
        here = (up_line == first // width) & (up_lane >= there) & (up_lane < there + QUART * rows)
        ups = jnp.where(here, moved, ups)
    source = lax.broadcasted_iota(jnp.int32, (width, rows), 0)
    target = lax.broadcasted_iota(jnp.int32, (width, rows), 1)
    fold = sum(jnp.where(source == target + place * rows, 1.0, 0.0) for place in range(across))
    narrow = mm(spread[...], fold.astype(BF16)).astype(BF16)
    entry = lax.broadcasted_iota(jnp.int32, (rows, width), 0)
    column = lax.broadcasted_iota(jnp.int32, (rows, width), 1)
    total = None
    for slot in range(plan.shards):
        at = slot * groups * across
        place = jnp.where(column == entry + devs[slot] * rows, 1.0, 0.0).astype(BF16)
        term = mm(narrow[at : at + groups * across], place)
        total = term if total is None else total + term
    out_ref[...] = jnp.zeros_like(out_ref)
    out_ref[:8, :] = total[:8]
    out_ref[8 : 8 + QUART, :] = ups
    entry = lax.broadcasted_iota(jnp.int32, total.shape, 0)
    for item in range(plan.items):
        picked = jnp.where(entry == 12 + lead[item], total, 0.0)
        out_ref[12 + item : 13 + item, :] = jnp.sum(picked, 0, keepdims=True)


def unpack_kernel(grads_ref, up_ref, down_ref):
    _, rows, width = grads_ref.shape
    for part in range(QUART):
        up_ref[:, part * width : (part + 1) * width] = grads_ref[part].astype(F32)
        down_ref[part * rows : (part + 1) * rows, :] = grads_ref[QUART + part].astype(F32)


def add_kernel(work, *refs):
    outs, at = refs[len(refs) - len(work) :], 0
    for (low, high, first), out in zip(work, outs):
        mine, other = refs[at], refs[at + 1]
        at += 2
        cuts, came = [low, high], None
        if first is not None:
            came = refs[at]
            at += 1
            cuts = sorted({low, first, first + came.shape[0], high})
        for start, end in zip(cuts, cuts[1:]):
            value = mine[0, start:end, :].astype(F32) + other[0, start:end, :].astype(F32)
            if came is not None and first <= start < first + came.shape[0]:
                value = value + came[start - first : end - first, :].astype(F32)
            out[start - low : end - low, :] = value.astype(BF16)


def total_kernel(many, mine, other, ahead, behind, qkv, out, *refs):
    width = mine.shape[2]
    rows = out.shape[0]

    def rows_of(low, count):
        here = slice(low, low + count)
        value = mine[0, here, :].astype(F32) + other[0, here, :].astype(F32)
        return value + (ahead[here, :].astype(F32) + behind[here, :].astype(F32))

    for part in range(OUT):
        qkv[:, part * width : (part + 1) * width] = rows_of(part * rows, rows)
    out[...] = rows_of(OUT * rows, rows)
    vectors, (up_bias, table, small) = refs[:8], refs[8:]
    lines = rows_of(FIRST * rows, EXTRA)
    for index in range(many):
        line, place = divmod(index, width // rows)
        small[index : index + 1, :] = lines[line : line + 1, place * rows : (place + 1) * rows]
    for index, vector in enumerate(vectors):
        vector[...] = small[index : index + 1, :]
    for part in range(QUART):
        up_bias[:, part * rows : (part + 1) * rows] = small[8 + part : 9 + part, :]
    table[...] = small[12:many, :]


SMEM = pl.BlockSpec(memory_space=pltpu.SMEM)
VMEM = pl.BlockSpec(memory_space=pltpu.VMEM)
HBM = pl.BlockSpec(memory_space=pltpu.HBM)
ANY = pl.BlockSpec(memory_space=pl.ANY)


def kept_shapes(plan):
    tokens, width = plan.tokens, plan.width
    return [
        ((tokens, width), BF16),
        ((tokens, 3 * width), BF16),
        ((tokens, width), BF16),
        ((tokens, width), F32),
        ((tokens, width), BF16),
        ((plan.items * plan.pairs, 2 * plan.length, plan.length), F32),
        ((tokens, 4 * width), BF16),
        ((tokens, 4 * width), F32),
    ]


def held_blocks(plan, blocks):
    return pltpu.VMEM((blocks, plan.shards, plan.rows, plan.width), BF16)


def call(kernel, outs, in_specs, out_specs, scratch, name, work, limit, args):
    args = [
        pltpu.with_memory_space_constraint(arg, pltpu.HBM) if spec is HBM else arg
        for arg, spec in zip(args, in_specs)
    ]
    return pl.pallas_call(
        kernel,
        out_shape=outs,
        in_specs=in_specs,
        out_specs=out_specs,
        scratch_shapes=scratch,
        compiler_params=pltpu.CompilerParams(vmem_limit_bytes=limit * 1024 * 1024),
        cost_estimate=pl.CostEstimate(flops=2 * work[0], bytes_accessed=work[1], transcendentals=0),
        name=name,
    )(*args)


def of(shape):
    return jax.ShapeDtypeStruct(*shape)


def inside(shape):
    return pltpu.VMEM(*shape)


def run_attend(plan, lengths, flag, devs, x, vec, pieces):
    kept = kept_shapes(plan)
    block = plan.width * plan.width
    return call(
        functools.partial(attend_kernel, plan),
        [of(kept[3]), of(kept[4])],
        [SMEM, SMEM, SMEM, VMEM, VMEM] + [HBM] * len(pieces),
        [VMEM, VMEM],
        [held_blocks(plan, FIRST)] + [inside(shape) for shape in kept[:3]] + [pltpu.SemaphoreType.DMA((2,))],
        "attend",
        (FIRST * block * plan.tokens, FIRST * block * 2),
        14,
        (lengths, flag, devs, x, vec, *pieces),
    )


def run_vectors(plan, many, devs, lead, pieces):
    groups = pl.cdiv(many, plan.width // plan.rows) * (plan.width // plan.rows)
    return call(
        functools.partial(vectors_kernel, plan, many),
        jax.ShapeDtypeStruct((16, plan.width), F32),
        [SMEM, SMEM] + [HBM] * len(pieces),
        VMEM,
        [
            pltpu.VMEM((plan.shards, EXTRA, plan.width), BF16),
            pltpu.VMEM((plan.shards * groups, plan.width), BF16),
            pltpu.SemaphoreType.DMA((1,)),
        ],
        "vectors",
        (plan.width * plan.width * plan.rows, plan.width * plan.width * 4),
        12,
        (devs, lead, *pieces),
    )


def run_mlp(plan, middle, hidden, vec, gathered):
    block = plan.width * plan.width
    return call(
        functools.partial(mlp_kernel, plan),
        jax.ShapeDtypeStruct(hidden.shape, BF16),
        [VMEM, VMEM, VMEM, HBM],
        VMEM,
        [held_blocks(plan, SECOND), pltpu.SemaphoreType.DMA((QUART,)), pltpu.SemaphoreType.DMA((QUART,))],
        "mlp",
        (SECOND * block * plan.tokens, SECOND * block * 2),
        16,
        (middle, hidden, vec, gathered),
    )


def run_load(plan, devs, after, firsts, gathered):
    block = plan.width * plan.width
    return call(
        functools.partial(load_kernel, plan),
        [held_blocks(plan, FIRST), held_blocks(plan, SECOND)],
        [SMEM, ANY] + [HBM] * (1 + len(firsts)),
        [VMEM, VMEM],
        [pltpu.SemaphoreType.DMA((2,)), pltpu.SemaphoreType.DMA((QUART,))],
        "load",
        (0, (FIRST + SECOND) * block * 4),
        2,
        (devs, after, gathered, *firsts),
    )


def run_chain(plan, lengths, flag, x, recv, cot, vec, held1, held2):
    shapes = kept_shapes(plan)
    block = plan.width * plan.width
    rest = [shapes[index] for index in (0, 0, 1, 2, 3, 5)]
    return call(
        functools.partial(chain_kernel, plan),
        [of(shapes[0]), of(shapes[0])]
        + [inside(shapes[index]) for index in (4, 6, 7)]
        + [pltpu.HBM(*shape) for shape in rest],
        [SMEM] * 2 + [VMEM] * 6,
        [VMEM] * 5 + [HBM] * len(rest),
        [inside(shape) for shape in rest]
        + [inside(shapes[0]), inside(shapes[1]), pltpu.SemaphoreType.DMA((len(rest),))],
        "chain",
        (24 * block * plan.tokens, 12 * block),
        14,
        (lengths, flag, x, recv, cot, vec, held1, held2),
    )


def grad_shapes(plan, extra=0):
    rows = FIRST * plan.rows + (extra if plan.parts == 2 else 0)
    return [pltpu.HBM((plan.shards // plan.parts, rows, plan.width), BF16)] * plan.parts


def stage_scratch(plan):
    return [
        pltpu.VMEM((2, plan.shards, plan.rows, plan.width), BF16),
        pltpu.SemaphoreType.DMA((2,)),
    ]


def run_mlp_back(plan, flag, arriving, cot, held2, hidden, act, slope):
    shapes = kept_shapes(plan)
    block = plan.width * plan.width
    return call(
        functools.partial(mlp_back_kernel, plan),
        [
            of(shapes[3]),
            jax.ShapeDtypeStruct((16, plan.width), F32),
            pltpu.HBM((plan.shards, SECOND, plan.rows, plan.width), BF16),
        ],
        [SMEM] + [VMEM] * 6,
        [VMEM, VMEM, HBM],
        [inside(shapes[6])] + stage_scratch(plan),
        "mlp_back",
        (2 * SECOND * block * plan.tokens, SECOND * block * 2),
        10,
        (flag, arriving, cot, held2, hidden, act, slope),
    )


def run_rest(plan, many, flag, devs, lead, arriving, cot, grad_hidden, small, vec, kept, pieces):
    shapes = kept_shapes(plan)
    block = plan.width * plan.width
    across = plan.width // plan.rows
    high = pl.cdiv(many, across) * across
    lines = (plan.shards, EXTRA, plan.width)
    rest = [shapes[index] for index in (0, 0, 1, 2, 3, 5)]
    input_grad, small, *grads = call(
        functools.partial(rest_kernel, plan, many),
        [of(shapes[3]), jax.ShapeDtypeStruct((16, plan.width), F32)] + grad_shapes(plan, EXTRA),
        [SMEM] * 3 + [VMEM] * 5 + [HBM] * (len(rest) + len(pieces)),
        [VMEM] * 2 + [HBM] * plan.parts,
        [inside(shape) for shape in rest]
        + [held_blocks(plan, FIRST)]
        + [inside(shapes[index]) for index in (3, 0, 1)]
        + [pltpu.SemaphoreType.DMA((2,)), pltpu.SemaphoreType.DMA((len(rest),))]
        + stage_scratch(plan)
        + [pltpu.SemaphoreType.DMA((1,)), pltpu.VMEM((plan.shards * high, plan.rows), BF16)]
        + [pltpu.VMEM(lines, F32), pltpu.VMEM(lines, BF16)],
        "rest",
        (2 * FIRST * block * plan.tokens, 2 * FIRST * block * 2),
        26,
        (flag, devs, lead, arriving, cot, grad_hidden, small, vec, *kept, *pieces),
    )
    return input_grad, small, grads


def run_add(mine, other, work):
    _, rows, width = mine.shape
    mine, other = (pltpu.with_memory_space_constraint(array, pltpu.HBM) for array in (mine, other))
    specs, args, plans, outs = [], [], [], []
    for way, (slot, low, high, came) in enumerate(work):
        one = pl.BlockSpec((1, rows, width), lambda index, slot=slot: (slot, 0, 0))
        specs += [one, one]
        args += [mine, other]
        first = None
        if came is not None:
            specs.append(pl.BlockSpec(came.shape, lambda index: (0, 0)))
            args.append(came)
            first = rows - came.shape[0] if way else 0
        plans.append((low, high, first))
        outs.append((high - low, width))
    return pl.pallas_call(
        functools.partial(add_kernel, plans),
        out_shape=[jax.ShapeDtypeStruct(shape, BF16) for shape in outs],
        grid=(1,),
        in_specs=specs,
        out_specs=[pl.BlockSpec(shape, lambda index: (0, 0)) for shape in outs],
        compiler_params=pltpu.CompilerParams(vmem_limit_bytes=14 * 1024 * 1024),
        name="add",
    )(*args)


def run_total(one, many, shapes):
    args = [pltpu.with_memory_space_constraint(array, pltpu.HBM) for array in (one.mine, one.other)]
    _, rows, width = one.mine.shape
    first = pl.BlockSpec((1, rows, width), lambda index: (0, 0, 0))
    whole = pl.BlockSpec((rows, width), lambda index: (0, 0))
    return pl.pallas_call(
        functools.partial(total_kernel, many),
        out_shape=[jax.ShapeDtypeStruct(shape, F32) for shape in shapes],
        grid=(1,),
        in_specs=[first, first, whole, whole],
        out_specs=[pl.BlockSpec(shape, lambda index: (0, 0)) for shape in shapes],
        scratch_shapes=[pltpu.VMEM((many, shapes[2][1]), F32)],
        compiler_params=pltpu.CompilerParams(vmem_limit_bytes=14 * 1024 * 1024),
        name="total",
    )(*args, *one.carried)


def after(value, *others):
    return lax.optimization_barrier((value, *others))[0]


def shifted(value, axis, steps):
    count = lax.axis_size(axis)
    first, last = (max(0, -steps), min(count, count - steps))
    return lax.ppermute(value, axis, [(source, source + steps) for source in range(first, last)])


class Ring:
    def __init__(self, count):
        self.count, self.chips = count, count // 2
        self.walk = list(range(0, self.chips, 2)) + list(range(self.chips - 1, 0, -2))
        self.order = [2 * chip + core for chip in self.walk for core in range(2)]
        after = self.walk[1:] + self.walk[:1]
        self.onward = [
            (2 * here + core, 2 * there + core)
            for here, there in zip(self.walk, after)
            for core in range(2)
        ]
        self.back = [(there, here) for here, there in self.onward]
        self.sibling = [(index, index ^ 1) for index in range(count)]

    def slots(self):
        index = lax.axis_index("dp")
        chip, core = index // 2, index % 2
        place_of = lambda chip: jnp.where(chip % 2 == 0, chip // 2, self.chips - 1 - chip // 2)
        steps = jnp.arange(self.chips, dtype=jnp.int32)
        ahead = (place_of(chip) + steps) % self.chips
        chips = jnp.where(ahead < (self.chips + 1) // 2, 2 * ahead, 2 * (self.chips - 1 - ahead) + 1)
        devs = jnp.concatenate([2 * chips + core, 2 * chips + 1 - core]).astype(jnp.int32)
        return devs

    def step(self, ahead, behind):
        return lax.ppermute(ahead, "dp", self.onward), lax.ppermute(behind, "dp", self.back)

    def gather(self, shard, low):
        half = self.chips // 2
        own = [[shard]] + [None] * (self.chips - 1)
        ahead = behind = shard
        for step in range(1, half):
            ahead, behind = self.step(ahead, behind)
            own[self.chips - step], own[step] = [ahead], [behind]
            ahead, behind = lax.optimization_barrier((ahead, behind))
        own[half] = list(self.step(ahead[:low], behind[low:]))
        return [piece for pieces in own for piece in pieces]

    def siblings(self, pieces):
        return [lax.ppermute(piece, "dp", self.sibling) for piece in pieces]


class RingSum:
    def __init__(self, ring, mine, other, low):
        self.ring, self.mine, self.other, self.low = ring, mine, other, low
        self.time = ring.chips // 2
        self.carried = [None, None]

    def add(self):
        rows = self.mine.shape[1]
        if self.carried[0] is None:
            work = [(self.time, 0, self.low, None), (self.time, self.low, rows, None)]
        else:
            work = [
                (self.time, 0, rows, self.carried[0]),
                (self.ring.chips - self.time, 0, rows, self.carried[1]),
            ]
        self.carried = run_add(self.mine, self.other, work)

    def send(self):
        self.carried = self.ring.step(*self.carried)
        self.time -= 1


def body(
    block_input, cotangent, lengths, leads,
    norm_gain1, norm_bias1, lead_table, qkv_weight, query_bias, value_bias, out_weight, out_bias,
    norm_gain2, norm_bias2, up_weight, up_bias, down_weight, down_bias,
):
    count = lax.axis_size("dp")
    micro, local, length, width = block_input.shape
    items = micro * local
    rows = width // count
    leads_count = lead_table.shape[2]
    flag = lax.axis_index("section").astype(jnp.int32).reshape(1)
    flat = lambda value: value.reshape(items * length, width)
    x, cot = flat(block_input), flat(cotangent)
    lens, lead = lengths.reshape(items), leads.reshape(items)

    vectors = (
        norm_gain1, norm_bias1, query_bias, value_bias, out_bias, norm_gain2, norm_bias2, down_bias
    )
    many = 12 + leads_count
    aligned = rows % 16 == 0 and count % 4 == 0 and pl.cdiv(many, width // rows) <= EXTRA
    if aligned:
        ring = Ring(count)
        first, second = pl.pallas_call(
            pack_kernel,
            out_shape=[jax.ShapeDtypeStruct((FIRST * rows + EXTRA, width), BF16)]
            + [jax.ShapeDtypeStruct((SECOND, rows, width), BF16)],
            scratch_shapes=[pltpu.VMEM((many, rows), F32), pltpu.VMEM((EXTRA, width), F32)],
            name="pack",
        )(qkv_weight[0], out_weight[0], up_weight[0], down_weight[0], *vectors, up_bias, lead_table[0].T)
        gathered = lax.all_gather(second, "dp", axis=0, tiled=True, axis_index_groups=[ring.order])
        gathered = gathered.reshape(count, SECOND, rows, width)
        firsts = ring.gather(first, LOW * rows)
        firsts = firsts + ring.siblings(firsts)
        devs = ring.slots()
        plan = Plan(ring.order, rows, items, length, width)
        vec = run_vectors(plan, many, devs, lead, firsts)
    else:
        wide_blocks = lambda value: value[0].reshape(rows, -1, width).transpose(1, 0, 2)
        packed = jnp.concatenate(
            [wide_blocks(qkv_weight), out_weight, wide_blocks(up_weight), down_weight.reshape(QUART, rows, width)], 0
        )
        everything = lax.all_gather(packed.astype(BF16), "dp", axis=0)
        across_blocks = lambda value: value.transpose(1, 0, 2, 3).reshape(-1, width, width)
        firsts = [across_blocks(everything[:, :FIRST])]
        gathered = jnp.concatenate(
            [
                across_blocks(everything[:, FIRST : FIRST + QUART]),
                everything[:, FIRST + QUART :].reshape(QUART, width, width),
            ],
            0,
        )[None]
        devs = jnp.zeros((1,), jnp.int32)
        plan = Plan([0], width, items, length, width)
        small = jnp.concatenate([*vectors, up_bias.reshape(4, rows), lead_table[0].T], 0).astype(BF16)
        wide = lax.all_gather(small, "dp", axis=1, tiled=True).astype(F32)
        vec = jnp.concatenate(
            [wide[:8], wide[8:12].reshape(4, count, rows).transpose(1, 0, 2).reshape(4, width)]
            + [lax.dynamic_slice_in_dim(wide, 12 + lead[item], 1, 0) for item in range(items)]
            + [jnp.zeros((4 - items, width), F32)],
            0,
        )

    middle, hidden = run_attend(plan, lens, flag, devs, x, vec, firsts)
    first_out = run_mlp(plan, middle, hidden, vec, gathered)
    recv = shifted(first_out, "section", 1)
    held1, held2 = run_load(plan, devs, first_out, firsts, gathered)
    output, first_grad, hidden, act, slope, *kept = run_chain(
        plan, lens, flag, x, recv, cot, vec, held1, held2
    )
    arriving = shifted(first_grad, "section", -1)
    grad_hidden, sums, grads2 = run_mlp_back(plan, flag, arriving, cot, held2, hidden, act, slope)
    input_grad, sums, grads1 = run_rest(
        plan, many, flag, devs, lead, arriving, cot, grad_hidden, sums, vec, kept, firsts
    )
    if aligned:
        first_sum = RingSum(ring, grads1[0], *ring.siblings(grads1[1:]), LOW * rows)
        while first_sum.time:
            first_sum.add()
            first_sum.send()
        grads2 = lax.psum_scatter(
            grads2.reshape(count * SECOND, rows, width),
            "dp", scatter_dimension=0, tiled=True, axis_index_groups=[ring.order],
        )
        grad_up, grad_down = pl.pallas_call(
            unpack_kernel,
            out_shape=[
                jax.ShapeDtypeStruct((rows, QUART * width), F32),
                jax.ShapeDtypeStruct((QUART * rows, width), F32),
            ],
            name="unpack",
        )(grads2)
        grad_qkv, grad_out, *small_grads = run_total(
            first_sum, many,
            [(rows, OUT * width), (rows, width)] + [(1, rows)] * 8 + [(1, QUART * rows), (leads_count, rows)],
        )
    else:
        split = lambda value: value[0].reshape(-1, count, rows, width).transpose(1, 0, 2, 3)
        grads = jnp.concatenate(
            [
                split(grads1[0]),
                split(grads2[0, :QUART].reshape(1, QUART * width, width)),
                grads2[0, QUART:].reshape(count, QUART, rows, width),
            ],
            1,
        )
        grads = lax.psum_scatter(grads, "dp", scatter_dimension=0, tiled=False).astype(F32)
        across = lambda value: value.transpose(1, 0, 2).reshape(rows, -1)
        grad_qkv, grad_out = across(grads[:OUT]), grads[OUT]
        grad_up = across(grads[FIRST : FIRST + QUART])
        grad_down = grads[FIRST + QUART :].reshape(QUART * rows, width)
        hot = (jnp.arange(leads_count)[:, None] == lead[None, :]).astype(F32)
        table = sum(hot[:, item : item + 1] * sums[12 + item : 13 + item] for item in range(items))
        up_sums = sums[8:12].reshape(count, 4, rows).transpose(1, 0, 2).reshape(4, width)
        spread = lax.psum_scatter(
            jnp.concatenate([sums[:8], up_sums, table], 0), "dp", scatter_dimension=1, tiled=True
        )
        small_grads = [spread[index : index + 1] for index in range(8)]
        small_grads += [spread[8:12].reshape(1, 4 * rows), spread[12:]]
    vector = small_grads
    shape = (1, micro, local, length, width)
    return (
        output.reshape(shape),
        input_grad.reshape(shape),
        vector[0],
        vector[1],
        vector[9].T[None],
        grad_qkv[None],
        vector[2],
        vector[3],
        grad_out[None],
        vector[4],
        vector[5],
        vector[6],
        grad_up[None],
        vector[8],
        grad_down[None],
        vector[7],
    )


def solution(mesh):
    weights = (
        P("section", "dp"),
        P("section", "dp"),
        P("section", "dp", None),
        P("section", "dp", None),
        P("section", "dp"),
        P("section", "dp"),
        P("section", "dp", None),
        P("section", "dp"),
        P("section", "dp"),
        P("section", "dp"),
        P("section", "dp", None),
        P("section", "dp"),
        P("section", "dp", None),
        P("section", "dp"),
    )
    rows = P(None, "dp", None, None)
    layers = P("section", None, "dp", None, None)
    return jax.shard_map(
        body,
        mesh=mesh,
        in_specs=(rows, rows, P(None, "dp"), P(None, "dp")) + weights,
        out_specs=(layers, layers) + weights,
        check_vma=False,
    )
```

```python
import functools

import jax
import jax.numpy as jnp
from jax import lax
from jax.experimental import pallas as pl
from jax.experimental.pallas import tpu as pltpu
from jax.sharding import PartitionSpec as P

HEAD = 64
PAIR = 2 * HEAD
EPS = 1e-06
SCALE_FACTOR = 0.125
GELU_A = 0.7978845608028654
GELU_B = 0.044715
F32 = jnp.float32
BF16 = jnp.bfloat16
OUT = 3
FIRST = 4
SECOND = 8
QUART = 4
EXTRA = 16
LOW = 2
SLOTS = 4


def mm(left, right):
    return jnp.dot(left, right, preferred_element_type=F32)


def mm_nt(left, right):
    return lax.dot_general(left, right, (((1,), (1,)), ((), ())), preferred_element_type=F32)


def mm_tn(left, right):
    return lax.dot_general(left, right, (((0,), (0,)), ((), ())), preferred_element_type=F32)


def normalised(values):
    mean = jnp.mean(values, -1, keepdims=True)
    centred = values - mean
    variance = jnp.mean(centred * centred, -1, keepdims=True)
    rstd = lax.rsqrt(variance + EPS)
    return centred * rstd, rstd


def norm_back(grad, xhat, rstd, gain):
    scaled = grad * gain
    first = jnp.mean(scaled, -1, keepdims=True)
    second = jnp.mean(scaled * xhat, -1, keepdims=True)
    return rstd * (scaled - first - xhat * second)


def gelu_both(values):
    square = values * values
    slope = GELU_A * (1.0 + 3.0 * GELU_B * square)
    bend = jnp.tanh(GELU_A * values * (1.0 + GELU_B * square))
    half = 0.5 * (1.0 + bend)
    return values * half, half + 0.5 * values * (1.0 - bend * bend) * slope


def split_pair(rows):
    lane = lax.broadcasted_iota(jnp.int32, rows.shape, 1)
    zero = jnp.zeros_like(rows)
    return jnp.concatenate(
        [jnp.where(lane < HEAD, rows, zero), jnp.where(lane < HEAD, zero, rows)], 0
    )


def join_pair(stacked):
    count = stacked.shape[0] // 2
    lane = lax.broadcasted_iota(jnp.int32, (count, PAIR), 1)
    return jnp.where(lane < HEAD, stacked[:count], stacked[count:])


def runs_of(order):
    if all(order[at + 1] == order[at] + 1 for at in range(0, len(order) - 1, 2)) and len(order) > 1:
        return [(at, order[at], 2) for at in range(0, len(order), 2)]
    return [(at, device, 1) for at, device in enumerate(order)]


class Plan:
    def __init__(self, order, rows, items, length, width):
        self.order, self.shards, self.rows = order, len(order), rows
        self.items, self.length, self.width = items, length, width
        self.tokens = items * length
        self.low = LOW * rows
        self.pairs = width // PAIR
        whole = self.shards % QUART == 0
        self.runs = [(0, QUART)] if whole else [(block, 1) for block in range(QUART)]
        self.parts = 3 if self.shards > 1 else 1


def slot_pieces(plan, refs):
    if plan.shards == 1:
        return [[(0, refs[0])]]
    refs, slots, half = list(refs), [], plan.shards // 4
    for slot in range(plan.shards):
        parts = [(0, refs.pop(0))]
        if slot % (plan.shards // 2) == half:
            parts.append((plan.low, refs.pop(0)))
        slots.append(parts)
    return slots


def piece_rows(parts, row, count):
    start, ref = [part for part in parts if part[0] <= row][-1]
    return ref.at[pl.ds(row - start, count)]


def first_copies(plan, refs, devs, held, sem, blocks):
    if plan.shards == 1:
        return block_copies(refs, devs, held, sem, blocks)
    return [
        pltpu.make_async_copy(
            piece_rows(parts, block * plan.rows, plan.rows), held.at[block, devs[slot]], sem
        )
        for slot, parts in enumerate(slot_pieces(plan, refs))
        for block in range(blocks.start, blocks.start + blocks.size)
    ]


def block_copies(pieces, devs, held, sem, blocks, at=0):
    return [
        pltpu.make_async_copy(
            piece.at[blocks], held.at[pl.ds(at + blocks.start, blocks.size), devs[slot]], sem
        )
        for slot, piece in enumerate(pieces)
    ]


def up_copies(plan, gathered, held, sem, part):
    return [
        pltpu.make_async_copy(
            gathered.at[pl.ds(place, count), part], held.at[part, pl.ds(device, count)], sem
        )
        for place, device, count in runs_of(plan.order)
    ]


def down_copies(plan, pieces, devs, held, sems):
    copies = []
    for slot, piece in enumerate(pieces):
        for first, count in plan.runs:
            block, row = divmod(QUART * devs[slot] + first, plan.shards)
            copy = pltpu.make_async_copy(
                piece.at[pl.ds(first, count)],
                held.at[QUART + block, pl.ds(row, count)],
                sems.at[block],
            )
            copies.append((block, copy))
    return copies


def second_pieces(plan, gathered):
    ups = [gathered.at[place, pl.ds(0, QUART)] for place in range(plan.shards)]
    downs = [gathered.at[place, pl.ds(QUART, QUART)] for place in range(plan.shards)]
    return ups, downs


def start_all(copies):
    for copy in copies:
        copy.start()


def wait_bytes(part, sem):
    pltpu.make_async_copy(part, part, sem).wait()


def block_of(plan, held, index):
    return held[index].reshape(plan.width, plan.width)


def columns_of(plan, index):
    return slice(index * plan.width, (index + 1) * plan.width)


def attention_forward(plan, lengths, qkv_ref, attended_ref, probs_ref):
    width, length = plan.width, plan.length
    key_index = lax.broadcasted_iota(jnp.int32, (2 * length, length), 1)
    for item in range(plan.items):
        rows = slice(item * length, (item + 1) * length)
        valid = key_index < lengths[item]
        for pair in range(plan.pairs):
            at = pair * PAIR
            query = split_pair(qkv_ref[rows, at : at + PAIR])
            key = qkv_ref[rows, width + at : width + at + PAIR]
            value = qkv_ref[rows, 2 * width + at : 2 * width + at + PAIR]
            logits = jnp.where(valid, mm_nt(query, key) * SCALE_FACTOR, -1000000000.0)
            expo = jnp.exp(logits - jnp.max(logits, -1, keepdims=True))
            probs = expo / jnp.sum(expo, -1, keepdims=True)
            if probs_ref is not None:
                probs_ref[item * plan.pairs + pair] = probs
            attended_ref[rows, at : at + PAIR] = join_pair(mm(probs.astype(BF16), value)).astype(
                BF16
            )


def first_half(plan, inputs, lengths, vec, held, wait, normed_ref, qkv_ref, attended_ref, probs_ref, hidden_ref):
    width, length = plan.width, plan.length
    values = inputs.astype(F32)
    xhat, _ = normalised(values)
    base = xhat * vec[0:1, :] + vec[1:2, :]
    for item in range(plan.items):
        rows = slice(item * length, (item + 1) * length)
        normed_ref[rows, :] = (base[rows] + vec[12 + item : 13 + item, :]).astype(BF16)
    wait(0)
    for part, bias in enumerate((2, None, 3)):
        joined = mm(normed_ref[...], block_of(plan, held, part))
        if bias is not None:
            joined = joined + vec[bias : bias + 1, :]
        qkv_ref[:, columns_of(plan, part)] = joined.astype(BF16)
    attention_forward(plan, lengths, qkv_ref, attended_ref, probs_ref)
    wait(1)
    middle = values + (mm(attended_ref[...], block_of(plan, held, OUT)) + vec[4:5, :])
    xhat, _ = normalised(middle)
    hidden_ref[...] = (xhat * vec[5:6, :] + vec[6:7, :]).astype(BF16)
    return middle


def second_half(plan, hidden_ref, vec, held, act_ref=None, slope_ref=None, wait=None):
    total = None
    for part in range(QUART):
        if wait is not None:
            wait(part)
        pre_act = mm(hidden_ref[...], block_of(plan, held, part)) + vec[8 + part : 9 + part, :]
        act, slope = gelu_both(pre_act)
        act = act.astype(BF16)
        if act_ref is not None:
            act_ref[:, columns_of(plan, part)] = act
            slope_ref[:, columns_of(plan, part)] = slope
        if wait is not None:
            wait(QUART + part)
        term = mm(act, block_of(plan, held, QUART + part))
        total = term if total is None else total + term
    return total + vec[7:8, :]


def attention_back(plan, probs_ref, qkv_ref, grad_attended_ref, rows_ref):
    width, length = plan.width, plan.length
    for item in range(plan.items):
        rows = slice(item * length, (item + 1) * length)
        for pair in range(plan.pairs):
            at = pair * PAIR
            query = split_pair(qkv_ref[rows, at : at + PAIR])
            key = qkv_ref[rows, width + at : width + at + PAIR]
            value = qkv_ref[rows, 2 * width + at : 2 * width + at + PAIR]
            grad = split_pair(grad_attended_ref[rows, at : at + PAIR])
            probs = probs_ref[item * plan.pairs + pair]
            grad_probs = mm_nt(grad, value)
            centre = jnp.sum(grad_probs * probs, -1, keepdims=True)
            grad_logits = (probs * (grad_probs - centre)).astype(BF16)
            grad_query = join_pair(mm(grad_logits, key)) * SCALE_FACTOR
            grad_key = mm_tn(grad_logits, query) * SCALE_FACTOR
            grad_value = mm_tn(probs.astype(BF16), grad)
            rows_ref[rows, at : at + PAIR] = grad_query.astype(BF16)
            rows_ref[rows, width + at : width + at + PAIR] = grad_key.astype(BF16)
            rows_ref[rows, 2 * width + at : 2 * width + at + PAIR] = grad_value.astype(BF16)


def column_sum(values):
    return jnp.sum(values.astype(F32), 0, keepdims=True)


def attend_kernel(plan, lengths, flag, devs, x_ref, vec, *refs):
    pieces, (middle_ref, hidden_ref, held, normed, qkv, attended, sems) = refs[:-7], refs[-7:]
    start_all(first_copies(plan, pieces, devs, held, sems.at[0], pl.ds(0, OUT)))
    start_all(first_copies(plan, pieces, devs, held, sems.at[1], pl.ds(OUT, 1)))

    def wait(group):
        blocks = pl.ds(OUT, 1) if group else pl.ds(0, OUT)
        wait_bytes(held.at[blocks], sems.at[group])

    middle_ref[...] = first_half(
        plan, x_ref[...], lengths, vec, held, wait, normed, qkv, attended, None, hidden_ref
    )


def mlp_kernel(plan, middle_ref, hidden_ref, vec, gathered, y_ref, held, sems, down_sems):
    _, downs = second_pieces(plan, gathered)
    down = down_copies(plan, downs, plan.order, held, down_sems)
    for part in range(QUART):
        start_all(up_copies(plan, gathered, held, sems.at[part], part))
        start_all([copy for block, copy in down if block == part])

    def wait(block):
        sem = sems.at[block] if block < QUART else down_sems.at[block - QUART]
        wait_bytes(held.at[block], sem)

    total = second_half(plan, hidden_ref, vec, held, wait=wait)
    y_ref[...] = (middle_ref[...] + total).astype(BF16)


def load_kernel(plan, devs, after, cot_ref, gathered, *refs):
    firsts, (held1, held2, grad_act, sems, down_sems) = refs[:-5], refs[-5:]
    ups, downs = second_pieces(plan, gathered)
    start_all([copy for _, copy in down_copies(plan, downs, plan.order, held2, down_sems)])
    start_all(block_copies(ups, plan.order, held2, sems.at[1], pl.ds(0, QUART)))
    start_all(first_copies(plan, firsts, devs, held1, sems.at[0], pl.ds(0, FIRST)))
    for part in range(QUART):
        wait_bytes(held2.at[QUART + part], down_sems.at[part])
        grad_act[:, columns_of(plan, part)] = mm_nt(
            cot_ref[...], block_of(plan, held2, QUART + part)
        )
    wait_bytes(held2.at[pl.ds(0, QUART)], sems.at[1])
    wait_bytes(held1, sems.at[0])


def chain_kernel(
    plan, lengths, flag, x_ref, recv_ref, cot_ref, vec, held1, held2, grad_act,
    y_out, dx_ref, hidden, act, slope, *refs,
):
    outs, (xin_ref, normed, qkv, attended, middle, probs, y_ref, grad_attended, grad_rows, sems) = refs[:6], refs[6:]
    kept = (xin_ref, normed, qkv, attended, middle, probs)
    copies = [
        pltpu.make_async_copy(source, target, sems.at[index])
        for index, (source, target) in enumerate(zip(kept, outs))
    ]
    xin_ref[...] = jnp.where(flag[0] == 0, x_ref[...], recv_ref[...])
    middle[...] = first_half(
        plan, xin_ref[...], lengths, vec, held1, lambda group: None, normed, qkv, attended, probs, hidden
    )
    start_all(copies)
    y_ref[...] = (middle[...] + second_half(plan, hidden, vec, held2, act, slope)).astype(BF16)
    copies.append(pltpu.make_async_copy(y_ref, y_out, sems.at[len(copies)]))
    copies[-1].start()
    branch = cot_ref[...]
    grad_hidden = None
    for part in range(QUART):
        grad_pre = (slope[:, columns_of(plan, part)] * grad_act[:, columns_of(plan, part)]).astype(BF16)
        term = mm_nt(grad_pre, block_of(plan, held2, part))
        grad_hidden = term if grad_hidden is None else grad_hidden + term
    xhat, rstd = normalised(middle[...])
    grad_middle = branch.astype(F32) + norm_back(grad_hidden, xhat, rstd, vec[5:6, :])
    grad_attended[...] = mm_nt(grad_middle.astype(BF16), block_of(plan, held1, OUT)).astype(BF16)
    attention_back(plan, probs, qkv, grad_attended, grad_rows)
    grad_normed = None
    for part in range(OUT):
        term = mm_nt(grad_rows[:, columns_of(plan, part)], block_of(plan, held1, part))
        grad_normed = term if grad_normed is None else grad_normed + term
    xhat, rstd = normalised(xin_ref[...].astype(F32))
    dx_ref[...] = (grad_middle + norm_back(grad_normed, xhat, rstd, vec[0:1, :])).astype(BF16)
    for copy in copies:
        copy.wait()


class Stage:
    def __init__(self, plan, stage, sems):
        self.plan, self.stage, self.sems, self.sent = plan, stage, sems, 0

    def put(self, value, copies_of):
        slot = self.sent % SLOTS
        if self.sent >= SLOTS:
            wait_bytes(self.stage.at[slot], self.sems.at[slot])
        self.sent += 1
        plan = self.plan
        self.stage[slot] = value.astype(BF16).reshape(plan.shards, plan.rows, plan.width)
        start_all(copies_of(self.stage.at[slot], self.sems.at[slot]))

    def drain(self):
        for slot in range(min(SLOTS, self.sent)):
            wait_bytes(self.stage.at[slot], self.sems.at[slot])


def mlp_back_kernel(
    plan, flag, arr_ref, cot_ref, held2, hidden, act, slope,
    grad_hidden_ref, small_ref, grads, grad_pre_ref, stage, stage_sems,
):
    branch = jnp.where(flag[0] == 0, arr_ref[...], cot_ref[...])
    small_ref[...] = jnp.zeros_like(small_ref)
    small_ref[7:8, :] = column_sum(branch)
    out = Stage(plan, stage, stage_sems)

    def copies_of_up(part):
        def copies(source, sem):
            return [
                pltpu.make_async_copy(
                    source.at[pl.ds(device, count)], grads.at[pl.ds(place, count), part], sem
                )
                for place, device, count in runs_of(plan.order)
            ]

        return copies

    def copies_of_down(part):
        def copies(source, sem):
            made = []
            for place, device in enumerate(plan.order):
                for first, count in plan.runs:
                    block, row = divmod(QUART * device + first, plan.shards)
                    if block == part:
                        made.append(
                            pltpu.make_async_copy(
                                source.at[pl.ds(row, count)],
                                grads.at[place, pl.ds(QUART + first, count)],
                                sem,
                            )
                        )
            return made

        return copies

    grad_hidden = None
    for part in range(QUART):
        columns = columns_of(plan, part)
        grad_act = mm_nt(branch, block_of(plan, held2, QUART + part))
        grad_pre = (slope[:, columns] * grad_act).astype(BF16)
        grad_pre_ref[:, columns] = grad_pre
        small_ref[8 + part : 9 + part, :] = column_sum(grad_pre)
        term = mm_nt(grad_pre, block_of(plan, held2, part))
        grad_hidden = term if grad_hidden is None else grad_hidden + term
        out.put(mm_tn(act[:, columns], branch), copies_of_down(part))
    grad_hidden_ref[...] = grad_hidden
    for part in range(QUART):
        out.put(mm_tn(hidden[...], grad_pre_ref[:, columns_of(plan, part)]), copies_of_up(part))
    out.drain()


def slot_target(plan, grads, slot):
    if plan.parts == 1:
        return grads[0].at[0]
    half = plan.shards // 2
    if slot == half + half // 2:
        return grads[2].at[0]
    return grads[slot // half].at[slot % half]


def slot_copies(plan, devs, grads, block):
    def copies(source, sem):
        return [
            pltpu.make_async_copy(
                source.at[devs[slot]],
                slot_target(plan, grads, slot).at[pl.ds(block * plan.rows, plan.rows)],
                sem,
            )
            for slot in range(plan.shards)
        ]

    return copies


def pack_sums(plan, lead, many, sums, stack, lines):
    rows, width = plan.rows, plan.width
    across = width // rows
    groups = pl.cdiv(many, across)
    high = groups * across
    leads = many - 12
    entry = lax.broadcasted_iota(jnp.int32, (high - 12, width), 0)
    table = jnp.zeros((high - 12, width), F32)
    for item in range(plan.items):
        table = table + jnp.where(entry == lead[item], sums[12 + item : 13 + item], 0.0)
    top, ups = sums[:8], sums[8:12]
    for device in range(plan.shards):
        columns = slice(device * rows, (device + 1) * rows)
        line, place = divmod(QUART * device * rows, width)
        parts = [
            ups[line : line + 1, place + part * rows : place + (part + 1) * rows]
            for part in range(QUART)
        ]
        share = jnp.concatenate([top[:, columns], *parts, table[:, columns]], 0)
        stack[device * high : (device + 1) * high, :] = share.astype(BF16)
    entry = lax.broadcasted_iota(jnp.int32, (rows, width), 0)
    column = lax.broadcasted_iota(jnp.int32, (rows, width), 1)
    tile = jnp.where(lax.rem(column, rows) == entry, 1.0, 0.0).astype(BF16)
    line = lax.broadcasted_iota(jnp.int32, (high, width), 0)
    lane = lax.broadcasted_iota(jnp.int32, (high, width), 1)
    place = lax.rem(line, across) * rows
    chosen = (lane >= place) & (lane < place + rows)
    lines[...] = jnp.zeros_like(lines)
    for device in range(plan.shards):
        spread = mm(stack[device * high : (device + 1) * high, :], tile)
        spread = jnp.where(chosen, spread, 0.0).reshape(groups, across, width)
        lines[device, 0:groups, :] = jnp.sum(spread, 1)


def rest_kernel(
    plan, many, flag, devs, lead, arr_ref, cot_ref, grad_hidden_ref, small_in, vec, *refs,
):
    count = plan.shards + (2 if plan.parts > 1 else 0)
    kept_in, pieces, refs = refs[:6], refs[6 : 6 + count], refs[6 + count :]
    dx_ref, small_ref = refs[:2]
    grads, refs = refs[2 : 2 + plan.parts], refs[2 + plan.parts :]
    kept, refs = refs[:6], refs[6:]
    held, grad_middle_ref, grad_attended, grad_rows, sems, kept_sems, stage, stage_sems, out_sem, stack, lines, packed = refs
    xin_ref, normed, qkv, attended, middle_ref, probs = kept
    start_all(first_copies(plan, pieces, devs, held, sems.at[1], pl.ds(OUT, 1)))
    copies = [
        pltpu.make_async_copy(source, target, kept_sems.at[index])
        for index, (source, target) in enumerate(zip(kept_in, kept))
    ]
    for index in (4, 3, 2, 5, 1, 0):
        copies[index].start()
    start_all(first_copies(plan, pieces, devs, held, sems.at[0], pl.ds(0, OUT)))
    length = plan.length
    branch = jnp.where(flag[0] == 0, arr_ref[...], cot_ref[...])
    out = Stage(plan, stage, stage_sems)
    small_ref[...] = small_in[...]
    grad_hidden = grad_hidden_ref[...]
    copies[4].wait()
    xhat, rstd = normalised(middle_ref[...])
    small_ref[5:6, :] = column_sum(grad_hidden * xhat)
    small_ref[6:7, :] = column_sum(grad_hidden)
    grad_middle = branch.astype(F32) + norm_back(grad_hidden, xhat, rstd, vec[5:6, :])
    grad_middle_ref[...] = grad_middle
    attn_grad = grad_middle.astype(BF16)
    small_ref[4:5, :] = column_sum(attn_grad)
    wait_bytes(held.at[pl.ds(OUT, 1)], sems.at[1])
    grad_attended[...] = mm_nt(attn_grad, block_of(plan, held, OUT)).astype(BF16)
    copies[3].wait()
    out.put(mm_tn(attended[...], attn_grad), slot_copies(plan, devs, grads, OUT))
    copies[2].wait()
    copies[5].wait()
    attention_back(plan, probs, qkv, grad_attended, grad_rows)
    copies[1].wait()
    copies[0].wait()
    wait_bytes(held.at[pl.ds(0, OUT)], sems.at[0])
    grad_normed = None
    for part in range(OUT):
        rows = grad_rows[:, columns_of(plan, part)]
        term = mm_nt(rows, block_of(plan, held, part))
        grad_normed = term if grad_normed is None else grad_normed + term
        if part != 1:
            small_ref[2 + part // 2 : 3 + part // 2, :] = column_sum(rows)
        out.put(mm_tn(normed[...], rows), slot_copies(plan, devs, grads, part))
    xhat, rstd = normalised(xin_ref[...].astype(F32))
    small_ref[0:1, :] = column_sum(grad_normed * xhat)
    small_ref[1:2, :] = column_sum(grad_normed)
    for item in range(plan.items):
        small_ref[12 + item : 13 + item, :] = column_sum(
            grad_normed[item * length : (item + 1) * length]
        )
    dx_ref[...] = grad_middle_ref[...] + norm_back(grad_normed, xhat, rstd, vec[0:1, :])
    if plan.parts > 1:
        pack_sums(plan, lead, many, small_ref[...], stack, lines)
        packed[...] = lines[...].astype(BF16)
        start_all(
            [
                pltpu.make_async_copy(
                    packed.at[devs[slot]],
                    slot_target(plan, grads, slot).at[pl.ds(FIRST * plan.rows, EXTRA)],
                    out_sem.at[0],
                )
                for slot in range(plan.shards)
            ]
        )
        wait_bytes(packed, out_sem.at[0])
    out.drain()


def pack_kernel(qkv_ref, out_ref, up_ref, down_ref, *refs):
    rows, width = out_ref.shape
    vectors, (up_bias, table, first_ref, second_ref, small, wide) = refs[:8], refs[8:]
    for index, vector in enumerate(vectors):
        small[index : index + 1, :] = vector[...]
    for part in range(QUART):
        small[8 + part : 9 + part, :] = up_bias[:, part * rows : (part + 1) * rows]
    many = 12 + table.shape[0]
    small[12:many, :] = table[...]
    across = width // rows
    wide[...] = jnp.zeros_like(wide)
    for index in range(many):
        line, place = divmod(index, across)
        wide[line : line + 1, place * rows : (place + 1) * rows] = small[index : index + 1, :]
    for part in range(OUT):
        first_ref[part * rows : (part + 1) * rows, :] = qkv_ref[:, part * width : (part + 1) * width].astype(BF16)
    first_ref[OUT * rows : FIRST * rows, :] = out_ref[...].astype(BF16)
    first_ref[FIRST * rows :, :] = wide[...].astype(BF16)
    for part in range(QUART):
        second_ref[part] = up_ref[:, part * width : (part + 1) * width].astype(BF16)
        second_ref[QUART + part] = down_ref[part * rows : (part + 1) * rows, :].astype(BF16)


def vectors_kernel(plan, many, devs, lead, *refs):
    pieces, (out_ref, lines, spread, sem) = slot_pieces(plan, refs[:-4]), refs[-4:]
    rows, width = plan.rows, plan.width
    across = width // rows
    groups = pl.cdiv(many, across)
    start_all(
        [
            pltpu.make_async_copy(piece_rows(parts, FIRST * rows, EXTRA), lines.at[slot], sem.at[0])
            for slot, parts in enumerate(pieces)
        ]
    )
    wait_bytes(lines, sem.at[0])
    line = lax.broadcasted_iota(jnp.int32, (across, width), 0)
    lane = lax.broadcasted_iota(jnp.int32, (across, width), 1)
    chosen = (lane >= line * rows) & (lane < (line + 1) * rows)
    up_line = lax.broadcasted_iota(jnp.int32, (QUART, width), 0)
    up_lane = lax.broadcasted_iota(jnp.int32, (QUART, width), 1)
    ups = jnp.zeros((QUART, width), F32)
    for slot in range(plan.shards):
        values = lines[slot].astype(F32)
        for group in range(groups):
            at = (slot * groups + group) * across
            picked = jnp.where(chosen, jnp.broadcast_to(values[group : group + 1], chosen.shape), 0.0)
            spread[at : at + across, :] = picked.astype(BF16)
        first = QUART * rows * devs[slot]
        there = lax.rem(first, width)
        moved = jnp.broadcast_to(values[8 // across : 8 // across + 1], (8, width))
        moved = pltpu.roll(moved, lax.rem(there + width - 8 % across * rows, width), 1)[:QUART]
        here = (up_line == first // width) & (up_lane >= there) & (up_lane < there + QUART * rows)
        ups = jnp.where(here, moved, ups)
    source = lax.broadcasted_iota(jnp.int32, (width, rows), 0)
    target = lax.broadcasted_iota(jnp.int32, (width, rows), 1)
    fold = sum(jnp.where(source == target + place * rows, 1.0, 0.0) for place in range(across))
    narrow = mm(spread[...], fold.astype(BF16)).astype(BF16)
    entry = lax.broadcasted_iota(jnp.int32, (rows, width), 0)
    column = lax.broadcasted_iota(jnp.int32, (rows, width), 1)
    total = None
    for slot in range(plan.shards):
        at = slot * groups * across
        place = jnp.where(column == entry + devs[slot] * rows, 1.0, 0.0).astype(BF16)
        term = mm(narrow[at : at + groups * across], place)
        total = term if total is None else total + term
    out_ref[...] = jnp.zeros_like(out_ref)
    out_ref[:8, :] = total[:8]
    out_ref[8 : 8 + QUART, :] = ups
    entry = lax.broadcasted_iota(jnp.int32, total.shape, 0)
    for item in range(plan.items):
        picked = jnp.where(entry == 12 + lead[item], total, 0.0)
        out_ref[12 + item : 13 + item, :] = jnp.sum(picked, 0, keepdims=True)


def unpack_kernel(grads_ref, up_ref, down_ref):
    _, rows, width = grads_ref.shape
    for part in range(QUART):
        up_ref[:, part * width : (part + 1) * width] = grads_ref[part].astype(F32)
        down_ref[part * rows : (part + 1) * rows, :] = grads_ref[QUART + part].astype(F32)


def add_kernel(work, *refs):
    outs, at = refs[len(refs) - len(work) :], 0
    for (low, high, first), out in zip(work, outs):
        mine, other = refs[at], refs[at + 1]
        at += 2
        cuts, came = [low, high], None
        if first is not None:
            came = refs[at]
            at += 1
            cuts = sorted({low, first, first + came.shape[0], high})
        for start, end in zip(cuts, cuts[1:]):
            value = mine[0, start:end, :].astype(F32) + other[0, start:end, :].astype(F32)
            if came is not None and first <= start < first + came.shape[0]:
                value = value + came[start - first : end - first, :].astype(F32)
            out[start - low : end - low, :] = value.astype(BF16)


def total_kernel(many, mine, other, ahead, behind, qkv, out, *refs):
    width = mine.shape[2]
    rows = out.shape[0]

    def rows_of(low, count):
        here = slice(low, low + count)
        value = mine[0, here, :].astype(F32) + other[0, here, :].astype(F32)
        return value + (ahead[here, :].astype(F32) + behind[here, :].astype(F32))

    for part in range(OUT):
        qkv[:, part * width : (part + 1) * width] = rows_of(part * rows, rows)
    out[...] = rows_of(OUT * rows, rows)
    vectors, (up_bias, table, small) = refs[:8], refs[8:]
    lines = rows_of(FIRST * rows, EXTRA)
    for index in range(many):
        line, place = divmod(index, width // rows)
        small[index : index + 1, :] = lines[line : line + 1, place * rows : (place + 1) * rows]
    for index, vector in enumerate(vectors):
        vector[...] = small[index : index + 1, :]
    for part in range(QUART):
        up_bias[:, part * rows : (part + 1) * rows] = small[8 + part : 9 + part, :]
    table[...] = small[12:many, :]


SMEM = pl.BlockSpec(memory_space=pltpu.SMEM)
VMEM = pl.BlockSpec(memory_space=pltpu.VMEM)
HBM = pl.BlockSpec(memory_space=pltpu.HBM)
ANY = pl.BlockSpec(memory_space=pl.ANY)


def kept_shapes(plan):
    tokens, width = plan.tokens, plan.width
    return [
        ((tokens, width), BF16),
        ((tokens, 3 * width), BF16),
        ((tokens, width), BF16),
        ((tokens, width), F32),
        ((tokens, width), BF16),
        ((plan.items * plan.pairs, 2 * plan.length, plan.length), F32),
        ((tokens, 4 * width), BF16),
        ((tokens, 4 * width), F32),
    ]


def held_blocks(plan, blocks):
    return pltpu.VMEM((blocks, plan.shards, plan.rows, plan.width), BF16)


def call(kernel, outs, in_specs, out_specs, scratch, name, work, limit, args):
    args = [
        pltpu.with_memory_space_constraint(arg, pltpu.HBM) if spec is HBM else arg
        for arg, spec in zip(args, in_specs)
    ]
    return pl.pallas_call(
        kernel,
        out_shape=outs,
        in_specs=in_specs,
        out_specs=out_specs,
        scratch_shapes=scratch,
        compiler_params=pltpu.CompilerParams(vmem_limit_bytes=limit * 1024 * 1024),
        cost_estimate=pl.CostEstimate(flops=2 * work[0], bytes_accessed=work[1], transcendentals=0),
        name=name,
    )(*args)


def of(shape):
    return jax.ShapeDtypeStruct(*shape)


def inside(shape):
    return pltpu.VMEM(*shape)


def run_attend(plan, lengths, flag, devs, x, vec, pieces):
    kept = kept_shapes(plan)
    block = plan.width * plan.width
    return call(
        functools.partial(attend_kernel, plan),
        [of(kept[3]), of(kept[4])],
        [SMEM, SMEM, SMEM, VMEM, VMEM] + [HBM] * len(pieces),
        [VMEM, VMEM],
        [held_blocks(plan, FIRST)] + [inside(shape) for shape in kept[:3]] + [pltpu.SemaphoreType.DMA((2,))],
        "attend",
        (FIRST * block * plan.tokens, FIRST * block * 2),
        14,
        (lengths, flag, devs, x, vec, *pieces),
    )


def run_vectors(plan, many, devs, lead, pieces):
    groups = pl.cdiv(many, plan.width // plan.rows) * (plan.width // plan.rows)
    return call(
        functools.partial(vectors_kernel, plan, many),
        jax.ShapeDtypeStruct((16, plan.width), F32),
        [SMEM, SMEM] + [HBM] * len(pieces),
        VMEM,
        [
            pltpu.VMEM((plan.shards, EXTRA, plan.width), BF16),
            pltpu.VMEM((plan.shards * groups, plan.width), BF16),
            pltpu.SemaphoreType.DMA((1,)),
        ],
        "vectors",
        (plan.width * plan.width * plan.rows, plan.width * plan.width * 4),
        12,
        (devs, lead, *pieces),
    )


def run_mlp(plan, middle, hidden, vec, gathered):
    block = plan.width * plan.width
    return call(
        functools.partial(mlp_kernel, plan),
        jax.ShapeDtypeStruct(hidden.shape, BF16),
        [VMEM, VMEM, VMEM, HBM],
        VMEM,
        [held_blocks(plan, SECOND), pltpu.SemaphoreType.DMA((QUART,)), pltpu.SemaphoreType.DMA((QUART,))],
        "mlp",
        (SECOND * block * plan.tokens, SECOND * block * 2),
        16,
        (middle, hidden, vec, gathered),
    )


def run_load(plan, devs, after, cot, firsts, gathered):
    block = plan.width * plan.width
    return call(
        functools.partial(load_kernel, plan),
        [held_blocks(plan, FIRST), held_blocks(plan, SECOND), inside(kept_shapes(plan)[7])],
        [SMEM, ANY, VMEM] + [HBM] * (1 + len(firsts)),
        [VMEM] * 3,
        [pltpu.SemaphoreType.DMA((2,)), pltpu.SemaphoreType.DMA((QUART,))],
        "load",
        (QUART * block * plan.tokens, (FIRST + SECOND) * block * 4),
        4,
        (devs, after, cot, gathered, *firsts),
    )


def run_chain(plan, lengths, flag, x, recv, cot, vec, held1, held2, grad_act):
    shapes = kept_shapes(plan)
    block = plan.width * plan.width
    rest = [shapes[index] for index in (0, 0, 1, 2, 3, 5)]
    return call(
        functools.partial(chain_kernel, plan),
        [pltpu.HBM(*shapes[0]), of(shapes[0])]
        + [inside(shapes[index]) for index in (4, 6, 7)]
        + [pltpu.HBM(*shape) for shape in rest],
        [SMEM] * 2 + [VMEM] * 7,
        [HBM] + [VMEM] * 4 + [HBM] * len(rest),
        [inside(shape) for shape in rest]
        + [inside(shapes[0]), inside(shapes[0]), inside(shapes[1])]
        + [pltpu.SemaphoreType.DMA((len(rest) + 1,))],
        "chain",
        (24 * block * plan.tokens, 12 * block),
        14,
        (lengths, flag, x, recv, cot, vec, held1, held2, grad_act),
    )


def grad_shapes(plan):
    if plan.parts == 1:
        return [pltpu.HBM((1, FIRST * plan.rows, plan.width), BF16)]
    rows = FIRST * plan.rows + EXTRA
    return [
        pltpu.HBM((count, rows, plan.width), BF16)
        for count in (plan.shards // 2, plan.shards // 2, 1)
    ]


def stage_scratch(plan):
    return [
        pltpu.VMEM((SLOTS, plan.shards, plan.rows, plan.width), BF16),
        pltpu.SemaphoreType.DMA((SLOTS,)),
    ]


def run_mlp_back(plan, flag, arriving, cot, held2, hidden, act, slope):
    shapes = kept_shapes(plan)
    block = plan.width * plan.width
    return call(
        functools.partial(mlp_back_kernel, plan),
        [
            of(shapes[3]),
            jax.ShapeDtypeStruct((16, plan.width), F32),
            pltpu.HBM((plan.shards, SECOND, plan.rows, plan.width), BF16),
        ],
        [SMEM] + [VMEM] * 6,
        [VMEM, VMEM, HBM],
        [inside(shapes[6])] + stage_scratch(plan),
        "mlp_back",
        (2 * SECOND * block * plan.tokens, SECOND * block * 2),
        10,
        (flag, arriving, cot, held2, hidden, act, slope),
    )


def run_rest(plan, many, flag, devs, lead, arriving, cot, grad_hidden, small, vec, kept, pieces):
    shapes = kept_shapes(plan)
    block = plan.width * plan.width
    across = plan.width // plan.rows
    high = pl.cdiv(many, across) * across
    lines = (plan.shards, EXTRA, plan.width)
    rest = [shapes[index] for index in (0, 0, 1, 2, 3, 5)]
    input_grad, small, *grads = call(
        functools.partial(rest_kernel, plan, many),
        [of(shapes[3]), jax.ShapeDtypeStruct((16, plan.width), F32)] + grad_shapes(plan),
        [SMEM] * 3 + [VMEM] * 5 + [HBM] * (len(rest) + len(pieces)),
        [VMEM] * 2 + [HBM] * plan.parts,
        [inside(shape) for shape in rest]
        + [held_blocks(plan, FIRST)]
        + [inside(shapes[index]) for index in (3, 0, 1)]
        + [pltpu.SemaphoreType.DMA((2,)), pltpu.SemaphoreType.DMA((len(rest),))]
        + stage_scratch(plan)
        + [pltpu.SemaphoreType.DMA((1,)), pltpu.VMEM((plan.shards * high, plan.rows), BF16)]
        + [pltpu.VMEM(lines, F32), pltpu.VMEM(lines, BF16)],
        "rest",
        (2 * FIRST * block * plan.tokens, 2 * FIRST * block * 2),
        26,
        (flag, devs, lead, arriving, cot, grad_hidden, small, vec, *kept, *pieces),
    )
    return input_grad, small, grads


def run_add(mine, other, work):
    _, rows, width = mine.shape
    mine = pltpu.with_memory_space_constraint(mine, pltpu.HBM)
    specs, args, plans, outs = [], [], [], []
    for way, (slot, low, high, came) in enumerate(work):
        there = slot if other.shape[0] > 1 else 0
        specs += [
            pl.BlockSpec((1, rows, width), lambda index, slot=slot: (slot, 0, 0))
            for slot in (slot, there)
        ]
        args += [mine, other]
        first = None
        if came is not None:
            specs.append(pl.BlockSpec(came.shape, lambda index: (0, 0)))
            args.append(came)
            first = rows - came.shape[0] if way else 0
        plans.append((low, high, first))
        outs.append((high - low, width))
    return pl.pallas_call(
        functools.partial(add_kernel, plans),
        out_shape=[jax.ShapeDtypeStruct(shape, BF16) for shape in outs],
        grid=(1,),
        in_specs=specs,
        out_specs=[pl.BlockSpec(shape, lambda index: (0, 0)) for shape in outs],
        compiler_params=pltpu.CompilerParams(vmem_limit_bytes=14 * 1024 * 1024),
        name="add",
    )(*args)


def run_total(one, many, shapes):
    args = [pltpu.with_memory_space_constraint(one.mine, pltpu.HBM), one.other]
    _, rows, width = one.mine.shape
    first = pl.BlockSpec((1, rows, width), lambda index: (0, 0, 0))
    whole = pl.BlockSpec((rows, width), lambda index: (0, 0))
    return pl.pallas_call(
        functools.partial(total_kernel, many),
        out_shape=[jax.ShapeDtypeStruct(shape, F32) for shape in shapes],
        grid=(1,),
        in_specs=[first, first, whole, whole],
        out_specs=[pl.BlockSpec(shape, lambda index: (0, 0)) for shape in shapes],
        scratch_shapes=[pltpu.VMEM((many, shapes[2][1]), F32)],
        compiler_params=pltpu.CompilerParams(vmem_limit_bytes=14 * 1024 * 1024),
        name="total",
    )(*args, *one.carried)


def after(value, *others):
    return lax.optimization_barrier((value, *others))[0]


def shifted(value, axis, steps):
    count = lax.axis_size(axis)
    first, last = (max(0, -steps), min(count, count - steps))
    return lax.ppermute(value, axis, [(source, source + steps) for source in range(first, last)])


class Ring:
    def __init__(self, count):
        self.count, self.chips = count, count // 2
        self.walk = list(range(0, self.chips, 2)) + list(range(self.chips - 1, 0, -2))
        self.order = [2 * chip + core for chip in self.walk for core in range(2)]
        after = self.walk[1:] + self.walk[:1]
        self.onward = [
            (2 * here + core, 2 * there + core)
            for here, there in zip(self.walk, after)
            for core in range(2)
        ]
        self.back = [(there, here) for here, there in self.onward]
        self.sibling = [(index, index ^ 1) for index in range(count)]

    def slots(self):
        index = lax.axis_index("dp")
        chip, core = index // 2, index % 2
        place_of = lambda chip: jnp.where(chip % 2 == 0, chip // 2, self.chips - 1 - chip // 2)
        steps = jnp.arange(self.chips, dtype=jnp.int32)
        ahead = (place_of(chip) + steps) % self.chips
        chips = jnp.where(ahead < (self.chips + 1) // 2, 2 * ahead, 2 * (self.chips - 1 - ahead) + 1)
        devs = jnp.concatenate([2 * chips + core, 2 * chips + 1 - core]).astype(jnp.int32)
        return devs

    def step(self, ahead, behind):
        return lax.ppermute(ahead, "dp", self.onward), lax.ppermute(behind, "dp", self.back)

    def gather(self, shard, low):
        half = self.chips // 2
        own = [[shard]] + [None] * (self.chips - 1)
        ahead = behind = shard
        for step in range(1, half):
            ahead, behind = self.step(ahead, behind)
            own[self.chips - step], own[step] = [ahead], [behind]
            ahead, behind = lax.optimization_barrier((ahead, behind))
        own[half] = list(self.step(ahead[:low], behind[low:]))
        return [piece for pieces in own for piece in pieces]

    def siblings(self, pieces):
        return [lax.ppermute(piece, "dp", self.sibling) for piece in pieces]


class RingSum:
    def __init__(self, ring, mine, other, opposite, low):
        self.ring, self.mine, self.low = ring, mine, low
        self.other, self.opposite = other, opposite
        self.time = ring.chips // 2
        self.carried = [None, None]

    def add(self):
        rows = self.mine.shape[1]
        other = self.other
        if self.carried[0] is None:
            other = self.opposite
            work = [(self.time, 0, self.low, None), (self.time, self.low, rows, None)]
        else:
            work = [
                (self.time, 0, rows, self.carried[0]),
                (self.ring.chips - self.time, 0, rows, self.carried[1]),
            ]
        self.carried = run_add(self.mine, other, work)

    def send(self):
        self.carried = self.ring.step(*self.carried)
        self.time -= 1


def body(
    block_input, cotangent, lengths, leads,
    norm_gain1, norm_bias1, lead_table, qkv_weight, query_bias, value_bias, out_weight, out_bias,
    norm_gain2, norm_bias2, up_weight, up_bias, down_weight, down_bias,
):
    count = lax.axis_size("dp")
    micro, local, length, width = block_input.shape
    items = micro * local
    rows = width // count
    leads_count = lead_table.shape[2]
    flag = lax.axis_index("section").astype(jnp.int32).reshape(1)
    flat = lambda value: value.reshape(items * length, width)
    x, cot = flat(block_input), flat(cotangent)
    lens, lead = lengths.reshape(items), leads.reshape(items)

    vectors = (
        norm_gain1, norm_bias1, query_bias, value_bias, out_bias, norm_gain2, norm_bias2, down_bias
    )
    many = 12 + leads_count
    aligned = rows % 16 == 0 and count % 4 == 0 and pl.cdiv(many, width // rows) <= EXTRA
    if aligned:
        ring = Ring(count)
        first, second = pl.pallas_call(
            pack_kernel,
            out_shape=[
                jax.ShapeDtypeStruct((FIRST * rows + EXTRA, width), BF16),
                jax.ShapeDtypeStruct((SECOND, rows, width), BF16),
            ],
            scratch_shapes=[pltpu.VMEM((many, rows), F32), pltpu.VMEM((EXTRA, width), F32)],
            name="pack",
        )(qkv_weight[0], out_weight[0], up_weight[0], down_weight[0], *vectors, up_bias, lead_table[0].T)
        gathered = lax.all_gather(second, "dp", axis=0, tiled=True, axis_index_groups=[ring.order])
        gathered = gathered.reshape(count, SECOND, rows, width)
        firsts = ring.gather(first, LOW * rows)
        firsts = firsts + ring.siblings(firsts)
        devs = ring.slots()
        plan = Plan(ring.order, rows, items, length, width)
        vec = run_vectors(plan, many, devs, lead, firsts)
    else:
        wide_blocks = lambda value: value[0].reshape(rows, -1, width).transpose(1, 0, 2)
        packed = jnp.concatenate(
            [wide_blocks(qkv_weight), out_weight, wide_blocks(up_weight), down_weight.reshape(QUART, rows, width)], 0
        )
        everything = lax.all_gather(packed.astype(BF16), "dp", axis=0)
        across_blocks = lambda value: value.transpose(1, 0, 2, 3).reshape(-1, width, width)
        firsts = [across_blocks(everything[:, :FIRST])]
        gathered = jnp.concatenate(
            [
                across_blocks(everything[:, FIRST : FIRST + QUART]),
                everything[:, FIRST + QUART :].reshape(QUART, width, width),
            ],
            0,
        )[None]
        devs = jnp.zeros((1,), jnp.int32)
        plan = Plan([0], width, items, length, width)
        small = jnp.concatenate([*vectors, up_bias.reshape(4, rows), lead_table[0].T], 0).astype(BF16)
        wide = lax.all_gather(small, "dp", axis=1, tiled=True).astype(F32)
        vec = jnp.concatenate(
            [wide[:8], wide[8:12].reshape(4, count, rows).transpose(1, 0, 2).reshape(4, width)]
            + [lax.dynamic_slice_in_dim(wide, 12 + lead[item], 1, 0) for item in range(items)]
            + [jnp.zeros((4 - items, width), F32)],
            0,
        )

    middle, hidden = run_attend(plan, lens, flag, devs, x, vec, firsts)
    first_out = run_mlp(plan, middle, hidden, vec, gathered)
    recv = shifted(first_out, "section", 1)
    held1, held2, grad_act = run_load(plan, devs, first_out, cot, firsts, gathered)
    output, first_grad, hidden, act, slope, *kept = run_chain(
        plan, lens, flag, x, recv, cot, vec, held1, held2, grad_act
    )
    arriving = shifted(first_grad, "section", -1)
    grad_hidden, sums, grads2 = run_mlp_back(plan, flag, arriving, cot, held2, hidden, act, slope)
    input_grad, sums, grads1 = run_rest(
        plan, many, flag, devs, lead, arriving, cot, grad_hidden, sums, vec, kept, firsts
    )
    if aligned:
        (opposite,) = ring.siblings(grads1[2:])
        (other,) = ring.siblings([after(grads1[1], opposite)])
        first_sum = RingSum(ring, grads1[0], other, opposite, LOW * rows)
        while first_sum.time:
            first_sum.add()
            first_sum.send()
        grads2 = lax.psum_scatter(
            grads2.reshape(count * SECOND, rows, width),
            "dp", scatter_dimension=0, tiled=True, axis_index_groups=[ring.order],
        )
        grad_up, grad_down = pl.pallas_call(
            unpack_kernel,
            out_shape=[
                jax.ShapeDtypeStruct((rows, QUART * width), F32),
                jax.ShapeDtypeStruct((QUART * rows, width), F32),
            ],
            name="unpack",
        )(grads2)
        grad_qkv, grad_out, *small_grads = run_total(
            first_sum, many,
            [(rows, OUT * width), (rows, width)] + [(1, rows)] * 8 + [(1, QUART * rows), (leads_count, rows)],
        )
    else:
        split = lambda value: value[0].reshape(-1, count, rows, width).transpose(1, 0, 2, 3)
        grads = jnp.concatenate(
            [
                split(grads1[0]),
                split(grads2[0, :QUART].reshape(1, QUART * width, width)),
                grads2[0, QUART:].reshape(count, QUART, rows, width),
            ],
            1,
        )
        grads = lax.psum_scatter(grads, "dp", scatter_dimension=0, tiled=False).astype(F32)
        across = lambda value: value.transpose(1, 0, 2).reshape(rows, -1)
        grad_qkv, grad_out = across(grads[:OUT]), grads[OUT]
        grad_up = across(grads[FIRST : FIRST + QUART])
        grad_down = grads[FIRST + QUART :].reshape(QUART * rows, width)
        hot = (jnp.arange(leads_count)[:, None] == lead[None, :]).astype(F32)
        table = sum(hot[:, item : item + 1] * sums[12 + item : 13 + item] for item in range(items))
        up_sums = sums[8:12].reshape(count, 4, rows).transpose(1, 0, 2).reshape(4, width)
        spread = lax.psum_scatter(
            jnp.concatenate([sums[:8], up_sums, table], 0), "dp", scatter_dimension=1, tiled=True
        )
        small_grads = [spread[index : index + 1] for index in range(8)]
        small_grads += [spread[8:12].reshape(1, 4 * rows), spread[12:]]
    vector = small_grads
    shape = (1, micro, local, length, width)
    return (
        output.reshape(shape),
        input_grad.reshape(shape),
        vector[0],
        vector[1],
        vector[9].T[None],
        grad_qkv[None],
        vector[2],
        vector[3],
        grad_out[None],
        vector[4],
        vector[5],
        vector[6],
        grad_up[None],
        vector[8],
        grad_down[None],
        vector[7],
    )


def solution(mesh):
    weights = (
        P("section", "dp"),
        P("section", "dp"),
        P("section", "dp", None),
        P("section", "dp", None),
        P("section", "dp"),
        P("section", "dp"),
        P("section", "dp", None),
        P("section", "dp"),
        P("section", "dp"),
        P("section", "dp"),
        P("section", "dp", None),
        P("section", "dp"),
        P("section", "dp", None),
        P("section", "dp"),
    )
    rows = P(None, "dp", None, None)
    layers = P("section", None, "dp", None, None)
    return jax.shard_map(
        body,
        mesh=mesh,
        in_specs=(rows, rows, P(None, "dp"), P(None, "dp")) + weights,
        out_specs=(layers, layers) + weights,
        check_vma=False,
    )
```

```python
import functools

import jax
import jax.numpy as jnp
from jax import lax
from jax.experimental import pallas as pl
from jax.experimental.pallas import tpu as pltpu
from jax.sharding import PartitionSpec as P

HEAD = 64
PAIR = 2 * HEAD
EPS = 1e-06
SCALE_FACTOR = 0.125
GELU_A = 0.7978845608028654
GELU_B = 0.044715
F32 = jnp.float32
BF16 = jnp.bfloat16
OUT = 3
FIRST = 4
SECOND = 8
QUART = 4
EXTRA = 16
LOW = 2


def mm(left, right):
    return jnp.dot(left, right, preferred_element_type=F32)


def mm_nt(left, right):
    return lax.dot_general(left, right, (((1,), (1,)), ((), ())), preferred_element_type=F32)


def mm_tn(left, right):
    return lax.dot_general(left, right, (((0,), (0,)), ((), ())), preferred_element_type=F32)


def normalised(values):
    mean = jnp.mean(values, -1, keepdims=True)
    centred = values - mean
    variance = jnp.mean(centred * centred, -1, keepdims=True)
    rstd = lax.rsqrt(variance + EPS)
    return centred * rstd, rstd


def norm_back(grad, xhat, rstd, gain):
    scaled = grad * gain
    first = jnp.mean(scaled, -1, keepdims=True)
    second = jnp.mean(scaled * xhat, -1, keepdims=True)
    return rstd * (scaled - first - xhat * second)


def gelu_both(values):
    square = values * values
    slope = GELU_A * (1.0 + 3.0 * GELU_B * square)
    bend = jnp.tanh(GELU_A * values * (1.0 + GELU_B * square))
    half = 0.5 * (1.0 + bend)
    return values * half, half + 0.5 * values * (1.0 - bend * bend) * slope


def split_pair(rows):
    lane = lax.broadcasted_iota(jnp.int32, rows.shape, 1)
    zero = jnp.zeros_like(rows)
    return jnp.concatenate(
        [jnp.where(lane < HEAD, rows, zero), jnp.where(lane < HEAD, zero, rows)], 0
    )


def join_pair(stacked):
    count = stacked.shape[0] // 2
    lane = lax.broadcasted_iota(jnp.int32, (count, PAIR), 1)
    return jnp.where(lane < HEAD, stacked[:count], stacked[count:])


def runs_of(order):
    if all(order[at + 1] == order[at] + 1 for at in range(0, len(order) - 1, 2)) and len(order) > 1:
        return [(at, order[at], 2) for at in range(0, len(order), 2)]
    return [(at, device, 1) for at, device in enumerate(order)]


class Plan:
    def __init__(self, order, rows, items, length, width):
        self.order, self.shards, self.rows = order, len(order), rows
        self.items, self.length, self.width = items, length, width
        self.tokens = items * length
        self.low = LOW * rows
        self.pairs = width // PAIR
        whole = self.shards % QUART == 0
        self.runs = [(0, QUART)] if whole else [(block, 1) for block in range(QUART)]
        self.parts = 3 if self.shards > 1 else 1


def slot_pieces(plan, refs):
    if plan.shards == 1:
        return [[(0, refs[0])]]
    refs, slots, half = list(refs), [], plan.shards // 4
    for slot in range(plan.shards):
        parts = [(0, refs.pop(0))]
        if slot % (plan.shards // 2) == half:
            parts.append((plan.low, refs.pop(0)))
        slots.append(parts)
    return slots


def piece_rows(parts, row, count):
    start, ref = [part for part in parts if part[0] <= row][-1]
    return ref.at[pl.ds(row - start, count)]


def first_copies(plan, refs, devs, held, sem, blocks):
    if plan.shards == 1:
        return block_copies(refs, devs, held, sem, blocks)
    return [
        pltpu.make_async_copy(
            piece_rows(parts, block * plan.rows, plan.rows), held.at[block, devs[slot]], sem
        )
        for slot, parts in enumerate(slot_pieces(plan, refs))
        for block in range(blocks.start, blocks.start + blocks.size)
    ]


def block_copies(pieces, devs, held, sem, blocks, at=0):
    return [
        pltpu.make_async_copy(
            piece.at[blocks], held.at[pl.ds(at + blocks.start, blocks.size), devs[slot]], sem
        )
        for slot, piece in enumerate(pieces)
    ]


def up_copies(plan, gathered, held, sem, part):
    return [
        pltpu.make_async_copy(
            gathered.at[pl.ds(place, count), part], held.at[part, pl.ds(device, count)], sem
        )
        for place, device, count in runs_of(plan.order)
    ]


def down_copies(plan, pieces, devs, held, sems):
    copies = []
    for slot, piece in enumerate(pieces):
        for first, count in plan.runs:
            block, row = divmod(QUART * devs[slot] + first, plan.shards)
            copy = pltpu.make_async_copy(
                piece.at[pl.ds(first, count)],
                held.at[QUART + block, pl.ds(row, count)],
                sems.at[block],
            )
            copies.append((block, copy))
    return copies


def second_pieces(plan, gathered):
    ups = [gathered.at[place, pl.ds(0, QUART)] for place in range(plan.shards)]
    downs = [gathered.at[place, pl.ds(QUART, QUART)] for place in range(plan.shards)]
    return ups, downs


def start_all(copies):
    for copy in copies:
        copy.start()


def wait_bytes(part, sem):
    pltpu.make_async_copy(part, part, sem).wait()


def block_of(plan, held, index):
    return held[index].reshape(plan.width, plan.width)


def columns_of(plan, index):
    return slice(index * plan.width, (index + 1) * plan.width)


def attention_forward(plan, lengths, qkv_ref, attended_ref, probs_ref):
    width, length = plan.width, plan.length
    key_index = lax.broadcasted_iota(jnp.int32, (2 * length, length), 1)
    for item in range(plan.items):
        rows = slice(item * length, (item + 1) * length)
        valid = key_index < lengths[item]
        for pair in range(plan.pairs):
            at = pair * PAIR
            query = split_pair(qkv_ref[rows, at : at + PAIR])
            key = qkv_ref[rows, width + at : width + at + PAIR]
            value = qkv_ref[rows, 2 * width + at : 2 * width + at + PAIR]
            logits = jnp.where(valid, mm_nt(query, key) * SCALE_FACTOR, -1000000000.0)
            expo = jnp.exp(logits - jnp.max(logits, -1, keepdims=True))
            probs = expo / jnp.sum(expo, -1, keepdims=True)
            if probs_ref is not None:
                probs_ref[item * plan.pairs + pair] = probs
            attended_ref[rows, at : at + PAIR] = join_pair(mm(probs.astype(BF16), value)).astype(
                BF16
            )


def first_half(plan, inputs, lengths, vec, held, wait, normed_ref, qkv_ref, attended_ref, probs_ref, hidden_ref):
    width, length = plan.width, plan.length
    values = inputs.astype(F32)
    xhat, _ = normalised(values)
    base = xhat * vec[0:1, :] + vec[1:2, :]
    for item in range(plan.items):
        rows = slice(item * length, (item + 1) * length)
        normed_ref[rows, :] = (base[rows] + vec[12 + item : 13 + item, :]).astype(BF16)
    wait(0)
    for part, bias in enumerate((2, None, 3)):
        joined = mm(normed_ref[...], block_of(plan, held, part))
        if bias is not None:
            joined = joined + vec[bias : bias + 1, :]
        qkv_ref[:, columns_of(plan, part)] = joined.astype(BF16)
    attention_forward(plan, lengths, qkv_ref, attended_ref, probs_ref)
    wait(1)
    middle = values + (mm(attended_ref[...], block_of(plan, held, OUT)) + vec[4:5, :])
    xhat, _ = normalised(middle)
    hidden_ref[...] = (xhat * vec[5:6, :] + vec[6:7, :]).astype(BF16)
    return middle


def second_half(plan, hidden_ref, vec, held, act_ref=None, slope_ref=None, wait=None):
    total = None
    for part in range(QUART):
        if wait is not None:
            wait(part)
        pre_act = mm(hidden_ref[...], block_of(plan, held, part)) + vec[8 + part : 9 + part, :]
        act, slope = gelu_both(pre_act)
        act = act.astype(BF16)
        if act_ref is not None:
            act_ref[:, columns_of(plan, part)] = act
            slope_ref[:, columns_of(plan, part)] = slope
        if wait is not None:
            wait(QUART + part)
        term = mm(act, block_of(plan, held, QUART + part))
        total = term if total is None else total + term
    return total + vec[7:8, :]


def attention_back(plan, probs_ref, qkv_ref, grad_attended_ref, rows_ref, items=None):
    width, length = plan.width, plan.length
    for item in range(plan.items) if items is None else items:
        rows = slice(item * length, (item + 1) * length)
        for pair in range(plan.pairs):
            at = pair * PAIR
            query = split_pair(qkv_ref[rows, at : at + PAIR])
            key = qkv_ref[rows, width + at : width + at + PAIR]
            value = qkv_ref[rows, 2 * width + at : 2 * width + at + PAIR]
            grad = split_pair(grad_attended_ref[rows, at : at + PAIR])
            probs = probs_ref[item * plan.pairs + pair]
            grad_probs = mm_nt(grad, value)
            centre = jnp.sum(grad_probs * probs, -1, keepdims=True)
            grad_logits = (probs * (grad_probs - centre)).astype(BF16)
            grad_query = join_pair(mm(grad_logits, key)) * SCALE_FACTOR
            grad_key = mm_tn(grad_logits, query) * SCALE_FACTOR
            grad_value = mm_tn(probs.astype(BF16), grad)
            rows_ref[rows, at : at + PAIR] = grad_query.astype(BF16)
            rows_ref[rows, width + at : width + at + PAIR] = grad_key.astype(BF16)
            rows_ref[rows, 2 * width + at : 2 * width + at + PAIR] = grad_value.astype(BF16)


def column_sum(values):
    return jnp.sum(values.astype(F32), 0, keepdims=True)


def attend_kernel(plan, lengths, flag, devs, x_ref, vec, *refs):
    pieces, (middle_ref, hidden_ref, held, normed, qkv, attended, sems) = refs[:-7], refs[-7:]
    start_all(first_copies(plan, pieces, devs, held, sems.at[0], pl.ds(0, OUT)))
    start_all(first_copies(plan, pieces, devs, held, sems.at[1], pl.ds(OUT, 1)))

    def wait(group):
        blocks = pl.ds(OUT, 1) if group else pl.ds(0, OUT)
        wait_bytes(held.at[blocks], sems.at[group])

    middle_ref[...] = first_half(
        plan, x_ref[...], lengths, vec, held, wait, normed, qkv, attended, None, hidden_ref
    )


def mlp_kernel(plan, flag, middle_ref, hidden_ref, vec, gathered, y_ref, held, sems, down_sems):
    @pl.when(flag[0] == 0)
    def _():
        _, downs = second_pieces(plan, gathered)
        down = down_copies(plan, downs, plan.order, held, down_sems)
        for part in range(QUART):
            start_all(up_copies(plan, gathered, held, sems.at[part], part))
            start_all([copy for block, copy in down if block == part])

        def wait(block):
            sem = sems.at[block] if block < QUART else down_sems.at[block - QUART]
            wait_bytes(held.at[block], sem)

        total = second_half(plan, hidden_ref, vec, held, wait=wait)
        y_ref[...] = (middle_ref[...] + total).astype(BF16)


def load_kernel(plan, devs, after, cot_ref, gathered, *refs):
    firsts, (held1, held2, grad_act, sems, down_sems) = refs[:-5], refs[-5:]
    ups, downs = second_pieces(plan, gathered)
    start_all([copy for _, copy in down_copies(plan, downs, plan.order, held2, down_sems)])
    start_all(block_copies(ups, plan.order, held2, sems.at[1], pl.ds(0, QUART)))
    start_all(first_copies(plan, firsts, devs, held1, sems.at[0], pl.ds(0, FIRST)))
    for part in range(QUART):
        wait_bytes(held2.at[QUART + part], down_sems.at[part])
        grad_act[:, columns_of(plan, part)] = mm_nt(
            cot_ref[...], block_of(plan, held2, QUART + part)
        )
    wait_bytes(held2.at[pl.ds(0, QUART)], sems.at[1])
    wait_bytes(held1, sems.at[0])


def input_grad(plan, items, vec, held1, xin_ref, qkv, probs, grad_middle, grad_attended, grad_rows, dx_ref):
    attention_back(plan, probs, qkv, grad_attended, grad_rows, items)
    rows = slice(items.start * plan.length, items.stop * plan.length)
    grad_normed = None
    for part in range(OUT):
        term = mm_nt(grad_rows[rows, columns_of(plan, part)], block_of(plan, held1, part))
        grad_normed = term if grad_normed is None else grad_normed + term
    xhat, rstd = normalised(xin_ref[rows, :].astype(F32))
    dx_ref[...] = (grad_middle[rows, :] + norm_back(grad_normed, xhat, rstd, vec[0:1, :])).astype(BF16)


def chain_kernel(
    plan, lengths, flag, x_ref, recv_ref, cot_ref, vec, held1, held2, grad_act,
    y_out, dx_ref, hidden, act, slope, xin_ref, qkv, probs, grad_middle, grad_attended, *refs,
):
    outs, (normed, attended, middle, y_ref, grad_rows, sems) = refs[:6], refs[6:]
    kept = (xin_ref, normed, qkv, attended, middle, probs)
    copies = [
        pltpu.make_async_copy(source, target, sems.at[index])
        for index, (source, target) in enumerate(zip(kept, outs))
    ]
    xin_ref[...] = jnp.where(flag[0] == 0, x_ref[...], recv_ref[...])
    middle[...] = first_half(
        plan, xin_ref[...], lengths, vec, held1, lambda group: None, normed, qkv, attended, probs, hidden
    )
    start_all(copies)
    y_ref[...] = (middle[...] + second_half(plan, hidden, vec, held2, act, slope)).astype(BF16)
    copies.append(pltpu.make_async_copy(y_ref, y_out, sems.at[len(copies)]))
    copies[-1].start()

    @pl.when(flag[0] == 1)
    def _():
        branch = cot_ref[...]
        grad_hidden = None
        for part in range(QUART):
            grad_pre = (slope[:, columns_of(plan, part)] * grad_act[:, columns_of(plan, part)]).astype(BF16)
            term = mm_nt(grad_pre, block_of(plan, held2, part))
            grad_hidden = term if grad_hidden is None else grad_hidden + term
        xhat, rstd = normalised(middle[...])
        grad_middle[...] = branch.astype(F32) + norm_back(grad_hidden, xhat, rstd, vec[5:6, :])
        grad_attended[...] = mm_nt(grad_middle[...].astype(BF16), block_of(plan, held1, OUT)).astype(BF16)
        input_grad(
            plan, range(plan.items // 2), vec, held1, xin_ref, qkv, probs, grad_middle, grad_attended, grad_rows, dx_ref
        )

    for copy in copies:
        copy.wait()


def chain_end_kernel(plan, flag, vec, held1, xin_ref, qkv, probs, grad_middle, grad_attended, dx_ref, grad_rows):
    @pl.when(flag[0] == 1)
    def _():
        input_grad(
            plan, range(plan.items // 2, plan.items), vec, held1, xin_ref, qkv, probs, grad_middle, grad_attended,
            grad_rows, dx_ref,
        )


class Stage:
    def __init__(self, plan, stage, sems):
        self.plan, self.stage, self.sems, self.sent = plan, stage, sems, 0

    def put(self, value, copies_of):
        slots = self.stage.shape[0]
        slot = self.sent % slots
        if self.sent >= slots:
            wait_bytes(self.stage.at[slot], self.sems.at[slot])
        self.sent += 1
        plan = self.plan
        self.stage[slot] = value.astype(BF16).reshape(plan.shards, plan.rows, plan.width)
        start_all(copies_of(self.stage.at[slot], self.sems.at[slot]))

    def drain(self):
        for slot in range(min(self.stage.shape[0], self.sent)):
            wait_bytes(self.stage.at[slot], self.sems.at[slot])


def mlp_back_kernel(
    plan, flag, some_ref, other_ref, cot_ref, held2, hidden, act, slope,
    grad_pre_out, small_ref, grads, grad_pre_ref, stage, stage_sems, pre_sem,
):
    arrived = jnp.concatenate([some_ref[...], other_ref[...]], 0)
    branch = jnp.where(flag[0] == 0, arrived, cot_ref[...])
    out = Stage(plan, stage, stage_sems)

    def copies_of_up(part):
        def copies(source, sem):
            return [
                pltpu.make_async_copy(
                    source.at[pl.ds(device, count)], grads.at[pl.ds(place, count), part], sem
                )
                for place, device, count in runs_of(plan.order)
            ]

        return copies

    def copies_of_down(part):
        def copies(source, sem):
            made = []
            for place, device in enumerate(plan.order):
                for first, count in plan.runs:
                    block, row = divmod(QUART * device + first, plan.shards)
                    if block == part:
                        made.append(
                            pltpu.make_async_copy(
                                source.at[pl.ds(row, count)],
                                grads.at[place, pl.ds(QUART + first, count)],
                                sem,
                            )
                        )
            return made

        return copies

    for part in range(QUART):
        columns = columns_of(plan, part)
        grad_act = mm_nt(branch, block_of(plan, held2, QUART + part))
        grad_pre = (slope[:, columns] * grad_act).astype(BF16)
        grad_pre_ref[:, columns] = grad_pre
        out.put(mm_tn(act[:, columns], branch), copies_of_down(part))
        out.put(mm_tn(hidden[...], grad_pre), copies_of_up(part))
    copy = pltpu.make_async_copy(grad_pre_ref, grad_pre_out, pre_sem.at[0])
    copy.start()
    small_ref[...] = jnp.zeros_like(small_ref)
    small_ref[7:8, :] = column_sum(branch)
    for part in range(QUART):
        small_ref[8 + part : 9 + part, :] = column_sum(grad_pre_ref[:, columns_of(plan, part)])
    out.drain()
    copy.wait()


def slot_target(plan, grads, slot):
    if plan.parts == 1:
        return grads[0].at[0]
    half = plan.shards // 2
    if slot == half + half // 2:
        return grads[2].at[0]
    return grads[slot // half].at[slot % half]


def slot_copies(plan, devs, grads, block):
    def copies(source, sem):
        return [
            pltpu.make_async_copy(
                source.at[devs[slot]],
                slot_target(plan, grads, slot).at[pl.ds(block * plan.rows, plan.rows)],
                sem,
            )
            for slot in range(plan.shards)
        ]

    return copies


def pack_sums(plan, lead, many, sums, stack, lines):
    rows, width = plan.rows, plan.width
    across = width // rows
    groups = pl.cdiv(many, across)
    high = groups * across
    leads = many - 12
    entry = lax.broadcasted_iota(jnp.int32, (high - 12, width), 0)
    table = jnp.zeros((high - 12, width), F32)
    for item in range(plan.items):
        table = table + jnp.where(entry == lead[item], sums[12 + item : 13 + item], 0.0)
    top, ups = sums[:8], sums[8:12]
    for device in range(plan.shards):
        columns = slice(device * rows, (device + 1) * rows)
        line, place = divmod(QUART * device * rows, width)
        parts = [
            ups[line : line + 1, place + part * rows : place + (part + 1) * rows]
            for part in range(QUART)
        ]
        share = jnp.concatenate([top[:, columns], *parts, table[:, columns]], 0)
        stack[device * high : (device + 1) * high, :] = share.astype(BF16)
    entry = lax.broadcasted_iota(jnp.int32, (rows, width), 0)
    column = lax.broadcasted_iota(jnp.int32, (rows, width), 1)
    tile = jnp.where(lax.rem(column, rows) == entry, 1.0, 0.0).astype(BF16)
    line = lax.broadcasted_iota(jnp.int32, (high, width), 0)
    lane = lax.broadcasted_iota(jnp.int32, (high, width), 1)
    place = lax.rem(line, across) * rows
    chosen = (lane >= place) & (lane < place + rows)
    lines[...] = jnp.zeros_like(lines)
    for device in range(plan.shards):
        spread = mm(stack[device * high : (device + 1) * high, :], tile)
        spread = jnp.where(chosen, spread, 0.0).reshape(groups, across, width)
        lines[device, 0:groups, :] = jnp.sum(spread, 1)


def rest_kernel(
    plan, many, flag, devs, lead, some_ref, other_ref, cot_ref, small_in, vec, gathered, grad_pre_in, *refs,
):
    count = plan.shards + (2 if plan.parts > 1 else 0)
    kept_in, pieces, refs = refs[:6], refs[6 : 6 + count], refs[6 + count :]
    dx_ref, small_ref = refs[:2]
    grads, refs = refs[2 : 2 + plan.parts], refs[2 + plan.parts :]
    kept, (held2, grad_pre, up_sems, pre_sem), refs = refs[:6], refs[6:10], refs[10:]
    held, grad_middle_ref, grad_attended, grad_rows, sems, kept_sems, stage, stage_sems, out_sem, stack, lines, packed = refs
    xin_ref, normed, qkv, attended, middle_ref, probs = kept
    pre_copy = pltpu.make_async_copy(grad_pre_in, grad_pre, pre_sem.at[0])
    pre_copy.start()
    for part in range(QUART):
        start_all(up_copies(plan, gathered, held2, up_sems.at[part], part))
    start_all(first_copies(plan, pieces, devs, held, sems.at[1], pl.ds(OUT, 1)))
    copies = [
        pltpu.make_async_copy(source, target, kept_sems.at[index])
        for index, (source, target) in enumerate(zip(kept_in, kept))
    ]
    for index in (4, 3, 2, 5, 1, 0):
        copies[index].start()
    start_all(first_copies(plan, pieces, devs, held, sems.at[0], pl.ds(0, OUT)))
    length = plan.length
    arrived = jnp.concatenate([some_ref[...], other_ref[...]], 0)
    branch = jnp.where(flag[0] == 0, arrived, cot_ref[...])
    out = Stage(plan, stage, stage_sems)
    small_ref[...] = small_in[...]
    pre_copy.wait()
    grad_hidden = None
    for part in range(QUART):
        wait_bytes(held2.at[part], up_sems.at[part])
        term = mm_nt(grad_pre[:, columns_of(plan, part)], block_of(plan, held2, part))
        grad_hidden = term if grad_hidden is None else grad_hidden + term
    copies[4].wait()
    xhat, rstd = normalised(middle_ref[...])
    small_ref[5:6, :] = column_sum(grad_hidden * xhat)
    small_ref[6:7, :] = column_sum(grad_hidden)
    grad_middle = branch.astype(F32) + norm_back(grad_hidden, xhat, rstd, vec[5:6, :])
    grad_middle_ref[...] = grad_middle
    attn_grad = grad_middle.astype(BF16)
    small_ref[4:5, :] = column_sum(attn_grad)
    wait_bytes(held.at[pl.ds(OUT, 1)], sems.at[1])
    grad_attended[...] = mm_nt(attn_grad, block_of(plan, held, OUT)).astype(BF16)
    copies[3].wait()
    out.put(mm_tn(attended[...], attn_grad), slot_copies(plan, devs, grads, OUT))
    copies[2].wait()
    copies[5].wait()
    attention_back(plan, probs, qkv, grad_attended, grad_rows)
    copies[1].wait()
    copies[0].wait()
    wait_bytes(held.at[pl.ds(0, OUT)], sems.at[0])
    grad_normed = None
    for part in range(OUT):
        rows = grad_rows[:, columns_of(plan, part)]
        term = mm_nt(rows, block_of(plan, held, part))
        grad_normed = term if grad_normed is None else grad_normed + term
        if part != 1:
            small_ref[2 + part // 2 : 3 + part // 2, :] = column_sum(rows)
        out.put(mm_tn(normed[...], rows), slot_copies(plan, devs, grads, part))
    xhat, rstd = normalised(xin_ref[...].astype(F32))
    small_ref[0:1, :] = column_sum(grad_normed * xhat)
    small_ref[1:2, :] = column_sum(grad_normed)
    for item in range(plan.items):
        small_ref[12 + item : 13 + item, :] = column_sum(
            grad_normed[item * length : (item + 1) * length]
        )
    dx_ref[...] = grad_middle_ref[...] + norm_back(grad_normed, xhat, rstd, vec[0:1, :])
    if plan.parts > 1:
        pack_sums(plan, lead, many, small_ref[...], stack, lines)
        packed[...] = lines[...].astype(BF16)
        start_all(
            [
                pltpu.make_async_copy(
                    packed.at[devs[slot]],
                    slot_target(plan, grads, slot).at[pl.ds(FIRST * plan.rows, EXTRA)],
                    out_sem.at[0],
                )
                for slot in range(plan.shards)
            ]
        )
        wait_bytes(packed, out_sem.at[0])
    out.drain()


def pack_kernel(qkv_ref, out_ref, up_ref, down_ref, *refs):
    rows, width = out_ref.shape
    vectors, (up_bias, table, first_ref, second_ref, small, wide) = refs[:8], refs[8:]
    for index, vector in enumerate(vectors):
        small[index : index + 1, :] = vector[...]
    for part in range(QUART):
        small[8 + part : 9 + part, :] = up_bias[:, part * rows : (part + 1) * rows]
    many = 12 + table.shape[0]
    small[12:many, :] = table[...]
    across = width // rows
    wide[...] = jnp.zeros_like(wide)
    for index in range(many):
        line, place = divmod(index, across)
        wide[line : line + 1, place * rows : (place + 1) * rows] = small[index : index + 1, :]
    for part in range(OUT):
        first_ref[part * rows : (part + 1) * rows, :] = qkv_ref[:, part * width : (part + 1) * width].astype(BF16)
    first_ref[OUT * rows : FIRST * rows, :] = out_ref[...].astype(BF16)
    first_ref[FIRST * rows :, :] = wide[...].astype(BF16)
    for part in range(QUART):
        second_ref[part] = up_ref[:, part * width : (part + 1) * width].astype(BF16)
        second_ref[QUART + part] = down_ref[part * rows : (part + 1) * rows, :].astype(BF16)


def vectors_kernel(plan, many, devs, lead, *refs):
    pieces, (out_ref, lines, spread, sem) = slot_pieces(plan, refs[:-4]), refs[-4:]
    rows, width = plan.rows, plan.width
    across = width // rows
    groups = pl.cdiv(many, across)
    start_all(
        [
            pltpu.make_async_copy(piece_rows(parts, FIRST * rows, EXTRA), lines.at[slot], sem.at[0])
            for slot, parts in enumerate(pieces)
        ]
    )
    wait_bytes(lines, sem.at[0])
    line = lax.broadcasted_iota(jnp.int32, (across, width), 0)
    lane = lax.broadcasted_iota(jnp.int32, (across, width), 1)
    chosen = (lane >= line * rows) & (lane < (line + 1) * rows)
    up_line = lax.broadcasted_iota(jnp.int32, (QUART, width), 0)
    up_lane = lax.broadcasted_iota(jnp.int32, (QUART, width), 1)
    ups = jnp.zeros((QUART, width), F32)
    for slot in range(plan.shards):
        values = lines[slot].astype(F32)
        for group in range(groups):
            at = (slot * groups + group) * across
            picked = jnp.where(chosen, jnp.broadcast_to(values[group : group + 1], chosen.shape), 0.0)
            spread[at : at + across, :] = picked.astype(BF16)
        first = QUART * rows * devs[slot]
        there = lax.rem(first, width)
        moved = jnp.broadcast_to(values[8 // across : 8 // across + 1], (8, width))
        moved = pltpu.roll(moved, lax.rem(there + width - 8 % across * rows, width), 1)[:QUART]
        here = (up_line == first // width) & (up_lane >= there) & (up_lane < there + QUART * rows)
        ups = jnp.where(here, moved, ups)
    source = lax.broadcasted_iota(jnp.int32, (width, rows), 0)
    target = lax.broadcasted_iota(jnp.int32, (width, rows), 1)
    fold = sum(jnp.where(source == target + place * rows, 1.0, 0.0) for place in range(across))
    narrow = mm(spread[...], fold.astype(BF16)).astype(BF16)
    entry = lax.broadcasted_iota(jnp.int32, (rows, width), 0)
    column = lax.broadcasted_iota(jnp.int32, (rows, width), 1)
    total = None
    for slot in range(plan.shards):
        at = slot * groups * across
        place = jnp.where(column == entry + devs[slot] * rows, 1.0, 0.0).astype(BF16)
        term = mm(narrow[at : at + groups * across], place)
        total = term if total is None else total + term
    out_ref[...] = jnp.zeros_like(out_ref)
    out_ref[:8, :] = total[:8]
    out_ref[8 : 8 + QUART, :] = ups
    entry = lax.broadcasted_iota(jnp.int32, total.shape, 0)
    for item in range(plan.items):
        picked = jnp.where(entry == 12 + lead[item], total, 0.0)
        out_ref[12 + item : 13 + item, :] = jnp.sum(picked, 0, keepdims=True)


def unpack_kernel(grads_ref, up_ref, down_ref):
    _, rows, width = grads_ref.shape
    for part in range(QUART):
        up_ref[:, part * width : (part + 1) * width] = grads_ref[part].astype(F32)
        down_ref[part * rows : (part + 1) * rows, :] = grads_ref[QUART + part].astype(F32)


def add_kernel(work, *refs):
    outs, at = refs[len(refs) - len(work) :], 0
    for (low, high, first), out in zip(work, outs):
        mine, other = refs[at], refs[at + 1]
        at += 2
        cuts, came = [low, high], None
        if first is not None:
            came = refs[at]
            at += 1
            cuts = sorted({low, first, first + came.shape[0], high})
        for start, end in zip(cuts, cuts[1:]):
            value = mine[0, start:end, :].astype(F32) + other[0, start:end, :].astype(F32)
            if came is not None and first <= start < first + came.shape[0]:
                value = value + came[start - first : end - first, :].astype(F32)
            out[start - low : end - low, :] = value.astype(BF16)


def total_kernel(many, mine, other, ahead, behind, qkv, out, *refs):
    width = mine.shape[2]
    rows = out.shape[0]

    def rows_of(low, count):
        here = slice(low, low + count)
        value = mine[0, here, :].astype(F32) + other[0, here, :].astype(F32)
        return value + (ahead[here, :].astype(F32) + behind[here, :].astype(F32))

    for part in range(OUT):
        qkv[:, part * width : (part + 1) * width] = rows_of(part * rows, rows)
    out[...] = rows_of(OUT * rows, rows)
    vectors, (up_bias, table, small) = refs[:8], refs[8:]
    lines = rows_of(FIRST * rows, EXTRA)
    for index in range(many):
        line, place = divmod(index, width // rows)
        small[index : index + 1, :] = lines[line : line + 1, place * rows : (place + 1) * rows]
    for index, vector in enumerate(vectors):
        vector[...] = small[index : index + 1, :]
    for part in range(QUART):
        up_bias[:, part * rows : (part + 1) * rows] = small[8 + part : 9 + part, :]
    table[...] = small[12:many, :]


SMEM = pl.BlockSpec(memory_space=pltpu.SMEM)
VMEM = pl.BlockSpec(memory_space=pltpu.VMEM)
HBM = pl.BlockSpec(memory_space=pltpu.HBM)
ANY = pl.BlockSpec(memory_space=pl.ANY)


def kept_shapes(plan):
    tokens, width = plan.tokens, plan.width
    return [
        ((tokens, width), BF16),
        ((tokens, 3 * width), BF16),
        ((tokens, width), BF16),
        ((tokens, width), F32),
        ((tokens, width), BF16),
        ((plan.items * plan.pairs, 2 * plan.length, plan.length), F32),
        ((tokens, 4 * width), BF16),
        ((tokens, 4 * width), F32),
    ]


def held_blocks(plan, blocks):
    return pltpu.VMEM((blocks, plan.shards, plan.rows, plan.width), BF16)


def call(kernel, outs, in_specs, out_specs, scratch, name, work, limit, args):
    args = [
        pltpu.with_memory_space_constraint(arg, pltpu.HBM) if spec is HBM else arg
        for arg, spec in zip(args, in_specs)
    ]
    return pl.pallas_call(
        kernel,
        out_shape=outs,
        in_specs=in_specs,
        out_specs=out_specs,
        scratch_shapes=scratch,
        compiler_params=pltpu.CompilerParams(vmem_limit_bytes=limit * 1024 * 1024),
        cost_estimate=pl.CostEstimate(flops=2 * work[0], bytes_accessed=work[1], transcendentals=0),
        name=name,
    )(*args)


def of(shape):
    return jax.ShapeDtypeStruct(*shape)


def inside(shape):
    return pltpu.VMEM(*shape)


def run_attend(plan, lengths, flag, devs, x, vec, pieces):
    kept = kept_shapes(plan)
    block = plan.width * plan.width
    return call(
        functools.partial(attend_kernel, plan),
        [of(kept[3]), of(kept[4])],
        [SMEM, SMEM, SMEM, VMEM, VMEM] + [HBM] * len(pieces),
        [VMEM, VMEM],
        [held_blocks(plan, FIRST)] + [inside(shape) for shape in kept[:3]] + [pltpu.SemaphoreType.DMA((2,))],
        "attend",
        (FIRST * block * plan.tokens, FIRST * block * 2),
        14,
        (lengths, flag, devs, x, vec, *pieces),
    )


def run_vectors(plan, many, devs, lead, pieces):
    groups = pl.cdiv(many, plan.width // plan.rows) * (plan.width // plan.rows)
    return call(
        functools.partial(vectors_kernel, plan, many),
        jax.ShapeDtypeStruct((16, plan.width), F32),
        [SMEM, SMEM] + [HBM] * len(pieces),
        VMEM,
        [
            pltpu.VMEM((plan.shards, EXTRA, plan.width), BF16),
            pltpu.VMEM((plan.shards * groups, plan.width), BF16),
            pltpu.SemaphoreType.DMA((1,)),
        ],
        "vectors",
        (plan.width * plan.width * plan.rows, plan.width * plan.width * 4),
        12,
        (devs, lead, *pieces),
    )


def run_mlp(plan, flag, middle, hidden, vec, gathered):
    block = plan.width * plan.width
    return call(
        functools.partial(mlp_kernel, plan),
        jax.ShapeDtypeStruct(hidden.shape, BF16),
        [SMEM, VMEM, VMEM, VMEM, HBM],
        VMEM,
        [held_blocks(plan, SECOND), pltpu.SemaphoreType.DMA((QUART,)), pltpu.SemaphoreType.DMA((QUART,))],
        "mlp",
        (SECOND * block * plan.tokens, SECOND * block * 2),
        16,
        (flag, middle, hidden, vec, gathered),
    )


def run_load(plan, devs, after, cot, firsts, gathered):
    block = plan.width * plan.width
    return call(
        functools.partial(load_kernel, plan),
        [held_blocks(plan, FIRST), held_blocks(plan, SECOND), inside(kept_shapes(plan)[7])],
        [SMEM, ANY, VMEM] + [HBM] * (1 + len(firsts)),
        [VMEM] * 3,
        [pltpu.SemaphoreType.DMA((2,)), pltpu.SemaphoreType.DMA((QUART,))],
        "load",
        (QUART * block * plan.tokens, (FIRST + SECOND) * block * 4),
        4,
        (devs, after, cot, gathered, *firsts),
    )


def run_chain(plan, lengths, flag, x, recv, cot, vec, held1, held2, grad_act):
    shapes = kept_shapes(plan)
    block = plan.width * plan.width
    rest = [shapes[index] for index in (0, 0, 1, 2, 3, 5)]
    some = ((plan.items // 2 * plan.length, plan.width), BF16)
    results = call(
        functools.partial(chain_kernel, plan),
        [pltpu.HBM(*shapes[0]), of(some)]
        + [inside(shapes[index]) for index in (4, 6, 7, 0, 1, 5, 3, 0)]
        + [pltpu.HBM(*shape) for shape in rest],
        [SMEM] * 2 + [VMEM] * 7,
        [HBM] + [VMEM] * 9 + [HBM] * len(rest),
        [inside(shapes[index]) for index in (0, 2, 3, 0, 1)]
        + [pltpu.SemaphoreType.DMA((len(rest) + 1,))],
        "chain",
        (20 * block * plan.tokens, 12 * block),
        12,
        (lengths, flag, x, recv, cot, vec, held1, held2, grad_act),
    )
    return results[0], results[1], results[2:5], results[5:10], results[10:]


def run_chain_end(plan, flag, vec, held1, end):
    shapes = kept_shapes(plan)
    block = plan.width * plan.width
    left = plan.items - plan.items // 2
    return call(
        functools.partial(chain_end_kernel, plan),
        of(((left * plan.length, plan.width), BF16)),
        [SMEM] + [VMEM] * 7,
        VMEM,
        [inside(shapes[1])],
        "chain_end",
        (2 * block * plan.tokens, 3 * block),
        6,
        (flag, vec, held1, *end),
    )


def grad_shapes(plan):
    if plan.parts == 1:
        return [pltpu.HBM((1, FIRST * plan.rows, plan.width), BF16)]
    rows = FIRST * plan.rows + EXTRA
    return [
        pltpu.HBM((count, rows, plan.width), BF16)
        for count in (plan.shards // 2, plan.shards // 2, 1)
    ]


def stage_scratch(plan, slots):
    return [
        pltpu.VMEM((slots, plan.shards, plan.rows, plan.width), BF16),
        pltpu.SemaphoreType.DMA((slots,)),
    ]


def run_mlp_back(plan, flag, arriving, cot, held2, hidden, act, slope):
    shapes = kept_shapes(plan)
    block = plan.width * plan.width
    return call(
        functools.partial(mlp_back_kernel, plan),
        [
            pltpu.HBM(*shapes[6]),
            jax.ShapeDtypeStruct((16, plan.width), F32),
            pltpu.HBM((plan.shards, SECOND, plan.rows, plan.width), BF16),
        ],
        [SMEM] + [VMEM] * 7,
        [HBM, VMEM, HBM],
        [inside(shapes[6])] + stage_scratch(plan, SECOND) + [pltpu.SemaphoreType.DMA((1,))],
        "mlp_back",
        (2 * SECOND * block * plan.tokens, SECOND * block * 2),
        16,
        (flag, *arriving, cot, held2, hidden, act, slope),
    )


def run_rest(plan, many, flag, devs, lead, arriving, cot, small, vec, gathered, grad_pre, kept, pieces):
    shapes = kept_shapes(plan)
    block = plan.width * plan.width
    across = plan.width // plan.rows
    high = pl.cdiv(many, across) * across
    lines = (plan.shards, EXTRA, plan.width)
    rest = [shapes[index] for index in (0, 0, 1, 2, 3, 5)]
    input_grad, small, *grads = call(
        functools.partial(rest_kernel, plan, many),
        [of(shapes[3]), jax.ShapeDtypeStruct((16, plan.width), F32)] + grad_shapes(plan),
        [SMEM] * 3 + [VMEM] * 5 + [HBM] * (2 + len(rest) + len(pieces)),
        [VMEM] * 2 + [HBM] * plan.parts,
        [inside(shape) for shape in rest]
        + [held_blocks(plan, QUART), inside(shapes[6])]
        + [pltpu.SemaphoreType.DMA((QUART,)), pltpu.SemaphoreType.DMA((1,))]
        + [held_blocks(plan, FIRST)]
        + [inside(shapes[index]) for index in (3, 0, 1)]
        + [pltpu.SemaphoreType.DMA((2,)), pltpu.SemaphoreType.DMA((len(rest),))]
        + stage_scratch(plan, FIRST)
        + [pltpu.SemaphoreType.DMA((1,)), pltpu.VMEM((plan.shards * high, plan.rows), BF16)]
        + [pltpu.VMEM(lines, F32), pltpu.VMEM(lines, BF16)],
        "rest",
        (3 * FIRST * block * plan.tokens, 3 * FIRST * block * 2),
        34,
        (flag, devs, lead, *arriving, cot, small, vec, gathered, grad_pre, *kept, *pieces),
    )
    return input_grad, small, grads


def run_add(mine, other, work):
    _, rows, width = mine.shape
    mine = pltpu.with_memory_space_constraint(mine, pltpu.HBM)
    specs, args, plans, outs = [], [], [], []
    for way, (slot, low, high, came) in enumerate(work):
        there = slot if other.shape[0] > 1 else 0
        specs += [
            pl.BlockSpec((1, rows, width), lambda index, slot=slot: (slot, 0, 0))
            for slot in (slot, there)
        ]
        args += [mine, other]
        first = None
        if came is not None:
            specs.append(pl.BlockSpec(came.shape, lambda index: (0, 0)))
            args.append(came)
            first = rows - came.shape[0] if way else 0
        plans.append((low, high, first))
        outs.append((high - low, width))
    return pl.pallas_call(
        functools.partial(add_kernel, plans),
        out_shape=[jax.ShapeDtypeStruct(shape, BF16) for shape in outs],
        grid=(1,),
        in_specs=specs,
        out_specs=[pl.BlockSpec(shape, lambda index: (0, 0)) for shape in outs],
        compiler_params=pltpu.CompilerParams(vmem_limit_bytes=14 * 1024 * 1024),
        name="add",
    )(*args)


def run_total(one, many, shapes):
    args = [pltpu.with_memory_space_constraint(one.mine, pltpu.HBM), one.other]
    _, rows, width = one.mine.shape
    first = pl.BlockSpec((1, rows, width), lambda index: (0, 0, 0))
    whole = pl.BlockSpec((rows, width), lambda index: (0, 0))
    return pl.pallas_call(
        functools.partial(total_kernel, many),
        out_shape=[jax.ShapeDtypeStruct(shape, F32) for shape in shapes],
        grid=(1,),
        in_specs=[first, first, whole, whole],
        out_specs=[pl.BlockSpec(shape, lambda index: (0, 0)) for shape in shapes],
        scratch_shapes=[pltpu.VMEM((many, shapes[2][1]), F32)],
        compiler_params=pltpu.CompilerParams(vmem_limit_bytes=14 * 1024 * 1024),
        name="total",
    )(*args, *one.carried)


def after(value, *others):
    return lax.optimization_barrier((value, *others))[0]


def shifted(value, axis, steps):
    count = lax.axis_size(axis)
    first, last = (max(0, -steps), min(count, count - steps))
    return lax.ppermute(value, axis, [(source, source + steps) for source in range(first, last)])


class Ring:
    def __init__(self, count):
        self.count, self.chips = count, count // 2
        self.walk = list(range(0, self.chips, 2)) + list(range(self.chips - 1, 0, -2))
        self.order = [2 * chip + core for chip in self.walk for core in range(2)]
        after = self.walk[1:] + self.walk[:1]
        self.onward = [
            (2 * here + core, 2 * there + core)
            for here, there in zip(self.walk, after)
            for core in range(2)
        ]
        self.back = [(there, here) for here, there in self.onward]
        self.sibling = [(index, index ^ 1) for index in range(count)]

    def slots(self):
        index = lax.axis_index("dp")
        chip, core = index // 2, index % 2
        place_of = lambda chip: jnp.where(chip % 2 == 0, chip // 2, self.chips - 1 - chip // 2)
        steps = jnp.arange(self.chips, dtype=jnp.int32)
        ahead = (place_of(chip) + steps) % self.chips
        chips = jnp.where(ahead < (self.chips + 1) // 2, 2 * ahead, 2 * (self.chips - 1 - ahead) + 1)
        devs = jnp.concatenate([2 * chips + core, 2 * chips + 1 - core]).astype(jnp.int32)
        return devs

    def step(self, ahead, behind):
        return lax.ppermute(ahead, "dp", self.onward), lax.ppermute(behind, "dp", self.back)

    def gather(self, shard, low):
        half = self.chips // 2
        own = [[shard]] + [None] * (self.chips - 1)
        ahead = behind = shard
        for step in range(1, half):
            ahead, behind = self.step(ahead, behind)
            own[self.chips - step], own[step] = [ahead], [behind]
            ahead, behind = lax.optimization_barrier((ahead, behind))
        own[half] = list(self.step(ahead[:low], behind[low:]))
        return [piece for pieces in own for piece in pieces]

    def siblings(self, pieces):
        return [lax.ppermute(piece, "dp", self.sibling) for piece in pieces]


class RingSum:
    def __init__(self, ring, mine, other, opposite, low):
        self.ring, self.mine, self.low = ring, mine, low
        self.other, self.opposite = other, opposite
        self.time = ring.chips // 2
        self.carried = [None, None]

    def add(self):
        rows = self.mine.shape[1]
        other = self.other
        if self.carried[0] is None:
            other = self.opposite
            work = [(self.time, 0, self.low, None), (self.time, self.low, rows, None)]
        else:
            work = [
                (self.time, 0, rows, self.carried[0]),
                (self.ring.chips - self.time, 0, rows, self.carried[1]),
            ]
        self.carried = run_add(self.mine, other, work)

    def send(self):
        self.carried = self.ring.step(*self.carried)
        self.time -= 1


def body(
    block_input, cotangent, lengths, leads,
    norm_gain1, norm_bias1, lead_table, qkv_weight, query_bias, value_bias, out_weight, out_bias,
    norm_gain2, norm_bias2, up_weight, up_bias, down_weight, down_bias,
):
    count = lax.axis_size("dp")
    micro, local, length, width = block_input.shape
    items = micro * local
    rows = width // count
    leads_count = lead_table.shape[2]
    flag = lax.axis_index("section").astype(jnp.int32).reshape(1)
    flat = lambda value: value.reshape(items * length, width)
    x, cot = flat(block_input), flat(cotangent)
    lens, lead = lengths.reshape(items), leads.reshape(items)

    vectors = (
        norm_gain1, norm_bias1, query_bias, value_bias, out_bias, norm_gain2, norm_bias2, down_bias
    )
    many = 12 + leads_count
    aligned = rows % 16 == 0 and count % 4 == 0 and pl.cdiv(many, width // rows) <= EXTRA
    if aligned:
        ring = Ring(count)
        first, second = pl.pallas_call(
            pack_kernel,
            out_shape=[
                jax.ShapeDtypeStruct((FIRST * rows + EXTRA, width), BF16),
                jax.ShapeDtypeStruct((SECOND, rows, width), BF16),
            ],
            scratch_shapes=[pltpu.VMEM((many, rows), F32), pltpu.VMEM((EXTRA, width), F32)],
            name="pack",
        )(qkv_weight[0], out_weight[0], up_weight[0], down_weight[0], *vectors, up_bias, lead_table[0].T)
        gathered = lax.all_gather(second, "dp", axis=0, tiled=True, axis_index_groups=[ring.order])
        gathered = gathered.reshape(count, SECOND, rows, width)
        firsts = ring.gather(first, LOW * rows)
        firsts = firsts + ring.siblings(firsts)
        devs = ring.slots()
        plan = Plan(ring.order, rows, items, length, width)
        vec = run_vectors(plan, many, devs, lead, firsts)
    else:
        wide_blocks = lambda value: value[0].reshape(rows, -1, width).transpose(1, 0, 2)
        packed = jnp.concatenate(
            [wide_blocks(qkv_weight), out_weight, wide_blocks(up_weight), down_weight.reshape(QUART, rows, width)], 0
        )
        everything = lax.all_gather(packed.astype(BF16), "dp", axis=0)
        across_blocks = lambda value: value.transpose(1, 0, 2, 3).reshape(-1, width, width)
        firsts = [across_blocks(everything[:, :FIRST])]
        gathered = jnp.concatenate(
            [
                across_blocks(everything[:, FIRST : FIRST + QUART]),
                everything[:, FIRST + QUART :].reshape(QUART, width, width),
            ],
            0,
        )[None]
        devs = jnp.zeros((1,), jnp.int32)
        plan = Plan([0], width, items, length, width)
        small = jnp.concatenate([*vectors, up_bias.reshape(4, rows), lead_table[0].T], 0).astype(BF16)
        wide = lax.all_gather(small, "dp", axis=1, tiled=True).astype(F32)
        vec = jnp.concatenate(
            [wide[:8], wide[8:12].reshape(4, count, rows).transpose(1, 0, 2).reshape(4, width)]
            + [lax.dynamic_slice_in_dim(wide, 12 + lead[item], 1, 0) for item in range(items)]
            + [jnp.zeros((4 - items, width), F32)],
            0,
        )

    middle, hidden = run_attend(plan, lens, flag, devs, x, vec, firsts)
    first_out = run_mlp(plan, flag, middle, hidden, vec, gathered)
    recv = shifted(first_out, "section", 1)
    held1, held2, grad_act = run_load(plan, devs, first_out, cot, firsts, gathered)
    output, some_grad, (hidden, act, slope), end, kept = run_chain(
        plan, lens, flag, x, recv, cot, vec, held1, held2, grad_act
    )
    other_grad = run_chain_end(plan, flag, vec, held1, end)
    arriving = [shifted(grad, "section", -1) for grad in (some_grad, other_grad)]
    grad_pre, sums, grads2 = run_mlp_back(plan, flag, arriving, cot, held2, hidden, act, slope)
    input_grad, sums, grads1 = run_rest(
        plan, many, flag, devs, lead, arriving, cot, sums, vec, gathered, grad_pre, kept, firsts
    )
    if aligned:
        (opposite,) = ring.siblings(grads1[2:])
        (other,) = ring.siblings([after(grads1[1], opposite)])
        first_sum = RingSum(ring, grads1[0], other, opposite, LOW * rows)
        while first_sum.time:
            first_sum.add()
            first_sum.send()
        grads2 = lax.psum_scatter(
            grads2.reshape(count * SECOND, rows, width),
            "dp", scatter_dimension=0, tiled=True, axis_index_groups=[ring.order],
        )
        grad_up, grad_down = pl.pallas_call(
            unpack_kernel,
            out_shape=[
                jax.ShapeDtypeStruct((rows, QUART * width), F32),
                jax.ShapeDtypeStruct((QUART * rows, width), F32),
            ],
            name="unpack",
        )(grads2)
        grad_qkv, grad_out, *small_grads = run_total(
            first_sum, many,
            [(rows, OUT * width), (rows, width)] + [(1, rows)] * 8 + [(1, QUART * rows), (leads_count, rows)],
        )
    else:
        split = lambda value: value[0].reshape(-1, count, rows, width).transpose(1, 0, 2, 3)
        grads = jnp.concatenate(
            [
                split(grads1[0]),
                split(grads2[0, :QUART].reshape(1, QUART * width, width)),
                grads2[0, QUART:].reshape(count, QUART, rows, width),
            ],
            1,
        )
        grads = lax.psum_scatter(grads, "dp", scatter_dimension=0, tiled=False).astype(F32)
        across = lambda value: value.transpose(1, 0, 2).reshape(rows, -1)
        grad_qkv, grad_out = across(grads[:OUT]), grads[OUT]
        grad_up = across(grads[FIRST : FIRST + QUART])
        grad_down = grads[FIRST + QUART :].reshape(QUART * rows, width)
        hot = (jnp.arange(leads_count)[:, None] == lead[None, :]).astype(F32)
        table = sum(hot[:, item : item + 1] * sums[12 + item : 13 + item] for item in range(items))
        up_sums = sums[8:12].reshape(count, 4, rows).transpose(1, 0, 2).reshape(4, width)
        spread = lax.psum_scatter(
            jnp.concatenate([sums[:8], up_sums, table], 0), "dp", scatter_dimension=1, tiled=True
        )
        small_grads = [spread[index : index + 1] for index in range(8)]
        small_grads += [spread[8:12].reshape(1, 4 * rows), spread[12:]]
    vector = small_grads
    shape = (1, micro, local, length, width)
    return (
        output.reshape(shape),
        input_grad.reshape(shape),
        vector[0],
        vector[1],
        vector[9].T[None],
        grad_qkv[None],
        vector[2],
        vector[3],
        grad_out[None],
        vector[4],
        vector[5],
        vector[6],
        grad_up[None],
        vector[8],
        grad_down[None],
        vector[7],
    )


def solution(mesh):
    weights = (
        P("section", "dp"),
        P("section", "dp"),
        P("section", "dp", None),
        P("section", "dp", None),
        P("section", "dp"),
        P("section", "dp"),
        P("section", "dp", None),
        P("section", "dp"),
        P("section", "dp"),
        P("section", "dp"),
        P("section", "dp", None),
        P("section", "dp"),
        P("section", "dp", None),
        P("section", "dp"),
    )
    rows = P(None, "dp", None, None)
    layers = P("section", None, "dp", None, None)
    return jax.shard_map(
        body,
        mesh=mesh,
        in_specs=(rows, rows, P(None, "dp"), P(None, "dp")) + weights,
        out_specs=(layers, layers) + weights,
        check_vma=False,
    )
```

```python
import functools

import jax
import jax.numpy as jnp
from jax import lax
from jax.experimental import pallas as pl
from jax.experimental.pallas import tpu as pltpu
from jax.sharding import PartitionSpec as P

HEAD = 64
PAIR = 2 * HEAD
EPS = 1e-06
SCALE_FACTOR = 0.125
GELU_A = 0.7978845608028654
GELU_B = 0.044715
F32 = jnp.float32
BF16 = jnp.bfloat16
OUT = 3
FIRST = 4
SECOND = 8
QUART = 4
EXTRA = 16
LOW = 2


def mm(left, right):
    return jnp.dot(left, right, preferred_element_type=F32)


def mm_nt(left, right):
    return lax.dot_general(left, right, (((1,), (1,)), ((), ())), preferred_element_type=F32)


def mm_tn(left, right):
    return lax.dot_general(left, right, (((0,), (0,)), ((), ())), preferred_element_type=F32)


def normalised(values):
    mean = jnp.mean(values, -1, keepdims=True)
    centred = values - mean
    variance = jnp.mean(centred * centred, -1, keepdims=True)
    rstd = lax.rsqrt(variance + EPS)
    return centred * rstd, rstd


def norm_back(grad, xhat, rstd, gain):
    scaled = grad * gain
    first = jnp.mean(scaled, -1, keepdims=True)
    second = jnp.mean(scaled * xhat, -1, keepdims=True)
    return rstd * (scaled - first - xhat * second)


def gelu_both(values):
    square = values * values
    slope = GELU_A * (1.0 + 3.0 * GELU_B * square)
    bend = jnp.tanh(GELU_A * values * (1.0 + GELU_B * square))
    half = 0.5 * (1.0 + bend)
    return values * half, half + 0.5 * values * (1.0 - bend * bend) * slope


def split_pair(rows):
    lane = lax.broadcasted_iota(jnp.int32, rows.shape, 1)
    zero = jnp.zeros_like(rows)
    return jnp.concatenate(
        [jnp.where(lane < HEAD, rows, zero), jnp.where(lane < HEAD, zero, rows)], 0
    )


def join_pair(stacked):
    count = stacked.shape[0] // 2
    lane = lax.broadcasted_iota(jnp.int32, (count, PAIR), 1)
    return jnp.where(lane < HEAD, stacked[:count], stacked[count:])


def runs_of(order):
    if all(order[at + 1] == order[at] + 1 for at in range(0, len(order) - 1, 2)) and len(order) > 1:
        return [(at, order[at], 2) for at in range(0, len(order), 2)]
    return [(at, device, 1) for at, device in enumerate(order)]


class Plan:
    def __init__(self, order, rows, items, length, width):
        self.order, self.shards, self.rows = order, len(order), rows
        self.items, self.length, self.width = items, length, width
        self.tokens = items * length
        self.low = LOW * rows
        self.pairs = width // PAIR
        whole = self.shards % QUART == 0
        self.runs = [(0, QUART)] if whole else [(block, 1) for block in range(QUART)]
        self.parts = 3 if self.shards > 1 else 1


def slot_pieces(plan, refs):
    if plan.shards == 1:
        return [[(0, refs[0])]]
    refs, slots, half = list(refs), [], plan.shards // 4
    for slot in range(plan.shards):
        parts = [(0, refs.pop(0))]
        if slot % (plan.shards // 2) == half:
            parts.append((plan.low, refs.pop(0)))
        slots.append(parts)
    return slots


def piece_rows(parts, row, count):
    start, ref = [part for part in parts if part[0] <= row][-1]
    return ref.at[pl.ds(row - start, count)]


def first_copies(plan, refs, devs, held, sem, blocks):
    if plan.shards == 1:
        return block_copies(refs, devs, held, sem, blocks)
    return [
        pltpu.make_async_copy(
            piece_rows(parts, block * plan.rows, plan.rows), held.at[block, devs[slot]], sem
        )
        for slot, parts in enumerate(slot_pieces(plan, refs))
        for block in range(blocks.start, blocks.start + blocks.size)
    ]


def block_copies(pieces, devs, held, sem, blocks, at=0):
    return [
        pltpu.make_async_copy(
            piece.at[blocks], held.at[pl.ds(at + blocks.start, blocks.size), devs[slot]], sem
        )
        for slot, piece in enumerate(pieces)
    ]


def up_copies(plan, gathered, held, sem, part):
    return [
        pltpu.make_async_copy(
            gathered.at[pl.ds(place, count), part], held.at[part, pl.ds(device, count)], sem
        )
        for place, device, count in runs_of(plan.order)
    ]


def down_copies(plan, pieces, devs, held, sems):
    copies = []
    for slot, piece in enumerate(pieces):
        for first, count in plan.runs:
            block, row = divmod(QUART * devs[slot] + first, plan.shards)
            copy = pltpu.make_async_copy(
                piece.at[pl.ds(first, count)],
                held.at[QUART + block, pl.ds(row, count)],
                sems.at[block],
            )
            copies.append((block, copy))
    return copies


def second_pieces(plan, gathered):
    ups = [gathered.at[place, pl.ds(0, QUART)] for place in range(plan.shards)]
    downs = [gathered.at[place, pl.ds(QUART, QUART)] for place in range(plan.shards)]
    return ups, downs


def start_all(copies):
    for copy in copies:
        copy.start()


def wait_bytes(part, sem):
    pltpu.make_async_copy(part, part, sem).wait()


def block_of(plan, held, index):
    return held[index].reshape(plan.width, plan.width)


def columns_of(plan, index):
    return slice(index * plan.width, (index + 1) * plan.width)


def attention_forward(plan, lengths, qkv_ref, attended_ref, probs_ref):
    width, length = plan.width, plan.length
    key_index = lax.broadcasted_iota(jnp.int32, (2 * length, length), 1)
    for item in range(plan.items):
        rows = slice(item * length, (item + 1) * length)
        valid = key_index < lengths[item]
        for pair in range(plan.pairs):
            at = pair * PAIR
            query = split_pair(qkv_ref[rows, at : at + PAIR])
            key = qkv_ref[rows, width + at : width + at + PAIR]
            value = qkv_ref[rows, 2 * width + at : 2 * width + at + PAIR]
            logits = jnp.where(valid, mm_nt(query, key) * SCALE_FACTOR, -1000000000.0)
            expo = jnp.exp(logits - jnp.max(logits, -1, keepdims=True))
            probs = expo / jnp.sum(expo, -1, keepdims=True)
            if probs_ref is not None:
                probs_ref[item * plan.pairs + pair] = probs
            attended_ref[rows, at : at + PAIR] = join_pair(mm(probs.astype(BF16), value)).astype(
                BF16
            )


def first_half(plan, inputs, lengths, vec, held, wait, normed_ref, qkv_ref, attended_ref, probs_ref, hidden_ref):
    width, length = plan.width, plan.length
    values = inputs.astype(F32)
    xhat, _ = normalised(values)
    base = xhat * vec[0:1, :] + vec[1:2, :]
    for item in range(plan.items):
        rows = slice(item * length, (item + 1) * length)
        normed_ref[rows, :] = (base[rows] + vec[12 + item : 13 + item, :]).astype(BF16)
    wait(0)
    for part, bias in enumerate((2, None, 3)):
        joined = mm(normed_ref[...], block_of(plan, held, part))
        if bias is not None:
            joined = joined + vec[bias : bias + 1, :]
        qkv_ref[:, columns_of(plan, part)] = joined.astype(BF16)
    attention_forward(plan, lengths, qkv_ref, attended_ref, probs_ref)
    wait(1)
    middle = values + (mm(attended_ref[...], block_of(plan, held, OUT)) + vec[4:5, :])
    xhat, _ = normalised(middle)
    hidden_ref[...] = (xhat * vec[5:6, :] + vec[6:7, :]).astype(BF16)
    return middle


def activate(plan, part, hidden_ref, vec, held):
    pre_act = mm(hidden_ref[...], block_of(plan, held, part)) + vec[8 + part : 9 + part, :]
    act, slope = gelu_both(pre_act)
    return act.astype(BF16), slope


def second_half(plan, hidden_ref, vec, held, wait):
    total = None
    for part in range(QUART):
        wait(part)
        act, _ = activate(plan, part, hidden_ref, vec, held)
        wait(QUART + part)
        term = mm(act, block_of(plan, held, QUART + part))
        total = term if total is None else total + term
    return total + vec[7:8, :]


def attention_back(plan, probs_ref, qkv_ref, grad_attended_ref, rows_ref, items=None):
    width, length = plan.width, plan.length
    for item in range(plan.items) if items is None else items:
        rows = slice(item * length, (item + 1) * length)
        for pair in range(plan.pairs):
            at = pair * PAIR
            query = split_pair(qkv_ref[rows, at : at + PAIR])
            key = qkv_ref[rows, width + at : width + at + PAIR]
            value = qkv_ref[rows, 2 * width + at : 2 * width + at + PAIR]
            grad = split_pair(grad_attended_ref[rows, at : at + PAIR])
            probs = probs_ref[item * plan.pairs + pair]
            grad_probs = mm_nt(grad, value)
            centre = jnp.sum(grad_probs * probs, -1, keepdims=True)
            grad_logits = (probs * (grad_probs - centre)).astype(BF16)
            grad_query = join_pair(mm(grad_logits, key)) * SCALE_FACTOR
            grad_key = mm_tn(grad_logits, query) * SCALE_FACTOR
            grad_value = mm_tn(probs.astype(BF16), grad)
            rows_ref[rows, at : at + PAIR] = grad_query.astype(BF16)
            rows_ref[rows, width + at : width + at + PAIR] = grad_key.astype(BF16)
            rows_ref[rows, 2 * width + at : 2 * width + at + PAIR] = grad_value.astype(BF16)


def column_sum(values):
    return jnp.sum(values.astype(F32), 0, keepdims=True)


def attend_kernel(plan, lengths, flag, devs, x_ref, vec, *refs):
    pieces, (middle_ref, hidden_ref, held, normed, qkv, attended, sems) = refs[:-7], refs[-7:]
    start_all(first_copies(plan, pieces, devs, held, sems.at[0], pl.ds(0, OUT)))
    start_all(first_copies(plan, pieces, devs, held, sems.at[1], pl.ds(OUT, 1)))

    def wait(group):
        blocks = pl.ds(OUT, 1) if group else pl.ds(0, OUT)
        wait_bytes(held.at[blocks], sems.at[group])

    middle_ref[...] = first_half(
        plan, x_ref[...], lengths, vec, held, wait, normed, qkv, attended, None, hidden_ref
    )


def mlp_kernel(plan, flag, middle_ref, hidden_ref, vec, gathered, y_ref, held, sems, down_sems):
    @pl.when(flag[0] == 0)
    def _():
        _, downs = second_pieces(plan, gathered)
        down = down_copies(plan, downs, plan.order, held, down_sems)
        for part in range(QUART):
            start_all(up_copies(plan, gathered, held, sems.at[part], part))
            start_all([copy for block, copy in down if block == part])

        def wait(block):
            sem = sems.at[block] if block < QUART else down_sems.at[block - QUART]
            wait_bytes(held.at[block], sem)

        total = second_half(plan, hidden_ref, vec, held, wait)
        y_ref[...] = (middle_ref[...] + total).astype(BF16)


def load_kernel(plan, devs, after, cot_ref, gathered, *refs):
    firsts, (held1, held2, grad_act, sems, down_sems) = refs[:-5], refs[-5:]
    ups, downs = second_pieces(plan, gathered)
    start_all([copy for _, copy in down_copies(plan, downs, plan.order, held2, down_sems)])
    start_all(block_copies(ups, plan.order, held2, sems.at[1], pl.ds(0, QUART)))
    start_all(first_copies(plan, firsts, devs, held1, sems.at[0], pl.ds(0, FIRST)))
    for part in range(QUART):
        wait_bytes(held2.at[QUART + part], down_sems.at[part])
        grad_act[:, columns_of(plan, part)] = mm_nt(
            cot_ref[...], block_of(plan, held2, QUART + part)
        )
    wait_bytes(held2.at[pl.ds(0, QUART)], sems.at[1])
    wait_bytes(held1, sems.at[0])


def input_grad(plan, items, vec, held1, xin_ref, qkv, probs, grad_middle, grad_attended, grad_rows, dx_ref):
    attention_back(plan, probs, qkv, grad_attended, grad_rows, items)
    rows = slice(items.start * plan.length, items.stop * plan.length)
    grad_normed = None
    for part in range(OUT):
        term = mm_nt(grad_rows[rows, columns_of(plan, part)], block_of(plan, held1, part))
        grad_normed = term if grad_normed is None else grad_normed + term
    xhat, rstd = normalised(xin_ref[rows, :].astype(F32))
    dx_ref[...] = (grad_middle[rows, :] + norm_back(grad_normed, xhat, rstd, vec[0:1, :])).astype(BF16)


def chain_kernel(
    plan, lengths, flag, x_ref, recv_ref, cot_ref, vec, held1, held2, grad_act,
    dx_ref, hidden, act, slope, xin_ref, qkv, probs, grad_middle, grad_attended, middle, *refs,
):
    outs, (normed, attended, grad_rows, sems) = refs[:6], refs[6:]
    kept = (xin_ref, normed, qkv, attended, middle, probs)
    copies = [
        pltpu.make_async_copy(source, target, sems.at[index])
        for index, (source, target) in enumerate(zip(kept, outs))
    ]
    xin_ref[...] = jnp.where(flag[0] == 0, x_ref[...], recv_ref[...])
    middle[...] = first_half(
        plan, xin_ref[...], lengths, vec, held1, lambda group: None, normed, qkv, attended, probs, hidden
    )
    start_all(copies)
    for part in range(QUART):
        columns = columns_of(plan, part)
        act[:, columns], slope[:, columns] = activate(plan, part, hidden, vec, held2)

    @pl.when(flag[0] == 1)
    def _():
        branch = cot_ref[...]
        grad_hidden = None
        for part in range(QUART):
            grad_pre = (slope[:, columns_of(plan, part)] * grad_act[:, columns_of(plan, part)]).astype(BF16)
            term = mm_nt(grad_pre, block_of(plan, held2, part))
            grad_hidden = term if grad_hidden is None else grad_hidden + term
        xhat, rstd = normalised(middle[...])
        grad_middle[...] = branch.astype(F32) + norm_back(grad_hidden, xhat, rstd, vec[5:6, :])
        grad_attended[...] = mm_nt(grad_middle[...].astype(BF16), block_of(plan, held1, OUT)).astype(BF16)
        input_grad(
            plan, range(plan.items // 2), vec, held1, xin_ref, qkv, probs, grad_middle, grad_attended, grad_rows, dx_ref
        )

    for copy in copies:
        copy.wait()


def chain_end_kernel(plan, flag, vec, held1, xin_ref, qkv, probs, grad_middle, grad_attended, dx_ref, grad_rows):
    @pl.when(flag[0] == 1)
    def _():
        input_grad(
            plan, range(plan.items // 2, plan.items), vec, held1, xin_ref, qkv, probs, grad_middle, grad_attended,
            grad_rows, dx_ref,
        )


def output_kernel(plan, flag, act, middle_ref, vec, held2, y_ref):
    total = None
    for part in range(QUART):
        term = mm(act[:, columns_of(plan, part)], block_of(plan, held2, QUART + part))
        total = term if total is None else total + term
    y_ref[...] = (middle_ref[...] + (total + vec[7:8, :])).astype(BF16)


class Stage:
    def __init__(self, plan, stage, sems):
        self.plan, self.stage, self.sems, self.sent = plan, stage, sems, 0

    def put(self, value, copies_of):
        slots = self.stage.shape[0]
        slot = self.sent % slots
        if self.sent >= slots:
            wait_bytes(self.stage.at[slot], self.sems.at[slot])
        self.sent += 1
        plan = self.plan
        self.stage[slot] = value.astype(BF16).reshape(plan.shards, plan.rows, plan.width)
        start_all(copies_of(self.stage.at[slot], self.sems.at[slot]))

    def drain(self):
        for slot in range(min(self.stage.shape[0], self.sent)):
            wait_bytes(self.stage.at[slot], self.sems.at[slot])


def mlp_back_kernel(
    plan, flag, beside, some_ref, other_ref, cot_ref, held2, hidden, act, slope,
    grad_pre_out, small_ref, grads, grad_pre_ref, stage, stage_sems, pre_sem,
):
    arrived = jnp.concatenate([some_ref[...], other_ref[...]], 0)
    branch = jnp.where(flag[0] == 0, arrived, cot_ref[...])
    out = Stage(plan, stage, stage_sems)

    def copies_of_up(part):
        def copies(source, sem):
            return [
                pltpu.make_async_copy(
                    source.at[pl.ds(device, count)], grads.at[pl.ds(place, count), part], sem
                )
                for place, device, count in runs_of(plan.order)
            ]

        return copies

    def copies_of_down(part):
        def copies(source, sem):
            made = []
            for place, device in enumerate(plan.order):
                for first, count in plan.runs:
                    block, row = divmod(QUART * device + first, plan.shards)
                    if block == part:
                        made.append(
                            pltpu.make_async_copy(
                                source.at[pl.ds(row, count)],
                                grads.at[place, pl.ds(QUART + first, count)],
                                sem,
                            )
                        )
            return made

        return copies

    for part in range(QUART):
        columns = columns_of(plan, part)
        grad_act = mm_nt(branch, block_of(plan, held2, QUART + part))
        grad_pre = (slope[:, columns] * grad_act).astype(BF16)
        grad_pre_ref[:, columns] = grad_pre
        out.put(mm_tn(act[:, columns], branch), copies_of_down(part))
        out.put(mm_tn(hidden[...], grad_pre), copies_of_up(part))
    copy = pltpu.make_async_copy(grad_pre_ref, grad_pre_out, pre_sem.at[0])
    copy.start()
    small_ref[...] = jnp.zeros_like(small_ref)
    small_ref[7:8, :] = column_sum(branch)
    for part in range(QUART):
        small_ref[8 + part : 9 + part, :] = column_sum(grad_pre_ref[:, columns_of(plan, part)])
    out.drain()
    copy.wait()


def slot_target(plan, grads, slot):
    if plan.parts == 1:
        return grads[0].at[0]
    half = plan.shards // 2
    if slot == half + half // 2:
        return grads[2].at[0]
    return grads[slot // half].at[slot % half]


def slot_copies(plan, devs, grads, block):
    def copies(source, sem):
        return [
            pltpu.make_async_copy(
                source.at[devs[slot]],
                slot_target(plan, grads, slot).at[pl.ds(block * plan.rows, plan.rows)],
                sem,
            )
            for slot in range(plan.shards)
        ]

    return copies


def pack_sums(plan, lead, many, sums, stack, lines):
    rows, width = plan.rows, plan.width
    across = width // rows
    groups = pl.cdiv(many, across)
    high = groups * across
    leads = many - 12
    entry = lax.broadcasted_iota(jnp.int32, (high - 12, width), 0)
    table = jnp.zeros((high - 12, width), F32)
    for item in range(plan.items):
        table = table + jnp.where(entry == lead[item], sums[12 + item : 13 + item], 0.0)
    top, ups = sums[:8], sums[8:12]
    for device in range(plan.shards):
        columns = slice(device * rows, (device + 1) * rows)
        line, place = divmod(QUART * device * rows, width)
        parts = [
            ups[line : line + 1, place + part * rows : place + (part + 1) * rows]
            for part in range(QUART)
        ]
        share = jnp.concatenate([top[:, columns], *parts, table[:, columns]], 0)
        stack[device * high : (device + 1) * high, :] = share.astype(BF16)
    entry = lax.broadcasted_iota(jnp.int32, (rows, width), 0)
    column = lax.broadcasted_iota(jnp.int32, (rows, width), 1)
    tile = jnp.where(lax.rem(column, rows) == entry, 1.0, 0.0).astype(BF16)
    line = lax.broadcasted_iota(jnp.int32, (high, width), 0)
    lane = lax.broadcasted_iota(jnp.int32, (high, width), 1)
    place = lax.rem(line, across) * rows
    chosen = (lane >= place) & (lane < place + rows)
    lines[...] = jnp.zeros_like(lines)
    for device in range(plan.shards):
        spread = mm(stack[device * high : (device + 1) * high, :], tile)
        spread = jnp.where(chosen, spread, 0.0).reshape(groups, across, width)
        lines[device, 0:groups, :] = jnp.sum(spread, 1)


def rest_kernel(
    plan, many, flag, devs, lead, some_ref, other_ref, cot_ref, small_in, vec, gathered, grad_pre_in, *refs,
):
    count = plan.shards + (2 if plan.parts > 1 else 0)
    kept_in, pieces, refs = refs[:6], refs[6 : 6 + count], refs[6 + count :]
    dx_ref, small_ref = refs[:2]
    grads, refs = refs[2 : 2 + plan.parts], refs[2 + plan.parts :]
    kept, (held2, grad_pre, up_sems, pre_sem), refs = refs[:6], refs[6:10], refs[10:]
    held, grad_middle_ref, grad_attended, grad_rows, sems, kept_sems, stage, stage_sems, out_sem, stack, lines, packed = refs
    xin_ref, normed, qkv, attended, middle_ref, probs = kept
    pre_copy = pltpu.make_async_copy(grad_pre_in, grad_pre, pre_sem.at[0])
    pre_copy.start()
    for part in range(QUART):
        start_all(up_copies(plan, gathered, held2, up_sems.at[part], part))
    start_all(first_copies(plan, pieces, devs, held, sems.at[1], pl.ds(OUT, 1)))
    copies = [
        pltpu.make_async_copy(source, target, kept_sems.at[index])
        for index, (source, target) in enumerate(zip(kept_in, kept))
    ]
    for index in (4, 3, 2, 5, 1, 0):
        copies[index].start()
    start_all(first_copies(plan, pieces, devs, held, sems.at[0], pl.ds(0, OUT)))
    length = plan.length
    arrived = jnp.concatenate([some_ref[...], other_ref[...]], 0)
    branch = jnp.where(flag[0] == 0, arrived, cot_ref[...])
    out = Stage(plan, stage, stage_sems)
    small_ref[...] = small_in[...]
    pre_copy.wait()
    grad_hidden = None
    for part in range(QUART):
        wait_bytes(held2.at[part], up_sems.at[part])
        term = mm_nt(grad_pre[:, columns_of(plan, part)], block_of(plan, held2, part))
        grad_hidden = term if grad_hidden is None else grad_hidden + term
    copies[4].wait()
    xhat, rstd = normalised(middle_ref[...])
    small_ref[5:6, :] = column_sum(grad_hidden * xhat)
    small_ref[6:7, :] = column_sum(grad_hidden)
    grad_middle = branch.astype(F32) + norm_back(grad_hidden, xhat, rstd, vec[5:6, :])
    grad_middle_ref[...] = grad_middle
    attn_grad = grad_middle.astype(BF16)
    small_ref[4:5, :] = column_sum(attn_grad)
    wait_bytes(held.at[pl.ds(OUT, 1)], sems.at[1])
    grad_attended[...] = mm_nt(attn_grad, block_of(plan, held, OUT)).astype(BF16)
    copies[3].wait()
    out.put(mm_tn(attended[...], attn_grad), slot_copies(plan, devs, grads, OUT))
    copies[2].wait()
    copies[5].wait()
    attention_back(plan, probs, qkv, grad_attended, grad_rows)
    copies[1].wait()
    copies[0].wait()
    wait_bytes(held.at[pl.ds(0, OUT)], sems.at[0])
    grad_normed = None
    for part in range(OUT):
        rows = grad_rows[:, columns_of(plan, part)]
        term = mm_nt(rows, block_of(plan, held, part))
        grad_normed = term if grad_normed is None else grad_normed + term
        if part != 1:
            small_ref[2 + part // 2 : 3 + part // 2, :] = column_sum(rows)
        out.put(mm_tn(normed[...], rows), slot_copies(plan, devs, grads, part))
    xhat, rstd = normalised(xin_ref[...].astype(F32))
    small_ref[0:1, :] = column_sum(grad_normed * xhat)
    small_ref[1:2, :] = column_sum(grad_normed)
    for item in range(plan.items):
        small_ref[12 + item : 13 + item, :] = column_sum(
            grad_normed[item * length : (item + 1) * length]
        )
    dx_ref[...] = grad_middle_ref[...] + norm_back(grad_normed, xhat, rstd, vec[0:1, :])
    if plan.parts > 1:
        pack_sums(plan, lead, many, small_ref[...], stack, lines)
        packed[...] = lines[...].astype(BF16)
        start_all(
            [
                pltpu.make_async_copy(
                    packed.at[devs[slot]],
                    slot_target(plan, grads, slot).at[pl.ds(FIRST * plan.rows, EXTRA)],
                    out_sem.at[0],
                )
                for slot in range(plan.shards)
            ]
        )
        wait_bytes(packed, out_sem.at[0])
    out.drain()


def pack_kernel(qkv_ref, out_ref, up_ref, down_ref, *refs):
    rows, width = out_ref.shape
    vectors, (up_bias, table, first_ref, second_ref, small, wide) = refs[:8], refs[8:]
    for index, vector in enumerate(vectors):
        small[index : index + 1, :] = vector[...]
    for part in range(QUART):
        small[8 + part : 9 + part, :] = up_bias[:, part * rows : (part + 1) * rows]
    many = 12 + table.shape[0]
    small[12:many, :] = table[...]
    across = width // rows
    wide[...] = jnp.zeros_like(wide)
    for index in range(many):
        line, place = divmod(index, across)
        wide[line : line + 1, place * rows : (place + 1) * rows] = small[index : index + 1, :]
    for part in range(OUT):
        first_ref[part * rows : (part + 1) * rows, :] = qkv_ref[:, part * width : (part + 1) * width].astype(BF16)
    first_ref[OUT * rows : FIRST * rows, :] = out_ref[...].astype(BF16)
    first_ref[FIRST * rows :, :] = wide[...].astype(BF16)
    for part in range(QUART):
        second_ref[part] = up_ref[:, part * width : (part + 1) * width].astype(BF16)
        second_ref[QUART + part] = down_ref[part * rows : (part + 1) * rows, :].astype(BF16)


def vectors_kernel(plan, many, devs, lead, *refs):
    pieces, (out_ref, lines, spread, sem) = slot_pieces(plan, refs[:-4]), refs[-4:]
    rows, width = plan.rows, plan.width
    across = width // rows
    groups = pl.cdiv(many, across)
    start_all(
        [
            pltpu.make_async_copy(piece_rows(parts, FIRST * rows, EXTRA), lines.at[slot], sem.at[0])
            for slot, parts in enumerate(pieces)
        ]
    )
    wait_bytes(lines, sem.at[0])
    line = lax.broadcasted_iota(jnp.int32, (across, width), 0)
    lane = lax.broadcasted_iota(jnp.int32, (across, width), 1)
    chosen = (lane >= line * rows) & (lane < (line + 1) * rows)
    up_line = lax.broadcasted_iota(jnp.int32, (QUART, width), 0)
    up_lane = lax.broadcasted_iota(jnp.int32, (QUART, width), 1)
    ups = jnp.zeros((QUART, width), F32)
    for slot in range(plan.shards):
        values = lines[slot].astype(F32)
        for group in range(groups):
            at = (slot * groups + group) * across
            picked = jnp.where(chosen, jnp.broadcast_to(values[group : group + 1], chosen.shape), 0.0)
            spread[at : at + across, :] = picked.astype(BF16)
        first = QUART * rows * devs[slot]
        there = lax.rem(first, width)
        moved = jnp.broadcast_to(values[8 // across : 8 // across + 1], (8, width))
        moved = pltpu.roll(moved, lax.rem(there + width - 8 % across * rows, width), 1)[:QUART]
        here = (up_line == first // width) & (up_lane >= there) & (up_lane < there + QUART * rows)
        ups = jnp.where(here, moved, ups)
    source = lax.broadcasted_iota(jnp.int32, (width, rows), 0)
    target = lax.broadcasted_iota(jnp.int32, (width, rows), 1)
    fold = sum(jnp.where(source == target + place * rows, 1.0, 0.0) for place in range(across))
    narrow = mm(spread[...], fold.astype(BF16)).astype(BF16)
    entry = lax.broadcasted_iota(jnp.int32, (rows, width), 0)
    column = lax.broadcasted_iota(jnp.int32, (rows, width), 1)
    total = None
    for slot in range(plan.shards):
        at = slot * groups * across
        place = jnp.where(column == entry + devs[slot] * rows, 1.0, 0.0).astype(BF16)
        term = mm(narrow[at : at + groups * across], place)
        total = term if total is None else total + term
    out_ref[...] = jnp.zeros_like(out_ref)
    out_ref[:8, :] = total[:8]
    out_ref[8 : 8 + QUART, :] = ups
    entry = lax.broadcasted_iota(jnp.int32, total.shape, 0)
    for item in range(plan.items):
        picked = jnp.where(entry == 12 + lead[item], total, 0.0)
        out_ref[12 + item : 13 + item, :] = jnp.sum(picked, 0, keepdims=True)


def unpack_kernel(grads_ref, up_ref, down_ref):
    _, rows, width = grads_ref.shape
    for part in range(QUART):
        up_ref[:, part * width : (part + 1) * width] = grads_ref[part].astype(F32)
        down_ref[part * rows : (part + 1) * rows, :] = grads_ref[QUART + part].astype(F32)


def add_kernel(work, *refs):
    outs, at = refs[len(refs) - len(work) :], 0
    for (low, high, first), out in zip(work, outs):
        mine, other = refs[at], refs[at + 1]
        at += 2
        cuts, came = [low, high], None
        if first is not None:
            came = refs[at]
            at += 1
            cuts = sorted({low, first, first + came.shape[0], high})
        for start, end in zip(cuts, cuts[1:]):
            value = mine[0, start:end, :].astype(F32) + other[0, start:end, :].astype(F32)
            if came is not None and first <= start < first + came.shape[0]:
                value = value + came[start - first : end - first, :].astype(F32)
            out[start - low : end - low, :] = value.astype(BF16)


def total_kernel(many, mine, other, ahead, behind, qkv, out, *refs):
    width = mine.shape[2]
    rows = out.shape[0]

    def rows_of(low, count):
        here = slice(low, low + count)
        value = mine[0, here, :].astype(F32) + other[0, here, :].astype(F32)
        return value + (ahead[here, :].astype(F32) + behind[here, :].astype(F32))

    for part in range(OUT):
        qkv[:, part * width : (part + 1) * width] = rows_of(part * rows, rows)
    out[...] = rows_of(OUT * rows, rows)
    vectors, (up_bias, table, small) = refs[:8], refs[8:]
    lines = rows_of(FIRST * rows, EXTRA)
    for index in range(many):
        line, place = divmod(index, width // rows)
        small[index : index + 1, :] = lines[line : line + 1, place * rows : (place + 1) * rows]
    for index, vector in enumerate(vectors):
        vector[...] = small[index : index + 1, :]
    for part in range(QUART):
        up_bias[:, part * rows : (part + 1) * rows] = small[8 + part : 9 + part, :]
    table[...] = small[12:many, :]


SMEM = pl.BlockSpec(memory_space=pltpu.SMEM)
VMEM = pl.BlockSpec(memory_space=pltpu.VMEM)
HBM = pl.BlockSpec(memory_space=pltpu.HBM)
ANY = pl.BlockSpec(memory_space=pl.ANY)


def kept_shapes(plan):
    tokens, width = plan.tokens, plan.width
    return [
        ((tokens, width), BF16),
        ((tokens, 3 * width), BF16),
        ((tokens, width), BF16),
        ((tokens, width), F32),
        ((tokens, width), BF16),
        ((plan.items * plan.pairs, 2 * plan.length, plan.length), F32),
        ((tokens, 4 * width), BF16),
        ((tokens, 4 * width), F32),
    ]


def held_blocks(plan, blocks):
    return pltpu.VMEM((blocks, plan.shards, plan.rows, plan.width), BF16)


def call(kernel, outs, in_specs, out_specs, scratch, name, work, limit, args):
    args = [
        pltpu.with_memory_space_constraint(arg, pltpu.HBM) if spec is HBM else arg
        for arg, spec in zip(args, in_specs)
    ]
    return pl.pallas_call(
        kernel,
        out_shape=outs,
        in_specs=in_specs,
        out_specs=out_specs,
        scratch_shapes=scratch,
        compiler_params=pltpu.CompilerParams(vmem_limit_bytes=limit * 1024 * 1024),
        cost_estimate=pl.CostEstimate(flops=2 * work[0], bytes_accessed=work[1], transcendentals=0),
        name=name,
    )(*args)


def of(shape):
    return jax.ShapeDtypeStruct(*shape)


def inside(shape):
    return pltpu.VMEM(*shape)


def run_attend(plan, lengths, flag, devs, x, vec, pieces):
    kept = kept_shapes(plan)
    block = plan.width * plan.width
    return call(
        functools.partial(attend_kernel, plan),
        [of(kept[3]), of(kept[4])],
        [SMEM, SMEM, SMEM, VMEM, VMEM] + [HBM] * len(pieces),
        [VMEM, VMEM],
        [held_blocks(plan, FIRST)] + [inside(shape) for shape in kept[:3]] + [pltpu.SemaphoreType.DMA((2,))],
        "attend",
        (FIRST * block * plan.tokens, FIRST * block * 2),
        14,
        (lengths, flag, devs, x, vec, *pieces),
    )


def run_vectors(plan, many, devs, lead, pieces):
    groups = pl.cdiv(many, plan.width // plan.rows) * (plan.width // plan.rows)
    return call(
        functools.partial(vectors_kernel, plan, many),
        jax.ShapeDtypeStruct((16, plan.width), F32),
        [SMEM, SMEM] + [HBM] * len(pieces),
        VMEM,
        [
            pltpu.VMEM((plan.shards, EXTRA, plan.width), BF16),
            pltpu.VMEM((plan.shards * groups, plan.width), BF16),
            pltpu.SemaphoreType.DMA((1,)),
        ],
        "vectors",
        (plan.width * plan.width * plan.rows, plan.width * plan.width * 4),
        12,
        (devs, lead, *pieces),
    )


def run_mlp(plan, flag, middle, hidden, vec, gathered):
    block = plan.width * plan.width
    return call(
        functools.partial(mlp_kernel, plan),
        jax.ShapeDtypeStruct(hidden.shape, BF16),
        [SMEM, VMEM, VMEM, VMEM, HBM],
        VMEM,
        [held_blocks(plan, SECOND), pltpu.SemaphoreType.DMA((QUART,)), pltpu.SemaphoreType.DMA((QUART,))],
        "mlp",
        (SECOND * block * plan.tokens, SECOND * block * 2),
        16,
        (flag, middle, hidden, vec, gathered),
    )


def run_load(plan, devs, after, cot, firsts, gathered):
    block = plan.width * plan.width
    return call(
        functools.partial(load_kernel, plan),
        [held_blocks(plan, FIRST), held_blocks(plan, SECOND), inside(kept_shapes(plan)[7])],
        [SMEM, ANY, VMEM] + [HBM] * (1 + len(firsts)),
        [VMEM] * 3,
        [pltpu.SemaphoreType.DMA((2,)), pltpu.SemaphoreType.DMA((QUART,))],
        "load",
        (QUART * block * plan.tokens, (FIRST + SECOND) * block * 4),
        4,
        (devs, after, cot, gathered, *firsts),
    )


def run_chain(plan, lengths, flag, x, recv, cot, vec, held1, held2, grad_act):
    shapes = kept_shapes(plan)
    block = plan.width * plan.width
    rest = [shapes[index] for index in (0, 0, 1, 2, 3, 5)]
    some = ((plan.items // 2 * plan.length, plan.width), BF16)
    results = call(
        functools.partial(chain_kernel, plan),
        [of(some)]
        + [inside(shapes[index]) for index in (4, 6, 7, 0, 1, 5, 3, 0, 3)]
        + [pltpu.HBM(*shape) for shape in rest],
        [SMEM] * 2 + [VMEM] * 7,
        [VMEM] * 10 + [HBM] * len(rest),
        [inside(shapes[index]) for index in (0, 2, 1)]
        + [pltpu.SemaphoreType.DMA((len(rest),))],
        "chain",
        (20 * block * plan.tokens, 12 * block),
        12,
        (lengths, flag, x, recv, cot, vec, held1, held2, grad_act),
    )
    return results[0], results[1:4], results[4:9], results[9], results[10:]


def run_output(plan, flag, act, middle, vec, held2):
    block = plan.width * plan.width
    return call(
        functools.partial(output_kernel, plan),
        of(kept_shapes(plan)[0]),
        [SMEM] + [VMEM] * 4,
        VMEM,
        [],
        "output",
        (QUART * block * plan.tokens, QUART * block),
        4,
        (flag, act, middle, vec, held2),
    )


def run_chain_end(plan, flag, vec, held1, end):
    shapes = kept_shapes(plan)
    block = plan.width * plan.width
    left = plan.items - plan.items // 2
    return call(
        functools.partial(chain_end_kernel, plan),
        of(((left * plan.length, plan.width), BF16)),
        [SMEM] + [VMEM] * 7,
        VMEM,
        [inside(shapes[1])],
        "chain_end",
        (2 * block * plan.tokens, 3 * block),
        6,
        (flag, vec, held1, *end),
    )


def grad_shapes(plan):
    if plan.parts == 1:
        return [pltpu.HBM((1, FIRST * plan.rows, plan.width), BF16)]
    rows = FIRST * plan.rows + EXTRA
    return [
        pltpu.HBM((count, rows, plan.width), BF16)
        for count in (plan.shards // 2, plan.shards // 2, 1)
    ]


def stage_scratch(plan, slots):
    return [
        pltpu.VMEM((slots, plan.shards, plan.rows, plan.width), BF16),
        pltpu.SemaphoreType.DMA((slots,)),
    ]


def run_mlp_back(plan, flag, beside, arriving, cot, held2, hidden, act, slope):
    shapes = kept_shapes(plan)
    block = plan.width * plan.width
    return call(
        functools.partial(mlp_back_kernel, plan),
        [
            pltpu.HBM(*shapes[6]),
            jax.ShapeDtypeStruct((16, plan.width), F32),
            pltpu.HBM((plan.shards, SECOND, plan.rows, plan.width), BF16),
        ],
        [SMEM, HBM] + [VMEM] * 7,
        [HBM, VMEM, HBM],
        [inside(shapes[6])] + stage_scratch(plan, SECOND) + [pltpu.SemaphoreType.DMA((1,))],
        "mlp_back",
        (2 * SECOND * block * plan.tokens, SECOND * block * 2),
        16,
        (flag, beside, *arriving, cot, held2, hidden, act, slope),
    )


def run_rest(plan, many, flag, devs, lead, arriving, cot, small, vec, gathered, grad_pre, kept, pieces):
    shapes = kept_shapes(plan)
    block = plan.width * plan.width
    across = plan.width // plan.rows
    high = pl.cdiv(many, across) * across
    lines = (plan.shards, EXTRA, plan.width)
    rest = [shapes[index] for index in (0, 0, 1, 2, 3, 5)]
    input_grad, small, *grads = call(
        functools.partial(rest_kernel, plan, many),
        [of(shapes[3]), jax.ShapeDtypeStruct((16, plan.width), F32)] + grad_shapes(plan),
        [SMEM] * 3 + [VMEM] * 5 + [HBM] * (2 + len(rest) + len(pieces)),
        [VMEM] * 2 + [HBM] * plan.parts,
        [inside(shape) for shape in rest]
        + [held_blocks(plan, QUART), inside(shapes[6])]
        + [pltpu.SemaphoreType.DMA((QUART,)), pltpu.SemaphoreType.DMA((1,))]
        + [held_blocks(plan, FIRST)]
        + [inside(shapes[index]) for index in (3, 0, 1)]
        + [pltpu.SemaphoreType.DMA((2,)), pltpu.SemaphoreType.DMA((len(rest),))]
        + stage_scratch(plan, FIRST)
        + [pltpu.SemaphoreType.DMA((1,)), pltpu.VMEM((plan.shards * high, plan.rows), BF16)]
        + [pltpu.VMEM(lines, F32), pltpu.VMEM(lines, BF16)],
        "rest",
        (3 * FIRST * block * plan.tokens, 3 * FIRST * block * 2),
        34,
        (flag, devs, lead, *arriving, cot, small, vec, gathered, grad_pre, *kept, *pieces),
    )
    return input_grad, small, grads


def run_add(mine, other, work):
    _, rows, width = mine.shape
    mine = pltpu.with_memory_space_constraint(mine, pltpu.HBM)
    specs, args, plans, outs = [], [], [], []
    for way, (slot, low, high, came) in enumerate(work):
        there = slot if other.shape[0] > 1 else 0
        specs += [
            pl.BlockSpec((1, rows, width), lambda index, slot=slot: (slot, 0, 0))
            for slot in (slot, there)
        ]
        args += [mine, other]
        first = None
        if came is not None:
            specs.append(pl.BlockSpec(came.shape, lambda index: (0, 0)))
            args.append(came)
            first = rows - came.shape[0] if way else 0
        plans.append((low, high, first))
        outs.append((high - low, width))
    return pl.pallas_call(
        functools.partial(add_kernel, plans),
        out_shape=[jax.ShapeDtypeStruct(shape, BF16) for shape in outs],
        grid=(1,),
        in_specs=specs,
        out_specs=[pl.BlockSpec(shape, lambda index: (0, 0)) for shape in outs],
        compiler_params=pltpu.CompilerParams(vmem_limit_bytes=14 * 1024 * 1024),
        name="add",
    )(*args)


def run_total(one, many, shapes):
    args = [pltpu.with_memory_space_constraint(one.mine, pltpu.HBM), one.other]
    _, rows, width = one.mine.shape
    first = pl.BlockSpec((1, rows, width), lambda index: (0, 0, 0))
    whole = pl.BlockSpec((rows, width), lambda index: (0, 0))
    return pl.pallas_call(
        functools.partial(total_kernel, many),
        out_shape=[jax.ShapeDtypeStruct(shape, F32) for shape in shapes],
        grid=(1,),
        in_specs=[first, first, whole, whole],
        out_specs=[pl.BlockSpec(shape, lambda index: (0, 0)) for shape in shapes],
        scratch_shapes=[pltpu.VMEM((many, shapes[2][1]), F32)],
        compiler_params=pltpu.CompilerParams(vmem_limit_bytes=14 * 1024 * 1024),
        name="total",
    )(*args, *one.carried)


def after(value, *others):
    return lax.optimization_barrier((value, *others))[0]


def shifted(value, axis, steps):
    count = lax.axis_size(axis)
    first, last = (max(0, -steps), min(count, count - steps))
    return lax.ppermute(value, axis, [(source, source + steps) for source in range(first, last)])


class Ring:
    def __init__(self, count):
        self.count, self.chips = count, count // 2
        self.walk = list(range(0, self.chips, 2)) + list(range(self.chips - 1, 0, -2))
        self.order = [2 * chip + core for chip in self.walk for core in range(2)]
        after = self.walk[1:] + self.walk[:1]
        self.onward = [
            (2 * here + core, 2 * there + core)
            for here, there in zip(self.walk, after)
            for core in range(2)
        ]
        self.back = [(there, here) for here, there in self.onward]
        self.sibling = [(index, index ^ 1) for index in range(count)]

    def slots(self):
        index = lax.axis_index("dp")
        chip, core = index // 2, index % 2
        place_of = lambda chip: jnp.where(chip % 2 == 0, chip // 2, self.chips - 1 - chip // 2)
        steps = jnp.arange(self.chips, dtype=jnp.int32)
        ahead = (place_of(chip) + steps) % self.chips
        chips = jnp.where(ahead < (self.chips + 1) // 2, 2 * ahead, 2 * (self.chips - 1 - ahead) + 1)
        devs = jnp.concatenate([2 * chips + core, 2 * chips + 1 - core]).astype(jnp.int32)
        return devs

    def step(self, ahead, behind):
        return lax.ppermute(ahead, "dp", self.onward), lax.ppermute(behind, "dp", self.back)

    def gather(self, shard, low):
        half = self.chips // 2
        own = [[shard]] + [None] * (self.chips - 1)
        ahead = behind = shard
        for step in range(1, half):
            ahead, behind = self.step(ahead, behind)
            own[self.chips - step], own[step] = [ahead], [behind]
            ahead, behind = lax.optimization_barrier((ahead, behind))
        own[half] = list(self.step(ahead[:low], behind[low:]))
        return [piece for pieces in own for piece in pieces]

    def siblings(self, pieces):
        return [lax.ppermute(piece, "dp", self.sibling) for piece in pieces]


class RingSum:
    def __init__(self, ring, mine, other, opposite, low):
        self.ring, self.mine, self.low = ring, mine, low
        self.other, self.opposite = other, opposite
        self.time = ring.chips // 2
        self.carried = [None, None]

    def add(self):
        rows = self.mine.shape[1]
        other = self.other
        if self.carried[0] is None:
            other = self.opposite
            work = [(self.time, 0, self.low, None), (self.time, self.low, rows, None)]
        else:
            work = [
                (self.time, 0, rows, self.carried[0]),
                (self.ring.chips - self.time, 0, rows, self.carried[1]),
            ]
        self.carried = run_add(self.mine, other, work)

    def send(self):
        self.carried = self.ring.step(*self.carried)
        self.time -= 1


def body(
    block_input, cotangent, lengths, leads,
    norm_gain1, norm_bias1, lead_table, qkv_weight, query_bias, value_bias, out_weight, out_bias,
    norm_gain2, norm_bias2, up_weight, up_bias, down_weight, down_bias,
):
    count = lax.axis_size("dp")
    micro, local, length, width = block_input.shape
    items = micro * local
    rows = width // count
    leads_count = lead_table.shape[2]
    flag = lax.axis_index("section").astype(jnp.int32).reshape(1)
    flat = lambda value: value.reshape(items * length, width)
    x, cot = flat(block_input), flat(cotangent)
    lens, lead = lengths.reshape(items), leads.reshape(items)

    vectors = (
        norm_gain1, norm_bias1, query_bias, value_bias, out_bias, norm_gain2, norm_bias2, down_bias
    )
    many = 12 + leads_count
    aligned = rows % 16 == 0 and count % 4 == 0 and pl.cdiv(many, width // rows) <= EXTRA
    if aligned:
        ring = Ring(count)
        first, second = pl.pallas_call(
            pack_kernel,
            out_shape=[
                jax.ShapeDtypeStruct((FIRST * rows + EXTRA, width), BF16),
                jax.ShapeDtypeStruct((SECOND, rows, width), BF16),
            ],
            scratch_shapes=[pltpu.VMEM((many, rows), F32), pltpu.VMEM((EXTRA, width), F32)],
            name="pack",
        )(qkv_weight[0], out_weight[0], up_weight[0], down_weight[0], *vectors, up_bias, lead_table[0].T)
        gathered = lax.all_gather(second, "dp", axis=0, tiled=True, axis_index_groups=[ring.order])
        gathered = gathered.reshape(count, SECOND, rows, width)
        firsts = ring.gather(first, LOW * rows)
        firsts = firsts + ring.siblings(firsts)
        devs = ring.slots()
        plan = Plan(ring.order, rows, items, length, width)
        vec = run_vectors(plan, many, devs, lead, firsts)
    else:
        wide_blocks = lambda value: value[0].reshape(rows, -1, width).transpose(1, 0, 2)
        packed = jnp.concatenate(
            [wide_blocks(qkv_weight), out_weight, wide_blocks(up_weight), down_weight.reshape(QUART, rows, width)], 0
        )
        everything = lax.all_gather(packed.astype(BF16), "dp", axis=0)
        across_blocks = lambda value: value.transpose(1, 0, 2, 3).reshape(-1, width, width)
        firsts = [across_blocks(everything[:, :FIRST])]
        gathered = jnp.concatenate(
            [
                across_blocks(everything[:, FIRST : FIRST + QUART]),
                everything[:, FIRST + QUART :].reshape(QUART, width, width),
            ],
            0,
        )[None]
        devs = jnp.zeros((1,), jnp.int32)
        plan = Plan([0], width, items, length, width)
        small = jnp.concatenate([*vectors, up_bias.reshape(4, rows), lead_table[0].T], 0).astype(BF16)
        wide = lax.all_gather(small, "dp", axis=1, tiled=True).astype(F32)
        vec = jnp.concatenate(
            [wide[:8], wide[8:12].reshape(4, count, rows).transpose(1, 0, 2).reshape(4, width)]
            + [lax.dynamic_slice_in_dim(wide, 12 + lead[item], 1, 0) for item in range(items)]
            + [jnp.zeros((4 - items, width), F32)],
            0,
        )

    middle, hidden = run_attend(plan, lens, flag, devs, x, vec, firsts)
    first_out = run_mlp(plan, flag, middle, hidden, vec, gathered)
    recv = shifted(first_out, "section", 1)
    held1, held2, grad_act = run_load(plan, devs, first_out, cot, firsts, gathered)
    some_grad, (hidden, act, slope), end, middle, kept = run_chain(
        plan, lens, flag, x, recv, cot, vec, held1, held2, grad_act
    )
    other_grad = run_chain_end(plan, flag, vec, held1, end)
    arriving = [shifted(grad, "section", -1) for grad in (some_grad, other_grad)]
    output = run_output(plan, flag, act, middle, vec, held2)
    grad_pre, sums, grads2 = run_mlp_back(
        plan, flag, output, arriving, cot, held2, hidden, act, slope
    )
    input_grad, sums, grads1 = run_rest(
        plan, many, flag, devs, lead, arriving, cot, sums, vec, gathered, grad_pre, kept, firsts
    )
    if aligned:
        (opposite,) = ring.siblings(grads1[2:])
        (other,) = ring.siblings([after(grads1[1], opposite)])
        first_sum = RingSum(ring, grads1[0], other, opposite, LOW * rows)
        while first_sum.time:
            first_sum.add()
            first_sum.send()
        grads2 = lax.psum_scatter(
            grads2.reshape(count * SECOND, rows, width),
            "dp", scatter_dimension=0, tiled=True, axis_index_groups=[ring.order],
        )
        grad_up, grad_down = pl.pallas_call(
            unpack_kernel,
            out_shape=[
                jax.ShapeDtypeStruct((rows, QUART * width), F32),
                jax.ShapeDtypeStruct((QUART * rows, width), F32),
            ],
            name="unpack",
        )(grads2)
        grad_qkv, grad_out, *small_grads = run_total(
            first_sum, many,
            [(rows, OUT * width), (rows, width)] + [(1, rows)] * 8 + [(1, QUART * rows), (leads_count, rows)],
        )
    else:
        split = lambda value: value[0].reshape(-1, count, rows, width).transpose(1, 0, 2, 3)
        grads = jnp.concatenate(
            [
                split(grads1[0]),
                split(grads2[0, :QUART].reshape(1, QUART * width, width)),
                grads2[0, QUART:].reshape(count, QUART, rows, width),
            ],
            1,
        )
        grads = lax.psum_scatter(grads, "dp", scatter_dimension=0, tiled=False).astype(F32)
        across = lambda value: value.transpose(1, 0, 2).reshape(rows, -1)
        grad_qkv, grad_out = across(grads[:OUT]), grads[OUT]
        grad_up = across(grads[FIRST : FIRST + QUART])
        grad_down = grads[FIRST + QUART :].reshape(QUART * rows, width)
        hot = (jnp.arange(leads_count)[:, None] == lead[None, :]).astype(F32)
        table = sum(hot[:, item : item + 1] * sums[12 + item : 13 + item] for item in range(items))
        up_sums = sums[8:12].reshape(count, 4, rows).transpose(1, 0, 2).reshape(4, width)
        spread = lax.psum_scatter(
            jnp.concatenate([sums[:8], up_sums, table], 0), "dp", scatter_dimension=1, tiled=True
        )
        small_grads = [spread[index : index + 1] for index in range(8)]
        small_grads += [spread[8:12].reshape(1, 4 * rows), spread[12:]]
    vector = small_grads
    shape = (1, micro, local, length, width)
    return (
        output.reshape(shape),
        input_grad.reshape(shape),
        vector[0],
        vector[1],
        vector[9].T[None],
        grad_qkv[None],
        vector[2],
        vector[3],
        grad_out[None],
        vector[4],
        vector[5],
        vector[6],
        grad_up[None],
        vector[8],
        grad_down[None],
        vector[7],
    )


def solution(mesh):
    weights = (
        P("section", "dp"),
        P("section", "dp"),
        P("section", "dp", None),
        P("section", "dp", None),
        P("section", "dp"),
        P("section", "dp"),
        P("section", "dp", None),
        P("section", "dp"),
        P("section", "dp"),
        P("section", "dp"),
        P("section", "dp", None),
        P("section", "dp"),
        P("section", "dp", None),
        P("section", "dp"),
    )
    rows = P(None, "dp", None, None)
    layers = P("section", None, "dp", None, None)
    return jax.shard_map(
        body,
        mesh=mesh,
        in_specs=(rows, rows, P(None, "dp"), P(None, "dp")) + weights,
        out_specs=(layers, layers) + weights,
        check_vma=False,
    )
```

```python
import functools

import jax
import jax.numpy as jnp
from jax import lax
from jax.experimental import pallas as pl
from jax.experimental.pallas import tpu as pltpu
from jax.sharding import PartitionSpec as P

HEAD = 64
PAIR = 2 * HEAD
EPS = 1e-06
SCALE_FACTOR = 0.125
GELU_A = 0.7978845608028654
GELU_B = 0.044715
F32 = jnp.float32
BF16 = jnp.bfloat16
OUT = 3
FIRST = 4
SECOND = 8
QUART = 4
EXTRA = 16
LOW = 2


def mm(left, right):
    return jnp.dot(left, right, preferred_element_type=F32)


def mm_nt(left, right):
    return lax.dot_general(left, right, (((1,), (1,)), ((), ())), preferred_element_type=F32)


def mm_tn(left, right):
    return lax.dot_general(left, right, (((0,), (0,)), ((), ())), preferred_element_type=F32)


def normalised(values):
    mean = jnp.mean(values, -1, keepdims=True)
    centred = values - mean
    variance = jnp.mean(centred * centred, -1, keepdims=True)
    rstd = lax.rsqrt(variance + EPS)
    return centred * rstd, rstd


def norm_back(grad, xhat, rstd, gain):
    scaled = grad * gain
    first = jnp.mean(scaled, -1, keepdims=True)
    second = jnp.mean(scaled * xhat, -1, keepdims=True)
    return rstd * (scaled - first - xhat * second)


def gelu_both(values):
    square = values * values
    slope = GELU_A * (1.0 + 3.0 * GELU_B * square)
    bend = jnp.tanh(GELU_A * values * (1.0 + GELU_B * square))
    half = 0.5 * (1.0 + bend)
    return values * half, half + 0.5 * values * (1.0 - bend * bend) * slope


def split_pair(rows):
    lane = lax.broadcasted_iota(jnp.int32, rows.shape, 1)
    zero = jnp.zeros_like(rows)
    return jnp.concatenate(
        [jnp.where(lane < HEAD, rows, zero), jnp.where(lane < HEAD, zero, rows)], 0
    )


def join_pair(stacked):
    count = stacked.shape[0] // 2
    lane = lax.broadcasted_iota(jnp.int32, (count, PAIR), 1)
    return jnp.where(lane < HEAD, stacked[:count], stacked[count:])


def runs_of(order):
    if all(order[at + 1] == order[at] + 1 for at in range(0, len(order) - 1, 2)) and len(order) > 1:
        return [(at, order[at], 2) for at in range(0, len(order), 2)]
    return [(at, device, 1) for at, device in enumerate(order)]


class Plan:
    def __init__(self, order, rows, items, length, width):
        self.order, self.shards, self.rows = order, len(order), rows
        self.items, self.length, self.width = items, length, width
        self.tokens = items * length
        self.low = LOW * rows
        self.pairs = width // PAIR
        whole = self.shards % QUART == 0
        self.runs = [(0, QUART)] if whole else [(block, 1) for block in range(QUART)]
        self.parts = 3 if self.shards > 1 else 1


def slot_pieces(plan, refs):
    if plan.shards == 1:
        return [[(0, refs[0])]]
    refs, slots, half = list(refs), [], plan.shards // 4
    for slot in range(plan.shards):
        parts = [(0, refs.pop(0))]
        if slot % (plan.shards // 2) == half:
            parts.append((plan.low, refs.pop(0)))
        slots.append(parts)
    return slots


def piece_rows(parts, row, count):
    start, ref = [part for part in parts if part[0] <= row][-1]
    return ref.at[pl.ds(row - start, count)]


def first_copies(plan, refs, devs, held, sem, blocks):
    if plan.shards == 1:
        return block_copies(refs, devs, held, sem, blocks)
    return [
        pltpu.make_async_copy(
            piece_rows(parts, block * plan.rows, plan.rows), held.at[block, devs[slot]], sem
        )
        for slot, parts in enumerate(slot_pieces(plan, refs))
        for block in range(blocks.start, blocks.start + blocks.size)
    ]


def block_copies(pieces, devs, held, sem, blocks, at=0):
    return [
        pltpu.make_async_copy(
            piece.at[blocks], held.at[pl.ds(at + blocks.start, blocks.size), devs[slot]], sem
        )
        for slot, piece in enumerate(pieces)
    ]


def up_copies(plan, gathered, held, sem, part):
    return [
        pltpu.make_async_copy(
            gathered.at[pl.ds(place, count), part], held.at[part, pl.ds(device, count)], sem
        )
        for place, device, count in runs_of(plan.order)
    ]


def down_copies(plan, pieces, devs, held, sems):
    copies = []
    for slot, piece in enumerate(pieces):
        for first, count in plan.runs:
            block, row = divmod(QUART * devs[slot] + first, plan.shards)
            copy = pltpu.make_async_copy(
                piece.at[pl.ds(first, count)],
                held.at[QUART + block, pl.ds(row, count)],
                sems.at[block],
            )
            copies.append((block, copy))
    return copies


def second_pieces(plan, gathered):
    ups = [gathered.at[place, pl.ds(0, QUART)] for place in range(plan.shards)]
    downs = [gathered.at[place, pl.ds(QUART, QUART)] for place in range(plan.shards)]
    return ups, downs


def start_all(copies):
    for copy in copies:
        copy.start()


def wait_bytes(part, sem):
    pltpu.make_async_copy(part, part, sem).wait()


def block_of(plan, held, index):
    return held[index].reshape(plan.width, plan.width)


def columns_of(plan, index):
    return slice(index * plan.width, (index + 1) * plan.width)


def attention_forward(plan, lengths, qkv_ref, attended_ref, probs_ref):
    width, length = plan.width, plan.length
    key_index = lax.broadcasted_iota(jnp.int32, (2 * length, length), 1)
    for item in range(plan.items):
        rows = slice(item * length, (item + 1) * length)
        valid = key_index < lengths[item]
        for pair in range(plan.pairs):
            at = pair * PAIR
            query = split_pair(qkv_ref[rows, at : at + PAIR])
            key = qkv_ref[rows, width + at : width + at + PAIR]
            value = qkv_ref[rows, 2 * width + at : 2 * width + at + PAIR]
            logits = jnp.where(valid, mm_nt(query, key) * SCALE_FACTOR, -1000000000.0)
            expo = jnp.exp(logits - jnp.max(logits, -1, keepdims=True))
            probs = expo / jnp.sum(expo, -1, keepdims=True)
            if probs_ref is not None:
                probs_ref[item * plan.pairs + pair] = probs
            attended_ref[rows, at : at + PAIR] = join_pair(mm(probs.astype(BF16), value)).astype(
                BF16
            )


def first_half(plan, inputs, lengths, vec, held, wait, normed_ref, qkv_ref, attended_ref, probs_ref, hidden_ref):
    width, length = plan.width, plan.length
    values = inputs.astype(F32)
    xhat, _ = normalised(values)
    base = xhat * vec[0:1, :] + vec[1:2, :]
    for item in range(plan.items):
        rows = slice(item * length, (item + 1) * length)
        normed_ref[rows, :] = (base[rows] + vec[12 + item : 13 + item, :]).astype(BF16)
    wait(0)
    for part, bias in enumerate((2, None, 3)):
        joined = mm(normed_ref[...], block_of(plan, held, part))
        if bias is not None:
            joined = joined + vec[bias : bias + 1, :]
        qkv_ref[:, columns_of(plan, part)] = joined.astype(BF16)
    attention_forward(plan, lengths, qkv_ref, attended_ref, probs_ref)
    wait(1)
    middle = values + (mm(attended_ref[...], block_of(plan, held, OUT)) + vec[4:5, :])
    xhat, _ = normalised(middle)
    hidden_ref[...] = (xhat * vec[5:6, :] + vec[6:7, :]).astype(BF16)
    return middle


def activate(plan, part, hidden_ref, vec, held):
    pre_act = mm(hidden_ref[...], block_of(plan, held, part)) + vec[8 + part : 9 + part, :]
    act, slope = gelu_both(pre_act)
    return act.astype(BF16), slope


def second_half(plan, hidden_ref, vec, held, wait):
    total = None
    for part in range(QUART):
        wait(part)
        act, _ = activate(plan, part, hidden_ref, vec, held)
        wait(QUART + part)
        term = mm(act, block_of(plan, held, QUART + part))
        total = term if total is None else total + term
    return total + vec[7:8, :]


def attention_back(plan, probs_ref, qkv_ref, grad_attended_ref, rows_ref, items=None):
    width, length = plan.width, plan.length
    for item in range(plan.items) if items is None else items:
        rows = slice(item * length, (item + 1) * length)
        for pair in range(plan.pairs):
            at = pair * PAIR
            query = split_pair(qkv_ref[rows, at : at + PAIR])
            key = qkv_ref[rows, width + at : width + at + PAIR]
            value = qkv_ref[rows, 2 * width + at : 2 * width + at + PAIR]
            grad = split_pair(grad_attended_ref[rows, at : at + PAIR])
            probs = probs_ref[item * plan.pairs + pair]
            grad_probs = mm_nt(grad, value)
            centre = jnp.sum(grad_probs * probs, -1, keepdims=True)
            grad_logits = (probs * (grad_probs - centre)).astype(BF16)
            grad_query = join_pair(mm(grad_logits, key)) * SCALE_FACTOR
            grad_key = mm_tn(grad_logits, query) * SCALE_FACTOR
            grad_value = mm_tn(probs.astype(BF16), grad)
            rows_ref[rows, at : at + PAIR] = grad_query.astype(BF16)
            rows_ref[rows, width + at : width + at + PAIR] = grad_key.astype(BF16)
            rows_ref[rows, 2 * width + at : 2 * width + at + PAIR] = grad_value.astype(BF16)


def column_sum(values):
    return jnp.sum(values.astype(F32), 0, keepdims=True)


def attend_kernel(plan, lengths, flag, devs, x_ref, vec, *refs):
    pieces, (middle_ref, hidden_ref, held, normed, qkv, attended, sems) = refs[:-7], refs[-7:]
    start_all(first_copies(plan, pieces, devs, held, sems.at[0], pl.ds(0, OUT)))
    start_all(first_copies(plan, pieces, devs, held, sems.at[1], pl.ds(OUT, 1)))

    def wait(group):
        blocks = pl.ds(OUT, 1) if group else pl.ds(0, OUT)
        wait_bytes(held.at[blocks], sems.at[group])

    middle_ref[...] = first_half(
        plan, x_ref[...], lengths, vec, held, wait, normed, qkv, attended, None, hidden_ref
    )


def mlp_kernel(plan, flag, middle_ref, hidden_ref, vec, gathered, y_ref, held, sems, down_sems):
    @pl.when(flag[0] == 0)
    def _():
        _, downs = second_pieces(plan, gathered)
        down = down_copies(plan, downs, plan.order, held, down_sems)
        for part in range(QUART):
            start_all(up_copies(plan, gathered, held, sems.at[part], part))
            start_all([copy for block, copy in down if block == part])

        def wait(block):
            sem = sems.at[block] if block < QUART else down_sems.at[block - QUART]
            wait_bytes(held.at[block], sem)

        total = second_half(plan, hidden_ref, vec, held, wait)
        y_ref[...] = (middle_ref[...] + total).astype(BF16)


def load_kernel(plan, devs, flag, after, cot_ref, gathered, *refs):
    firsts, (held1, held2, grad_act, turned, sems, down_sems) = refs[:-6], refs[-6:]
    ups, downs = second_pieces(plan, gathered)
    start_all([copy for _, copy in down_copies(plan, downs, plan.order, held2, down_sems)])
    start_all(block_copies(ups, plan.order, held2, sems.at[1], pl.ds(0, QUART)))
    start_all(first_copies(plan, firsts, devs, held1, sems.at[0], pl.ds(0, FIRST)))
    for part in range(QUART):
        wait_bytes(held2.at[QUART + part], down_sems.at[part])
        grad_act[:, columns_of(plan, part)] = mm_nt(
            cot_ref[...], block_of(plan, held2, QUART + part)
        )
    wait_bytes(held2.at[pl.ds(0, QUART)], sems.at[1])
    wait_bytes(held1, sems.at[0])

    @pl.when(flag[0] == 1)
    def _():
        for block in range(FIRST):
            turned[block] = block_of(plan, held1, block).T
        for part in range(QUART):
            turned[FIRST + part] = block_of(plan, held2, part).T


def input_grad(plan, items, vec, turned, xin_ref, qkv, probs, grad_middle, grad_attended, grad_rows, dx_ref):
    attention_back(plan, probs, qkv, grad_attended, grad_rows, items)
    rows = slice(items.start * plan.length, items.stop * plan.length)
    grad_normed = None
    for part in range(OUT):
        term = mm(grad_rows[rows, columns_of(plan, part)], turned[part])
        grad_normed = term if grad_normed is None else grad_normed + term
    xhat, rstd = normalised(xin_ref[rows, :].astype(F32))
    dx_ref[...] = (grad_middle[rows, :] + norm_back(grad_normed, xhat, rstd, vec[0:1, :])).astype(BF16)


def chain_kernel(
    plan, lengths, flag, x_ref, recv_ref, cot_ref, vec, held1, held2, grad_act, turned,
    dx_ref, hidden, act, slope, xin_ref, qkv, probs, grad_middle, grad_attended, middle, *refs,
):
    outs, (normed, attended, grad_rows, sems) = refs[:6], refs[6:]
    kept = (xin_ref, normed, qkv, attended, middle, probs)
    copies = [
        pltpu.make_async_copy(source, target, sems.at[index])
        for index, (source, target) in enumerate(zip(kept, outs))
    ]
    xin_ref[...] = jnp.where(flag[0] == 0, x_ref[...], recv_ref[...])
    middle[...] = first_half(
        plan, xin_ref[...], lengths, vec, held1, lambda group: None, normed, qkv, attended, probs, hidden
    )
    start_all(copies)
    for part in range(QUART):
        columns = columns_of(plan, part)
        act[:, columns], slope[:, columns] = activate(plan, part, hidden, vec, held2)

    @pl.when(flag[0] == 1)
    def _():
        branch = cot_ref[...]
        grad_hidden = None
        for part in range(QUART):
            grad_pre = (slope[:, columns_of(plan, part)] * grad_act[:, columns_of(plan, part)]).astype(BF16)
            term = mm(grad_pre, turned[FIRST + part])
            grad_hidden = term if grad_hidden is None else grad_hidden + term
        xhat, rstd = normalised(middle[...])
        grad_middle[...] = branch.astype(F32) + norm_back(grad_hidden, xhat, rstd, vec[5:6, :])
        grad_attended[...] = mm(grad_middle[...].astype(BF16), turned[OUT]).astype(BF16)
        input_grad(
            plan, range(plan.items // 2), vec, turned, xin_ref, qkv, probs, grad_middle, grad_attended, grad_rows, dx_ref
        )

    for copy in copies:
        copy.wait()


def chain_end_kernel(plan, flag, vec, turned, xin_ref, qkv, probs, grad_middle, grad_attended, dx_ref, grad_rows):
    @pl.when(flag[0] == 1)
    def _():
        input_grad(
            plan, range(plan.items // 2, plan.items), vec, turned, xin_ref, qkv, probs, grad_middle, grad_attended,
            grad_rows, dx_ref,
        )


def output_kernel(plan, flag, act, middle_ref, vec, held2, y_ref):
    total = None
    for part in range(QUART):
        term = mm(act[:, columns_of(plan, part)], block_of(plan, held2, QUART + part))
        total = term if total is None else total + term
    y_ref[...] = (middle_ref[...] + (total + vec[7:8, :])).astype(BF16)


class Stage:
    def __init__(self, plan, stage, sems):
        self.plan, self.stage, self.sems, self.sent = plan, stage, sems, 0

    def put(self, value, copies_of):
        slots = self.stage.shape[0]
        slot = self.sent % slots
        if self.sent >= slots:
            wait_bytes(self.stage.at[slot], self.sems.at[slot])
        self.sent += 1
        plan = self.plan
        self.stage[slot] = value.astype(BF16).reshape(plan.shards, plan.rows, plan.width)
        start_all(copies_of(self.stage.at[slot], self.sems.at[slot]))

    def drain(self):
        for slot in range(min(self.stage.shape[0], self.sent)):
            wait_bytes(self.stage.at[slot], self.sems.at[slot])


def mlp_back_kernel(
    plan, flag, beside, some_ref, other_ref, cot_ref, held2, hidden, act, slope,
    grad_pre_out, small_ref, grads, grad_pre_ref, stage, stage_sems, pre_sem,
):
    arrived = jnp.concatenate([some_ref[...], other_ref[...]], 0)
    branch = jnp.where(flag[0] == 0, arrived, cot_ref[...])
    out = Stage(plan, stage, stage_sems)

    def copies_of_up(part):
        def copies(source, sem):
            return [
                pltpu.make_async_copy(
                    source.at[pl.ds(device, count)], grads.at[pl.ds(place, count), part], sem
                )
                for place, device, count in runs_of(plan.order)
            ]

        return copies

    def copies_of_down(part):
        def copies(source, sem):
            made = []
            for place, device in enumerate(plan.order):
                for first, count in plan.runs:
                    block, row = divmod(QUART * device + first, plan.shards)
                    if block == part:
                        made.append(
                            pltpu.make_async_copy(
                                source.at[pl.ds(row, count)],
                                grads.at[place, pl.ds(QUART + first, count)],
                                sem,
                            )
                        )
            return made

        return copies

    for part in range(QUART):
        columns = columns_of(plan, part)
        grad_act = mm_nt(branch, block_of(plan, held2, QUART + part))
        grad_pre = (slope[:, columns] * grad_act).astype(BF16)
        grad_pre_ref[:, columns] = grad_pre
        out.put(mm_tn(act[:, columns], branch), copies_of_down(part))
        out.put(mm_tn(hidden[...], grad_pre), copies_of_up(part))
    copy = pltpu.make_async_copy(grad_pre_ref, grad_pre_out, pre_sem.at[0])
    copy.start()
    small_ref[...] = jnp.zeros_like(small_ref)
    small_ref[7:8, :] = column_sum(branch)
    for part in range(QUART):
        small_ref[8 + part : 9 + part, :] = column_sum(grad_pre_ref[:, columns_of(plan, part)])
    out.drain()
    copy.wait()


def slot_target(plan, grads, slot):
    if plan.parts == 1:
        return grads[0].at[0]
    half = plan.shards // 2
    if slot == half + half // 2:
        return grads[2].at[0]
    return grads[slot // half].at[slot % half]


def slot_copies(plan, devs, grads, block):
    def copies(source, sem):
        return [
            pltpu.make_async_copy(
                source.at[devs[slot]],
                slot_target(plan, grads, slot).at[pl.ds(block * plan.rows, plan.rows)],
                sem,
            )
            for slot in range(plan.shards)
        ]

    return copies


def pack_sums(plan, lead, many, sums, stack, lines):
    rows, width = plan.rows, plan.width
    across = width // rows
    groups = pl.cdiv(many, across)
    high = groups * across
    leads = many - 12
    entry = lax.broadcasted_iota(jnp.int32, (high - 12, width), 0)
    table = jnp.zeros((high - 12, width), F32)
    for item in range(plan.items):
        table = table + jnp.where(entry == lead[item], sums[12 + item : 13 + item], 0.0)
    top, ups = sums[:8], sums[8:12]
    for device in range(plan.shards):
        columns = slice(device * rows, (device + 1) * rows)
        line, place = divmod(QUART * device * rows, width)
        parts = [
            ups[line : line + 1, place + part * rows : place + (part + 1) * rows]
            for part in range(QUART)
        ]
        share = jnp.concatenate([top[:, columns], *parts, table[:, columns]], 0)
        stack[device * high : (device + 1) * high, :] = share.astype(BF16)
    entry = lax.broadcasted_iota(jnp.int32, (rows, width), 0)
    column = lax.broadcasted_iota(jnp.int32, (rows, width), 1)
    tile = jnp.where(lax.rem(column, rows) == entry, 1.0, 0.0).astype(BF16)
    line = lax.broadcasted_iota(jnp.int32, (high, width), 0)
    lane = lax.broadcasted_iota(jnp.int32, (high, width), 1)
    place = lax.rem(line, across) * rows
    chosen = (lane >= place) & (lane < place + rows)
    lines[...] = jnp.zeros_like(lines)
    for device in range(plan.shards):
        spread = mm(stack[device * high : (device + 1) * high, :], tile)
        spread = jnp.where(chosen, spread, 0.0).reshape(groups, across, width)
        lines[device, 0:groups, :] = jnp.sum(spread, 1)


def rest_kernel(
    plan, many, flag, devs, lead, some_ref, other_ref, cot_ref, small_in, vec, gathered, grad_pre_in, *refs,
):
    count = plan.shards + (2 if plan.parts > 1 else 0)
    kept_in, pieces, refs = refs[:6], refs[6 : 6 + count], refs[6 + count :]
    dx_ref, small_ref = refs[:2]
    grads, refs = refs[2 : 2 + plan.parts], refs[2 + plan.parts :]
    kept, (held2, grad_pre, up_sems, pre_sem), refs = refs[:6], refs[6:10], refs[10:]
    held, grad_middle_ref, grad_attended, grad_rows, sems, kept_sems, stage, stage_sems, out_sem, stack, lines, packed = refs
    xin_ref, normed, qkv, attended, middle_ref, probs = kept
    pre_copy = pltpu.make_async_copy(grad_pre_in, grad_pre, pre_sem.at[0])
    pre_copy.start()
    for part in range(QUART):
        start_all(up_copies(plan, gathered, held2, up_sems.at[part], part))
    start_all(first_copies(plan, pieces, devs, held, sems.at[1], pl.ds(OUT, 1)))
    copies = [
        pltpu.make_async_copy(source, target, kept_sems.at[index])
        for index, (source, target) in enumerate(zip(kept_in, kept))
    ]
    for index in (4, 3, 2, 5, 1, 0):
        copies[index].start()
    start_all(first_copies(plan, pieces, devs, held, sems.at[0], pl.ds(0, OUT)))
    length = plan.length
    arrived = jnp.concatenate([some_ref[...], other_ref[...]], 0)
    branch = jnp.where(flag[0] == 0, arrived, cot_ref[...])
    out = Stage(plan, stage, stage_sems)
    small_ref[...] = small_in[...]
    pre_copy.wait()
    grad_hidden = None
    for part in range(QUART):
        wait_bytes(held2.at[part], up_sems.at[part])
        term = mm_nt(grad_pre[:, columns_of(plan, part)], block_of(plan, held2, part))
        grad_hidden = term if grad_hidden is None else grad_hidden + term
    copies[4].wait()
    xhat, rstd = normalised(middle_ref[...])
    small_ref[5:6, :] = column_sum(grad_hidden * xhat)
    small_ref[6:7, :] = column_sum(grad_hidden)
    grad_middle = branch.astype(F32) + norm_back(grad_hidden, xhat, rstd, vec[5:6, :])
    grad_middle_ref[...] = grad_middle
    attn_grad = grad_middle.astype(BF16)
    small_ref[4:5, :] = column_sum(attn_grad)
    wait_bytes(held.at[pl.ds(OUT, 1)], sems.at[1])
    grad_attended[...] = mm_nt(attn_grad, block_of(plan, held, OUT)).astype(BF16)
    copies[3].wait()
    out.put(mm_tn(attended[...], attn_grad), slot_copies(plan, devs, grads, OUT))
    copies[2].wait()
    copies[5].wait()
    attention_back(plan, probs, qkv, grad_attended, grad_rows)
    copies[1].wait()
    copies[0].wait()
    wait_bytes(held.at[pl.ds(0, OUT)], sems.at[0])
    grad_normed = None
    for part in range(OUT):
        rows = grad_rows[:, columns_of(plan, part)]
        term = mm_nt(rows, block_of(plan, held, part))
        grad_normed = term if grad_normed is None else grad_normed + term
        if part != 1:
            small_ref[2 + part // 2 : 3 + part // 2, :] = column_sum(rows)
        out.put(mm_tn(normed[...], rows), slot_copies(plan, devs, grads, part))
    xhat, rstd = normalised(xin_ref[...].astype(F32))
    small_ref[0:1, :] = column_sum(grad_normed * xhat)
    small_ref[1:2, :] = column_sum(grad_normed)
    for item in range(plan.items):
        small_ref[12 + item : 13 + item, :] = column_sum(
            grad_normed[item * length : (item + 1) * length]
        )
    dx_ref[...] = grad_middle_ref[...] + norm_back(grad_normed, xhat, rstd, vec[0:1, :])
    if plan.parts > 1:
        pack_sums(plan, lead, many, small_ref[...], stack, lines)
        packed[...] = lines[...].astype(BF16)
        start_all(
            [
                pltpu.make_async_copy(
                    packed.at[devs[slot]],
                    slot_target(plan, grads, slot).at[pl.ds(FIRST * plan.rows, EXTRA)],
                    out_sem.at[0],
                )
                for slot in range(plan.shards)
            ]
        )
        wait_bytes(packed, out_sem.at[0])
    out.drain()


def pack_kernel(qkv_ref, out_ref, up_ref, down_ref, *refs):
    rows, width = out_ref.shape
    vectors, (up_bias, table, first_ref, second_ref, small, wide) = refs[:8], refs[8:]
    for index, vector in enumerate(vectors):
        small[index : index + 1, :] = vector[...]
    for part in range(QUART):
        small[8 + part : 9 + part, :] = up_bias[:, part * rows : (part + 1) * rows]
    many = 12 + table.shape[0]
    small[12:many, :] = table[...]
    across = width // rows
    wide[...] = jnp.zeros_like(wide)
    for index in range(many):
        line, place = divmod(index, across)
        wide[line : line + 1, place * rows : (place + 1) * rows] = small[index : index + 1, :]
    for part in range(OUT):
        first_ref[part * rows : (part + 1) * rows, :] = qkv_ref[:, part * width : (part + 1) * width].astype(BF16)
    first_ref[OUT * rows : FIRST * rows, :] = out_ref[...].astype(BF16)
    first_ref[FIRST * rows :, :] = wide[...].astype(BF16)
    for part in range(QUART):
        second_ref[part] = up_ref[:, part * width : (part + 1) * width].astype(BF16)
        second_ref[QUART + part] = down_ref[part * rows : (part + 1) * rows, :].astype(BF16)


def vectors_kernel(plan, many, devs, lead, *refs):
    pieces, (out_ref, lines, spread, sem) = slot_pieces(plan, refs[:-4]), refs[-4:]
    rows, width = plan.rows, plan.width
    across = width // rows
    groups = pl.cdiv(many, across)
    start_all(
        [
            pltpu.make_async_copy(piece_rows(parts, FIRST * rows, EXTRA), lines.at[slot], sem.at[0])
            for slot, parts in enumerate(pieces)
        ]
    )
    wait_bytes(lines, sem.at[0])
    line = lax.broadcasted_iota(jnp.int32, (across, width), 0)
    lane = lax.broadcasted_iota(jnp.int32, (across, width), 1)
    chosen = (lane >= line * rows) & (lane < (line + 1) * rows)
    up_line = lax.broadcasted_iota(jnp.int32, (QUART, width), 0)
    up_lane = lax.broadcasted_iota(jnp.int32, (QUART, width), 1)
    ups = jnp.zeros((QUART, width), F32)
    for slot in range(plan.shards):
        values = lines[slot].astype(F32)
        for group in range(groups):
            at = (slot * groups + group) * across
            picked = jnp.where(chosen, jnp.broadcast_to(values[group : group + 1], chosen.shape), 0.0)
            spread[at : at + across, :] = picked.astype(BF16)
        first = QUART * rows * devs[slot]
        there = lax.rem(first, width)
        moved = jnp.broadcast_to(values[8 // across : 8 // across + 1], (8, width))
        moved = pltpu.roll(moved, lax.rem(there + width - 8 % across * rows, width), 1)[:QUART]
        here = (up_line == first // width) & (up_lane >= there) & (up_lane < there + QUART * rows)
        ups = jnp.where(here, moved, ups)
    source = lax.broadcasted_iota(jnp.int32, (width, rows), 0)
    target = lax.broadcasted_iota(jnp.int32, (width, rows), 1)
    fold = sum(jnp.where(source == target + place * rows, 1.0, 0.0) for place in range(across))
    narrow = mm(spread[...], fold.astype(BF16)).astype(BF16)
    entry = lax.broadcasted_iota(jnp.int32, (rows, width), 0)
    column = lax.broadcasted_iota(jnp.int32, (rows, width), 1)
    total = None
    for slot in range(plan.shards):
        at = slot * groups * across
        place = jnp.where(column == entry + devs[slot] * rows, 1.0, 0.0).astype(BF16)
        term = mm(narrow[at : at + groups * across], place)
        total = term if total is None else total + term
    out_ref[...] = jnp.zeros_like(out_ref)
    out_ref[:8, :] = total[:8]
    out_ref[8 : 8 + QUART, :] = ups
    entry = lax.broadcasted_iota(jnp.int32, total.shape, 0)
    for item in range(plan.items):
        picked = jnp.where(entry == 12 + lead[item], total, 0.0)
        out_ref[12 + item : 13 + item, :] = jnp.sum(picked, 0, keepdims=True)


def unpack_kernel(grads_ref, up_ref, down_ref):
    _, rows, width = grads_ref.shape
    for part in range(QUART):
        up_ref[:, part * width : (part + 1) * width] = grads_ref[part].astype(F32)
        down_ref[part * rows : (part + 1) * rows, :] = grads_ref[QUART + part].astype(F32)


def add_kernel(work, *refs):
    outs, at = refs[len(refs) - len(work) :], 0
    for (low, high, first), out in zip(work, outs):
        mine, other = refs[at], refs[at + 1]
        at += 2
        cuts, came = [low, high], None
        if first is not None:
            came = refs[at]
            at += 1
            cuts = sorted({low, first, first + came.shape[0], high})
        for start, end in zip(cuts, cuts[1:]):
            value = mine[0, start:end, :].astype(F32) + other[0, start:end, :].astype(F32)
            if came is not None and first <= start < first + came.shape[0]:
                value = value + came[start - first : end - first, :].astype(F32)
            out[start - low : end - low, :] = value.astype(BF16)


def total_kernel(many, mine, other, ahead, behind, qkv, out, *refs):
    width = mine.shape[2]
    rows = out.shape[0]

    def rows_of(low, count):
        here = slice(low, low + count)
        value = mine[0, here, :].astype(F32) + other[0, here, :].astype(F32)
        return value + (ahead[here, :].astype(F32) + behind[here, :].astype(F32))

    for part in range(OUT):
        qkv[:, part * width : (part + 1) * width] = rows_of(part * rows, rows)
    out[...] = rows_of(OUT * rows, rows)
    vectors, (up_bias, table, small) = refs[:8], refs[8:]
    lines = rows_of(FIRST * rows, EXTRA)
    for index in range(many):
        line, place = divmod(index, width // rows)
        small[index : index + 1, :] = lines[line : line + 1, place * rows : (place + 1) * rows]
    for index, vector in enumerate(vectors):
        vector[...] = small[index : index + 1, :]
    for part in range(QUART):
        up_bias[:, part * rows : (part + 1) * rows] = small[8 + part : 9 + part, :]
    table[...] = small[12:many, :]


SMEM = pl.BlockSpec(memory_space=pltpu.SMEM)
VMEM = pl.BlockSpec(memory_space=pltpu.VMEM)
HBM = pl.BlockSpec(memory_space=pltpu.HBM)
ANY = pl.BlockSpec(memory_space=pl.ANY)


def kept_shapes(plan):
    tokens, width = plan.tokens, plan.width
    return [
        ((tokens, width), BF16),
        ((tokens, 3 * width), BF16),
        ((tokens, width), BF16),
        ((tokens, width), F32),
        ((tokens, width), BF16),
        ((plan.items * plan.pairs, 2 * plan.length, plan.length), F32),
        ((tokens, 4 * width), BF16),
        ((tokens, 4 * width), F32),
    ]


def held_blocks(plan, blocks):
    return pltpu.VMEM((blocks, plan.shards, plan.rows, plan.width), BF16)


def call(kernel, outs, in_specs, out_specs, scratch, name, work, limit, args):
    args = [
        pltpu.with_memory_space_constraint(arg, pltpu.HBM) if spec is HBM else arg
        for arg, spec in zip(args, in_specs)
    ]
    return pl.pallas_call(
        kernel,
        out_shape=outs,
        in_specs=in_specs,
        out_specs=out_specs,
        scratch_shapes=scratch,
        compiler_params=pltpu.CompilerParams(vmem_limit_bytes=limit * 1024 * 1024),
        cost_estimate=pl.CostEstimate(flops=2 * work[0], bytes_accessed=work[1], transcendentals=0),
        name=name,
    )(*args)


def of(shape):
    return jax.ShapeDtypeStruct(*shape)


def inside(shape):
    return pltpu.VMEM(*shape)


def run_attend(plan, lengths, flag, devs, x, vec, pieces):
    kept = kept_shapes(plan)
    block = plan.width * plan.width
    return call(
        functools.partial(attend_kernel, plan),
        [of(kept[3]), of(kept[4])],
        [SMEM, SMEM, SMEM, VMEM, VMEM] + [HBM] * len(pieces),
        [VMEM, VMEM],
        [held_blocks(plan, FIRST)] + [inside(shape) for shape in kept[:3]] + [pltpu.SemaphoreType.DMA((2,))],
        "attend",
        (FIRST * block * plan.tokens, FIRST * block * 2),
        14,
        (lengths, flag, devs, x, vec, *pieces),
    )


def run_vectors(plan, many, devs, lead, pieces):
    groups = pl.cdiv(many, plan.width // plan.rows) * (plan.width // plan.rows)
    return call(
        functools.partial(vectors_kernel, plan, many),
        jax.ShapeDtypeStruct((16, plan.width), F32),
        [SMEM, SMEM] + [HBM] * len(pieces),
        VMEM,
        [
            pltpu.VMEM((plan.shards, EXTRA, plan.width), BF16),
            pltpu.VMEM((plan.shards * groups, plan.width), BF16),
            pltpu.SemaphoreType.DMA((1,)),
        ],
        "vectors",
        (plan.width * plan.width * plan.rows, plan.width * plan.width * 4),
        12,
        (devs, lead, *pieces),
    )


def run_mlp(plan, flag, middle, hidden, vec, gathered):
    block = plan.width * plan.width
    return call(
        functools.partial(mlp_kernel, plan),
        jax.ShapeDtypeStruct(hidden.shape, BF16),
        [SMEM, VMEM, VMEM, VMEM, HBM],
        VMEM,
        [held_blocks(plan, SECOND), pltpu.SemaphoreType.DMA((QUART,)), pltpu.SemaphoreType.DMA((QUART,))],
        "mlp",
        (SECOND * block * plan.tokens, SECOND * block * 2),
        16,
        (flag, middle, hidden, vec, gathered),
    )


def run_load(plan, devs, flag, after, cot, firsts, gathered):
    block = plan.width * plan.width
    return call(
        functools.partial(load_kernel, plan),
        [held_blocks(plan, FIRST), held_blocks(plan, SECOND), inside(kept_shapes(plan)[7])]
        + [pltpu.VMEM((FIRST + QUART, plan.width, plan.width), BF16)],
        [SMEM, SMEM, ANY, VMEM] + [HBM] * (1 + len(firsts)),
        [VMEM] * 4,
        [pltpu.SemaphoreType.DMA((2,)), pltpu.SemaphoreType.DMA((QUART,))],
        "load",
        (QUART * block * plan.tokens, (FIRST + SECOND) * block * 4),
        4,
        (devs, flag, after, cot, gathered, *firsts),
    )


def run_chain(plan, lengths, flag, x, recv, cot, vec, held1, held2, grad_act, turned):
    shapes = kept_shapes(plan)
    block = plan.width * plan.width
    rest = [shapes[index] for index in (0, 0, 1, 2, 3, 5)]
    some = ((plan.items // 2 * plan.length, plan.width), BF16)
    results = call(
        functools.partial(chain_kernel, plan),
        [of(some)]
        + [inside(shapes[index]) for index in (4, 6, 7, 0, 1, 5, 3, 0, 3)]
        + [pltpu.HBM(*shape) for shape in rest],
        [SMEM] * 2 + [VMEM] * 8,
        [VMEM] * 10 + [HBM] * len(rest),
        [inside(shapes[index]) for index in (0, 2, 1)]
        + [pltpu.SemaphoreType.DMA((len(rest),))],
        "chain",
        (20 * block * plan.tokens, 12 * block),
        12,
        (lengths, flag, x, recv, cot, vec, held1, held2, grad_act, turned),
    )
    return results[0], results[1:4], results[4:9], results[9], results[10:]


def run_output(plan, flag, act, middle, vec, held2):
    block = plan.width * plan.width
    return call(
        functools.partial(output_kernel, plan),
        of(kept_shapes(plan)[0]),
        [SMEM] + [VMEM] * 4,
        VMEM,
        [],
        "output",
        (QUART * block * plan.tokens, QUART * block),
        4,
        (flag, act, middle, vec, held2),
    )


def run_chain_end(plan, flag, vec, turned, end):
    shapes = kept_shapes(plan)
    block = plan.width * plan.width
    left = plan.items - plan.items // 2
    return call(
        functools.partial(chain_end_kernel, plan),
        of(((left * plan.length, plan.width), BF16)),
        [SMEM] + [VMEM] * 7,
        VMEM,
        [inside(shapes[1])],
        "chain_end",
        (2 * block * plan.tokens, 3 * block),
        6,
        (flag, vec, turned, *end),
    )


def grad_shapes(plan):
    if plan.parts == 1:
        return [pltpu.HBM((1, FIRST * plan.rows, plan.width), BF16)]
    rows = FIRST * plan.rows + EXTRA
    return [
        pltpu.HBM((count, rows, plan.width), BF16)
        for count in (plan.shards // 2, plan.shards // 2, 1)
    ]


def stage_scratch(plan, slots):
    return [
        pltpu.VMEM((slots, plan.shards, plan.rows, plan.width), BF16),
        pltpu.SemaphoreType.DMA((slots,)),
    ]


def run_mlp_back(plan, flag, beside, arriving, cot, held2, hidden, act, slope):
    shapes = kept_shapes(plan)
    block = plan.width * plan.width
    return call(
        functools.partial(mlp_back_kernel, plan),
        [
            pltpu.HBM(*shapes[6]),
            jax.ShapeDtypeStruct((16, plan.width), F32),
            pltpu.HBM((plan.shards, SECOND, plan.rows, plan.width), BF16),
        ],
        [SMEM, HBM] + [VMEM] * 7,
        [HBM, VMEM, HBM],
        [inside(shapes[6])] + stage_scratch(plan, SECOND) + [pltpu.SemaphoreType.DMA((1,))],
        "mlp_back",
        (2 * SECOND * block * plan.tokens, SECOND * block * 2),
        16,
        (flag, beside, *arriving, cot, held2, hidden, act, slope),
    )


def run_rest(plan, many, flag, devs, lead, arriving, cot, small, vec, gathered, grad_pre, kept, pieces):
    shapes = kept_shapes(plan)
    block = plan.width * plan.width
    across = plan.width // plan.rows
    high = pl.cdiv(many, across) * across
    lines = (plan.shards, EXTRA, plan.width)
    rest = [shapes[index] for index in (0, 0, 1, 2, 3, 5)]
    input_grad, small, *grads = call(
        functools.partial(rest_kernel, plan, many),
        [of(shapes[3]), jax.ShapeDtypeStruct((16, plan.width), F32)] + grad_shapes(plan),
        [SMEM] * 3 + [VMEM] * 5 + [HBM] * (2 + len(rest) + len(pieces)),
        [VMEM] * 2 + [HBM] * plan.parts,
        [inside(shape) for shape in rest]
        + [held_blocks(plan, QUART), inside(shapes[6])]
        + [pltpu.SemaphoreType.DMA((QUART,)), pltpu.SemaphoreType.DMA((1,))]
        + [held_blocks(plan, FIRST)]
        + [inside(shapes[index]) for index in (3, 0, 1)]
        + [pltpu.SemaphoreType.DMA((2,)), pltpu.SemaphoreType.DMA((len(rest),))]
        + stage_scratch(plan, FIRST)
        + [pltpu.SemaphoreType.DMA((1,)), pltpu.VMEM((plan.shards * high, plan.rows), BF16)]
        + [pltpu.VMEM(lines, F32), pltpu.VMEM(lines, BF16)],
        "rest",
        (3 * FIRST * block * plan.tokens, 3 * FIRST * block * 2),
        34,
        (flag, devs, lead, *arriving, cot, small, vec, gathered, grad_pre, *kept, *pieces),
    )
    return input_grad, small, grads


def run_add(mine, other, work):
    _, rows, width = mine.shape
    mine = pltpu.with_memory_space_constraint(mine, pltpu.HBM)
    specs, args, plans, outs = [], [], [], []
    for way, (slot, low, high, came) in enumerate(work):
        there = slot if other.shape[0] > 1 else 0
        specs += [
            pl.BlockSpec((1, rows, width), lambda index, slot=slot: (slot, 0, 0))
            for slot in (slot, there)
        ]
        args += [mine, other]
        first = None
        if came is not None:
            specs.append(pl.BlockSpec(came.shape, lambda index: (0, 0)))
            args.append(came)
            first = rows - came.shape[0] if way else 0
        plans.append((low, high, first))
        outs.append((high - low, width))
    return pl.pallas_call(
        functools.partial(add_kernel, plans),
        out_shape=[jax.ShapeDtypeStruct(shape, BF16) for shape in outs],
        grid=(1,),
        in_specs=specs,
        out_specs=[pl.BlockSpec(shape, lambda index: (0, 0)) for shape in outs],
        compiler_params=pltpu.CompilerParams(vmem_limit_bytes=14 * 1024 * 1024),
        name="add",
    )(*args)


def run_total(one, many, shapes):
    args = [pltpu.with_memory_space_constraint(one.mine, pltpu.HBM), one.other]
    _, rows, width = one.mine.shape
    first = pl.BlockSpec((1, rows, width), lambda index: (0, 0, 0))
    whole = pl.BlockSpec((rows, width), lambda index: (0, 0))
    return pl.pallas_call(
        functools.partial(total_kernel, many),
        out_shape=[jax.ShapeDtypeStruct(shape, F32) for shape in shapes],
        grid=(1,),
        in_specs=[first, first, whole, whole],
        out_specs=[pl.BlockSpec(shape, lambda index: (0, 0)) for shape in shapes],
        scratch_shapes=[pltpu.VMEM((many, shapes[2][1]), F32)],
        compiler_params=pltpu.CompilerParams(vmem_limit_bytes=14 * 1024 * 1024),
        name="total",
    )(*args, *one.carried)


def after(value, *others):
    return lax.optimization_barrier((value, *others))[0]


def shifted(value, axis, steps):
    count = lax.axis_size(axis)
    first, last = (max(0, -steps), min(count, count - steps))
    return lax.ppermute(value, axis, [(source, source + steps) for source in range(first, last)])


class Ring:
    def __init__(self, count):
        self.count, self.chips = count, count // 2
        self.walk = list(range(0, self.chips, 2)) + list(range(self.chips - 1, 0, -2))
        self.order = [2 * chip + core for chip in self.walk for core in range(2)]
        after = self.walk[1:] + self.walk[:1]
        self.onward = [
            (2 * here + core, 2 * there + core)
            for here, there in zip(self.walk, after)
            for core in range(2)
        ]
        self.back = [(there, here) for here, there in self.onward]
        self.sibling = [(index, index ^ 1) for index in range(count)]

    def slots(self):
        index = lax.axis_index("dp")
        chip, core = index // 2, index % 2
        place_of = lambda chip: jnp.where(chip % 2 == 0, chip // 2, self.chips - 1 - chip // 2)
        steps = jnp.arange(self.chips, dtype=jnp.int32)
        ahead = (place_of(chip) + steps) % self.chips
        chips = jnp.where(ahead < (self.chips + 1) // 2, 2 * ahead, 2 * (self.chips - 1 - ahead) + 1)
        devs = jnp.concatenate([2 * chips + core, 2 * chips + 1 - core]).astype(jnp.int32)
        return devs

    def step(self, ahead, behind):
        return lax.ppermute(ahead, "dp", self.onward), lax.ppermute(behind, "dp", self.back)

    def gather(self, shard, low):
        half = self.chips // 2
        own = [[shard]] + [None] * (self.chips - 1)
        ahead = behind = shard
        for step in range(1, half):
            ahead, behind = self.step(ahead, behind)
            own[self.chips - step], own[step] = [ahead], [behind]
            ahead, behind = lax.optimization_barrier((ahead, behind))
        own[half] = list(self.step(ahead[:low], behind[low:]))
        return [piece for pieces in own for piece in pieces]

    def siblings(self, pieces):
        return [lax.ppermute(piece, "dp", self.sibling) for piece in pieces]


class RingSum:
    def __init__(self, ring, mine, other, opposite, low):
        self.ring, self.mine, self.low = ring, mine, low
        self.other, self.opposite = other, opposite
        self.time = ring.chips // 2
        self.carried = [None, None]

    def add(self):
        rows = self.mine.shape[1]
        other = self.other
        if self.carried[0] is None:
            other = self.opposite
            work = [(self.time, 0, self.low, None), (self.time, self.low, rows, None)]
        else:
            work = [
                (self.time, 0, rows, self.carried[0]),
                (self.ring.chips - self.time, 0, rows, self.carried[1]),
            ]
        self.carried = run_add(self.mine, other, work)

    def send(self):
        self.carried = self.ring.step(*self.carried)
        self.time -= 1


def body(
    block_input, cotangent, lengths, leads,
    norm_gain1, norm_bias1, lead_table, qkv_weight, query_bias, value_bias, out_weight, out_bias,
    norm_gain2, norm_bias2, up_weight, up_bias, down_weight, down_bias,
):
    count = lax.axis_size("dp")
    micro, local, length, width = block_input.shape
    items = micro * local
    rows = width // count
    leads_count = lead_table.shape[2]
    flag = lax.axis_index("section").astype(jnp.int32).reshape(1)
    flat = lambda value: value.reshape(items * length, width)
    x, cot = flat(block_input), flat(cotangent)
    lens, lead = lengths.reshape(items), leads.reshape(items)

    vectors = (
        norm_gain1, norm_bias1, query_bias, value_bias, out_bias, norm_gain2, norm_bias2, down_bias
    )
    many = 12 + leads_count
    aligned = rows % 16 == 0 and count % 4 == 0 and pl.cdiv(many, width // rows) <= EXTRA
    if aligned:
        ring = Ring(count)
        first, second = pl.pallas_call(
            pack_kernel,
            out_shape=[
                jax.ShapeDtypeStruct((FIRST * rows + EXTRA, width), BF16),
                jax.ShapeDtypeStruct((SECOND, rows, width), BF16),
            ],
            scratch_shapes=[pltpu.VMEM((many, rows), F32), pltpu.VMEM((EXTRA, width), F32)],
            name="pack",
        )(qkv_weight[0], out_weight[0], up_weight[0], down_weight[0], *vectors, up_bias, lead_table[0].T)
        gathered = lax.all_gather(second, "dp", axis=0, tiled=True, axis_index_groups=[ring.order])
        gathered = gathered.reshape(count, SECOND, rows, width)
        firsts = ring.gather(first, LOW * rows)
        firsts = firsts + ring.siblings(firsts)
        devs = ring.slots()
        plan = Plan(ring.order, rows, items, length, width)
        vec = run_vectors(plan, many, devs, lead, firsts)
    else:
        wide_blocks = lambda value: value[0].reshape(rows, -1, width).transpose(1, 0, 2)
        packed = jnp.concatenate(
            [wide_blocks(qkv_weight), out_weight, wide_blocks(up_weight), down_weight.reshape(QUART, rows, width)], 0
        )
        everything = lax.all_gather(packed.astype(BF16), "dp", axis=0)
        across_blocks = lambda value: value.transpose(1, 0, 2, 3).reshape(-1, width, width)
        firsts = [across_blocks(everything[:, :FIRST])]
        gathered = jnp.concatenate(
            [
                across_blocks(everything[:, FIRST : FIRST + QUART]),
                everything[:, FIRST + QUART :].reshape(QUART, width, width),
            ],
            0,
        )[None]
        devs = jnp.zeros((1,), jnp.int32)
        plan = Plan([0], width, items, length, width)
        small = jnp.concatenate([*vectors, up_bias.reshape(4, rows), lead_table[0].T], 0).astype(BF16)
        wide = lax.all_gather(small, "dp", axis=1, tiled=True).astype(F32)
        vec = jnp.concatenate(
            [wide[:8], wide[8:12].reshape(4, count, rows).transpose(1, 0, 2).reshape(4, width)]
            + [lax.dynamic_slice_in_dim(wide, 12 + lead[item], 1, 0) for item in range(items)]
            + [jnp.zeros((4 - items, width), F32)],
            0,
        )

    middle, hidden = run_attend(plan, lens, flag, devs, x, vec, firsts)
    first_out = run_mlp(plan, flag, middle, hidden, vec, gathered)
    recv = shifted(first_out, "section", 1)
    held1, held2, grad_act, turned = run_load(plan, devs, flag, first_out, cot, firsts, gathered)
    some_grad, (hidden, act, slope), end, middle, kept = run_chain(
        plan, lens, flag, x, recv, cot, vec, held1, held2, grad_act, turned
    )
    other_grad = run_chain_end(plan, flag, vec, turned, end)
    arriving = [shifted(grad, "section", -1) for grad in (some_grad, other_grad)]
    output = run_output(plan, flag, act, middle, vec, held2)
    grad_pre, sums, grads2 = run_mlp_back(
        plan, flag, output, arriving, cot, held2, hidden, act, slope
    )
    input_grad, sums, grads1 = run_rest(
        plan, many, flag, devs, lead, arriving, cot, sums, vec, gathered, grad_pre, kept, firsts
    )
    if aligned:
        (opposite,) = ring.siblings(grads1[2:])
        (other,) = ring.siblings([after(grads1[1], opposite)])
        first_sum = RingSum(ring, grads1[0], other, opposite, LOW * rows)
        while first_sum.time:
            first_sum.add()
            first_sum.send()
        grads2 = lax.psum_scatter(
            grads2.reshape(count * SECOND, rows, width),
            "dp", scatter_dimension=0, tiled=True, axis_index_groups=[ring.order],
        )
        grad_up, grad_down = pl.pallas_call(
            unpack_kernel,
            out_shape=[
                jax.ShapeDtypeStruct((rows, QUART * width), F32),
                jax.ShapeDtypeStruct((QUART * rows, width), F32),
            ],
            name="unpack",
        )(grads2)
        grad_qkv, grad_out, *small_grads = run_total(
            first_sum, many,
            [(rows, OUT * width), (rows, width)] + [(1, rows)] * 8 + [(1, QUART * rows), (leads_count, rows)],
        )
    else:
        split = lambda value: value[0].reshape(-1, count, rows, width).transpose(1, 0, 2, 3)
        grads = jnp.concatenate(
            [
                split(grads1[0]),
                split(grads2[0, :QUART].reshape(1, QUART * width, width)),
                grads2[0, QUART:].reshape(count, QUART, rows, width),
            ],
            1,
        )
        grads = lax.psum_scatter(grads, "dp", scatter_dimension=0, tiled=False).astype(F32)
        across = lambda value: value.transpose(1, 0, 2).reshape(rows, -1)
        grad_qkv, grad_out = across(grads[:OUT]), grads[OUT]
        grad_up = across(grads[FIRST : FIRST + QUART])
        grad_down = grads[FIRST + QUART :].reshape(QUART * rows, width)
        hot = (jnp.arange(leads_count)[:, None] == lead[None, :]).astype(F32)
        table = sum(hot[:, item : item + 1] * sums[12 + item : 13 + item] for item in range(items))
        up_sums = sums[8:12].reshape(count, 4, rows).transpose(1, 0, 2).reshape(4, width)
        spread = lax.psum_scatter(
            jnp.concatenate([sums[:8], up_sums, table], 0), "dp", scatter_dimension=1, tiled=True
        )
        small_grads = [spread[index : index + 1] for index in range(8)]
        small_grads += [spread[8:12].reshape(1, 4 * rows), spread[12:]]
    vector = small_grads
    shape = (1, micro, local, length, width)
    return (
        output.reshape(shape),
        input_grad.reshape(shape),
        vector[0],
        vector[1],
        vector[9].T[None],
        grad_qkv[None],
        vector[2],
        vector[3],
        grad_out[None],
        vector[4],
        vector[5],
        vector[6],
        grad_up[None],
        vector[8],
        grad_down[None],
        vector[7],
    )


def solution(mesh):
    weights = (
        P("section", "dp"),
        P("section", "dp"),
        P("section", "dp", None),
        P("section", "dp", None),
        P("section", "dp"),
        P("section", "dp"),
        P("section", "dp", None),
        P("section", "dp"),
        P("section", "dp"),
        P("section", "dp"),
        P("section", "dp", None),
        P("section", "dp"),
        P("section", "dp", None),
        P("section", "dp"),
    )
    rows = P(None, "dp", None, None)
    layers = P("section", None, "dp", None, None)
    return jax.shard_map(
        body,
        mesh=mesh,
        in_specs=(rows, rows, P(None, "dp"), P(None, "dp")) + weights,
        out_specs=(layers, layers) + weights,
        check_vma=False,
    )
```

```python
import functools

import jax
import jax.numpy as jnp
from jax import lax
from jax.experimental import pallas as pl
from jax.experimental.pallas import tpu as pltpu
from jax.sharding import PartitionSpec as P

HEAD = 64
PAIR = 2 * HEAD
EPS = 1e-06
SCALE_FACTOR = 0.125
GELU_A = 0.7978845608028654
GELU_B = 0.044715
F32 = jnp.float32
BF16 = jnp.bfloat16
OUT = 3
FIRST = 4
SECOND = 8
QUART = 4
EXTRA = 16
LOW = 2


def mm(left, right):
    return jnp.dot(left, right, preferred_element_type=F32)


def mm_nt(left, right):
    return lax.dot_general(left, right, (((1,), (1,)), ((), ())), preferred_element_type=F32)


def mm_tn(left, right):
    return lax.dot_general(left, right, (((0,), (0,)), ((), ())), preferred_element_type=F32)


def normalised(values):
    mean = jnp.mean(values, -1, keepdims=True)
    centred = values - mean
    variance = jnp.mean(centred * centred, -1, keepdims=True)
    rstd = lax.rsqrt(variance + EPS)
    return centred * rstd, rstd


def norm_back(grad, xhat, rstd, gain):
    scaled = grad * gain
    first = jnp.mean(scaled, -1, keepdims=True)
    second = jnp.mean(scaled * xhat, -1, keepdims=True)
    return rstd * (scaled - first - xhat * second)


def gelu_both(values):
    square = values * values
    slope = GELU_A * (1.0 + 3.0 * GELU_B * square)
    bend = jnp.tanh(GELU_A * values * (1.0 + GELU_B * square))
    half = 0.5 * (1.0 + bend)
    return values * half, half + 0.5 * values * (1.0 - bend * bend) * slope


def split_pair(rows):
    lane = lax.broadcasted_iota(jnp.int32, rows.shape, 1)
    zero = jnp.zeros_like(rows)
    return jnp.concatenate(
        [jnp.where(lane < HEAD, rows, zero), jnp.where(lane < HEAD, zero, rows)], 0
    )


def join_pair(stacked):
    count = stacked.shape[0] // 2
    lane = lax.broadcasted_iota(jnp.int32, (count, PAIR), 1)
    return jnp.where(lane < HEAD, stacked[:count], stacked[count:])


def runs_of(order):
    if all(order[at + 1] == order[at] + 1 for at in range(0, len(order) - 1, 2)) and len(order) > 1:
        return [(at, order[at], 2) for at in range(0, len(order), 2)]
    return [(at, device, 1) for at, device in enumerate(order)]


class Plan:
    def __init__(self, order, rows, items, length, width):
        self.order, self.shards, self.rows = order, len(order), rows
        self.items, self.length, self.width = items, length, width
        self.tokens = items * length
        self.low = LOW * rows
        self.pairs = width // PAIR
        whole = self.shards % QUART == 0
        self.runs = [(0, QUART)] if whole else [(block, 1) for block in range(QUART)]
        self.parts = 3 if self.shards > 1 else 1


def slot_pieces(plan, refs):
    if plan.shards == 1:
        return [[(0, refs[0])]]
    refs, slots, half = list(refs), [], plan.shards // 4
    for slot in range(plan.shards):
        parts = [(0, refs.pop(0))]
        if slot % (plan.shards // 2) == half:
            parts.append((plan.low, refs.pop(0)))
        slots.append(parts)
    return slots


def piece_rows(parts, row, count):
    start, ref = [part for part in parts if part[0] <= row][-1]
    return ref.at[pl.ds(row - start, count)]


def first_copies(plan, refs, devs, held, sem, blocks):
    if plan.shards == 1:
        return block_copies(refs, devs, held, sem, blocks)
    return [
        pltpu.make_async_copy(
            piece_rows(parts, block * plan.rows, plan.rows), held.at[block, devs[slot]], sem
        )
        for slot, parts in enumerate(slot_pieces(plan, refs))
        for block in range(blocks.start, blocks.start + blocks.size)
    ]


def block_copies(pieces, devs, held, sem, blocks, at=0):
    return [
        pltpu.make_async_copy(
            piece.at[blocks], held.at[pl.ds(at + blocks.start, blocks.size), devs[slot]], sem
        )
        for slot, piece in enumerate(pieces)
    ]


def up_copies(plan, gathered, held, sem, part):
    return [
        pltpu.make_async_copy(
            gathered.at[pl.ds(place, count), part], held.at[part, pl.ds(device, count)], sem
        )
        for place, device, count in runs_of(plan.order)
    ]


def down_copies(plan, pieces, devs, held, sems):
    copies = []
    for slot, piece in enumerate(pieces):
        for first, count in plan.runs:
            block, row = divmod(QUART * devs[slot] + first, plan.shards)
            copy = pltpu.make_async_copy(
                piece.at[pl.ds(first, count)],
                held.at[QUART + block, pl.ds(row, count)],
                sems.at[block],
            )
            copies.append((block, copy))
    return copies


def second_pieces(plan, gathered):
    ups = [gathered.at[place, pl.ds(0, QUART)] for place in range(plan.shards)]
    downs = [gathered.at[place, pl.ds(QUART, QUART)] for place in range(plan.shards)]
    return ups, downs


def start_all(copies):
    for copy in copies:
        copy.start()


def wait_bytes(part, sem):
    pltpu.make_async_copy(part, part, sem).wait()


def block_of(plan, held, index):
    return held[index].reshape(plan.width, plan.width)


def columns_of(plan, index):
    return slice(index * plan.width, (index + 1) * plan.width)


def attention_forward(plan, lengths, qkv_ref, attended_ref, probs_ref):
    width, length = plan.width, plan.length
    key_index = lax.broadcasted_iota(jnp.int32, (2 * length, length), 1)
    for item in range(plan.items):
        rows = slice(item * length, (item + 1) * length)
        valid = key_index < lengths[item]
        for pair in range(plan.pairs):
            at = pair * PAIR
            query = split_pair(qkv_ref[rows, at : at + PAIR])
            key = qkv_ref[rows, width + at : width + at + PAIR]
            value = qkv_ref[rows, 2 * width + at : 2 * width + at + PAIR]
            logits = jnp.where(valid, mm_nt(query, key) * SCALE_FACTOR, -1000000000.0)
            expo = jnp.exp(logits - jnp.max(logits, -1, keepdims=True))
            probs = expo / jnp.sum(expo, -1, keepdims=True)
            if probs_ref is not None:
                probs_ref[item * plan.pairs + pair] = probs
            attended_ref[rows, at : at + PAIR] = join_pair(mm(probs.astype(BF16), value)).astype(
                BF16
            )


def first_half(plan, inputs, lengths, vec, held, wait, normed_ref, qkv_ref, attended_ref, probs_ref, hidden_ref):
    width, length = plan.width, plan.length
    values = inputs.astype(F32)
    xhat, _ = normalised(values)
    base = xhat * vec[0:1, :] + vec[1:2, :]
    for item in range(plan.items):
        rows = slice(item * length, (item + 1) * length)
        normed_ref[rows, :] = (base[rows] + vec[12 + item : 13 + item, :]).astype(BF16)
    wait(0)
    for part, bias in enumerate((2, None, 3)):
        joined = mm(normed_ref[...], block_of(plan, held, part))
        if bias is not None:
            joined = joined + vec[bias : bias + 1, :]
        qkv_ref[:, columns_of(plan, part)] = joined.astype(BF16)
    attention_forward(plan, lengths, qkv_ref, attended_ref, probs_ref)
    wait(1)
    middle = values + (mm(attended_ref[...], block_of(plan, held, OUT)) + vec[4:5, :])
    xhat, _ = normalised(middle)
    hidden_ref[...] = (xhat * vec[5:6, :] + vec[6:7, :]).astype(BF16)
    return middle


def activate(plan, part, hidden_ref, vec, held):
    pre_act = mm(hidden_ref[...], block_of(plan, held, part)) + vec[8 + part : 9 + part, :]
    act, slope = gelu_both(pre_act)
    return act.astype(BF16), slope


def second_half(plan, hidden_ref, vec, held, wait):
    total = None
    for part in range(QUART):
        wait(part)
        act, _ = activate(plan, part, hidden_ref, vec, held)
        wait(QUART + part)
        term = mm(act, block_of(plan, held, QUART + part))
        total = term if total is None else total + term
    return total + vec[7:8, :]


def attention_back(plan, probs_ref, qkv_ref, grad_attended_ref, rows_ref, items=None):
    width, length = plan.width, plan.length
    for item in range(plan.items) if items is None else items:
        rows = slice(item * length, (item + 1) * length)
        for pair in range(plan.pairs):
            at = pair * PAIR
            query = split_pair(qkv_ref[rows, at : at + PAIR])
            key = qkv_ref[rows, width + at : width + at + PAIR]
            value = qkv_ref[rows, 2 * width + at : 2 * width + at + PAIR]
            grad = split_pair(grad_attended_ref[rows, at : at + PAIR])
            probs = probs_ref[item * plan.pairs + pair]
            grad_probs = mm_nt(grad, value)
            centre = jnp.sum(grad_probs * probs, -1, keepdims=True)
            grad_logits = (probs * (grad_probs - centre)).astype(BF16)
            grad_query = join_pair(mm(grad_logits, key)) * SCALE_FACTOR
            grad_key = mm_tn(grad_logits, query) * SCALE_FACTOR
            grad_value = mm_tn(probs.astype(BF16), grad)
            rows_ref[rows, at : at + PAIR] = grad_query.astype(BF16)
            rows_ref[rows, width + at : width + at + PAIR] = grad_key.astype(BF16)
            rows_ref[rows, 2 * width + at : 2 * width + at + PAIR] = grad_value.astype(BF16)


def column_sum(values):
    return jnp.sum(values.astype(F32), 0, keepdims=True)


def attend_kernel(plan, lengths, flag, devs, x_ref, vec, *refs):
    pieces, (middle_ref, hidden_ref, held, normed, qkv, attended, sems) = refs[:-7], refs[-7:]
    start_all(first_copies(plan, pieces, devs, held, sems.at[0], pl.ds(0, OUT)))
    start_all(first_copies(plan, pieces, devs, held, sems.at[1], pl.ds(OUT, 1)))

    def wait(group):
        blocks = pl.ds(OUT, 1) if group else pl.ds(0, OUT)
        wait_bytes(held.at[blocks], sems.at[group])

    middle_ref[...] = first_half(
        plan, x_ref[...], lengths, vec, held, wait, normed, qkv, attended, None, hidden_ref
    )


def mlp_kernel(plan, flag, middle_ref, hidden_ref, vec, gathered, y_ref, held, sems, down_sems):
    @pl.when(flag[0] == 0)
    def _():
        _, downs = second_pieces(plan, gathered)
        down = down_copies(plan, downs, plan.order, held, down_sems)
        for part in range(QUART):
            start_all(up_copies(plan, gathered, held, sems.at[part], part))
            start_all([copy for block, copy in down if block == part])

        def wait(block):
            sem = sems.at[block] if block < QUART else down_sems.at[block - QUART]
            wait_bytes(held.at[block], sem)

        total = second_half(plan, hidden_ref, vec, held, wait)
        y_ref[...] = (middle_ref[...] + total).astype(BF16)


def load_kernel(plan, devs, flag, after, cot_ref, gathered, *refs):
    firsts, (held1, held2, grad_act, turned, sems, down_sems) = refs[:-6], refs[-6:]
    ups, downs = second_pieces(plan, gathered)
    start_all([copy for _, copy in down_copies(plan, downs, plan.order, held2, down_sems)])
    start_all(block_copies(ups, plan.order, held2, sems.at[1], pl.ds(0, QUART)))
    start_all(first_copies(plan, firsts, devs, held1, sems.at[0], pl.ds(0, FIRST)))
    for part in range(QUART):
        wait_bytes(held2.at[QUART + part], down_sems.at[part])
        grad_act[:, columns_of(plan, part)] = mm_nt(
            cot_ref[...], block_of(plan, held2, QUART + part)
        )
    wait_bytes(held2.at[pl.ds(0, QUART)], sems.at[1])
    wait_bytes(held1, sems.at[0])

    @pl.when(flag[0] == 1)
    def _():
        for block in range(FIRST):
            turned[block] = block_of(plan, held1, block).T
        for part in range(QUART):
            turned[FIRST + part] = block_of(plan, held2, part).T


def input_grad(plan, items, vec, turned, xin_ref, qkv, probs, grad_middle, grad_attended, grad_rows, dx_ref):
    attention_back(plan, probs, qkv, grad_attended, grad_rows, items)
    rows = slice(items.start * plan.length, items.stop * plan.length)
    grad_normed = None
    for part in range(OUT):
        term = mm(grad_rows[rows, columns_of(plan, part)], turned[part])
        grad_normed = term if grad_normed is None else grad_normed + term
    xhat, rstd = normalised(xin_ref[rows, :].astype(F32))
    dx_ref[...] = (grad_middle[rows, :] + norm_back(grad_normed, xhat, rstd, vec[0:1, :])).astype(BF16)


def chain_kernel(
    plan, lengths, flag, x_ref, recv_ref, cot_ref, vec, held1, held2, grad_act, turned,
    dx_ref, hidden, act, slope, xin_ref, qkv, probs, grad_middle, grad_attended, middle, *refs,
):
    outs, (normed, attended, grad_rows, sems) = refs[:6], refs[6:]
    kept = (xin_ref, normed, qkv, attended, middle, probs)
    copies = [
        pltpu.make_async_copy(source, target, sems.at[index])
        for index, (source, target) in enumerate(zip(kept, outs))
    ]
    xin_ref[...] = jnp.where(flag[0] == 0, x_ref[...], recv_ref[...])
    middle[...] = first_half(
        plan, xin_ref[...], lengths, vec, held1, lambda group: None, normed, qkv, attended, probs, hidden
    )
    start_all(copies)
    for part in range(QUART):
        columns = columns_of(plan, part)
        act[:, columns], slope[:, columns] = activate(plan, part, hidden, vec, held2)

    @pl.when(flag[0] == 1)
    def _():
        branch = cot_ref[...]
        grad_hidden = None
        for part in range(QUART):
            grad_pre = (slope[:, columns_of(plan, part)] * grad_act[:, columns_of(plan, part)]).astype(BF16)
            term = mm(grad_pre, turned[FIRST + part])
            grad_hidden = term if grad_hidden is None else grad_hidden + term
        xhat, rstd = normalised(middle[...])
        grad_middle[...] = branch.astype(F32) + norm_back(grad_hidden, xhat, rstd, vec[5:6, :])
        grad_attended[...] = mm(grad_middle[...].astype(BF16), turned[OUT]).astype(BF16)
        input_grad(
            plan, range(plan.items // 2), vec, turned, xin_ref, qkv, probs, grad_middle, grad_attended, grad_rows, dx_ref
        )

    for copy in copies:
        copy.wait()


def chain_end_kernel(plan, flag, vec, turned, xin_ref, qkv, probs, grad_middle, grad_attended, dx_ref, grad_rows):
    @pl.when(flag[0] == 1)
    def _():
        input_grad(
            plan, range(plan.items // 2, plan.items), vec, turned, xin_ref, qkv, probs, grad_middle, grad_attended,
            grad_rows, dx_ref,
        )


def output_kernel(plan, flag, act, middle_ref, vec, held2, y_ref):
    total = None
    for part in range(QUART):
        term = mm(act[:, columns_of(plan, part)], block_of(plan, held2, QUART + part))
        total = term if total is None else total + term
    y_ref[...] = (middle_ref[...] + (total + vec[7:8, :])).astype(BF16)


class Stage:
    def __init__(self, plan, stage, sems):
        self.plan, self.stage, self.sems, self.sent = plan, stage, sems, 0

    def put(self, value, copies_of):
        slots = self.stage.shape[0]
        slot = self.sent % slots
        if self.sent >= slots:
            wait_bytes(self.stage.at[slot], self.sems.at[slot])
        self.sent += 1
        plan = self.plan
        self.stage[slot] = value.astype(BF16).reshape(plan.shards, plan.rows, plan.width)
        start_all(copies_of(self.stage.at[slot], self.sems.at[slot]))

    def drain(self):
        for slot in range(min(self.stage.shape[0], self.sent)):
            wait_bytes(self.stage.at[slot], self.sems.at[slot])


def mlp_back_kernel(
    plan, flag, beside, some_ref, other_ref, cot_ref, held2, hidden, act, slope,
    grad_pre_ref, small_ref, grads, stage, stage_sems,
):
    arrived = jnp.concatenate([some_ref[...], other_ref[...]], 0)
    branch = jnp.where(flag[0] == 0, arrived, cot_ref[...])
    out = Stage(plan, stage, stage_sems)

    def copies_of_up(part):
        def copies(source, sem):
            return [
                pltpu.make_async_copy(
                    source.at[pl.ds(device, count)], grads.at[pl.ds(place, count), part], sem
                )
                for place, device, count in runs_of(plan.order)
            ]

        return copies

    def copies_of_down(part):
        def copies(source, sem):
            made = []
            for place, device in enumerate(plan.order):
                for first, count in plan.runs:
                    block, row = divmod(QUART * device + first, plan.shards)
                    if block == part:
                        made.append(
                            pltpu.make_async_copy(
                                source.at[pl.ds(row, count)],
                                grads.at[place, pl.ds(QUART + first, count)],
                                sem,
                            )
                        )
            return made

        return copies

    for part in range(QUART):
        columns = columns_of(plan, part)
        grad_act = mm_nt(branch, block_of(plan, held2, QUART + part))
        grad_pre = (slope[:, columns] * grad_act).astype(BF16)
        grad_pre_ref[:, columns] = grad_pre
        out.put(mm_tn(act[:, columns], branch), copies_of_down(part))
        out.put(mm_tn(hidden[...], grad_pre), copies_of_up(part))
    small_ref[...] = jnp.zeros_like(small_ref)
    small_ref[7:8, :] = column_sum(branch)
    for part in range(QUART):
        small_ref[8 + part : 9 + part, :] = column_sum(grad_pre_ref[:, columns_of(plan, part)])
    out.drain()


def slot_target(plan, grads, slot):
    if plan.parts == 1:
        return grads[0].at[0]
    half = plan.shards // 2
    if slot == half + half // 2:
        return grads[2].at[0]
    return grads[slot // half].at[slot % half]


def slot_copies(plan, devs, grads, block):
    def copies(source, sem):
        return [
            pltpu.make_async_copy(
                source.at[devs[slot]],
                slot_target(plan, grads, slot).at[pl.ds(block * plan.rows, plan.rows)],
                sem,
            )
            for slot in range(plan.shards)
        ]

    return copies


def pack_sums(plan, lead, many, sums, stack, lines):
    rows, width = plan.rows, plan.width
    across = width // rows
    groups = pl.cdiv(many, across)
    high = groups * across
    leads = many - 12
    entry = lax.broadcasted_iota(jnp.int32, (high - 12, width), 0)
    table = jnp.zeros((high - 12, width), F32)
    for item in range(plan.items):
        table = table + jnp.where(entry == lead[item], sums[12 + item : 13 + item], 0.0)
    top, ups = sums[:8], sums[8:12]
    for device in range(plan.shards):
        columns = slice(device * rows, (device + 1) * rows)
        line, place = divmod(QUART * device * rows, width)
        parts = [
            ups[line : line + 1, place + part * rows : place + (part + 1) * rows]
            for part in range(QUART)
        ]
        share = jnp.concatenate([top[:, columns], *parts, table[:, columns]], 0)
        stack[device * high : (device + 1) * high, :] = share.astype(BF16)
    entry = lax.broadcasted_iota(jnp.int32, (rows, width), 0)
    column = lax.broadcasted_iota(jnp.int32, (rows, width), 1)
    tile = jnp.where(lax.rem(column, rows) == entry, 1.0, 0.0).astype(BF16)
    line = lax.broadcasted_iota(jnp.int32, (high, width), 0)
    lane = lax.broadcasted_iota(jnp.int32, (high, width), 1)
    place = lax.rem(line, across) * rows
    chosen = (lane >= place) & (lane < place + rows)
    lines[...] = jnp.zeros_like(lines)
    for device in range(plan.shards):
        spread = mm(stack[device * high : (device + 1) * high, :], tile)
        spread = jnp.where(chosen, spread, 0.0).reshape(groups, across, width)
        lines[device, 0:groups, :] = jnp.sum(spread, 1)


def rest_kernel(
    plan, many, flag, devs, lead, some_ref, other_ref, cot_ref, small_in, vec, grad_pre, gathered, *refs,
):
    count = plan.shards + (2 if plan.parts > 1 else 0)
    kept_in, pieces, refs = refs[:6], refs[6 : 6 + count], refs[6 + count :]
    dx_ref, small_ref = refs[:2]
    grads, refs = refs[2 : 2 + plan.parts], refs[2 + plan.parts :]
    kept, (held2, up_sems), refs = refs[:6], refs[6:8], refs[8:]
    held, grad_middle_ref, grad_attended, grad_rows, sems, kept_sems, stage, stage_sems, out_sem, stack, lines, packed = refs
    xin_ref, normed, qkv, attended, middle_ref, probs = kept
    for part in range(QUART):
        start_all(up_copies(plan, gathered, held2, up_sems.at[part], part))
    start_all(first_copies(plan, pieces, devs, held, sems.at[1], pl.ds(OUT, 1)))
    copies = [
        pltpu.make_async_copy(source, target, kept_sems.at[index])
        for index, (source, target) in enumerate(zip(kept_in, kept))
    ]
    for index in (4, 3, 2, 5, 1, 0):
        copies[index].start()
    start_all(first_copies(plan, pieces, devs, held, sems.at[0], pl.ds(0, OUT)))
    length = plan.length
    arrived = jnp.concatenate([some_ref[...], other_ref[...]], 0)
    branch = jnp.where(flag[0] == 0, arrived, cot_ref[...])
    out = Stage(plan, stage, stage_sems)
    small_ref[...] = small_in[...]
    grad_hidden = None
    for part in range(QUART):
        wait_bytes(held2.at[part], up_sems.at[part])
        term = mm_nt(grad_pre[:, columns_of(plan, part)], block_of(plan, held2, part))
        grad_hidden = term if grad_hidden is None else grad_hidden + term
    copies[4].wait()
    xhat, rstd = normalised(middle_ref[...])
    small_ref[5:6, :] = column_sum(grad_hidden * xhat)
    small_ref[6:7, :] = column_sum(grad_hidden)
    grad_middle = branch.astype(F32) + norm_back(grad_hidden, xhat, rstd, vec[5:6, :])
    grad_middle_ref[...] = grad_middle
    attn_grad = grad_middle.astype(BF16)
    small_ref[4:5, :] = column_sum(attn_grad)
    wait_bytes(held.at[pl.ds(OUT, 1)], sems.at[1])
    grad_attended[...] = mm_nt(attn_grad, block_of(plan, held, OUT)).astype(BF16)
    copies[3].wait()
    out.put(mm_tn(attended[...], attn_grad), slot_copies(plan, devs, grads, OUT))
    copies[2].wait()
    copies[5].wait()
    attention_back(plan, probs, qkv, grad_attended, grad_rows)
    copies[1].wait()
    copies[0].wait()
    wait_bytes(held.at[pl.ds(0, OUT)], sems.at[0])
    grad_normed = None
    for part in range(OUT):
        rows = grad_rows[:, columns_of(plan, part)]
        term = mm_nt(rows, block_of(plan, held, part))
        grad_normed = term if grad_normed is None else grad_normed + term
        if part != 1:
            small_ref[2 + part // 2 : 3 + part // 2, :] = column_sum(rows)
        out.put(mm_tn(normed[...], rows), slot_copies(plan, devs, grads, part))
    xhat, rstd = normalised(xin_ref[...].astype(F32))
    small_ref[0:1, :] = column_sum(grad_normed * xhat)
    small_ref[1:2, :] = column_sum(grad_normed)
    for item in range(plan.items):
        small_ref[12 + item : 13 + item, :] = column_sum(
            grad_normed[item * length : (item + 1) * length]
        )
    dx_ref[...] = grad_middle_ref[...] + norm_back(grad_normed, xhat, rstd, vec[0:1, :])
    if plan.parts > 1:
        pack_sums(plan, lead, many, small_ref[...], stack, lines)
        packed[...] = lines[...].astype(BF16)
        start_all(
            [
                pltpu.make_async_copy(
                    packed.at[devs[slot]],
                    slot_target(plan, grads, slot).at[pl.ds(FIRST * plan.rows, EXTRA)],
                    out_sem.at[0],
                )
                for slot in range(plan.shards)
            ]
        )
        wait_bytes(packed, out_sem.at[0])
    out.drain()


def pack_kernel(qkv_ref, out_ref, up_ref, down_ref, *refs):
    rows, width = out_ref.shape
    vectors, (up_bias, table, first_ref, second_ref, small, wide) = refs[:8], refs[8:]
    for index, vector in enumerate(vectors):
        small[index : index + 1, :] = vector[...]
    for part in range(QUART):
        small[8 + part : 9 + part, :] = up_bias[:, part * rows : (part + 1) * rows]
    many = 12 + table.shape[0]
    small[12:many, :] = table[...]
    across = width // rows
    wide[...] = jnp.zeros_like(wide)
    for index in range(many):
        line, place = divmod(index, across)
        wide[line : line + 1, place * rows : (place + 1) * rows] = small[index : index + 1, :]
    for part in range(OUT):
        first_ref[part * rows : (part + 1) * rows, :] = qkv_ref[:, part * width : (part + 1) * width].astype(BF16)
    first_ref[OUT * rows : FIRST * rows, :] = out_ref[...].astype(BF16)
    first_ref[FIRST * rows :, :] = wide[...].astype(BF16)
    for part in range(QUART):
        second_ref[part] = up_ref[:, part * width : (part + 1) * width].astype(BF16)
        second_ref[QUART + part] = down_ref[part * rows : (part + 1) * rows, :].astype(BF16)


def vectors_kernel(plan, many, devs, lead, *refs):
    pieces, (out_ref, lines, spread, sem) = slot_pieces(plan, refs[:-4]), refs[-4:]
    rows, width = plan.rows, plan.width
    across = width // rows
    groups = pl.cdiv(many, across)
    start_all(
        [
            pltpu.make_async_copy(piece_rows(parts, FIRST * rows, EXTRA), lines.at[slot], sem.at[0])
            for slot, parts in enumerate(pieces)
        ]
    )
    wait_bytes(lines, sem.at[0])
    line = lax.broadcasted_iota(jnp.int32, (across, width), 0)
    lane = lax.broadcasted_iota(jnp.int32, (across, width), 1)
    chosen = (lane >= line * rows) & (lane < (line + 1) * rows)
    up_line = lax.broadcasted_iota(jnp.int32, (QUART, width), 0)
    up_lane = lax.broadcasted_iota(jnp.int32, (QUART, width), 1)
    ups = jnp.zeros((QUART, width), F32)
    for slot in range(plan.shards):
        values = lines[slot].astype(F32)
        for group in range(groups):
            at = (slot * groups + group) * across
            picked = jnp.where(chosen, jnp.broadcast_to(values[group : group + 1], chosen.shape), 0.0)
            spread[at : at + across, :] = picked.astype(BF16)
        first = QUART * rows * devs[slot]
        there = lax.rem(first, width)
        moved = jnp.broadcast_to(values[8 // across : 8 // across + 1], (8, width))
        moved = pltpu.roll(moved, lax.rem(there + width - 8 % across * rows, width), 1)[:QUART]
        here = (up_line == first // width) & (up_lane >= there) & (up_lane < there + QUART * rows)
        ups = jnp.where(here, moved, ups)
    source = lax.broadcasted_iota(jnp.int32, (width, rows), 0)
    target = lax.broadcasted_iota(jnp.int32, (width, rows), 1)
    fold = sum(jnp.where(source == target + place * rows, 1.0, 0.0) for place in range(across))
    narrow = mm(spread[...], fold.astype(BF16)).astype(BF16)
    entry = lax.broadcasted_iota(jnp.int32, (rows, width), 0)
    column = lax.broadcasted_iota(jnp.int32, (rows, width), 1)
    total = None
    for slot in range(plan.shards):
        at = slot * groups * across
        place = jnp.where(column == entry + devs[slot] * rows, 1.0, 0.0).astype(BF16)
        term = mm(narrow[at : at + groups * across], place)
        total = term if total is None else total + term
    out_ref[...] = jnp.zeros_like(out_ref)
    out_ref[:8, :] = total[:8]
    out_ref[8 : 8 + QUART, :] = ups
    entry = lax.broadcasted_iota(jnp.int32, total.shape, 0)
    for item in range(plan.items):
        picked = jnp.where(entry == 12 + lead[item], total, 0.0)
        out_ref[12 + item : 13 + item, :] = jnp.sum(picked, 0, keepdims=True)


def unpack_kernel(grads_ref, up_ref, down_ref):
    _, rows, width = grads_ref.shape
    for part in range(QUART):
        up_ref[:, part * width : (part + 1) * width] = grads_ref[part].astype(F32)
        down_ref[part * rows : (part + 1) * rows, :] = grads_ref[QUART + part].astype(F32)


def add_kernel(work, *refs):
    outs, at = refs[len(refs) - len(work) :], 0
    for (low, high, first), out in zip(work, outs):
        mine, other = refs[at], refs[at + 1]
        at += 2
        cuts, came = [low, high], None
        if first is not None:
            came = refs[at]
            at += 1
            cuts = sorted({low, first, first + came.shape[0], high})
        for start, end in zip(cuts, cuts[1:]):
            value = mine[0, start:end, :].astype(F32) + other[0, start:end, :].astype(F32)
            if came is not None and first <= start < first + came.shape[0]:
                value = value + came[start - first : end - first, :].astype(F32)
            out[start - low : end - low, :] = value.astype(BF16)


def total_kernel(many, mine, other, ahead, behind, qkv, out, *refs):
    width = mine.shape[2]
    rows = out.shape[0]

    def rows_of(low, count):
        here = slice(low, low + count)
        value = mine[0, here, :].astype(F32) + other[0, here, :].astype(F32)
        return value + (ahead[here, :].astype(F32) + behind[here, :].astype(F32))

    for part in range(OUT):
        qkv[:, part * width : (part + 1) * width] = rows_of(part * rows, rows)
    out[...] = rows_of(OUT * rows, rows)
    vectors, (up_bias, table, small) = refs[:8], refs[8:]
    lines = rows_of(FIRST * rows, EXTRA)
    for index in range(many):
        line, place = divmod(index, width // rows)
        small[index : index + 1, :] = lines[line : line + 1, place * rows : (place + 1) * rows]
    for index, vector in enumerate(vectors):
        vector[...] = small[index : index + 1, :]
    for part in range(QUART):
        up_bias[:, part * rows : (part + 1) * rows] = small[8 + part : 9 + part, :]
    table[...] = small[12:many, :]


SMEM = pl.BlockSpec(memory_space=pltpu.SMEM)
VMEM = pl.BlockSpec(memory_space=pltpu.VMEM)
HBM = pl.BlockSpec(memory_space=pltpu.HBM)
ANY = pl.BlockSpec(memory_space=pl.ANY)


def kept_shapes(plan):
    tokens, width = plan.tokens, plan.width
    return [
        ((tokens, width), BF16),
        ((tokens, 3 * width), BF16),
        ((tokens, width), BF16),
        ((tokens, width), F32),
        ((tokens, width), BF16),
        ((plan.items * plan.pairs, 2 * plan.length, plan.length), F32),
        ((tokens, 4 * width), BF16),
        ((tokens, 4 * width), F32),
    ]


def held_blocks(plan, blocks):
    return pltpu.VMEM((blocks, plan.shards, plan.rows, plan.width), BF16)


def call(kernel, outs, in_specs, out_specs, scratch, name, work, limit, args):
    args = [
        pltpu.with_memory_space_constraint(arg, pltpu.HBM) if spec is HBM else arg
        for arg, spec in zip(args, in_specs)
    ]
    return pl.pallas_call(
        kernel,
        out_shape=outs,
        in_specs=in_specs,
        out_specs=out_specs,
        scratch_shapes=scratch,
        compiler_params=pltpu.CompilerParams(vmem_limit_bytes=limit * 1024 * 1024),
        cost_estimate=pl.CostEstimate(flops=2 * work[0], bytes_accessed=work[1], transcendentals=0),
        name=name,
    )(*args)


def of(shape):
    return jax.ShapeDtypeStruct(*shape)


def inside(shape):
    return pltpu.VMEM(*shape)


def run_attend(plan, lengths, flag, devs, x, vec, pieces):
    kept = kept_shapes(plan)
    block = plan.width * plan.width
    return call(
        functools.partial(attend_kernel, plan),
        [of(kept[3]), of(kept[4])],
        [SMEM, SMEM, SMEM, VMEM, VMEM] + [HBM] * len(pieces),
        [VMEM, VMEM],
        [held_blocks(plan, FIRST)] + [inside(shape) for shape in kept[:3]] + [pltpu.SemaphoreType.DMA((2,))],
        "attend",
        (FIRST * block * plan.tokens, FIRST * block * 2),
        14,
        (lengths, flag, devs, x, vec, *pieces),
    )


def run_vectors(plan, many, devs, lead, pieces):
    groups = pl.cdiv(many, plan.width // plan.rows) * (plan.width // plan.rows)
    return call(
        functools.partial(vectors_kernel, plan, many),
        jax.ShapeDtypeStruct((16, plan.width), F32),
        [SMEM, SMEM] + [HBM] * len(pieces),
        VMEM,
        [
            pltpu.VMEM((plan.shards, EXTRA, plan.width), BF16),
            pltpu.VMEM((plan.shards * groups, plan.width), BF16),
            pltpu.SemaphoreType.DMA((1,)),
        ],
        "vectors",
        (plan.width * plan.width * plan.rows, plan.width * plan.width * 4),
        12,
        (devs, lead, *pieces),
    )


def run_mlp(plan, flag, middle, hidden, vec, gathered):
    block = plan.width * plan.width
    return call(
        functools.partial(mlp_kernel, plan),
        jax.ShapeDtypeStruct(hidden.shape, BF16),
        [SMEM, VMEM, VMEM, VMEM, HBM],
        VMEM,
        [held_blocks(plan, SECOND), pltpu.SemaphoreType.DMA((QUART,)), pltpu.SemaphoreType.DMA((QUART,))],
        "mlp",
        (SECOND * block * plan.tokens, SECOND * block * 2),
        16,
        (flag, middle, hidden, vec, gathered),
    )


def run_load(plan, devs, flag, after, cot, firsts, gathered):
    block = plan.width * plan.width
    return call(
        functools.partial(load_kernel, plan),
        [held_blocks(plan, FIRST), held_blocks(plan, SECOND), inside(kept_shapes(plan)[7])]
        + [pltpu.VMEM((FIRST + QUART, plan.width, plan.width), BF16)],
        [SMEM, SMEM, ANY, VMEM] + [HBM] * (1 + len(firsts)),
        [VMEM] * 4,
        [pltpu.SemaphoreType.DMA((2,)), pltpu.SemaphoreType.DMA((QUART,))],
        "load",
        (QUART * block * plan.tokens, (FIRST + SECOND) * block * 4),
        4,
        (devs, flag, after, cot, gathered, *firsts),
    )


def run_chain(plan, lengths, flag, x, recv, cot, vec, held1, held2, grad_act, turned):
    shapes = kept_shapes(plan)
    block = plan.width * plan.width
    rest = [shapes[index] for index in (0, 0, 1, 2, 3, 5)]
    some = ((plan.items // 2 * plan.length, plan.width), BF16)
    results = call(
        functools.partial(chain_kernel, plan),
        [of(some)]
        + [inside(shapes[index]) for index in (4, 6, 7, 0, 1, 5, 3, 0, 3)]
        + [pltpu.HBM(*shape) for shape in rest],
        [SMEM] * 2 + [VMEM] * 8,
        [VMEM] * 10 + [HBM] * len(rest),
        [inside(shapes[index]) for index in (0, 2, 1)]
        + [pltpu.SemaphoreType.DMA((len(rest),))],
        "chain",
        (20 * block * plan.tokens, 12 * block),
        12,
        (lengths, flag, x, recv, cot, vec, held1, held2, grad_act, turned),
    )
    return results[0], results[1:4], results[4:9], results[9], results[10:]


def run_output(plan, flag, act, middle, vec, held2):
    block = plan.width * plan.width
    return call(
        functools.partial(output_kernel, plan),
        of(kept_shapes(plan)[0]),
        [SMEM] + [VMEM] * 4,
        VMEM,
        [],
        "output",
        (QUART * block * plan.tokens, QUART * block),
        4,
        (flag, act, middle, vec, held2),
    )


def run_chain_end(plan, flag, vec, turned, end):
    shapes = kept_shapes(plan)
    block = plan.width * plan.width
    left = plan.items - plan.items // 2
    return call(
        functools.partial(chain_end_kernel, plan),
        of(((left * plan.length, plan.width), BF16)),
        [SMEM] + [VMEM] * 7,
        VMEM,
        [inside(shapes[1])],
        "chain_end",
        (2 * block * plan.tokens, 3 * block),
        6,
        (flag, vec, turned, *end),
    )


def grad_shapes(plan):
    if plan.parts == 1:
        return [pltpu.HBM((1, FIRST * plan.rows, plan.width), BF16)]
    rows = FIRST * plan.rows + EXTRA
    return [
        pltpu.HBM((count, rows, plan.width), BF16)
        for count in (plan.shards // 2, plan.shards // 2, 1)
    ]


def stage_scratch(plan, slots):
    return [
        pltpu.VMEM((slots, plan.shards, plan.rows, plan.width), BF16),
        pltpu.SemaphoreType.DMA((slots,)),
    ]


def run_mlp_back(plan, flag, beside, arriving, cot, held2, hidden, act, slope):
    shapes = kept_shapes(plan)
    block = plan.width * plan.width
    return call(
        functools.partial(mlp_back_kernel, plan),
        [
            inside(shapes[6]),
            jax.ShapeDtypeStruct((16, plan.width), F32),
            pltpu.HBM((plan.shards, SECOND, plan.rows, plan.width), BF16),
        ],
        [SMEM, HBM] + [VMEM] * 7,
        [VMEM, VMEM, HBM],
        stage_scratch(plan, SECOND),
        "mlp_back",
        (2 * SECOND * block * plan.tokens, SECOND * block * 2),
        16,
        (flag, beside, *arriving, cot, held2, hidden, act, slope),
    )


def run_rest(plan, many, flag, devs, lead, arriving, cot, small, vec, gathered, grad_pre, kept, pieces):
    shapes = kept_shapes(plan)
    block = plan.width * plan.width
    across = plan.width // plan.rows
    high = pl.cdiv(many, across) * across
    lines = (plan.shards, EXTRA, plan.width)
    rest = [shapes[index] for index in (0, 0, 1, 2, 3, 5)]
    input_grad, small, *grads = call(
        functools.partial(rest_kernel, plan, many),
        [of(shapes[3]), jax.ShapeDtypeStruct((16, plan.width), F32)] + grad_shapes(plan),
        [SMEM] * 3 + [VMEM] * 6 + [HBM] * (1 + len(rest) + len(pieces)),
        [VMEM] * 2 + [HBM] * plan.parts,
        [inside(shape) for shape in rest]
        + [held_blocks(plan, QUART), pltpu.SemaphoreType.DMA((QUART,))]
        + [held_blocks(plan, FIRST)]
        + [inside(shapes[index]) for index in (3, 0, 1)]
        + [pltpu.SemaphoreType.DMA((2,)), pltpu.SemaphoreType.DMA((len(rest),))]
        + stage_scratch(plan, FIRST)
        + [pltpu.SemaphoreType.DMA((1,)), pltpu.VMEM((plan.shards * high, plan.rows), BF16)]
        + [pltpu.VMEM(lines, F32), pltpu.VMEM(lines, BF16)],
        "rest",
        (3 * FIRST * block * plan.tokens, 3 * FIRST * block * 2),
        34,
        (flag, devs, lead, *arriving, cot, small, vec, grad_pre, gathered, *kept, *pieces),
    )
    return input_grad, small, grads


def run_add(mine, other, work):
    _, rows, width = mine.shape
    mine = pltpu.with_memory_space_constraint(mine, pltpu.HBM)
    specs, args, plans, outs = [], [], [], []
    for way, (slot, low, high, came) in enumerate(work):
        there = slot if other.shape[0] > 1 else 0
        specs += [
            pl.BlockSpec((1, rows, width), lambda index, slot=slot: (slot, 0, 0))
            for slot in (slot, there)
        ]
        args += [mine, other]
        first = None
        if came is not None:
            specs.append(pl.BlockSpec(came.shape, lambda index: (0, 0)))
            args.append(came)
            first = rows - came.shape[0] if way else 0
        plans.append((low, high, first))
        outs.append((high - low, width))
    return pl.pallas_call(
        functools.partial(add_kernel, plans),
        out_shape=[jax.ShapeDtypeStruct(shape, BF16) for shape in outs],
        grid=(1,),
        in_specs=specs,
        out_specs=[pl.BlockSpec(shape, lambda index: (0, 0)) for shape in outs],
        compiler_params=pltpu.CompilerParams(vmem_limit_bytes=14 * 1024 * 1024),
        name="add",
    )(*args)


def run_total(one, many, shapes):
    args = [pltpu.with_memory_space_constraint(one.mine, pltpu.HBM), one.other]
    _, rows, width = one.mine.shape
    first = pl.BlockSpec((1, rows, width), lambda index: (0, 0, 0))
    whole = pl.BlockSpec((rows, width), lambda index: (0, 0))
    return pl.pallas_call(
        functools.partial(total_kernel, many),
        out_shape=[jax.ShapeDtypeStruct(shape, F32) for shape in shapes],
        grid=(1,),
        in_specs=[first, first, whole, whole],
        out_specs=[pl.BlockSpec(shape, lambda index: (0, 0)) for shape in shapes],
        scratch_shapes=[pltpu.VMEM((many, shapes[2][1]), F32)],
        compiler_params=pltpu.CompilerParams(vmem_limit_bytes=14 * 1024 * 1024),
        name="total",
    )(*args, *one.carried)


def after(value, *others):
    return lax.optimization_barrier((value, *others))[0]


def shifted(value, axis, steps):
    count = lax.axis_size(axis)
    first, last = (max(0, -steps), min(count, count - steps))
    return lax.ppermute(value, axis, [(source, source + steps) for source in range(first, last)])


class Ring:
    def __init__(self, count):
        self.count, self.chips = count, count // 2
        self.walk = list(range(0, self.chips, 2)) + list(range(self.chips - 1, 0, -2))
        self.order = [2 * chip + core for chip in self.walk for core in range(2)]
        after = self.walk[1:] + self.walk[:1]
        self.onward = [
            (2 * here + core, 2 * there + core)
            for here, there in zip(self.walk, after)
            for core in range(2)
        ]
        self.back = [(there, here) for here, there in self.onward]
        self.sibling = [(index, index ^ 1) for index in range(count)]

    def slots(self):
        index = lax.axis_index("dp")
        chip, core = index // 2, index % 2
        place_of = lambda chip: jnp.where(chip % 2 == 0, chip // 2, self.chips - 1 - chip // 2)
        steps = jnp.arange(self.chips, dtype=jnp.int32)
        ahead = (place_of(chip) + steps) % self.chips
        chips = jnp.where(ahead < (self.chips + 1) // 2, 2 * ahead, 2 * (self.chips - 1 - ahead) + 1)
        devs = jnp.concatenate([2 * chips + core, 2 * chips + 1 - core]).astype(jnp.int32)
        return devs

    def step(self, ahead, behind):
        return lax.ppermute(ahead, "dp", self.onward), lax.ppermute(behind, "dp", self.back)

    def gather(self, shard, low):
        half = self.chips // 2
        own = [[shard]] + [None] * (self.chips - 1)
        ahead = behind = shard
        for step in range(1, half):
            ahead, behind = self.step(ahead, behind)
            own[self.chips - step], own[step] = [ahead], [behind]
            ahead, behind = lax.optimization_barrier((ahead, behind))
        own[half] = list(self.step(ahead[:low], behind[low:]))
        return [piece for pieces in own for piece in pieces]

    def siblings(self, pieces):
        return [lax.ppermute(piece, "dp", self.sibling) for piece in pieces]


class RingSum:
    def __init__(self, ring, mine, other, opposite, low):
        self.ring, self.mine, self.low = ring, mine, low
        self.other, self.opposite = other, opposite
        self.time = ring.chips // 2
        self.carried = [None, None]

    def add(self):
        rows = self.mine.shape[1]
        other = self.other
        if self.carried[0] is None:
            other = self.opposite
            work = [(self.time, 0, self.low, None), (self.time, self.low, rows, None)]
        else:
            work = [
                (self.time, 0, rows, self.carried[0]),
                (self.ring.chips - self.time, 0, rows, self.carried[1]),
            ]
        self.carried = run_add(self.mine, other, work)

    def send(self):
        self.carried = self.ring.step(*self.carried)
        self.time -= 1


def body(
    block_input, cotangent, lengths, leads,
    norm_gain1, norm_bias1, lead_table, qkv_weight, query_bias, value_bias, out_weight, out_bias,
    norm_gain2, norm_bias2, up_weight, up_bias, down_weight, down_bias,
):
    count = lax.axis_size("dp")
    micro, local, length, width = block_input.shape
    items = micro * local
    rows = width // count
    leads_count = lead_table.shape[2]
    flag = lax.axis_index("section").astype(jnp.int32).reshape(1)
    flat = lambda value: value.reshape(items * length, width)
    x, cot = flat(block_input), flat(cotangent)
    lens, lead = lengths.reshape(items), leads.reshape(items)

    vectors = (
        norm_gain1, norm_bias1, query_bias, value_bias, out_bias, norm_gain2, norm_bias2, down_bias
    )
    many = 12 + leads_count
    aligned = rows % 16 == 0 and count % 4 == 0 and pl.cdiv(many, width // rows) <= EXTRA
    if aligned:
        ring = Ring(count)
        first, second = pl.pallas_call(
            pack_kernel,
            out_shape=[
                jax.ShapeDtypeStruct((FIRST * rows + EXTRA, width), BF16),
                jax.ShapeDtypeStruct((SECOND, rows, width), BF16),
            ],
            scratch_shapes=[pltpu.VMEM((many, rows), F32), pltpu.VMEM((EXTRA, width), F32)],
            name="pack",
        )(qkv_weight[0], out_weight[0], up_weight[0], down_weight[0], *vectors, up_bias, lead_table[0].T)
        gathered = lax.all_gather(second, "dp", axis=0, tiled=True, axis_index_groups=[ring.order])
        gathered = gathered.reshape(count, SECOND, rows, width)
        firsts = ring.gather(first, LOW * rows)
        firsts = firsts + ring.siblings(firsts)
        devs = ring.slots()
        plan = Plan(ring.order, rows, items, length, width)
        vec = run_vectors(plan, many, devs, lead, firsts)
    else:
        wide_blocks = lambda value: value[0].reshape(rows, -1, width).transpose(1, 0, 2)
        packed = jnp.concatenate(
            [wide_blocks(qkv_weight), out_weight, wide_blocks(up_weight), down_weight.reshape(QUART, rows, width)], 0
        )
        everything = lax.all_gather(packed.astype(BF16), "dp", axis=0)
        across_blocks = lambda value: value.transpose(1, 0, 2, 3).reshape(-1, width, width)
        firsts = [across_blocks(everything[:, :FIRST])]
        gathered = jnp.concatenate(
            [
                across_blocks(everything[:, FIRST : FIRST + QUART]),
                everything[:, FIRST + QUART :].reshape(QUART, width, width),
            ],
            0,
        )[None]
        devs = jnp.zeros((1,), jnp.int32)
        plan = Plan([0], width, items, length, width)
        small = jnp.concatenate([*vectors, up_bias.reshape(4, rows), lead_table[0].T], 0).astype(BF16)
        wide = lax.all_gather(small, "dp", axis=1, tiled=True).astype(F32)
        vec = jnp.concatenate(
            [wide[:8], wide[8:12].reshape(4, count, rows).transpose(1, 0, 2).reshape(4, width)]
            + [lax.dynamic_slice_in_dim(wide, 12 + lead[item], 1, 0) for item in range(items)]
            + [jnp.zeros((4 - items, width), F32)],
            0,
        )

    middle, hidden = run_attend(plan, lens, flag, devs, x, vec, firsts)
    first_out = run_mlp(plan, flag, middle, hidden, vec, gathered)
    recv = shifted(first_out, "section", 1)
    held1, held2, grad_act, turned = run_load(plan, devs, flag, first_out, cot, firsts, gathered)
    some_grad, (hidden, act, slope), end, middle, kept = run_chain(
        plan, lens, flag, x, recv, cot, vec, held1, held2, grad_act, turned
    )
    other_grad = run_chain_end(plan, flag, vec, turned, end)
    arriving = [shifted(grad, "section", -1) for grad in (some_grad, other_grad)]
    output = run_output(plan, flag, act, middle, vec, held2)
    grad_pre, sums, grads2 = run_mlp_back(
        plan, flag, output, arriving, cot, held2, hidden, act, slope
    )
    input_grad, sums, grads1 = run_rest(
        plan, many, flag, devs, lead, arriving, cot, sums, vec, gathered, grad_pre, kept, firsts
    )
    if aligned:
        (opposite,) = ring.siblings(grads1[2:])
        (other,) = ring.siblings([after(grads1[1], opposite)])
        first_sum = RingSum(ring, grads1[0], other, opposite, LOW * rows)
        while first_sum.time:
            first_sum.add()
            first_sum.send()
        grads2 = lax.psum_scatter(
            grads2.reshape(count * SECOND, rows, width),
            "dp", scatter_dimension=0, tiled=True, axis_index_groups=[ring.order],
        )
        grad_up, grad_down = pl.pallas_call(
            unpack_kernel,
            out_shape=[
                jax.ShapeDtypeStruct((rows, QUART * width), F32),
                jax.ShapeDtypeStruct((QUART * rows, width), F32),
            ],
            name="unpack",
        )(grads2)
        grad_qkv, grad_out, *small_grads = run_total(
            first_sum, many,
            [(rows, OUT * width), (rows, width)] + [(1, rows)] * 8 + [(1, QUART * rows), (leads_count, rows)],
        )
    else:
        split = lambda value: value[0].reshape(-1, count, rows, width).transpose(1, 0, 2, 3)
        grads = jnp.concatenate(
            [
                split(grads1[0]),
                split(grads2[0, :QUART].reshape(1, QUART * width, width)),
                grads2[0, QUART:].reshape(count, QUART, rows, width),
            ],
            1,
        )
        grads = lax.psum_scatter(grads, "dp", scatter_dimension=0, tiled=False).astype(F32)
        across = lambda value: value.transpose(1, 0, 2).reshape(rows, -1)
        grad_qkv, grad_out = across(grads[:OUT]), grads[OUT]
        grad_up = across(grads[FIRST : FIRST + QUART])
        grad_down = grads[FIRST + QUART :].reshape(QUART * rows, width)
        hot = (jnp.arange(leads_count)[:, None] == lead[None, :]).astype(F32)
        table = sum(hot[:, item : item + 1] * sums[12 + item : 13 + item] for item in range(items))
        up_sums = sums[8:12].reshape(count, 4, rows).transpose(1, 0, 2).reshape(4, width)
        spread = lax.psum_scatter(
            jnp.concatenate([sums[:8], up_sums, table], 0), "dp", scatter_dimension=1, tiled=True
        )
        small_grads = [spread[index : index + 1] for index in range(8)]
        small_grads += [spread[8:12].reshape(1, 4 * rows), spread[12:]]
    vector = small_grads
    shape = (1, micro, local, length, width)
    return (
        output.reshape(shape),
        input_grad.reshape(shape),
        vector[0],
        vector[1],
        vector[9].T[None],
        grad_qkv[None],
        vector[2],
        vector[3],
        grad_out[None],
        vector[4],
        vector[5],
        vector[6],
        grad_up[None],
        vector[8],
        grad_down[None],
        vector[7],
    )


def solution(mesh):
    weights = (
        P("section", "dp"),
        P("section", "dp"),
        P("section", "dp", None),
        P("section", "dp", None),
        P("section", "dp"),
        P("section", "dp"),
        P("section", "dp", None),
        P("section", "dp"),
        P("section", "dp"),
        P("section", "dp"),
        P("section", "dp", None),
        P("section", "dp"),
        P("section", "dp", None),
        P("section", "dp"),
    )
    rows = P(None, "dp", None, None)
    layers = P("section", None, "dp", None, None)
    return jax.shard_map(
        body,
        mesh=mesh,
        in_specs=(rows, rows, P(None, "dp"), P(None, "dp")) + weights,
        out_specs=(layers, layers) + weights,
        check_vma=False,
    )
```
